32 devices in a mesh: dp: 2 (over x), fsdp: 16 (over z, y, core).
Axes of the slice: x: 2, y: 2, z: 4, core: 2. Of those that a mesh axis runs over, the one named last changes fastest.
Arguments:
- inputs: bfloat16 [16384, 1024], P(('dp', 'fsdp')), may hold values from -6 to 6
- doc_lengths: int32 [32, 4], P(('dp', 'fsdp')), may hold values from 1 to 256, 512 in all within a row
- w_aq: bfloat16 [1024, 96], P(('dp', 'fsdp')), may hold values from -0.3125 to 0.3125
- w_bq: bfloat16 [1024, 384], P(('dp', 'fsdp')), may hold values from -0.3125 to 0.3125
- w_ak: bfloat16 [1024, 32], P(('dp', 'fsdp')), may hold values from -0.3125 to 0.3125
- w_bk: bfloat16 [1024, 128], P(('dp', 'fsdp')), may hold values from -0.3125 to 0.3125
- w_av: bfloat16 [1024, 32], P(('dp', 'fsdp')), may hold values from -0.1875 to 0.1875
- w_bv: bfloat16 [1024, 128], P(('dp', 'fsdp')), may hold values from -0.1875 to 0.1875
- w_out: bfloat16 [1024, 1024], P(('dp', 'fsdp')), may hold values from -1.5 to 1.5
- w_gate: bfloat16 [1024, 2816], P(('dp', 'fsdp')), may hold values from -0.1875 to 0.1875
- w_up: bfloat16 [1024, 2816], P(('dp', 'fsdp')), may hold values from -0.1875 to 0.1875
- w_down: bfloat16 [2816, 1024], P(('dp', 'fsdp')), may hold values from -0.109375 to 0.109375
- gain_attn: bfloat16 [1024], P(('dp', 'fsdp')), may hold values from 0.5 to 1.5
- gain_ffn: bfloat16 [1024], P(('dp', 'fsdp')), may hold values from 0.5 to 1.5
- cotangent: bfloat16 [16384, 1024], P(('dp', 'fsdp')), may hold values from -6 to 6
Outputs:
- outputs: bfloat16 [16384, 1024], P(('dp', 'fsdp'))
- input_grad: float32 [16384, 1024], P(('dp', 'fsdp'))
- grad_aq: float32 [1024, 96], P(('dp', 'fsdp'))
- grad_bq: float32 [1024, 384], P(('dp', 'fsdp'))
- grad_ak: float32 [1024, 32], P(('dp', 'fsdp'))
- grad_bk: float32 [1024, 128], P(('dp', 'fsdp'))
- grad_av: float32 [1024, 32], P(('dp', 'fsdp'))
- grad_bv: float32 [1024, 128], P(('dp', 'fsdp'))
- grad_out: float32 [1024, 1024], P(('dp', 'fsdp'))
- grad_gate: float32 [1024, 2816], P(('dp', 'fsdp'))
- grad_up: float32 [1024, 2816], P(('dp', 'fsdp'))
- grad_down: float32 [2816, 1024], P(('dp', 'fsdp'))
- grad_gain_attn: float32 [1024], P(('dp', 'fsdp'))
- grad_gain_ffn: float32 [1024], P(('dp', 'fsdp'))
The draws below stay inside these ranges and needn't reach their ends.
Inputs may be any that keep to these rules, and one draw needn't show every extreme that they name: `doc_lengths`: each row's 4 document lengths sum to 512.
All inputs are finite; a program needn't handle non-finite values.
Results may differ from the reference program's by a relative error of at most 0.013.
The reference program's roundings to bfloat16 on the way count: a program that leaves them out, or rounds other values in their place, can miss the bound.
Values may be sent and summed in bfloat16 or wider, within the bound.
A program may use at most 256 MiB of HBM per device.

```python
import math
from functools import partial
import jax
import jax.numpy as jnp
import numpy as np
from jax import lax

D = 1024
HEADS = 16
HEAD_DIM = 64
RANK_Q = 6
RANK_KV = 2
FF = 2816
TOK_DEV = 512
DOCS = 4
ROWS = 32
TOKENS = 16384


def levels(key, dims, cuts, smallest, high):
    factor_of, own = 1.0, jax.random.fold_in(key, 6)
    for axis_at, parts in cuts:
        heights = jnp.exp(jax.random.uniform(jax.random.fold_in(own, axis_at), (parts,), jnp.float32, smallest / len(cuts), high / len(cuts)))
        factor_of = factor_of * jnp.repeat(heights, dims[axis_at] // parts).reshape([-1 if axis == axis_at else 1 for axis in range(len(dims))])
    return factor_of


def split_up(amount, total, bound, skew):
    portions = [(1 << 20) // math.isqrt(rank ** skew) + 1 for rank in range(2, amount + 1)]
    rest, holding = total - bound - (amount - 1), [1] * (amount - 1)
    while rest > 0:
        free = [i for i in range(amount - 1) if holding[i] < bound]
        pool, left = sum([portions[i] for i in free]), rest
        for i in free:
            addition = min(bound - holding[i], max(1, left * portions[i] // pool), rest)
            holding[i] = holding[i] + addition
            rest = rest - addition
    return np.array([bound] + holding)


def ragged_sizes(key, amount, total, limit, skew):
    if amount == 2:
        one = jax.random.randint(key, (), max(1, total - limit), min(limit, total - 1) + 1)
        return jnp.stack([one, total - one])
    sizes = jnp.asarray(split_up(amount, total, limit, skew), jnp.int32)
    twos = (amount - 1) // 2
    donor, sink = sizes[1:1 + 2 * twos:2], sizes[2:2 + 2 * twos:2]
    room = jnp.minimum(donor - 1, limit - sink)
    passed = jax.random.randint(jax.random.fold_in(key, 1), (twos,), 0, 1 << 20) % (room + 1)
    sizes = sizes.at[1:1 + 2 * twos:2].set(donor - passed).at[2:2 + 2 * twos:2].set(sink + passed)
    return sizes[jax.random.permutation(jax.random.fold_in(key, 2), amount)]


def scatter_about(rng, extent, width, most, shards=(), kind=jnp.bfloat16):
    entries = width * jax.random.normal(rng, extent, jnp.float32)
    if shards:
        entries = entries * levels(rng, extent, shards, -0.22, 0.18)
    return jnp.clip(entries, -most, most).astype(kind)


def setup_inputs(seed: int = 0) -> dict:
    seeds = jax.random.split(jax.random.key(seed), 16)
    return {
        "inputs": scatter_about(seeds[0], (TOKENS, D), 1.0, 6.0, ((0, 32),)),
        "doc_lengths": jax.vmap(lambda own: ragged_sizes(own, DOCS, TOK_DEV, TOK_DEV // 2, 1))(jax.random.split(seeds[1], ROWS)).reshape((ROWS, DOCS)).astype(jnp.int32),
        "w_aq": scatter_about(seeds[2], (D, RANK_Q * HEADS), (D // 3) ** -0.5, 0.3125, ((0, 32),)),
        "w_bq": scatter_about(seeds[3], (D, RANK_Q * HEAD_DIM), (D // 3) ** -0.5, 0.3125, ((0, 32),)),
        "w_ak": scatter_about(seeds[4], (D, RANK_KV * HEADS), (D // 3) ** -0.5, 0.3125, ((0, 32),)),
        "w_bk": scatter_about(seeds[5], (D, RANK_KV * HEAD_DIM), (D // 3) ** -0.5, 0.3125, ((0, 32),)),
        "w_av": scatter_about(seeds[6], (D, RANK_KV * HEADS), D ** -0.5, 0.1875, ((0, 32),)),
        "w_bv": scatter_about(seeds[7], (D, RANK_KV * HEAD_DIM), D ** -0.5, 0.1875, ((0, 32),)),
        "w_out": scatter_about(seeds[8], (HEADS * HEAD_DIM, D), (max(1, HEADS * HEAD_DIM * 2 * DOCS // TOK_DEV)) ** -0.5, 1.5, ((0, 32),)),
        "w_gate": scatter_about(seeds[9], (D, FF), D ** -0.5, 0.1875, ((0, 32),)),
        "w_up": scatter_about(seeds[10], (D, FF), D ** -0.5, 0.1875, ((0, 32),)),
        "w_down": scatter_about(seeds[11], (FF, D), FF ** -0.5, 0.109375, ((0, 32),)),
        "gain_attn": jnp.clip(1.0 + 0.1 * jax.random.normal(seeds[12], (D,), jnp.float32), 0.5, 1.5).astype(jnp.bfloat16),
        "gain_ffn": jnp.clip(1.0 + 0.1 * jax.random.normal(seeds[13], (D,), jnp.float32), 0.5, 1.5).astype(jnp.bfloat16),
        "cotangent": scatter_about(seeds[14], (TOKENS, D), 1.0, 6.0, ((0, 32),)),
    }


EPSILON = 1e-06
PRECISE = lax.Precision.HIGHEST

@jax.custom_vjp
def low(v):
    return lax.optimization_barrier(v.astype(jnp.bfloat16)).astype(jnp.float32)

@jax.custom_vjp
def low_back(v):
    return v

def low_keep(v):
    return (low(v), None)

def low_pass(kept, grad):
    return (grad,)

def back_keep(v):
    return (v, None)

def back_low(kept, grad):
    return (low(grad),)
low.defvjp(low_keep, low_pass)
low_back.defvjp(back_keep, back_low)

def high_dot(left, right):
    return jnp.dot(left, right, precision=PRECISE, preferred_element_type=jnp.float32)

def doc_layout(lengths, length):
    doc_ends = jnp.cumsum(lengths).astype(jnp.int32)
    doc_starts = doc_ends - lengths
    places = jnp.arange(length, dtype=jnp.int32)
    segment = lax.optimization_barrier(jnp.sum((places[:, None] >= doc_ends[None, :]).astype(jnp.int32), axis=1))
    owner = segment[:, None] == jnp.arange(lengths.shape[0], dtype=jnp.int32)[None, :]
    doc_first = lax.optimization_barrier(jnp.sum(jnp.where(owner, doc_starts[None, :], 0), axis=1))
    return (segment, (places - doc_first).astype(jnp.float32))

def rotation(places):
    halfway = HEAD_DIM // 2
    freqs = jnp.exp(-math.log(10000.0) * jnp.arange(halfway, dtype=jnp.float32) / halfway)
    angles = places[..., None] * freqs
    return (jnp.cos(angles), jnp.sin(angles))

def rotate(factor, cos_table, sin_table):
    halfway = factor.shape[-1] // 2
    front_part = factor[..., :halfway]
    back_part = factor[..., halfway:]
    cos_part = cos_table[..., None, :]
    sin_part = sin_table[..., None, :]
    return jnp.concatenate([front_part * cos_part - back_part * sin_part, front_part * sin_part + back_part * cos_part], axis=-1)

def rms(values, gain):
    return values * lax.rsqrt(lax.optimization_barrier(jnp.mean(values * values, axis=-1, keepdims=True)) + EPSILON) * gain

def attend_row(row_item):
    queries, keys_low, values, segment = row_item
    length = queries.shape[0]
    places = jnp.arange(length, dtype=jnp.int32)
    scaling = HEAD_DIM ** (-0.5)
    scores = low_back(jnp.einsum('thd,shd->hts', queries, keys_low, precision=PRECISE) * scaling)
    allowed = (segment[:, None] == segment[None, :]) & (places[None, :] <= places[:, None])
    scores = jnp.where(allowed[None], scores, -1e+30)
    attn_probs = low(jax.nn.softmax(scores, axis=-1))
    return jnp.einsum('hts,shd->thd', attn_probs, values, precision=PRECISE)

def forward(inputs, segment, places, params):
    w_aq, w_bq, w_ak, w_bk, w_av, w_bv, w_out, w_gate, w_up, w_down, gain_attn, gain_ffn = params
    groups = inputs.shape[0]
    length = inputs.shape[1]
    flat = inputs.reshape(groups * length, D)
    normed_one = low(rms(flat, gain_attn))
    a_q = low_back(high_dot(normed_one, w_aq)).reshape(groups, length, RANK_Q, HEADS)
    b_q = low_back(high_dot(normed_one, w_bq)).reshape(groups, length, RANK_Q, HEAD_DIM)
    a_k = low_back(high_dot(normed_one, w_ak)).reshape(groups, length, RANK_KV, HEADS)
    b_k = low_back(high_dot(normed_one, w_bk)).reshape(groups, length, RANK_KV, HEAD_DIM)
    a_v = low_back(high_dot(normed_one, w_av)).reshape(groups, length, RANK_KV, HEADS)
    b_v = low_back(high_dot(normed_one, w_bv)).reshape(groups, length, RANK_KV, HEAD_DIM)
    cos_table, sin_table = rotation(places)
    bq_rot = rotate(b_q, cos_table, sin_table)
    bk_rot = rotate(b_k, cos_table, sin_table)
    queries = low(jnp.einsum('gtrh,gtrd->gthd', a_q, bq_rot, precision=PRECISE) / RANK_Q)
    keys_low = low(jnp.einsum('gtrh,gtrd->gthd', a_k, bk_rot, precision=PRECISE) / RANK_KV)
    values = low(jnp.einsum('gtrh,gtrd->gthd', a_v, b_v, precision=PRECISE) / RANK_KV)
    attended = lax.map(jax.checkpoint(attend_row), (queries, keys_low, values, segment))
    mixed = low(low_back(attended)).reshape(groups * length, HEADS * HEAD_DIM)
    resid = flat + low_back(high_dot(mixed, w_out))
    normed_two = low(rms(resid, gain_ffn))
    gate_act = low_back(high_dot(normed_two, w_gate))
    up_act = low_back(high_dot(normed_two, w_up))
    hidden = low(jax.nn.silu(gate_act) * up_act)
    result = resid + low_back(high_dot(hidden, w_down))
    return result.reshape(groups, length, D)

def reference(inputs, doc_lengths, w_aq, w_bq, w_ak, w_bk, w_av, w_bv, w_out, w_gate, w_up, w_down, gain_attn, gain_ffn, cotangent):
    params = tuple((weight.astype(jnp.float32) for weight in (w_aq, w_bq, w_ak, w_bk, w_av, w_bv, w_out, w_gate, w_up, w_down, gain_attn, gain_ffn)))
    rows_all = doc_lengths.shape[0]
    batch = math.gcd(rows_all, max(1, 4096 // TOK_DEV))
    count = rows_all // batch
    segment, places = jax.vmap(partial(doc_layout, length=TOK_DEV))(doc_lengths)
    blocks_in = inputs.reshape(count, batch, TOK_DEV, D)
    blocks_cot = cotangent.reshape(count, batch, TOK_DEV, D)
    blocks_seg = segment.reshape(count, batch, TOK_DEV)
    blocks_pos = places.reshape(count, batch, TOK_DEV)

    def advance(totals, block_item):
        block_in, block_seg, block_pos, block_cot = block_item

        def apply(values_in, weights):
            return forward(values_in, block_seg, block_pos, weights)
        result, pullback = jax.vjp(apply, block_in.astype(jnp.float32), params)
        grad_in, grad_params = pullback(block_cot.astype(jnp.float32))
        totals = jax.tree.map(jnp.add, totals, grad_params)
        return (totals, (result.astype(jnp.bfloat16), grad_in))
    zeros_init = tuple((jnp.zeros_like(weight) for weight in params))
    totals, (outputs, grads_in) = lax.scan(advance, zeros_init, (blocks_in, blocks_seg, blocks_pos, blocks_cot))
    return (outputs.reshape(TOKENS, D), grads_in.reshape(TOKENS, D), totals[0], totals[1], totals[2], totals[3], totals[4], totals[5], totals[6], totals[7], totals[8], totals[9], totals[10], totals[11])
```

```python
import math

import jax
import jax.numpy as jnp
from jax import lax
from jax.experimental import pallas as pl
from jax.experimental.pallas import tpu as pltpu
from jax.sharding import PartitionSpec as P

HEADS = 16
HEAD_DIM = 64
RANK_Q = 6
RANK_KV = 2
FF = 2816


EPSILON = 1e-06
PRECISE = lax.Precision.HIGHEST


def factor_columns():
    return [
        RANK_Q * HEADS,
        RANK_Q * HEAD_DIM,
        RANK_KV * HEADS,
        RANK_KV * HEAD_DIM,
        RANK_KV * HEADS,
        RANK_KV * HEAD_DIM,
    ]


def split_columns(matrix):
    pieces = []
    offset = 0
    for columns in factor_columns():
        pieces.append(matrix[:, offset : offset + columns])
        offset += columns
    return pieces


def doc_layout(lengths, length):
    order = jnp.arange(lengths.shape[0], dtype=jnp.int32)
    doc_ends = jnp.sum(jnp.where(order[:, None] >= order[None, :], lengths[None, :], 0), axis=1)
    doc_starts = doc_ends - lengths
    places = jnp.arange(length, dtype=jnp.int32)
    segment = jnp.sum((places[:, None] >= doc_ends[None, :]).astype(jnp.int32), axis=1)
    owner = segment[:, None] == jnp.arange(lengths.shape[0], dtype=jnp.int32)[None, :]
    doc_first = jnp.sum(jnp.where(owner, doc_starts[None, :], 0), axis=1)
    return (segment, (places - doc_first).astype(jnp.float32))


def rotation(places):
    halfway = HEAD_DIM // 2
    freqs = jnp.exp(-math.log(10000.0) * jnp.arange(halfway, dtype=jnp.float32) / halfway)
    angles = places[..., None] * freqs
    return (jnp.cos(angles), jnp.sin(angles))


def rotate(factor, cos_table, sin_table):
    halfway = factor.shape[-1] // 2
    front_part = factor[..., :halfway]
    back_part = factor[..., halfway:]
    cos_part = cos_table[..., None, :]
    sin_part = sin_table[..., None, :]
    return jnp.concatenate(
        [
            front_part * cos_part - back_part * sin_part,
            front_part * sin_part + back_part * cos_part,
        ],
        axis=-1,
    )


def normalize(values, gain):
    scaling = lax.rsqrt(jnp.mean(values * values, axis=-1, keepdims=True) + EPSILON)
    unit_vals = values * scaling
    return (unit_vals * gain, unit_vals, scaling)


def norm_back(incoming, unit_vals, scaling, gain):
    unit_grad = incoming * gain
    grad_in = scaling * (
        unit_grad - unit_vals * jnp.mean(unit_grad * unit_vals, axis=-1, keepdims=True)
    )
    return (grad_in, jnp.sum(incoming * unit_vals, axis=0))


def block_scores(query_part, keys_low, seg_part, segment, place_part, places):
    scaling = HEAD_DIM ** (-0.5)
    scores = (
        jnp.einsum("thd,shd->hts", query_part, keys_low, preferred_element_type=jnp.float32)
        * scaling
    )
    allowed = (seg_part[:, None] == segment[None, :]) & (places[None, :] <= place_part[:, None])
    return jnp.where(allowed[None], scores, -1e30)


def attend_forward(queries, keys_low, values, segment):
    length = queries.shape[0]
    block_rows = min(512, length)
    places = jnp.arange(length, dtype=jnp.int32)

    def one_block(block_index):
        masked = block_scores(queries, keys_low, segment, segment, places, places)
        row_peak = jnp.max(masked, axis=-1, keepdims=True)
        exp_terms = jnp.exp(masked - row_peak)
        row_total = jnp.sum(exp_terms, axis=-1, keepdims=True)
        attn_probs = (exp_terms / row_total).astype(jnp.bfloat16)
        attended = jnp.einsum(
            "hts,shd->thd", attn_probs, values, preferred_element_type=jnp.float32
        )
        return (attended, (row_peak + jnp.log(row_total))[..., 0])

    attended, log_totals = lax.map(one_block, jnp.arange(length // block_rows, dtype=jnp.int32))
    return (attended.reshape(length, HEADS, HEAD_DIM), log_totals)


def attend_backward(queries, keys_low, values, segment, log_totals, mixed_grad):
    length = queries.shape[0]
    block_rows = min(512, length)
    places = jnp.arange(length, dtype=jnp.int32)
    scaling = HEAD_DIM ** (-0.5)

    def one_block(running, block_index):
        key_grad, value_grad = running
        masked = block_scores(queries, keys_low, segment, segment, places, places)
        attn_probs = jnp.exp(masked - log_totals[block_index][..., None])
        probs_low = attn_probs.astype(jnp.bfloat16)
        value_grad = value_grad + jnp.einsum(
            "hts,thd->shd", probs_low, mixed_grad, preferred_element_type=jnp.float32
        )
        probs_grad = jnp.einsum(
            "thd,shd->hts", mixed_grad, values, preferred_element_type=jnp.float32
        )
        inner_sum = jnp.sum(attn_probs * probs_grad, axis=-1, keepdims=True)
        score_grad = (attn_probs * (probs_grad - inner_sum)).astype(jnp.bfloat16)
        query_grad = (
            jnp.einsum("hts,shd->thd", score_grad, keys_low, preferred_element_type=jnp.float32)
            * scaling
        )
        key_grad = (
            key_grad
            + jnp.einsum("hts,thd->shd", score_grad, queries, preferred_element_type=jnp.float32)
            * scaling
        )
        return ((key_grad, value_grad), query_grad)

    empty = jnp.zeros((length, HEADS, HEAD_DIM), jnp.float32)
    (key_grad, value_grad), query_grad = lax.scan(
        one_block, (empty, empty), jnp.arange(length // block_rows, dtype=jnp.int32)
    )
    return (query_grad.reshape(length, HEADS, HEAD_DIM), key_grad, value_grad)


def factor_back(full_grad, a_part, b_part, rank_count):
    a_grad = jnp.einsum("thd,trd->trh", full_grad, b_part, precision=PRECISE) / rank_count
    b_grad = jnp.einsum("thd,trh->trd", full_grad, a_part, precision=PRECISE) / rank_count
    return (a_grad, b_grad)


def local(
    inputs,
    doc_lengths,
    w_aq,
    w_bq,
    w_ak,
    w_bk,
    w_av,
    w_bv,
    w_out,
    w_gate,
    w_up,
    w_down,
    gain_attn,
    gain_ffn,
    cotangent,
):
    length = inputs.shape[0]
    joined_local = jnp.concatenate([w_aq, w_bq, w_ak, w_bk, w_av, w_bv], axis=1)
    factor_w, out_w, gain_one = (
        lax.all_gather(joined_local, ("dp", "fsdp"), axis=0, tiled=True),
        lax.all_gather(w_out, ("dp", "fsdp"), axis=0, tiled=True),
        lax.all_gather(gain_attn, ("dp", "fsdp"), axis=0, tiled=True),
    )
    segment, places = doc_layout(doc_lengths[0], length)
    cos_table, sin_table = rotation(places)
    start_vals = inputs.astype(jnp.float32)
    normed_one, unit_one, scale_one = normalize(start_vals, gain_one.astype(jnp.float32))
    normed_low = normed_one.astype(jnp.bfloat16)
    factors = jnp.dot(normed_low, factor_w, preferred_element_type=jnp.float32)
    pieces = split_columns(factors)
    a_q = pieces[0].reshape(length, RANK_Q, HEADS)
    b_q = pieces[1].reshape(length, RANK_Q, HEAD_DIM)
    a_k = pieces[2].reshape(length, RANK_KV, HEADS)
    b_k = pieces[3].reshape(length, RANK_KV, HEAD_DIM)
    a_v = pieces[4].reshape(length, RANK_KV, HEADS)
    b_v = pieces[5].reshape(length, RANK_KV, HEAD_DIM)
    bq_rot = rotate(b_q, cos_table, sin_table)
    bk_rot = rotate(b_k, cos_table, sin_table)
    queries = (jnp.einsum("trh,trd->thd", a_q, bq_rot, precision=PRECISE) / RANK_Q).astype(
        jnp.bfloat16
    )
    keys_low = (jnp.einsum("trh,trd->thd", a_k, bk_rot, precision=PRECISE) / RANK_KV).astype(
        jnp.bfloat16
    )
    values = (jnp.einsum("trh,trd->thd", a_v, b_v, precision=PRECISE) / RANK_KV).astype(
        jnp.bfloat16
    )
    attended, log_totals = attend_forward(queries, keys_low, values, segment)
    mixed = attended.astype(jnp.bfloat16).reshape(length, HEADS * HEAD_DIM)
    resid = start_vals + jnp.dot(mixed, out_w, preferred_element_type=jnp.float32)
    gate_w, up_w, down_w, gain_two = (
        lax.all_gather(w_gate, ("dp", "fsdp"), axis=0, tiled=True),
        lax.all_gather(w_up, ("dp", "fsdp"), axis=0, tiled=True),
        lax.all_gather(w_down, ("dp", "fsdp"), axis=0, tiled=True),
        lax.all_gather(gain_ffn, ("dp", "fsdp"), axis=0, tiled=True),
    )
    normed_two, unit_two, scale_two = normalize(resid, gain_two.astype(jnp.float32))
    normed_two_low = normed_two.astype(jnp.bfloat16)
    gate_act = jnp.dot(normed_two_low, gate_w, preferred_element_type=jnp.float32)
    up_act = jnp.dot(normed_two_low, up_w, preferred_element_type=jnp.float32)
    hidden = (jax.nn.silu(gate_act) * up_act).astype(jnp.bfloat16)
    result = resid + jnp.dot(hidden, down_w, preferred_element_type=jnp.float32)
    outputs = result.astype(jnp.bfloat16)
    gate_w, up_w, down_w, gain_two = (
        lax.all_gather(w_gate, ("dp", "fsdp"), axis=0, tiled=True),
        lax.all_gather(w_up, ("dp", "fsdp"), axis=0, tiled=True),
        lax.all_gather(w_down, ("dp", "fsdp"), axis=0, tiled=True),
        lax.all_gather(gain_ffn, ("dp", "fsdp"), axis=0, tiled=True),
    )
    hidden_grad = jnp.einsum("tc,fc->tf", cotangent, down_w, preferred_element_type=jnp.float32)
    down_wgrad = jnp.einsum("tf,tc->fc", hidden, cotangent, preferred_element_type=jnp.float32)
    sig_vals = jax.nn.sigmoid(gate_act)
    gate_grad = (hidden_grad * up_act * sig_vals * (1.0 + gate_act * (1.0 - sig_vals))).astype(
        jnp.bfloat16
    )
    up_grad = (hidden_grad * jax.nn.silu(gate_act)).astype(jnp.bfloat16)
    normed_two_grad = jnp.einsum("tf,cf->tc", gate_grad, gate_w, preferred_element_type=jnp.float32)
    normed_two_grad = normed_two_grad + jnp.einsum(
        "tf,cf->tc", up_grad, up_w, preferred_element_type=jnp.float32
    )
    resid_norm_grad, gain_two_grad = norm_back(
        normed_two_grad, unit_two, scale_two, gain_two.astype(jnp.float32)
    )
    resid_grad = cotangent.astype(jnp.float32) + resid_norm_grad
    gate_rows = jnp.einsum(
        "tc,tf->cf", normed_two_low, gate_grad, preferred_element_type=jnp.float32
    )
    up_rows = jnp.einsum("tc,tf->cf", normed_two_low, up_grad, preferred_element_type=jnp.float32)
    gate_up_shard = lax.psum_scatter(
        jnp.concatenate([gate_rows, up_rows], axis=1),
        ("dp", "fsdp"),
        scatter_dimension=0,
        tiled=True,
    )
    gate_shard = gate_up_shard[:, :FF]
    up_shard = gate_up_shard[:, FF:]
    down_shard, gain_two_shard = (
        lax.psum_scatter(down_wgrad, ("dp", "fsdp"), scatter_dimension=0, tiled=True),
        lax.psum_scatter(gain_two_grad, ("dp", "fsdp"), scatter_dimension=0, tiled=True),
    )
    factor_w, out_w, gain_one = (
        lax.all_gather(joined_local, ("dp", "fsdp"), axis=0, tiled=True),
        lax.all_gather(w_out, ("dp", "fsdp"), axis=0, tiled=True),
        lax.all_gather(gain_attn, ("dp", "fsdp"), axis=0, tiled=True),
    )
    branch_grad = resid_grad.astype(jnp.bfloat16)
    out_wgrad = jnp.einsum("tc,td->cd", mixed, branch_grad, preferred_element_type=jnp.float32)
    mixed_grad = jnp.einsum("td,cd->tc", branch_grad, out_w, preferred_element_type=jnp.float32)
    mixed_grad = mixed_grad.astype(jnp.bfloat16).reshape(length, HEADS, HEAD_DIM)
    query_grad, key_grad, value_grad = attend_backward(
        queries, keys_low, values, segment, log_totals, mixed_grad
    )
    a_q_grad, bq_rot_grad = factor_back(query_grad, a_q, bq_rot, RANK_Q)
    a_k_grad, bk_rot_grad = factor_back(key_grad, a_k, bk_rot, RANK_KV)
    a_v_grad, b_v_grad = factor_back(value_grad, a_v, b_v, RANK_KV)
    neg_sin = -sin_table
    b_q_grad = rotate(bq_rot_grad, cos_table, neg_sin)
    b_k_grad = rotate(bk_rot_grad, cos_table, neg_sin)
    factor_grad = jnp.concatenate(
        [
            part.reshape(length, -1)
            for part in (a_q_grad, b_q_grad, a_k_grad, b_k_grad, a_v_grad, b_v_grad)
        ],
        axis=1,
    ).astype(jnp.bfloat16)
    factor_wgrad = jnp.einsum(
        "td,tc->dc", normed_low, factor_grad, preferred_element_type=jnp.float32
    )
    normed_one_grad = jnp.einsum(
        "tc,dc->td", factor_grad, factor_w, preferred_element_type=jnp.float32
    )
    input_norm_grad, gain_one_grad = norm_back(
        normed_one_grad, unit_one, scale_one, gain_one.astype(jnp.float32)
    )
    input_grad = resid_grad + input_norm_grad
    factor_shard, out_shard, gain_one_shard = (
        lax.psum_scatter(factor_wgrad, ("dp", "fsdp"), scatter_dimension=0, tiled=True),
        lax.psum_scatter(out_wgrad, ("dp", "fsdp"), scatter_dimension=0, tiled=True),
        lax.psum_scatter(gain_one_grad, ("dp", "fsdp"), scatter_dimension=0, tiled=True),
    )
    shard_pieces = split_columns(factor_shard)
    return (
        outputs,
        input_grad,
        shard_pieces[0],
        shard_pieces[1],
        shard_pieces[2],
        shard_pieces[3],
        shard_pieces[4],
        shard_pieces[5],
        out_shard,
        gate_shard,
        up_shard,
        down_shard,
        gain_one_shard,
        gain_two_shard,
    )


MESH_IDS = pl.DeviceIdType.MESH
HALF = FF // 2
OWN_UNITS = 88
PAD_UNITS = 96
FACTOR_PAD = 896
MIB = 2**20


def fits_pairs(mesh):
    return dict(mesh.shape) == {"dp": 2, "fsdp": 16}


def place():
    x = lax.axis_index("dp")
    f = lax.axis_index("fsdp")
    return x, lax.div(f, 4), lax.rem(lax.div(f, 2), 2), lax.rem(f, 2)


def device(x, z, y, c):
    return (x, z * 4 + y * 2 + c)


def greet(x, z, y, c):
    partners = [
        device(x, z, y, 1 - c),
        device(1 - x, z, y, c),
        device(x, z, 1 - y, c),
        device(1 - x, z, y, 1 - c),
    ]
    for step in (1, 2, 3):
        other = lax.rem(z + step, 4)
        partners += [device(x, other, y, c), device(x, other, y, 1 - c)]
    barrier = pltpu.get_barrier_semaphore()
    for partner in partners:
        pl.semaphore_signal(barrier, inc=1, device_id=partner, device_id_type=MESH_IDS)
    pl.semaphore_wait(barrier, len(partners))


class Wires:
    def __init__(self, send_sems, recv_sems, local_sems):
        self.send_sems, self.recv_sems, self.local_sems = send_sems, recv_sems, local_sems
        self.sent, self.held = 0, 0
        self.open = []

    def make(self, src, dst, to):
        at = self.sent
        self.sent += 1
        return pltpu.make_async_remote_copy(
            src_ref=src,
            dst_ref=dst,
            send_sem=self.send_sems.at[at],
            recv_sem=self.recv_sems.at[at],
            device_id=to,
            device_id_type=MESH_IDS,
        )

    def send(self, src, dst, to):
        copy = self.make(src, dst, to)
        copy.start()
        self.open.append(copy)
        return copy

    def local(self, src, dst):
        copy = pltpu.make_async_copy(src, dst, self.local_sems.at[self.held])
        self.held += 1
        copy.start()
        return copy

    def drain(self):
        for copy in self.open:
            copy.wait_send()
        self.open = []


def arrive(copies):
    for copy in copies:
        copy.wait_recv()


def gather_kernel(fac, wo, wd, wg, wu, fac_all, out_all, down_all, gate_all, up_all, ss, rs, ls):
    x, z, y, c = place()
    x_peer, y_peer, twin = device(1 - x, z, y, c), device(x, z, 1 - y, c), device(x, z, y, 1 - c)
    z_peers = [lax.rem(z + step, 4) for step in (1, 2, 3)]
    greet(x, z, y, c)
    w = Wires(ss, rs, ls)
    mine = pl.ds(pl.multiple_of(c * HALF, 128), HALF)
    theirs = pl.ds(pl.multiple_of((1 - c) * HALF, 128), HALF)

    def full_z(src, ref):
        own = w.local(src, ref.at[x, z, y, c])
        return own, [w.send(src, ref.at[x, z, y, c], device(x, zz, y, c)) for zz in z_peers]

    def full_two(ref, own, first):
        own.wait()
        arrive(first)
        a = w.send(ref.at[x, :, y, c, 0:16], ref.at[x, :, y, c, 0:16], x_peer)
        b = w.send(ref.at[x, :, y, c, 16:32], ref.at[x, :, y, c, 16:32], y_peer)
        return a, b, [w.send(ref.at[x, :, y, c], ref.at[x, :, y, c], twin)]

    def full_three(ref, a, b, down):
        a.wait_recv()
        a2 = w.send(ref.at[:, :, y, c, 0:16], ref.at[:, :, y, c, 0:16], y_peer)
        b.wait_recv()
        b2 = w.send(ref.at[x, :, :, c, 16:32], ref.at[x, :, :, c, 16:32], x_peer)
        down.append(w.send(ref.at[1 - x, :, y, c, 0:16], ref.at[1 - x, :, y, c, 0:16], twin))
        down.append(w.send(ref.at[x, :, 1 - y, c, 16:32], ref.at[x, :, 1 - y, c, 16:32], twin))
        return a2, b2

    def full_end(ref, a2, b2, down):
        a2.wait_recv()
        down.append(w.send(ref.at[:, :, 1 - y, c, 0:16], ref.at[:, :, 1 - y, c, 0:16], twin))
        b2.wait_recv()
        down.append(w.send(ref.at[1 - x, :, :, c, 16:32], ref.at[1 - x, :, :, c, 16:32], twin))
        arrive(down)

    def pair_z(src, ref):
        own = w.local(src.at[:, mine], ref.at[x, z, y, c])
        first = []
        for zz in z_peers:
            first.append(w.send(src.at[:, mine], ref.at[x, z, y, c], device(x, zz, y, c)))
            first.append(w.send(src.at[:, theirs], ref.at[x, z, y, c], device(x, zz, y, 1 - c)))
        first.append(w.send(src.at[:, theirs], ref.at[x, z, y, c], twin))
        return own, first

    own_f, z_f = full_z(fac, fac_all)
    own_o, z_o = full_z(wo, out_all)
    swap = w.make(wd, down_all.at[z, y, 1 - x], device(1 - x, z, y, 1 - c))
    keep = pltpu.make_async_copy(wd, down_all.at[z, y, x], w.local_sems.at[w.held])
    w.held += 1

    @pl.when(x == c)
    def _():
        keep.start()

    @pl.when(x != c)
    def _():
        swap.start()

    a_f, b_f, d_f = full_two(fac_all, own_f, z_f)
    a_o, b_o, d_o = full_two(out_all, own_o, z_o)

    @pl.when(x == c)
    def _():
        keep.wait()

    @pl.when(x != c)
    def _():
        swap.wait()

    slot = down_all.at[z, y, x]
    z_d = [w.send(slot, slot, device(x, zz, y, c)) for zz in z_peers]
    a2_f, b2_f = full_three(fac_all, a_f, b_f, d_f)
    own_g, z_g = pair_z(wg, gate_all)
    a2_o, b2_o = full_three(out_all, a_o, b_o, d_o)
    own_u, z_u = pair_z(wu, up_all)
    arrive(z_d)
    upper, lower = pl.ds(0, PAD_UNITS // 2), pl.ds(PAD_UNITS // 2, PAD_UNITS // 2)
    view = down_all.at[:, y, x, upper]
    a_d = w.send(view, view, x_peer)
    view = down_all.at[:, y, x, lower]
    b_d = w.send(view, view, y_peer)
    own_g.wait()
    arrive(z_g)
    view = gate_all.at[x, :, y]
    a_g = w.send(view, view, x_peer)
    own_u.wait()
    arrive(z_u)
    view = up_all.at[x, :, y]
    b_u = w.send(view, view, y_peer)
    full_end(fac_all, a2_f, b2_f, d_f)
    full_end(out_all, a2_o, b2_o, d_o)
    a_d.wait_recv()
    view = down_all.at[:, y, :, upper]
    a2_d = w.send(view, view, y_peer)
    b_d.wait_recv()
    view = down_all.at[:, :, x, lower]
    b2_d = w.send(view, view, x_peer)
    a_g.wait_recv()
    view = gate_all.at[:, :, y]
    a2_g = w.send(view, view, y_peer)
    b_u.wait_recv()
    view = up_all.at[x]
    b2_u = w.send(view, view, x_peer)
    arrive([a2_d, b2_d, a2_g, b2_u])
    w.drain()


def gather_all(fac, wo, wd, wg, wu):
    bf16 = jnp.bfloat16
    shapes = [
        (2, 4, 2, 2, 32, FACTOR_PAD),
        (2, 4, 2, 2, 32, 1024),
        (4, 2, 2, PAD_UNITS, 1024),
        (2, 4, 2, 2, 32, HALF),
        (2, 4, 2, 2, 32, HALF),
    ]
    anywhere = pl.BlockSpec(memory_space=pl.ANY)
    return pl.pallas_call(
        gather_kernel,
        out_shape=[jax.ShapeDtypeStruct(s, bf16) for s in shapes],
        in_specs=[anywhere] * 5,
        out_specs=[anywhere] * 5,
        scratch_shapes=[
            pltpu.SemaphoreType.DMA((64,)),
            pltpu.SemaphoreType.DMA((64,)),
            pltpu.SemaphoreType.DMA((8,)),
        ],
        compiler_params=pltpu.CompilerParams(collective_id=0, has_side_effects=True),
        name="gather_all",
    )(fac, wo, wd, wg, wu)


BLOCKS = ((0, 512), (512, 512), (1024, 384))
TILE = 256
NT = (((1,), (1,)), ((), ()))
TN = (((0,), (0,)), ((), ()))
F32, BF16 = jnp.float32, jnp.bfloat16


def dot(a, b, dims=None):
    if dims is None:
        return jnp.dot(a, b, preferred_element_type=F32)
    return lax.dot_general(a, b, dims, preferred_element_type=F32)


def add_low(dst, src):
    dst[...] = (dst[...].astype(F32) + src[...].astype(F32)).astype(BF16)


def ffn_kernel(
    n2_in, cot_in, resid, gain, gate_hbm, up_hbm, down_hbm,
    outputs, resid_grad, gain_part, gate_out, up_out, down_out,
    n2, cot, n2_t, wg, wu, wd, hid, gg, ug, out_acc, ng_acc, out_twin, ng_twin,
    g_buf, u_buf, d_buf, d_acc, g1, u1, da1, db1, g2, u2, da2, db2, g3, u3, d3, d_sum,
    ss, rs, ls,
):
    x, z, y, c = place()
    x_peer, y_peer, twin = device(1 - x, z, y, c), device(x, z, 1 - y, c), device(x, z, y, 1 - c)
    z_peers = [lax.rem(z + step, 4) for step in (1, 2, 3)]
    w = Wires(ss, rs, ls)
    own_n2 = w.local(n2_in, n2.at[0:512])
    own_cot = w.local(cot_in, cot.at[0:512])
    loads = []
    for start, size in BLOCKS:
        cols = pl.ds(start, size)
        loads.append(
            [
                w.local(gate_hbm.at[:, cols], wg.at[:, cols]),
                w.local(up_hbm.at[:, cols], wu.at[:, cols]),
                w.local(down_hbm.at[cols], wd.at[cols]),
            ]
        )
    greet(x, z, y, c)
    n2_twin = w.send(n2_in, n2.at[512:1024], twin)
    cot_twin = w.send(cot_in, cot.at[512:1024], twin)
    own_n2.wait()
    own_cot.wait()

    def turn(i):
        rows = pl.ds(pl.multiple_of(i * TILE, TILE), TILE)
        n2_t[:, rows] = n2[rows, :].T

    def forward(b, low, high):
        start, size = BLOCKS[b]
        cols = pl.ds(start, size)

        def tile(i, _):
            rows = pl.ds(pl.multiple_of(i * TILE, TILE), TILE)
            n2_rows, cot_rows = n2[rows, :], cot[rows, :]
            gate = dot(n2_rows, wg[:, cols])
            up = dot(n2_rows, wu[:, cols])
            hid_grad = dot(cot_rows, wd[cols, :], NT)
            sig = jax.nn.sigmoid(gate)
            silu = gate * sig
            hidden = (silu * up).astype(BF16)
            gate_grad = (hid_grad * up * sig * (1.0 + gate * (1.0 - sig))).astype(BF16)
            up_grad = (hid_grad * silu).astype(BF16)
            hid[rows, 0:size] = hidden
            gg[rows, 0:size] = gate_grad
            ug[rows, 0:size] = up_grad
            out_part = dot(hidden, wd[cols, :])
            ng_part = dot(gate_grad, wg[:, cols], NT) + dot(up_grad, wu[:, cols], NT)
            if b == 0:
                out_acc[rows, :] = out_part
                ng_acc[rows, :] = ng_part
            else:
                out_acc[rows, :] += out_part
                ng_acc[rows, :] += ng_part
            return 0

        lax.fori_loop(low, high, tile, 0)

    def weight_grads(b):
        start, size = BLOCKS[b]
        cols = pl.ds(start, size)

        def side(i, _):
            rows = pl.ds(pl.multiple_of(i * 512, 512), 512)
            part = dot(n2_t[rows, :], ug[:, 0:size])
            u_buf[i, :, :, :, cols] = part.astype(BF16).reshape(4, 2, 64, size)
            part = dot(n2_t[rows, :], gg[:, 0:size])
            g_buf[i, :, :, :, cols] = part.astype(BF16).reshape(4, 2, 64, size)
            return 0

        lax.fori_loop(0, 2, side, 0)
        d_acc[cols, :] = dot(hid[:, 0:size], cot[...], TN)

    def phase_one(b):
        cols = pl.ds(*BLOCKS[b])
        u = w.send(u_buf.at[1 - x, :, :, :, cols], u1.at[:, :, :, cols], x_peer)
        g = w.send(g_buf.at[:, :, 1 - y, :, cols], g1.at[:, :, :, cols], y_peer)
        return u, g

    def phase_two(b, u, g):
        cols = pl.ds(*BLOCKS[b])
        u.wait_recv()

        def add_u(i, _):
            zz, yy = lax.div(i, 2), lax.rem(i, 2)
            add_low(u_buf.at[x, zz, yy, :, cols], u1.at[zz, yy, :, cols])
            return 0

        lax.fori_loop(0, 8, add_u, 0)
        u = w.send(u_buf.at[x, :, 1 - y, :, cols], u2.at[:, :, cols], y_peer)
        g.wait_recv()

        def add_g(i, _):
            xx, zz = lax.div(i, 4), lax.rem(i, 4)
            add_low(g_buf.at[xx, zz, y, :, cols], g1.at[xx, zz, :, cols])
            return 0

        lax.fori_loop(0, 8, add_g, 0)
        g = w.send(g_buf.at[1 - x, :, y, :, cols], g2.at[:, :, cols], x_peer)
        return u, g

    def phase_three(b, u, g):
        cols = pl.ds(*BLOCKS[b])
        last = []
        for copy, buf, two, three in ((u, u_buf, u2, u3), (g, g_buf, g2, g3)):
            copy.wait_recv()

            def add(i, _, buf=buf, two=two):
                add_low(buf.at[x, i, y, :, cols], two.at[i, :, cols])
                return 0

            lax.fori_loop(0, 4, add, 0)
            for core, rel in ((c, 0), (1 - c, 1)):
                rows = pl.ds(pl.multiple_of(core * 32, 32), 32)
                for step, zz in enumerate(z_peers):
                    last.append(
                        w.send(
                            buf.at[x, zz, y, rows, cols],
                            three.at[rel, step + 1, :, cols],
                            device(x, zz, y, core),
                        )
                    )
            rows = pl.ds(pl.multiple_of((1 - c) * 32, 32), 32)
            last.append(w.send(buf.at[x, z, y, rows, cols], three.at[1, 0, :, cols], twin))
        return last

    def finish(buf, three, out):
        rows = pl.ds(pl.multiple_of(c * 32, 32), 32)
        own = buf[x, z, y, rows, :].astype(F32)
        for step in (1, 2, 3):
            own += three[0, step].astype(F32)
        out[c] = own
        other = three[1, 0].astype(F32)
        for step in (1, 2, 3):
            other += three[1, step].astype(F32)
        out[1 - c] = other

    for copy in loads[0]:
        copy.wait()
    forward(0, 0, 2)
    turn(0)
    turn(1)
    arrive([n2_twin, cot_twin])
    forward(0, 2, 4)
    turn(2)
    turn(3)
    weight_grads(0)
    one_0 = phase_one(0)
    for copy in loads[1]:
        copy.wait()
    forward(1, 0, 4)
    weight_grads(1)
    one_1 = phase_one(1)
    two_0 = phase_two(0, *one_0)
    for copy in loads[2]:
        copy.wait()
    forward(2, 2, 4)
    ng_send = w.send(ng_acc.at[512:1024], ng_twin, twin)
    out_send = w.send(out_acc.at[512:1024], out_twin, twin)
    forward(2, 0, 2)
    weight_grads(2)
    one_2 = phase_one(2)

    def spread(s, _):
        rows = d_acc[pl.ds(pl.multiple_of(s * OWN_UNITS, 8), OWN_UNITS), :]
        rows = jnp.concatenate([rows, jnp.zeros((PAD_UNITS - OWN_UNITS, rows.shape[1]), F32)], axis=0)
        d_buf[lax.div(s, 4), lax.rem(lax.div(s, 2), 2), lax.rem(s, 2)] = rows.astype(BF16)
        return 0

    lax.fori_loop(0, 16, spread, 0)
    upper, lower = pl.ds(0, PAD_UNITS // 2), pl.ds(PAD_UNITS // 2, PAD_UNITS // 2)
    da = w.send(d_buf.at[:, 1 - y, :, upper], da1, y_peer)
    db = w.send(d_buf.at[:, :, 1 - x, lower], db1, x_peer)
    two_1 = phase_two(1, *one_1)
    arrive([ng_send, out_send])

    def close(i, total):
        rows = pl.ds(pl.multiple_of(i * 128, 128), 128)
        base = resid[rows, :]
        n2[rows, :] = (base + out_acc[rows, :] + out_twin[rows, :]).astype(BF16)
        grad = ng_acc[rows, :] + ng_twin[rows, :]
        scale = lax.rsqrt(jnp.mean(base * base, axis=-1, keepdims=True) + EPSILON)
        unit = base * scale
        unit_grad = grad * gain[...]
        back = scale * (unit_grad - unit * jnp.mean(unit_grad * unit, axis=-1, keepdims=True))
        out_acc[rows, :] = cot[rows, :].astype(F32) + back
        return total + jnp.sum((grad * unit).reshape(16, 8, 1024), axis=0)

    gain_part[...] = lax.fori_loop(0, 4, close, jnp.zeros((8, 1024), F32))
    results = [
        w.local(n2.at[0:512], outputs),
        w.local(out_acc.at[0:512], resid_grad),
    ]
    last = phase_three(0, *two_0)
    two_2 = phase_two(2, *one_2)
    last += phase_three(1, *two_1)
    da.wait_recv()
    db.wait_recv()

    def add_d(i, _):
        zz, s = lax.div(i, 2), lax.rem(i, 2)
        add_low(d_buf.at[zz, y, s, upper], da1.at[zz, s])
        add_low(d_buf.at[zz, s, x, lower], db1.at[zz, s])
        return 0

    lax.fori_loop(0, 8, add_d, 0)
    da = w.send(d_buf.at[:, y, 1 - x, upper], da2, x_peer)
    db = w.send(d_buf.at[:, 1 - y, x, lower], db2, y_peer)
    last += phase_three(2, *two_2)
    da.wait_recv()
    db.wait_recv()

    def add_d2(i, _):
        add_low(d_buf.at[i, y, x, upper], da2.at[i])
        add_low(d_buf.at[i, y, x, lower], db2.at[i])
        return 0

    lax.fori_loop(0, 4, add_d2, 0)
    last_d = [
        w.send(d_buf.at[zz, y, x], d3.at[step], device(x, zz, y, c))
        for step, zz in enumerate(z_peers)
    ]
    arrive(last)
    finish(u_buf, u3, up_out)
    finish(g_buf, g3, gate_out)
    arrive(last_d)
    d_sum[...] = (
        d_buf[z, y, x].astype(F32)
        + d3[0].astype(F32)
        + d3[1].astype(F32)
        + d3[2].astype(F32)
    )
    swap = w.make(d_sum, down_out, device(1 - x, z, y, 1 - c))
    keep = pltpu.make_async_copy(d_sum, down_out, w.local_sems.at[w.held])
    w.held += 1

    @pl.when(x == c)
    def _():
        keep.start()
        keep.wait()

    @pl.when(x != c)
    def _():
        swap.start()
        swap.wait()

    for copy in results:
        copy.wait()
    w.drain()


def ffn_all(n2, cot, resid, gain, gate_w, up_w, down_w):
    anywhere, vmem = pl.BlockSpec(memory_space=pl.ANY), pl.BlockSpec(memory_space=pltpu.VMEM)
    big = lambda *shape: pltpu.VMEM(shape, BF16)
    wide = lambda *shape: pltpu.VMEM(shape, F32)
    return pl.pallas_call(
        ffn_kernel,
        out_shape=[
            jax.ShapeDtypeStruct((512, 1024), BF16),
            jax.ShapeDtypeStruct((512, 1024), F32),
            jax.ShapeDtypeStruct((8, 1024), F32),
            jax.ShapeDtypeStruct((2, 32, HALF), F32),
            jax.ShapeDtypeStruct((2, 32, HALF), F32),
            jax.ShapeDtypeStruct((PAD_UNITS, 1024), F32),
        ],
        in_specs=[anywhere, anywhere, vmem, vmem, anywhere, anywhere, anywhere],
        out_specs=[anywhere, anywhere, vmem, vmem, vmem, vmem],
        scratch_shapes=[
            big(1024, 1024), big(1024, 1024), big(1024, 1024),
            big(1024, HALF), big(1024, HALF), big(HALF, 1024),
            big(1024, 512), big(1024, 512), big(1024, 512),
            wide(1024, 1024), wide(1024, 1024), wide(512, 1024), wide(512, 1024),
            big(2, 4, 2, 64, HALF), big(2, 4, 2, 64, HALF), big(4, 2, 2, PAD_UNITS, 1024), wide(HALF, 1024),
            big(2, 4, 64, HALF), big(4, 2, 64, HALF), big(4, 2, PAD_UNITS // 2, 1024), big(4, 2, PAD_UNITS // 2, 1024),
            big(4, 64, HALF), big(4, 64, HALF), big(4, PAD_UNITS // 2, 1024), big(4, PAD_UNITS // 2, 1024),
            big(2, 4, 32, HALF), big(2, 4, 32, HALF), big(3, PAD_UNITS, 1024), wide(PAD_UNITS, 1024),
            pltpu.SemaphoreType.DMA((80,)),
            pltpu.SemaphoreType.DMA((80,)),
            pltpu.SemaphoreType.DMA((16,)),
        ],
        compiler_params=pltpu.CompilerParams(
            collective_id=1, has_side_effects=True, vmem_limit_bytes=61 * MIB
        ),
        name="ffn_all",
    )(n2, cot, resid, gain, gate_w, up_w, down_w)


def sum_kernel(part, out, own, twin_part, one_a, one_b, two_a, two_b, three, ss, rs, ls):
    x, z, y, c = place()
    x_peer, y_peer, twin = device(1 - x, z, y, c), device(x, z, 1 - y, c), device(x, z, y, 1 - c)
    z_peers = [lax.rem(z + step, 4) for step in (1, 2, 3)]
    w = Wires(ss, rs, ls)
    load = w.local(part.at[:, :, :, c], own)
    greet(x, z, y, c)
    first = w.send(part.at[:, :, :, 1 - c], twin_part, twin)
    load.wait()
    first.wait_recv()

    def add(i, _):
        xx, zz, yy = lax.div(i, 8), lax.rem(lax.div(i, 2), 4), lax.rem(i, 2)
        add_low(own.at[xx, zz, yy], twin_part.at[xx, zz, yy])
        return 0

    lax.fori_loop(0, 16, add, 0)
    upper, lower = pl.ds(0, 16), pl.ds(16, 16)
    a = w.send(own.at[:, :, 1 - y, upper], one_a, y_peer)
    b = w.send(own.at[1 - x, :, :, lower], one_b, x_peer)
    a.wait_recv()
    b.wait_recv()

    def add_one(i, _):
        s, zz = lax.div(i, 4), lax.rem(i, 4)
        add_low(own.at[s, zz, y, upper], one_a.at[s, zz])
        add_low(own.at[x, zz, s, lower], one_b.at[zz, s])
        return 0

    lax.fori_loop(0, 8, add_one, 0)
    a = w.send(own.at[1 - x, :, y, upper], two_a, x_peer)
    b = w.send(own.at[x, :, 1 - y, lower], two_b, y_peer)
    a.wait_recv()
    b.wait_recv()

    def add_two(i, _):
        add_low(own.at[x, i, y, upper], two_a.at[i])
        add_low(own.at[x, i, y, lower], two_b.at[i])
        return 0

    lax.fori_loop(0, 4, add_two, 0)
    last = [
        w.send(own.at[x, zz, y], three.at[step], device(x, zz, y, c))
        for step, zz in enumerate(z_peers)
    ]
    arrive(last)
    out[...] = (
        own[x, z, y].astype(F32)
        + three[0].astype(F32)
        + three[1].astype(F32)
        + three[2].astype(F32)
    )
    w.drain()


def sum_all(part):
    width = part.shape[-1]
    big = lambda *shape: pltpu.VMEM(shape, BF16)
    return pl.pallas_call(
        sum_kernel,
        out_shape=jax.ShapeDtypeStruct((32, width), F32),
        in_specs=[pl.BlockSpec(memory_space=pl.ANY)],
        out_specs=pl.BlockSpec(memory_space=pltpu.VMEM),
        scratch_shapes=[
            big(2, 4, 2, 32, width), big(2, 4, 2, 32, width),
            big(2, 4, 16, width), big(4, 2, 16, width), big(4, 16, width), big(4, 16, width),
            big(3, 32, width),
            pltpu.SemaphoreType.DMA((16,)),
            pltpu.SemaphoreType.DMA((16,)),
            pltpu.SemaphoreType.DMA((2,)),
        ],
        compiler_params=pltpu.CompilerParams(
            collective_id=2, has_side_effects=True, vmem_limit_bytes=40 * MIB
        ),
        name="sum_all",
    )(part)


def local_paired(
    inputs, doc_lengths, w_aq, w_bq, w_ak, w_bk, w_av, w_bv,
    w_out, w_gate, w_up, w_down, gain_attn, gain_ffn, cotangent,
):
    length = inputs.shape[0]
    spare = jnp.zeros((32, FACTOR_PAD - 802), BF16)
    fac = jnp.concatenate(
        [w_aq, w_bq, w_ak, w_bk, w_av, w_bv, gain_attn[:, None], gain_ffn[:, None], spare], axis=1
    )
    wd = jnp.pad(w_down, ((0, PAD_UNITS - OWN_UNITS), (0, 0)))
    fac_all, out_all, down_all, gate_all, up_all = gather_all(fac, w_out, wd, w_gate, w_up)
    fac_all = fac_all.reshape(1024, FACTOR_PAD)
    factor_w = fac_all[:, :800]
    gain_one, gain_two = fac_all[:, 800].astype(F32), fac_all[:, 801].astype(F32)
    out_w = out_all.reshape(1024, 1024)
    gate_w = gate_all.reshape(1024, HALF)
    up_w = up_all.reshape(1024, HALF)
    down_w = down_all.reshape(16, PAD_UNITS, 1024)[:, :OWN_UNITS].reshape(HALF, 1024)

    segment, places = doc_layout(doc_lengths[0], length)
    cos_table, sin_table = rotation(places)
    start_vals = inputs.astype(jnp.float32)
    normed_one, unit_one, scale_one = normalize(start_vals, gain_one)
    normed_low = normed_one.astype(jnp.bfloat16)
    factors = jnp.dot(normed_low, factor_w, preferred_element_type=jnp.float32)
    pieces = split_columns(factors)
    a_q = pieces[0].reshape(length, RANK_Q, HEADS)
    b_q = pieces[1].reshape(length, RANK_Q, HEAD_DIM)
    a_k = pieces[2].reshape(length, RANK_KV, HEADS)
    b_k = pieces[3].reshape(length, RANK_KV, HEAD_DIM)
    a_v = pieces[4].reshape(length, RANK_KV, HEADS)
    b_v = pieces[5].reshape(length, RANK_KV, HEAD_DIM)
    bq_rot = rotate(b_q, cos_table, sin_table)
    bk_rot = rotate(b_k, cos_table, sin_table)
    queries = (jnp.einsum("trh,trd->thd", a_q, bq_rot, precision=PRECISE) / RANK_Q).astype(BF16)
    keys_low = (jnp.einsum("trh,trd->thd", a_k, bk_rot, precision=PRECISE) / RANK_KV).astype(BF16)
    values = (jnp.einsum("trh,trd->thd", a_v, b_v, precision=PRECISE) / RANK_KV).astype(BF16)
    attended, log_totals = attend_forward(queries, keys_low, values, segment)
    mixed = attended.astype(jnp.bfloat16).reshape(length, HEADS * HEAD_DIM)
    resid = start_vals + jnp.dot(mixed, out_w, preferred_element_type=jnp.float32)
    normed_two, _, _ = normalize(resid, gain_two)

    outputs, resid_grad, gain_two_part, gate_shard, up_shard, down_shard = ffn_all(
        normed_two.astype(BF16), cotangent, resid, gain_two[None, :], gate_w, up_w, down_w
    )
    gate_shard = jnp.concatenate([gate_shard[0], gate_shard[1]], axis=1)
    up_shard = jnp.concatenate([up_shard[0], up_shard[1]], axis=1)
    down_shard = down_shard[:OWN_UNITS]
    gain_two_grad = jnp.sum(gain_two_part, axis=0)

    branch_grad = resid_grad.astype(jnp.bfloat16)
    out_wgrad = jnp.einsum("tc,td->cd", mixed, branch_grad, preferred_element_type=jnp.float32)
    mixed_grad = jnp.einsum("td,cd->tc", branch_grad, out_w, preferred_element_type=jnp.float32)
    mixed_grad = mixed_grad.astype(jnp.bfloat16).reshape(length, HEADS, HEAD_DIM)
    query_grad, key_grad, value_grad = attend_backward(
        queries, keys_low, values, segment, log_totals, mixed_grad
    )
    a_q_grad, bq_rot_grad = factor_back(query_grad, a_q, bq_rot, RANK_Q)
    a_k_grad, bk_rot_grad = factor_back(key_grad, a_k, bk_rot, RANK_KV)
    a_v_grad, b_v_grad = factor_back(value_grad, a_v, b_v, RANK_KV)
    neg_sin = -sin_table
    b_q_grad = rotate(bq_rot_grad, cos_table, neg_sin)
    b_k_grad = rotate(bk_rot_grad, cos_table, neg_sin)
    factor_grad = jnp.concatenate(
        [
            part.reshape(length, -1)
            for part in (a_q_grad, b_q_grad, a_k_grad, b_k_grad, a_v_grad, b_v_grad)
        ],
        axis=1,
    ).astype(jnp.bfloat16)
    factor_wgrad = jnp.einsum(
        "td,tc->dc", normed_low, factor_grad, preferred_element_type=jnp.float32
    )
    normed_one_grad = jnp.einsum(
        "tc,dc->td", factor_grad, factor_w, preferred_element_type=jnp.float32
    )
    input_norm_grad, gain_one_grad = norm_back(normed_one_grad, unit_one, scale_one, gain_one)
    input_grad = resid_grad + input_norm_grad
    part = jnp.concatenate(
        [
            factor_wgrad,
            gain_one_grad[:, None],
            gain_two_grad[:, None],
            jnp.zeros((1024, FACTOR_PAD - 802), F32),
            out_wgrad,
        ],
        axis=1,
    ).astype(BF16)
    shard = sum_all(part.reshape(2, 4, 2, 2, 32, FACTOR_PAD + 1024))
    shard_pieces = split_columns(shard)
    return (
        outputs,
        input_grad,
        *shard_pieces,
        shard[:, FACTOR_PAD:],
        gate_shard,
        up_shard,
        down_shard,
        shard[:, 800],
        shard[:, 801],
    )


def solution(mesh):
    return jax.shard_map(
        local_paired if fits_pairs(mesh) else local,
        mesh=mesh,
        in_specs=(
            P(("dp", "fsdp"), None),
            P(("dp", "fsdp"), None),
            P(("dp", "fsdp"), None),
            P(("dp", "fsdp"), None),
            P(("dp", "fsdp"), None),
            P(("dp", "fsdp"), None),
            P(("dp", "fsdp"), None),
            P(("dp", "fsdp"), None),
            P(("dp", "fsdp"), None),
            P(("dp", "fsdp"), None),
            P(("dp", "fsdp"), None),
            P(("dp", "fsdp"), None),
            P(("dp", "fsdp")),
            P(("dp", "fsdp")),
            P(("dp", "fsdp"), None),
        ),
        out_specs=(
            P(("dp", "fsdp"), None),
            P(("dp", "fsdp"), None),
            P(("dp", "fsdp"), None),
            P(("dp", "fsdp"), None),
            P(("dp", "fsdp"), None),
            P(("dp", "fsdp"), None),
            P(("dp", "fsdp"), None),
            P(("dp", "fsdp"), None),
            P(("dp", "fsdp"), None),
            P(("dp", "fsdp"), None),
            P(("dp", "fsdp"), None),
            P(("dp", "fsdp"), None),
            P(("dp", "fsdp")),
            P(("dp", "fsdp")),
        ),
        check_vma=False,
    )
```

```python
import math

import jax
import jax.numpy as jnp
from jax import lax
from jax.experimental import pallas as pl
from jax.experimental.pallas import tpu as pltpu
from jax.sharding import PartitionSpec as P

HEADS = 16
HEAD_DIM = 64
RANK_Q = 6
RANK_KV = 2
FF = 2816


EPSILON = 1e-06
PRECISE = lax.Precision.HIGHEST


def factor_columns():
    return [
        RANK_Q * HEADS,
        RANK_Q * HEAD_DIM,
        RANK_KV * HEADS,
        RANK_KV * HEAD_DIM,
        RANK_KV * HEADS,
        RANK_KV * HEAD_DIM,
    ]


def split_columns(matrix):
    pieces = []
    offset = 0
    for columns in factor_columns():
        pieces.append(matrix[:, offset : offset + columns])
        offset += columns
    return pieces


def doc_layout(lengths, length):
    order = jnp.arange(lengths.shape[0], dtype=jnp.int32)
    doc_ends = jnp.sum(jnp.where(order[:, None] >= order[None, :], lengths[None, :], 0), axis=1)
    doc_starts = doc_ends - lengths
    places = jnp.arange(length, dtype=jnp.int32)
    segment = jnp.sum((places[:, None] >= doc_ends[None, :]).astype(jnp.int32), axis=1)
    owner = segment[:, None] == jnp.arange(lengths.shape[0], dtype=jnp.int32)[None, :]
    doc_first = jnp.sum(jnp.where(owner, doc_starts[None, :], 0), axis=1)
    return (segment, (places - doc_first).astype(jnp.float32))


def rotation(places):
    halfway = HEAD_DIM // 2
    freqs = jnp.exp(-math.log(10000.0) * jnp.arange(halfway, dtype=jnp.float32) / halfway)
    angles = places[..., None] * freqs
    return (jnp.cos(angles), jnp.sin(angles))


def rotate(factor, cos_table, sin_table):
    halfway = factor.shape[-1] // 2
    front_part = factor[..., :halfway]
    back_part = factor[..., halfway:]
    cos_part = cos_table[..., None, :]
    sin_part = sin_table[..., None, :]
    return jnp.concatenate(
        [
            front_part * cos_part - back_part * sin_part,
            front_part * sin_part + back_part * cos_part,
        ],
        axis=-1,
    )


def normalize(values, gain):
    scaling = lax.rsqrt(jnp.mean(values * values, axis=-1, keepdims=True) + EPSILON)
    unit_vals = values * scaling
    return (unit_vals * gain, unit_vals, scaling)


def norm_back(incoming, unit_vals, scaling, gain):
    unit_grad = incoming * gain
    grad_in = scaling * (
        unit_grad - unit_vals * jnp.mean(unit_grad * unit_vals, axis=-1, keepdims=True)
    )
    return (grad_in, jnp.sum(incoming * unit_vals, axis=0))


def block_scores(query_part, keys_low, seg_part, segment, place_part, places):
    scaling = HEAD_DIM ** (-0.5)
    scores = (
        jnp.einsum("thd,shd->hts", query_part, keys_low, preferred_element_type=jnp.float32)
        * scaling
    )
    allowed = (seg_part[:, None] == segment[None, :]) & (places[None, :] <= place_part[:, None])
    return jnp.where(allowed[None], scores, -1e30)


def attend_forward(queries, keys_low, values, segment):
    length = queries.shape[0]
    block_rows = min(512, length)
    places = jnp.arange(length, dtype=jnp.int32)

    def one_block(block_index):
        masked = block_scores(queries, keys_low, segment, segment, places, places)
        row_peak = jnp.max(masked, axis=-1, keepdims=True)
        exp_terms = jnp.exp(masked - row_peak)
        row_total = jnp.sum(exp_terms, axis=-1, keepdims=True)
        attn_probs = (exp_terms / row_total).astype(jnp.bfloat16)
        attended = jnp.einsum(
            "hts,shd->thd", attn_probs, values, preferred_element_type=jnp.float32
        )
        return (attended, (row_peak + jnp.log(row_total))[..., 0])

    attended, log_totals = lax.map(one_block, jnp.arange(length // block_rows, dtype=jnp.int32))
    return (attended.reshape(length, HEADS, HEAD_DIM), log_totals)


def attend_backward(queries, keys_low, values, segment, log_totals, mixed_grad):
    length = queries.shape[0]
    block_rows = min(512, length)
    places = jnp.arange(length, dtype=jnp.int32)
    scaling = HEAD_DIM ** (-0.5)

    def one_block(running, block_index):
        key_grad, value_grad = running
        masked = block_scores(queries, keys_low, segment, segment, places, places)
        attn_probs = jnp.exp(masked - log_totals[block_index][..., None])
        probs_low = attn_probs.astype(jnp.bfloat16)
        value_grad = value_grad + jnp.einsum(
            "hts,thd->shd", probs_low, mixed_grad, preferred_element_type=jnp.float32
        )
        probs_grad = jnp.einsum(
            "thd,shd->hts", mixed_grad, values, preferred_element_type=jnp.float32
        )
        inner_sum = jnp.sum(attn_probs * probs_grad, axis=-1, keepdims=True)
        score_grad = (attn_probs * (probs_grad - inner_sum)).astype(jnp.bfloat16)
        query_grad = (
            jnp.einsum("hts,shd->thd", score_grad, keys_low, preferred_element_type=jnp.float32)
            * scaling
        )
        key_grad = (
            key_grad
            + jnp.einsum("hts,thd->shd", score_grad, queries, preferred_element_type=jnp.float32)
            * scaling
        )
        return ((key_grad, value_grad), query_grad)

    empty = jnp.zeros((length, HEADS, HEAD_DIM), jnp.float32)
    (key_grad, value_grad), query_grad = lax.scan(
        one_block, (empty, empty), jnp.arange(length // block_rows, dtype=jnp.int32)
    )
    return (query_grad.reshape(length, HEADS, HEAD_DIM), key_grad, value_grad)


def factor_back(full_grad, a_part, b_part, rank_count):
    a_grad = jnp.einsum("thd,trd->trh", full_grad, b_part, precision=PRECISE) / rank_count
    b_grad = jnp.einsum("thd,trh->trd", full_grad, a_part, precision=PRECISE) / rank_count
    return (a_grad, b_grad)


def local(
    inputs,
    doc_lengths,
    w_aq,
    w_bq,
    w_ak,
    w_bk,
    w_av,
    w_bv,
    w_out,
    w_gate,
    w_up,
    w_down,
    gain_attn,
    gain_ffn,
    cotangent,
):
    length = inputs.shape[0]
    joined_local = jnp.concatenate([w_aq, w_bq, w_ak, w_bk, w_av, w_bv], axis=1)
    factor_w, out_w, gain_one = (
        lax.all_gather(joined_local, ("dp", "fsdp"), axis=0, tiled=True),
        lax.all_gather(w_out, ("dp", "fsdp"), axis=0, tiled=True),
        lax.all_gather(gain_attn, ("dp", "fsdp"), axis=0, tiled=True),
    )
    segment, places = doc_layout(doc_lengths[0], length)
    cos_table, sin_table = rotation(places)
    start_vals = inputs.astype(jnp.float32)
    normed_one, unit_one, scale_one = normalize(start_vals, gain_one.astype(jnp.float32))
    normed_low = normed_one.astype(jnp.bfloat16)
    factors = jnp.dot(normed_low, factor_w, preferred_element_type=jnp.float32)
    pieces = split_columns(factors)
    a_q = pieces[0].reshape(length, RANK_Q, HEADS)
    b_q = pieces[1].reshape(length, RANK_Q, HEAD_DIM)
    a_k = pieces[2].reshape(length, RANK_KV, HEADS)
    b_k = pieces[3].reshape(length, RANK_KV, HEAD_DIM)
    a_v = pieces[4].reshape(length, RANK_KV, HEADS)
    b_v = pieces[5].reshape(length, RANK_KV, HEAD_DIM)
    bq_rot = rotate(b_q, cos_table, sin_table)
    bk_rot = rotate(b_k, cos_table, sin_table)
    queries = (jnp.einsum("trh,trd->thd", a_q, bq_rot, precision=PRECISE) / RANK_Q).astype(
        jnp.bfloat16
    )
    keys_low = (jnp.einsum("trh,trd->thd", a_k, bk_rot, precision=PRECISE) / RANK_KV).astype(
        jnp.bfloat16
    )
    values = (jnp.einsum("trh,trd->thd", a_v, b_v, precision=PRECISE) / RANK_KV).astype(
        jnp.bfloat16
    )
    attended, log_totals = attend_forward(queries, keys_low, values, segment)
    mixed = attended.astype(jnp.bfloat16).reshape(length, HEADS * HEAD_DIM)
    resid = start_vals + jnp.dot(mixed, out_w, preferred_element_type=jnp.float32)
    gate_w, up_w, down_w, gain_two = (
        lax.all_gather(w_gate, ("dp", "fsdp"), axis=0, tiled=True),
        lax.all_gather(w_up, ("dp", "fsdp"), axis=0, tiled=True),
        lax.all_gather(w_down, ("dp", "fsdp"), axis=0, tiled=True),
        lax.all_gather(gain_ffn, ("dp", "fsdp"), axis=0, tiled=True),
    )
    normed_two, unit_two, scale_two = normalize(resid, gain_two.astype(jnp.float32))
    normed_two_low = normed_two.astype(jnp.bfloat16)
    gate_act = jnp.dot(normed_two_low, gate_w, preferred_element_type=jnp.float32)
    up_act = jnp.dot(normed_two_low, up_w, preferred_element_type=jnp.float32)
    hidden = (jax.nn.silu(gate_act) * up_act).astype(jnp.bfloat16)
    result = resid + jnp.dot(hidden, down_w, preferred_element_type=jnp.float32)
    outputs = result.astype(jnp.bfloat16)
    gate_w, up_w, down_w, gain_two = (
        lax.all_gather(w_gate, ("dp", "fsdp"), axis=0, tiled=True),
        lax.all_gather(w_up, ("dp", "fsdp"), axis=0, tiled=True),
        lax.all_gather(w_down, ("dp", "fsdp"), axis=0, tiled=True),
        lax.all_gather(gain_ffn, ("dp", "fsdp"), axis=0, tiled=True),
    )
    hidden_grad = jnp.einsum("tc,fc->tf", cotangent, down_w, preferred_element_type=jnp.float32)
    down_wgrad = jnp.einsum("tf,tc->fc", hidden, cotangent, preferred_element_type=jnp.float32)
    sig_vals = jax.nn.sigmoid(gate_act)
    gate_grad = (hidden_grad * up_act * sig_vals * (1.0 + gate_act * (1.0 - sig_vals))).astype(
        jnp.bfloat16
    )
    up_grad = (hidden_grad * jax.nn.silu(gate_act)).astype(jnp.bfloat16)
    normed_two_grad = jnp.einsum("tf,cf->tc", gate_grad, gate_w, preferred_element_type=jnp.float32)
    normed_two_grad = normed_two_grad + jnp.einsum(
        "tf,cf->tc", up_grad, up_w, preferred_element_type=jnp.float32
    )
    resid_norm_grad, gain_two_grad = norm_back(
        normed_two_grad, unit_two, scale_two, gain_two.astype(jnp.float32)
    )
    resid_grad = cotangent.astype(jnp.float32) + resid_norm_grad
    gate_rows = jnp.einsum(
        "tc,tf->cf", normed_two_low, gate_grad, preferred_element_type=jnp.float32
    )
    up_rows = jnp.einsum("tc,tf->cf", normed_two_low, up_grad, preferred_element_type=jnp.float32)
    gate_up_shard = lax.psum_scatter(
        jnp.concatenate([gate_rows, up_rows], axis=1),
        ("dp", "fsdp"),
        scatter_dimension=0,
        tiled=True,
    )
    gate_shard = gate_up_shard[:, :FF]
    up_shard = gate_up_shard[:, FF:]
    down_shard, gain_two_shard = (
        lax.psum_scatter(down_wgrad, ("dp", "fsdp"), scatter_dimension=0, tiled=True),
        lax.psum_scatter(gain_two_grad, ("dp", "fsdp"), scatter_dimension=0, tiled=True),
    )
    factor_w, out_w, gain_one = (
        lax.all_gather(joined_local, ("dp", "fsdp"), axis=0, tiled=True),
        lax.all_gather(w_out, ("dp", "fsdp"), axis=0, tiled=True),
        lax.all_gather(gain_attn, ("dp", "fsdp"), axis=0, tiled=True),
    )
    branch_grad = resid_grad.astype(jnp.bfloat16)
    out_wgrad = jnp.einsum("tc,td->cd", mixed, branch_grad, preferred_element_type=jnp.float32)
    mixed_grad = jnp.einsum("td,cd->tc", branch_grad, out_w, preferred_element_type=jnp.float32)
    mixed_grad = mixed_grad.astype(jnp.bfloat16).reshape(length, HEADS, HEAD_DIM)
    query_grad, key_grad, value_grad = attend_backward(
        queries, keys_low, values, segment, log_totals, mixed_grad
    )
    a_q_grad, bq_rot_grad = factor_back(query_grad, a_q, bq_rot, RANK_Q)
    a_k_grad, bk_rot_grad = factor_back(key_grad, a_k, bk_rot, RANK_KV)
    a_v_grad, b_v_grad = factor_back(value_grad, a_v, b_v, RANK_KV)
    neg_sin = -sin_table
    b_q_grad = rotate(bq_rot_grad, cos_table, neg_sin)
    b_k_grad = rotate(bk_rot_grad, cos_table, neg_sin)
    factor_grad = jnp.concatenate(
        [
            part.reshape(length, -1)
            for part in (a_q_grad, b_q_grad, a_k_grad, b_k_grad, a_v_grad, b_v_grad)
        ],
        axis=1,
    ).astype(jnp.bfloat16)
    factor_wgrad = jnp.einsum(
        "td,tc->dc", normed_low, factor_grad, preferred_element_type=jnp.float32
    )
    normed_one_grad = jnp.einsum(
        "tc,dc->td", factor_grad, factor_w, preferred_element_type=jnp.float32
    )
    input_norm_grad, gain_one_grad = norm_back(
        normed_one_grad, unit_one, scale_one, gain_one.astype(jnp.float32)
    )
    input_grad = resid_grad + input_norm_grad
    factor_shard, out_shard, gain_one_shard = (
        lax.psum_scatter(factor_wgrad, ("dp", "fsdp"), scatter_dimension=0, tiled=True),
        lax.psum_scatter(out_wgrad, ("dp", "fsdp"), scatter_dimension=0, tiled=True),
        lax.psum_scatter(gain_one_grad, ("dp", "fsdp"), scatter_dimension=0, tiled=True),
    )
    shard_pieces = split_columns(factor_shard)
    return (
        outputs,
        input_grad,
        shard_pieces[0],
        shard_pieces[1],
        shard_pieces[2],
        shard_pieces[3],
        shard_pieces[4],
        shard_pieces[5],
        out_shard,
        gate_shard,
        up_shard,
        down_shard,
        gain_one_shard,
        gain_two_shard,
    )


MESH_IDS = pl.DeviceIdType.MESH
HALF = FF // 2
OWN_UNITS = 88
PAD_UNITS = 96
FACTOR_PAD = 896
MIB = 2**20


def fits_pairs(mesh):
    return dict(mesh.shape) == {"dp": 2, "fsdp": 16}


def place():
    x = lax.axis_index("dp")
    f = lax.axis_index("fsdp")
    return x, lax.div(f, 4), lax.rem(lax.div(f, 2), 2), lax.rem(f, 2)


def device(x, z, y, c):
    return (x, z * 4 + y * 2 + c)


def greet(x, z, y, c):
    partners = [
        device(x, z, y, 1 - c),
        device(1 - x, z, y, c),
        device(x, z, 1 - y, c),
        device(1 - x, z, y, 1 - c),
    ]
    for step in (1, 2, 3):
        other = lax.rem(z + step, 4)
        partners += [device(x, other, y, c), device(x, other, y, 1 - c)]
    barrier = pltpu.get_barrier_semaphore()
    for partner in partners:
        pl.semaphore_signal(barrier, inc=1, device_id=partner, device_id_type=MESH_IDS)
    pl.semaphore_wait(barrier, len(partners))


class Wires:
    def __init__(self, send_sems, recv_sems, local_sems):
        self.send_sems, self.recv_sems, self.local_sems = send_sems, recv_sems, local_sems
        self.sent, self.held = 0, 0
        self.open = []

    def make(self, src, dst, to):
        at = self.sent
        self.sent += 1
        return pltpu.make_async_remote_copy(
            src_ref=src,
            dst_ref=dst,
            send_sem=self.send_sems.at[at],
            recv_sem=self.recv_sems.at[at],
            device_id=to,
            device_id_type=MESH_IDS,
        )

    def go(self, copy):
        copy.start()
        self.open.append(copy)
        return copy

    def send(self, src, dst, to):
        return self.go(self.make(src, dst, to))

    def local(self, src, dst):
        copy = pltpu.make_async_copy(src, dst, self.local_sems.at[self.held])
        self.held += 1
        copy.start()
        return copy

    def drain(self):
        for copy in self.open:
            copy.wait_send()
        self.open = []


def arrive(copies):
    for copy in copies:
        copy.wait_recv()


BLOCKS = ((0, 512), (512, 512), (1024, 384))
TILE = 256
NT = (((1,), (1,)), ((), ()))
TN = (((0,), (0,)), ((), ()))
F32, BF16 = jnp.float32, jnp.bfloat16


def dot(a, b, dims=None):
    if dims is None:
        return jnp.dot(a, b, preferred_element_type=F32)
    return lax.dot_general(a, b, dims, preferred_element_type=F32)


def add_low(dst, src):
    dst[...] = (dst[...].astype(F32) + src[...].astype(F32)).astype(BF16)


KEPT = 1152
COS_LANES = pl.ds(896, 128)
SIN_LANES = pl.ds(1024, 128)
A_LANES = pl.ds(640, 128)
V_LANES = pl.ds(768, 128)


def lane_iota(rows, lanes=128):
    return lax.broadcasted_iota(jnp.int32, (rows, lanes), 1)


def row_iota(rows, lanes=128):
    return lax.broadcasted_iota(jnp.int32, (rows, lanes), 0)


def doc_ends_of(lengths):
    one = lengths[0, 0]
    two = one + lengths[0, 1]
    return one, two, two + lengths[0, 2]


def make_tables(lengths, cos_ref, sin_ref):
    ends = doc_ends_of(lengths)

    def tile(i, _):
        rows = pl.ds(pl.multiple_of(i * 128, 128), 128)
        places = row_iota(128) + i * 128
        first = jnp.zeros((128, 128), jnp.int32)
        for end in ends:
            first = jnp.where(places >= end, end, first)
        lane = lane_iota(128)
        turn = lax.rem(lane, 32).astype(F32)
        freqs = jnp.exp(-math.log(10000.0) * turn / 32)
        angles = (places - first).astype(F32) * freqs
        cos_ref[rows, :] = jnp.cos(angles)
        sin_vals = jnp.sin(angles)
        sin_ref[rows, :] = jnp.where(lax.rem(lane, 64) < 32, -sin_vals, sin_vals)
        return 0

    lax.fori_loop(0, 4, tile, 0)


def make_bias(lengths, bias):
    ends = doc_ends_of(lengths)

    def tile(i, _):
        rows = pl.ds(pl.multiple_of(i * 128, 128), 128)
        t = row_iota(128, 512) + i * 128
        s = lane_iota(128, 512)
        own, key = jnp.zeros((128, 512), jnp.int32), jnp.zeros((128, 512), jnp.int32)
        for end in ends:
            own += (t >= end).astype(jnp.int32)
            key += (s >= end).astype(jnp.int32)
        bias[rows, :] = jnp.where((own == key) & (s <= t), 0.0, -1e30)
        return 0

    lax.fori_loop(0, 4, tile, 0)


def make_spread(spread):
    def rank(r, _):
        head = lax.div(lane_iota(128, 1024), HEAD_DIM) + r * HEADS
        spread[r] = jnp.where(row_iota(128, 1024) == head, 1.0, 0.0).astype(BF16)
        return 0

    lax.fori_loop(0, 8, rank, 0)


def swapped(tile):
    front = lax.rem(lane_iota(tile.shape[0]), 64) < 32
    return jnp.where(front, pltpu.roll(tile, 96, 1), pltpu.roll(tile, 32, 1))


def both_halves(tile, half):
    low = lane_iota(tile.shape[0]) < 64
    other = pltpu.roll(tile, 64, 1)
    return jnp.where(low, tile, other) if half == 0 else jnp.where(low, other, tile)


def two_terms(a):
    high = a.astype(BF16)
    return high, (a - high.astype(F32)).astype(BF16)


def expand(terms, spread_r):
    return dot(terms[0], spread_r) + dot(terms[1], spread_r)


def eight(tile):
    return jnp.concatenate([tile] * 8, axis=1)


def gain_rows(fac_all, gains):
    tile = fac_all[:, :, :, :, :, V_LANES].reshape(1024, 128).astype(F32)
    gains[...] = tile.T[32:40, :]


def make_factors(x_in, gains, fac_all, n1, kept):
    def tile(i, _):
        rows = pl.ds(pl.multiple_of(i * 256, 256), 256)
        vals = x_in[rows, :].astype(F32)
        scale = lax.rsqrt(jnp.mean(vals * vals, axis=-1, keepdims=True) + EPSILON)
        low = (vals * scale * gains[0:1, :]).astype(BF16)
        n1[rows, :] = low
        kept[rows, 0:FACTOR_PAD] = dot(low, fac_all[...].reshape(1024, FACTOR_PAD))
        return 0

    lax.fori_loop(0, 2, tile, 0)


def make_heads(kept, cos_ref, sin_ref, spread, q, k, v):
    def tile(i, _):
        rows = pl.ds(pl.multiple_of(i * 128, 128), 128)
        turned = []
        for j in range(4):
            lanes = pl.ds(j * 128, 128)
            part = kept[rows, lanes]
            part = part * cos_ref[rows, :] + swapped(part) * sin_ref[rows, :]
            kept[rows, lanes] = part
            turned.append(part)
        terms = two_terms(kept[rows, A_LANES])
        total = jnp.zeros((128, 1024), F32)
        for r in range(RANK_Q):
            total += expand(terms, spread[r]) * eight(both_halves(turned[r // 2], r % 2))
        q[rows, :] = (total * (1.0 / RANK_Q)).astype(BF16) * BF16(HEAD_DIM**-0.5)
        total = jnp.zeros((128, 1024), F32)
        for r in range(RANK_KV):
            total += expand(terms, spread[RANK_Q + r]) * eight(both_halves(turned[3], r))
        k[rows, :] = (total * (1.0 / RANK_KV)).astype(BF16)
        terms = two_terms(kept[rows, V_LANES])
        plain = kept[rows, pl.ds(512, 128)]
        total = jnp.zeros((128, 1024), F32)
        for r in range(RANK_KV):
            total += expand(terms, spread[r]) * eight(both_halves(plain, r))
        v[rows, :] = (total * (1.0 / RANK_KV)).astype(BF16)
        return 0

    lax.fori_loop(0, 4, tile, 0)


def only(tile, half):
    low = lane_iota(tile.shape[0]) < 64
    keep = low if half == 0 else jnp.logical_not(low)
    return jnp.where(keep, tile, jnp.zeros_like(tile))


def soft(q_rows, k_cols, bias_block):
    scores = dot(q_rows, k_cols, NT) + bias_block
    terms = jnp.exp(scores - jnp.max(scores, axis=-1, keepdims=True))
    return terms * (1.0 / jnp.sum(terms, axis=-1, keepdims=True))


def attend_pairs(q, k, v, bias, mixed, first, last):
    def pair(p, _):
        lanes = pl.ds(pl.multiple_of(p * 128, 128), 128)
        for start, extent in ((0, 256), (256, 512)):
            rows, cols = pl.ds(start, 256), pl.ds(0, extent)
            q_rows, k_cols, v_cols = q[rows, lanes], k[cols, lanes], v[cols, lanes]
            halves = []
            for half in (0, 1):
                probs = soft(only(q_rows, half), k_cols, bias[rows, cols]).astype(BF16)
                halves.append(dot(probs, v_cols))
            low = lane_iota(256) < 64
            mixed[rows, lanes] = jnp.where(low, halves[0], halves[1]).astype(BF16)
        return 0

    lax.fori_loop(first, last, pair, 0)


def make_resid(x_in, mixed, out_all, gains, resid, n2):
    def tile(i, _):
        rows = pl.ds(pl.multiple_of(i * 256, 256), 256)
        base = x_in[rows, :].astype(F32) + dot(mixed[rows, :], out_all[...].reshape(1024, 1024))
        resid[rows, :] = base
        scale = lax.rsqrt(jnp.mean(base * base, axis=-1, keepdims=True) + EPSILON)
        n2[rows, :] = (base * scale * gains[1:2, :]).astype(BF16)
        return 0

    lax.fori_loop(0, 2, tile, 0)


def front_kernel(
    x_in, lengths, fac, wo, wd, wg, wu,
    down_all, gate_all, up_all, fac_out, out_out, n1_out, kept_out, q_out, k_out, v_out, mixed_out, resid_out, n2_out, bias_out, spread_out, gains,
    fac_all, out_all, n1, kept, q, k, v, mixed, resid, n2, bias, spread,
    ss, rs, ls,
):
    x, z, y, c = place()
    x_peer, y_peer, twin = device(1 - x, z, y, c), device(x, z, 1 - y, c), device(x, z, y, 1 - c)
    z_peers = [lax.rem(z + step, 4) for step in (1, 2, 3)]
    w = Wires(ss, rs, ls)
    mine = pl.ds(pl.multiple_of(c * HALF, 128), HALF)
    theirs = pl.ds(pl.multiple_of((1 - c) * HALF, 128), HALF)
    one, two = pl.ds(0, 16), pl.ds(16, 16)

    def full_z(src, ref):
        own = w.local(src, ref.at[x, z, y, c])
        return own, [w.send(src, ref.at[x, z, y, c], device(x, zz, y, c)) for zz in z_peers]

    def same(view, to):
        return w.send(view, view, to)

    def full_two(ref, own, first):
        own.wait()
        arrive(first)
        a = same(ref.at[x, :, y, c, one], x_peer)
        b = same(ref.at[x, :, y, c, two], y_peer)
        return a, b, [same(ref.at[x, :, y, c], twin)]

    def full_three(ref, a, b, down):
        a.wait_recv()
        a2 = same(ref.at[:, :, y, c, one], y_peer)
        b.wait_recv()
        b2 = same(ref.at[x, :, :, c, two], x_peer)
        down.append(same(ref.at[1 - x, :, y, c, one], twin))
        down.append(same(ref.at[x, :, 1 - y, c, two], twin))
        return a2, b2

    def full_end(ref, a2, b2, down):
        a2.wait_recv()
        down.append(same(ref.at[:, :, 1 - y, c, one], twin))
        b2.wait_recv()
        down.append(same(ref.at[1 - x, :, :, c, two], twin))

    def pair_z(src, ref):
        own = w.local(src.at[:, mine], ref.at[x, z, y, c])
        first = []
        for zz in z_peers:
            first.append(w.send(src.at[:, mine], ref.at[x, z, y, c], device(x, zz, y, c)))
            first.append(w.send(src.at[:, theirs], ref.at[x, z, y, c], device(x, zz, y, 1 - c)))
        first.append(w.send(src.at[:, theirs], ref.at[x, z, y, c], twin))
        return own, first

    def pair_two(ref, own, first):
        own.wait()
        arrive(first)
        return same(ref.at[x, :, y, :, one], x_peer), same(ref.at[x, :, y, :, two], y_peer)

    def pair_three(ref, a, b):
        a.wait_recv()
        a2 = same(ref.at[:, :, y, :, one], y_peer)
        b.wait_recv()
        return a2, same(ref.at[x, :, :, :, two], x_peer)

    cos_ref, sin_ref = kept.at[:, COS_LANES], kept.at[:, SIN_LANES]
    greet(x, z, y, c)
    own_f, z_f = full_z(fac, fac_all)
    swap = w.make(wd, down_all.at[z, y, 1 - x], device(1 - x, z, y, 1 - c))
    keep = pltpu.make_async_copy(wd, down_all.at[z, y, x], w.local_sems.at[w.held])
    w.held += 1

    @pl.when(x == c)
    def _():
        keep.start()

    @pl.when(x != c)
    def _():
        swap.start()

    make_tables(lengths, cos_ref, sin_ref)
    a_f, b_f, d_f = full_two(fac_all, own_f, z_f)
    own_o, z_o = full_z(wo, out_all)

    @pl.when(x == c)
    def _():
        keep.wait()

    @pl.when(x != c)
    def _():
        swap.wait()

    slot = down_all.at[z, y, x]
    upper, lower = pl.ds(0, PAD_UNITS // 2), pl.ds(PAD_UNITS // 2, PAD_UNITS // 2)
    z_da = [
        w.send(slot.at[upper], slot.at[upper], device(x, zz, y, c)) for zz in z_peers
    ]
    make_spread(spread)
    a2_f, b2_f = full_three(fac_all, a_f, b_f, d_f)
    z_db = [
        w.send(slot.at[lower], slot.at[lower], device(x, zz, y, c)) for zz in z_peers
    ]
    make_bias(lengths, bias)
    a_o, b_o, d_o = full_two(out_all, own_o, z_o)
    full_end(fac_all, a2_f, b2_f, d_f)
    own_g, z_g = pair_z(wg, gate_all)
    arrive(z_da)
    a_d = same(down_all.at[:, y, x, upper], x_peer)
    arrive(d_f)
    saves = [w.local(fac_all, fac_out)]
    gain_rows(fac_all, gains)
    make_factors(x_in, gains, fac_all, n1, kept)
    a2_o, b2_o = full_three(out_all, a_o, b_o, d_o)
    arrive(z_db)
    b_d = same(down_all.at[:, y, x, lower], y_peer)
    saves.append(w.local(n1, n1_out))
    own_u, z_u = pair_z(wu, up_all)
    make_heads(kept, cos_ref, sin_ref, spread, q, k, v)
    for src, dst in (
        (kept, kept_out),
        (q, q_out),
        (k, k_out),
        (v, v_out),
        (bias, bias_out),
        (spread, spread_out),
    ):
        saves.append(w.local(src, dst))
    a_d.wait_recv()
    a2_d = same(down_all.at[:, y, :, upper], y_peer)
    full_end(out_all, a2_o, b2_o, d_o)
    attend_pairs(q, k, v, bias, mixed, 0, 2)
    b_d.wait_recv()
    b2_d = same(down_all.at[:, :, x, lower], x_peer)
    a_g, b_g = pair_two(gate_all, own_g, z_g)
    attend_pairs(q, k, v, bias, mixed, 2, 5)
    a2_g, b2_g = pair_three(gate_all, a_g, b_g)
    a_u, b_u = pair_two(up_all, own_u, z_u)
    attend_pairs(q, k, v, bias, mixed, 5, 8)
    saves.append(w.local(mixed, mixed_out))
    arrive(d_o)
    saves.append(w.local(out_all, out_out))
    make_resid(x_in, mixed, out_all, gains, resid, n2)
    saves.append(w.local(resid, resid_out))
    saves.append(w.local(n2, n2_out))
    a2_u, b2_u = pair_three(up_all, a_u, b_u)
    arrive([a2_d, b2_d, a2_g, b2_g, a2_u, b2_u])
    for copy in saves:
        copy.wait()
    w.drain()


def front_all(inputs, doc_lengths, fac, wo, wd, wg, wu):
    anywhere, vmem = pl.BlockSpec(memory_space=pl.ANY), pl.BlockSpec(memory_space=pltpu.VMEM)
    fac_shape, out_shape = (2, 4, 2, 2, 32, FACTOR_PAD), (2, 4, 2, 2, 32, 1024)
    row = (512, 1024)
    outs = [
        ((4, 2, 2, PAD_UNITS, 1024), BF16),
        ((2, 4, 2, 2, 32, HALF), BF16),
        ((2, 4, 2, 2, 32, HALF), BF16),
        (fac_shape, BF16),
        (out_shape, BF16),
        (row, BF16),
        ((512, KEPT), F32),
        (row, BF16),
        (row, BF16),
        (row, BF16),
        (row, BF16),
        (row, F32),
        (row, BF16),
        ((512, 512), F32),
        ((8, 128, 1024), BF16),
        ((8, 1024), F32),
    ]
    scratch = [
        (fac_shape, BF16),
        (out_shape, BF16),
        (row, BF16),
        ((512, KEPT), F32),
        (row, BF16),
        (row, BF16),
        (row, BF16),
        (row, BF16),
        (row, F32),
        (row, BF16),
        ((512, 512), F32),
        ((8, 128, 1024), BF16),
    ]
    return pl.pallas_call(
        front_kernel,
        out_shape=[jax.ShapeDtypeStruct(*o) for o in outs],
        in_specs=[vmem, pl.BlockSpec(memory_space=pltpu.SMEM)] + [anywhere] * 5,
        out_specs=[anywhere] * 15 + [vmem],
        scratch_shapes=[pltpu.VMEM(*s) for s in scratch]
        + [
            pltpu.SemaphoreType.DMA((72,)),
            pltpu.SemaphoreType.DMA((72,)),
            pltpu.SemaphoreType.DMA((20,)),
        ],
        compiler_params=pltpu.CompilerParams(
            collective_id=0, has_side_effects=True, vmem_limit_bytes=61 * MIB
        ),
        name="front_all",
    )(inputs, doc_lengths, fac, wo, wd, wg, wu)


def head_grads(q, q_t, k, v, mg, mg_t, bias, dq, dkv_t, first, last):
    def pair(p, _):
        at = pl.multiple_of(p * 128, 128)
        lanes = pl.ds(at, 128)
        for start, extent in ((256, 512), (0, 256)):
            rows, cols = pl.ds(start, 256), pl.ds(0, extent)
            q_rows, mg_rows = q[rows, lanes], mg[rows, lanes]
            k_cols, v_cols = k[cols, lanes], v[cols, lanes]
            halves = []
            for half in (0, 1):
                own = pl.ds(pl.multiple_of(at + half * 64, 64), 64)
                probs = soft(only(q_rows, half), k_cols, bias[rows, cols])
                probs_grad = dot(only(mg_rows, half), v_cols, NT)
                inner = jnp.sum(probs * probs_grad, axis=-1, keepdims=True)
                score_grad = (probs * (probs_grad - inner)).astype(BF16)
                dv = dot(mg_t[own, rows], probs.astype(BF16))
                dk = dot(q_t[own, rows], score_grad)
                if start:
                    dkv_t[own, 0:512] = dk
                    dkv_t[own, 512:1024] = dv
                else:
                    dkv_t[own, 0:256] += dk
                    dkv_t[own, 512:768] += dv
                halves.append(dot(score_grad, k_cols))
            low = lane_iota(256) < 64
            dq[rows, lanes] = jnp.where(low, halves[0], halves[1]) * HEAD_DIM**-0.5
        return 0

    lax.fori_loop(first, last, pair, 0)


def fold(product):
    total = product[:, 0:128]
    for j in range(1, 8):
        total += product[:, j * 128 : (j + 1) * 128]
    return total + pltpu.roll(total, 64, 1)


def rank_grads(full, terms, ranks, duplicates, spread):
    a_grad, b_grads = jnp.zeros((full.shape[0], 128), F32), []
    for r, twice in zip(ranks, duplicates, strict=True):
        spread_r = spread[r]
        a_grad += dot((full * eight(twice)).astype(BF16), spread_r, NT)
        b_grads.append(fold(full * expand(terms, spread_r)))
    return a_grad, b_grads


def pick(low_half, high_half):
    return jnp.where(lane_iota(low_half.shape[0]) < 64, low_half, high_half)


def factor_grads(dq, dkv_t, kept, spread, fg, fg_at):
    def tile(i, _):
        at = pl.multiple_of(i * 128, 128)
        rows = pl.ds(at, 128)
        out = pl.ds(pl.multiple_of(fg_at + i * 128, 128), 128)
        cos_rows, sin_rows = kept[rows, COS_LANES], kept[rows, SIN_LANES]

        def turn_back(part):
            return part * cos_rows - swapped(part) * sin_rows

        tiles = [kept[rows, pl.ds(j * 128, 128)] for j in range(5)]
        terms = two_terms(kept[rows, A_LANES])
        a_q, b_q = rank_grads(
            dq[rows, :],
            terms,
            range(RANK_Q),
            [both_halves(tiles[r // 2], r % 2) for r in range(RANK_Q)],
            spread,
        )
        for j in range(RANK_Q // 2):
            part = pick(b_q[2 * j], b_q[2 * j + 1]) * (1.0 / RANK_Q)
            fg[out, pl.ds(j * 128, 128)] = turn_back(part).astype(BF16)
        a_k, b_k = rank_grads(
            dkv_t[:, rows].T,
            terms,
            range(RANK_Q, RANK_Q + RANK_KV),
            [both_halves(tiles[3], r) for r in range(RANK_KV)],
            spread,
        )
        part = pick(b_k[0], b_k[1]) * (1.0 / RANK_KV)
        fg[out, pl.ds(384, 128)] = turn_back(part).astype(BF16)
        fg[out, A_LANES] = (a_q * (1.0 / RANK_Q) + a_k * (1.0 / RANK_KV)).astype(BF16)
        a_v, b_v = rank_grads(
            dkv_t[:, pl.ds(pl.multiple_of(512 + i * 128, 128), 128)].T,
            two_terms(kept[rows, V_LANES]),
            range(RANK_KV),
            [both_halves(tiles[4], r) for r in range(RANK_KV)],
            spread,
        )
        fg[out, pl.ds(512, 128)] = (pick(b_v[0], b_v[1]) * (1.0 / RANK_KV)).astype(BF16)
        fg[out, V_LANES] = (a_v * (1.0 / RANK_KV)).astype(BF16)
        return 0

    lax.fori_loop(0, 4, tile, 0)


def back_kernel(
    n2_in, cot_in, resid_in, gains, gate_hbm, up_hbm, down_hbm, fac_in, out_in, x_hbm,
    n1_in, kept_in, q_in, k_in, v_in, mixed_in, bias_in, spread_in,
    outputs, input_grad, gate_out, up_out, down_out, out_shard, fac_shard,
    n2, cot, out_acc, ng_acc, out_twin, ng_twin,
    g_buf, u_buf, d_buf, g1, u1, da1, db1, g2, u2, da2, db2, g3, u3, d3,
    po, po_twin, po_1a, po_1b, po_2a, po_2b, po_3,
    pf, pf_twin, pf_1a, pf_1b, pf_2a, pf_2b, pf_3,
    ss, rs, ls,
):
    x, z, y, c = place()
    x_peer, y_peer, twin = device(1 - x, z, y, c), device(x, z, 1 - y, c), device(x, z, y, 1 - c)
    z_peers = [lax.rem(z + step, 4) for step in (1, 2, 3)]
    w = Wires(ss, rs, ls)
    upper, lower = pl.ds(0, PAD_UNITS // 2), pl.ds(PAD_UNITS // 2, PAD_UNITS // 2)

    ones, twos = [], []
    for block in BLOCKS:
        cols = pl.ds(*block)
        ones.append(
            (
                w.make(u_buf.at[1 - x, :, :, :, cols], u1.at[:, :, :, cols], x_peer),
                w.make(g_buf.at[:, :, 1 - y, :, cols], g1.at[:, :, :, cols], y_peer),
            )
        )
        twos.append(
            (
                w.make(u_buf.at[x, :, 1 - y, :, cols], u2.at[:, :, cols], y_peer),
                w.make(g_buf.at[1 - x, :, y, :, cols], g2.at[:, :, cols], x_peer),
            )
        )
    n2_twin = w.make(n2_in, n2.at[512:1024], twin)
    cot_twin = w.make(cot_in, cot.at[512:1024], twin)
    ng_send = w.make(ng_acc.at[512:1024], ng_twin, twin)
    out_send = w.make(out_acc.at[512:1024], out_twin, twin)
    da_one = w.make(d_buf.at[:, 1 - y, :, upper], da1, y_peer)
    db_one = w.make(d_buf.at[:, :, 1 - x, lower], db1, x_peer)

    def phase_one(b):
        for copy in ones[b]:
            w.go(copy)

    def phase_two(b):
        cols = pl.ds(*BLOCKS[b])
        u, g = ones[b]
        u.wait_recv()

        def add_u(i, _):
            zz, yy = lax.div(i, 2), lax.rem(i, 2)
            add_low(u_buf.at[x, zz, yy, :, cols], u1.at[zz, yy, :, cols])
            return 0

        lax.fori_loop(0, 8, add_u, 0)
        w.go(twos[b][0])
        g.wait_recv()

        def add_g(i, _):
            xx, zz = lax.div(i, 4), lax.rem(i, 4)
            add_low(g_buf.at[xx, zz, y, :, cols], g1.at[xx, zz, :, cols])
            return 0

        lax.fori_loop(0, 8, add_g, 0)
        w.go(twos[b][1])

    def phase_three(b):
        u, g = twos[b]
        cols = pl.ds(*BLOCKS[b])
        last = []
        for copy, buf, two, three in ((u, u_buf, u2, u3), (g, g_buf, g2, g3)):
            copy.wait_recv()

            def add(i, _, buf=buf, two=two):
                add_low(buf.at[x, i, y, :, cols], two.at[i, :, cols])
                return 0

            lax.fori_loop(0, 4, add, 0)
            for core, rel in ((c, 0), (1 - c, 1)):
                rows = pl.ds(pl.multiple_of(core * 32, 32), 32)
                for step, zz in enumerate(z_peers):
                    last.append(
                        w.send(
                            buf.at[x, zz, y, rows, cols],
                            three.at[rel, step + 1, :, cols],
                            device(x, zz, y, core),
                        )
                    )
            rows = pl.ds(pl.multiple_of((1 - c) * 32, 32), 32)
            last.append(w.send(buf.at[x, z, y, rows, cols], three.at[1, 0, :, cols], twin))
        return last

    def finish(buf, three, out):
        rows = pl.ds(pl.multiple_of(c * 32, 32), 32)
        own = buf[x, z, y, rows, :].astype(F32)
        for step in (1, 2, 3):
            own += three[0, step].astype(F32)
        out[c] = own
        other = three[1, 0].astype(F32)
        for step in (1, 2, 3):
            other += three[1, step].astype(F32)
        out[1 - c] = other

    def down_two():
        da_one.wait_recv()
        db_one.wait_recv()

        def add(i, _):
            zz, s = lax.div(i, 2), lax.rem(i, 2)
            add_low(d_buf.at[zz, y, s, upper], da1.at[zz, s])
            add_low(d_buf.at[zz, s, x, lower], db1.at[zz, s])
            return 0

        lax.fori_loop(0, 8, add, 0)
        da = w.send(d_buf.at[:, y, 1 - x, upper], da2, x_peer)
        return da, w.send(d_buf.at[:, 1 - y, x, lower], db2, y_peer)

    def down_three(da, db):
        da.wait_recv()
        db.wait_recv()

        def add(i, _):
            add_low(d_buf.at[i, y, x, upper], da2.at[i])
            add_low(d_buf.at[i, y, x, lower], db2.at[i])
            return 0

        lax.fori_loop(0, 4, add, 0)
        return [
            w.send(d_buf.at[zz, y, x], d3.at[step], device(x, zz, y, c))
            for step, zz in enumerate(z_peers)
        ]

    first_rows, second_rows = pl.ds(0, 16), pl.ds(16, 16)

    def full_zero(buf, from_twin):
        return w.send(buf.at[:, :, :, 1 - c], from_twin, twin)

    def full_one(copy, buf, from_twin, one_a, one_b):
        copy.wait_recv()

        def add(i, _):
            xx, zz, yy = lax.div(i, 8), lax.rem(lax.div(i, 2), 4), lax.rem(i, 2)
            add_low(buf.at[xx, zz, yy, c], from_twin.at[xx, zz, yy])
            return 0

        lax.fori_loop(0, 16, add, 0)
        a = w.send(buf.at[:, :, 1 - y, c, first_rows], one_a, y_peer)
        return a, w.send(buf.at[1 - x, :, :, c, second_rows], one_b, x_peer)

    def full_two(a, b, buf, one_a, one_b, two_a, two_b):
        a.wait_recv()
        b.wait_recv()

        def add(i, _):
            s, zz = lax.div(i, 4), lax.rem(i, 4)
            add_low(buf.at[s, zz, y, c, first_rows], one_a.at[s, zz])
            add_low(buf.at[x, zz, s, c, second_rows], one_b.at[zz, s])
            return 0

        lax.fori_loop(0, 8, add, 0)
        a = w.send(buf.at[1 - x, :, y, c, first_rows], two_a, x_peer)
        return a, w.send(buf.at[x, :, 1 - y, c, second_rows], two_b, y_peer)

    def full_three(a, b, buf, two_a, two_b, three):
        a.wait_recv()
        b.wait_recv()

        def add(i, _):
            add_low(buf.at[x, i, y, c, first_rows], two_a.at[i])
            add_low(buf.at[x, i, y, c, second_rows], two_b.at[i])
            return 0

        lax.fori_loop(0, 4, add, 0)
        return [
            w.send(buf.at[x, zz, y, c], three.at[step], device(x, zz, y, c))
            for step, zz in enumerate(z_peers)
        ]

    def full_end(last, buf, three, out):
        arrive(last)
        out[...] = (
            buf[x, z, y, c].astype(F32)
            + three[0].astype(F32)
            + three[1].astype(F32)
            + three[2].astype(F32)
        )

    def feed_forward(n2_t, wg, wu, wd, hid, gg, ug, d_acc):
        own_n2 = w.local(n2_in, n2.at[0:512])
        own_cot = w.local(cot_in, cot.at[0:512])
        loads = []
        for start, size in BLOCKS:
            cols = pl.ds(start, size)
            loads.append(
                [
                    w.local(gate_hbm.at[:, cols], wg.at[:, cols]),
                    w.local(up_hbm.at[:, cols], wu.at[:, cols]),
                    w.local(down_hbm.at[cols], wd.at[cols]),
                ]
            )
        greet(x, z, y, c)
        w.go(n2_twin)
        w.go(cot_twin)
        own_n2.wait()
        own_cot.wait()

        def turn(i):
            rows = pl.ds(i * TILE, TILE)
            n2_t[:, rows] = n2[rows, :].T

        def forward(b, low, high):
            start, size = BLOCKS[b]
            cols = pl.ds(start, size)

            def tile(i, _):
                rows = pl.ds(pl.multiple_of(i * TILE, TILE), TILE)
                n2_rows, cot_rows = n2[rows, :], cot[rows, :]
                gate = dot(n2_rows, wg[:, cols])
                up = dot(n2_rows, wu[:, cols])
                hid_grad = dot(cot_rows, wd[cols, :], NT)
                sig = jax.nn.sigmoid(gate)
                silu = gate * sig
                hidden = (silu * up).astype(BF16)
                gate_grad = (hid_grad * up * sig * (1.0 + gate * (1.0 - sig))).astype(BF16)
                up_grad = (hid_grad * silu).astype(BF16)
                hid[rows, 0:size] = hidden
                gg[rows, 0:size] = gate_grad
                ug[rows, 0:size] = up_grad
                out_part = dot(hidden, wd[cols, :])
                ng_part = dot(gate_grad, wg[:, cols], NT) + dot(up_grad, wu[:, cols], NT)
                if b == 0:
                    out_acc[rows, :] = out_part
                    ng_acc[rows, :] = ng_part
                else:
                    out_acc[rows, :] += out_part
                    ng_acc[rows, :] += ng_part
                return 0

            lax.fori_loop(low, high, tile, 0)

        def weight_grads(b):
            start, size = BLOCKS[b]
            cols = pl.ds(start, size)

            def side(i, _):
                rows = pl.ds(pl.multiple_of(i * 512, 512), 512)
                part = dot(n2_t[rows, :], ug[:, 0:size])
                u_buf[i, :, :, :, cols] = part.astype(BF16).reshape(4, 2, 64, size)
                part = dot(n2_t[rows, :], gg[:, 0:size])
                g_buf[i, :, :, :, cols] = part.astype(BF16).reshape(4, 2, 64, size)
                return 0

            lax.fori_loop(0, 2, side, 0)
            d_acc[cols, :] = dot(hid[:, 0:size], cot[...], TN)

        for copy in loads[0]:
            copy.wait()
        forward(0, 0, 2)
        turn(0)
        turn(1)
        arrive([n2_twin, cot_twin])
        forward(0, 2, 4)
        turn(2)
        turn(3)
        weight_grads(0)
        phase_one(0)
        for copy in loads[1]:
            copy.wait()
        forward(1, 0, 4)
        weight_grads(1)
        phase_one(1)
        phase_two(0)
        for copy in loads[2]:
            copy.wait()
        forward(2, 2, 4)
        w.go(ng_send)
        w.go(out_send)
        forward(2, 0, 2)
        weight_grads(2)
        phase_one(2)

        def spread_rows(s, _):
            rows = d_acc[pl.ds(pl.multiple_of(s * OWN_UNITS, 8), OWN_UNITS), :]
            rows = jnp.concatenate(
                [rows, jnp.zeros((PAD_UNITS - OWN_UNITS, rows.shape[1]), F32)], axis=0
            )
            d_buf[lax.div(s, 4), lax.rem(lax.div(s, 2), 2), lax.rem(s, 2)] = rows.astype(BF16)
            return 0

        lax.fori_loop(0, 16, spread_rows, 0)
        w.go(da_one)
        w.go(db_one)

    pl.run_scoped(
        feed_forward,
        pltpu.VMEM((1024, 1024), BF16),
        pltpu.VMEM((1024, HALF), BF16),
        pltpu.VMEM((1024, HALF), BF16),
        pltpu.VMEM((HALF, 1024), BF16),
        pltpu.VMEM((1024, 512), BF16),
        pltpu.VMEM((1024, 512), BF16),
        pltpu.VMEM((1024, 512), BF16),
        pltpu.VMEM((HALF, 1024), F32),
    )
    branch, mg = cot.at[0:512], cot.at[512:1024]

    def attention(
        resid, x_in, mixed, out_w, q, k, v, bias, kept, spread, n1, q_t, mg_t, gain_two,
        gate_sum, up_sum, d_sum,
    ):
        swap = w.make(d_sum, down_out, device(1 - x, z, y, 1 - c))
        keep = pltpu.make_async_copy(d_sum, down_out, w.local_sems.at[w.held])
        w.held += 1

        def down_end(last):
            arrive(last)
            d_sum[...] = (
                d_buf[z, y, x].astype(F32)
                + d3[0].astype(F32)
                + d3[1].astype(F32)
                + d3[2].astype(F32)
            )

            @pl.when(x == c)
            def _():
                keep.start()

            @pl.when(x != c)
            def _():
                swap.start()

        def down_close():
            @pl.when(x == c)
            def _():
                keep.wait()

            @pl.when(x != c)
            def _():
                swap.wait()

        loads = [
            w.local(src, dst)
            for src, dst in (
                (resid_in, resid),
                (mixed_in, mixed),
                (out_in, out_w),
                (q_in, q),
                (k_in, k),
                (v_in, v),
                (bias_in, bias),
                (kept_in, kept),
                (spread_in, spread),
                (n1_in, n1),
                (x_hbm, x_in),
            )
        ]
        phase_two(1)
        loads[0].wait()
        arrive([ng_send, out_send])

        def close(i, total):
            rows = pl.ds(pl.multiple_of(i * 128, 128), 128)
            base = resid[rows, :]
            n2[rows, :] = (base + out_acc[rows, :] + out_twin[rows, :]).astype(BF16)
            grad = ng_acc[rows, :] + ng_twin[rows, :]
            scale = lax.rsqrt(jnp.mean(base * base, axis=-1, keepdims=True) + EPSILON)
            unit = base * scale
            unit_grad = grad * gains[1:2, :]
            back = scale * (unit_grad - unit * jnp.mean(unit_grad * unit, axis=-1, keepdims=True))
            full = cot[rows, :].astype(F32) + back
            out_acc[rows, :] = full
            branch[rows, :] = full.astype(BF16)
            return total + jnp.sum((grad * unit).reshape(16, 8, 1024), axis=0)

        gain_two[...] = lax.fori_loop(0, 4, close, jnp.zeros((8, 1024), F32))
        results = [w.local(n2.at[0:512], outputs)]
        last = phase_three(0)
        for copy in loads[1:4]:
            copy.wait()
        for side in range(2):
            part = dot(mixed[:, side * 512 : (side + 1) * 512], branch[...], TN)
            po[side] = part.astype(BF16).reshape(4, 2, 2, 32, 1024)
        o_zero = full_zero(po, po_twin)
        phase_two(2)
        for i in range(2):
            rows = pl.ds(i * 256, 256)
            part = dot(branch[rows, :], out_w[...].reshape(1024, 1024), NT).astype(BF16)
            mg[rows, :] = part
            mg_t[:, rows] = part.T
            q_t[:, rows] = q[rows, :].T
        fac_w = out_w.at[:, :, :, :, :, 0:FACTOR_PAD]
        loads.append(w.local(fac_in, fac_w))
        for copy in loads[4:7]:
            copy.wait()
        o_one = full_one(o_zero, po, po_twin, po_1a, po_1b)
        ng_send.wait_send()
        w.open = [copy for copy in w.open if copy is not ng_send]
        heads = (q, q_t, k, v, mg, mg_t, bias, out_twin, ng_acc)
        head_grads(*heads, 0, 1)
        last += phase_three(1)
        head_grads(*heads, 1, 3)
        d_two = down_two()
        head_grads(*heads, 3, 4)
        last += phase_three(2)
        head_grads(*heads, 4, 5)
        o_two = full_two(*o_one, po, po_1a, po_1b, po_2a, po_2b)
        head_grads(*heads, 5, 7)
        d_last = down_three(*d_two)
        head_grads(*heads, 7, 8)
        o_last = full_three(*o_two, po, po_2a, po_2b, po_3)
        for copy in loads[7:9]:
            copy.wait()
        results[0].wait()
        factor_grads(out_twin, ng_acc, kept, spread, n2, 512)
        fg = n2.at[512:1024, 0:FACTOR_PAD]
        for copy in loads[9:]:
            copy.wait()

        def first_norm(i, total):
            rows = pl.ds(pl.multiple_of(i * 128, 128), 128)
            incoming = dot(fg[rows, :], fac_w[...].reshape(1024, FACTOR_PAD), NT)
            vals = x_in[rows, :].astype(F32)
            scale = lax.rsqrt(jnp.mean(vals * vals, axis=-1, keepdims=True) + EPSILON)
            unit = vals * scale
            unit_grad = incoming * gains[0:1, :]
            back = scale * (unit_grad - unit * jnp.mean(unit_grad * unit, axis=-1, keepdims=True))
            out_acc[rows, :] += back
            return total + jnp.sum((incoming * unit).reshape(16, 8, 1024), axis=0)

        gain_one = jnp.sum(lax.fori_loop(0, 4, first_norm, jnp.zeros((8, 1024), F32)), axis=0, keepdims=True)
        place_row = row_iota(128, 1024)
        gain_tile = jnp.where(
            place_row == 32,
            gain_one,
            jnp.where(place_row == 33, jnp.sum(gain_two[...], axis=0, keepdims=True), 0.0),
        ).T
        for side in range(2):
            part = dot(n1[:, side * 512 : (side + 1) * 512], fg[...], TN)
            part = jnp.concatenate(
                [part[:, 0:768], part[:, 768:896] + gain_tile[side * 512 : (side + 1) * 512]], axis=1
            )
            pf[side] = part.astype(BF16).reshape(4, 2, 2, 32, FACTOR_PAD)
        f_zero = full_zero(pf, pf_twin)
        results.append(w.local(out_acc.at[0:512], input_grad))
        f_one = full_one(f_zero, pf, pf_twin, pf_1a, pf_1b)
        arrive(last)
        finish(u_buf, u3, up_sum)
        finish(g_buf, g3, gate_sum)
        results += [w.local(up_sum, up_out), w.local(gate_sum, gate_out)]
        down_end(d_last)
        f_two = full_two(*f_one, pf, pf_1a, pf_1b, pf_2a, pf_2b)
        shard = out_twin.at[0:32, :]
        full_end(o_last, po, po_3, shard)
        results.append(w.local(shard, out_shard))
        f_last = full_three(*f_two, pf, pf_2a, pf_2b, pf_3)
        down_close()
        shard = out_twin.at[32:64, 0:FACTOR_PAD]
        full_end(f_last, pf, pf_3, shard)
        results.append(w.local(shard, fac_shard))
        for copy in results[1:]:
            copy.wait()
        w.drain()

    pl.run_scoped(
        attention,
        pltpu.VMEM((512, 1024), F32),
        pltpu.VMEM((512, 1024), BF16),
        pltpu.VMEM((512, 1024), BF16),
        pltpu.VMEM((2, 4, 2, 2, 32, 1024), BF16),
        pltpu.VMEM((512, 1024), BF16),
        pltpu.VMEM((512, 1024), BF16),
        pltpu.VMEM((512, 1024), BF16),
        pltpu.VMEM((512, 512), F32),
        pltpu.VMEM((512, KEPT), F32),
        pltpu.VMEM((8, 128, 1024), BF16),
        pltpu.VMEM((512, 1024), BF16),
        pltpu.VMEM((1024, 512), BF16),
        pltpu.VMEM((1024, 512), BF16),
        pltpu.VMEM((8, 1024), F32),
        pltpu.VMEM((2, 32, HALF), F32),
        pltpu.VMEM((2, 32, HALF), F32),
        pltpu.VMEM((PAD_UNITS, 1024), F32),
    )


def back_all(*args):
    anywhere, vmem = pl.BlockSpec(memory_space=pl.ANY), pl.BlockSpec(memory_space=pltpu.VMEM)
    big = lambda *shape: pltpu.VMEM(shape, BF16)
    wide = lambda *shape: pltpu.VMEM(shape, F32)
    half = PAD_UNITS // 2

    def full_scratch(width):
        return [
            big(2, 4, 2, 2, 32, width), big(2, 4, 2, 32, width),
            big(2, 4, 16, width), big(4, 2, 16, width), big(4, 16, width), big(4, 16, width),
            big(3, 32, width),
        ]

    return pl.pallas_call(
        back_kernel,
        out_shape=[
            jax.ShapeDtypeStruct((512, 1024), BF16),
            jax.ShapeDtypeStruct((512, 1024), F32),
            jax.ShapeDtypeStruct((2, 32, HALF), F32),
            jax.ShapeDtypeStruct((2, 32, HALF), F32),
            jax.ShapeDtypeStruct((PAD_UNITS, 1024), F32),
            jax.ShapeDtypeStruct((32, 1024), F32),
            jax.ShapeDtypeStruct((32, FACTOR_PAD), F32),
        ],
        in_specs=[anywhere] * 3 + [vmem] + [anywhere] * 14,
        out_specs=[anywhere] * 7,
        scratch_shapes=[
            big(1024, 1024), big(1024, 1024),
            wide(1024, 1024), wide(1024, 1024), wide(512, 1024), wide(512, 1024),
            big(2, 4, 2, 64, HALF), big(2, 4, 2, 64, HALF), big(4, 2, 2, PAD_UNITS, 1024),
            big(2, 4, 64, HALF), big(4, 2, 64, HALF), big(4, 2, half, 1024), big(4, 2, half, 1024),
            big(4, 64, HALF), big(4, 64, HALF), big(4, half, 1024), big(4, half, 1024),
            big(2, 4, 32, HALF), big(2, 4, 32, HALF), big(3, PAD_UNITS, 1024),
            *full_scratch(1024),
            *full_scratch(FACTOR_PAD),
            pltpu.SemaphoreType.DMA((96,)),
            pltpu.SemaphoreType.DMA((96,)),
            pltpu.SemaphoreType.DMA((32,)),
        ],
        compiler_params=pltpu.CompilerParams(
            collective_id=1, has_side_effects=True, vmem_limit_bytes=62 * MIB
        ),
        name="back_all",
    )(*args)


def local_paired(
    inputs, doc_lengths, w_aq, w_bq, w_ak, w_bk, w_av, w_bv,
    w_out, w_gate, w_up, w_down, gain_attn, gain_ffn, cotangent,
):
    spare = jnp.zeros((32, FACTOR_PAD - 802), BF16)
    fac = jnp.concatenate(
        [w_bq, w_bk, w_bv, w_aq, w_ak, w_av, gain_attn[:, None], gain_ffn[:, None], spare], axis=1
    )
    wd = jnp.pad(w_down, ((0, PAD_UNITS - OWN_UNITS), (0, 0)))
    (
        down_all, gate_all, up_all, fac_all, out_all, n1, kept,
        q, k, v, mixed, resid, n2, bias, spread, gains,
    ) = front_all(inputs, doc_lengths, fac, w_out, wd, w_gate, w_up)
    down_w = down_all.reshape(16, PAD_UNITS, 1024)[:, :OWN_UNITS].reshape(HALF, 1024)
    outputs, input_grad, gate_shard, up_shard, down_shard, out_shard, shard = back_all(
        n2, cotangent, resid, gains,
        gate_all.reshape(1024, HALF), up_all.reshape(1024, HALF), down_w, fac_all, out_all, inputs,
        n1, kept, q, k, v, mixed, bias, spread,
    )
    return (
        outputs,
        input_grad,
        shard[:, 640:736],
        shard[:, :384],
        shard[:, 736:768],
        shard[:, 384:512],
        shard[:, 768:800],
        shard[:, 512:640],
        out_shard,
        jnp.concatenate([gate_shard[0], gate_shard[1]], axis=1),
        jnp.concatenate([up_shard[0], up_shard[1]], axis=1),
        down_shard[:OWN_UNITS],
        shard[:, 800],
        shard[:, 801],
    )


def solution(mesh):
    return jax.shard_map(
        local_paired if fits_pairs(mesh) else local,
        mesh=mesh,
        in_specs=(
            P(("dp", "fsdp"), None),
            P(("dp", "fsdp"), None),
            P(("dp", "fsdp"), None),
            P(("dp", "fsdp"), None),
            P(("dp", "fsdp"), None),
            P(("dp", "fsdp"), None),
            P(("dp", "fsdp"), None),
            P(("dp", "fsdp"), None),
            P(("dp", "fsdp"), None),
            P(("dp", "fsdp"), None),
            P(("dp", "fsdp"), None),
            P(("dp", "fsdp"), None),
            P(("dp", "fsdp")),
            P(("dp", "fsdp")),
            P(("dp", "fsdp"), None),
        ),
        out_specs=(
            P(("dp", "fsdp"), None),
            P(("dp", "fsdp"), None),
            P(("dp", "fsdp"), None),
            P(("dp", "fsdp"), None),
            P(("dp", "fsdp"), None),
            P(("dp", "fsdp"), None),
            P(("dp", "fsdp"), None),
            P(("dp", "fsdp"), None),
            P(("dp", "fsdp"), None),
            P(("dp", "fsdp"), None),
            P(("dp", "fsdp"), None),
            P(("dp", "fsdp"), None),
            P(("dp", "fsdp")),
            P(("dp", "fsdp")),
        ),
        check_vma=False,
    )
```

```python
import math

import jax
import jax.numpy as jnp
from jax import lax
from jax.experimental import pallas as pl
from jax.experimental.pallas import tpu as pltpu
from jax.sharding import PartitionSpec as P

HEADS = 16
HEAD_DIM = 64
RANK_Q = 6
RANK_KV = 2
FF = 2816


EPSILON = 1e-06
PRECISE = lax.Precision.HIGHEST


def factor_columns():
    return [
        RANK_Q * HEADS,
        RANK_Q * HEAD_DIM,
        RANK_KV * HEADS,
        RANK_KV * HEAD_DIM,
        RANK_KV * HEADS,
        RANK_KV * HEAD_DIM,
    ]


def split_columns(matrix):
    pieces = []
    offset = 0
    for columns in factor_columns():
        pieces.append(matrix[:, offset : offset + columns])
        offset += columns
    return pieces


def doc_layout(lengths, length):
    order = jnp.arange(lengths.shape[0], dtype=jnp.int32)
    doc_ends = jnp.sum(jnp.where(order[:, None] >= order[None, :], lengths[None, :], 0), axis=1)
    doc_starts = doc_ends - lengths
    places = jnp.arange(length, dtype=jnp.int32)
    segment = jnp.sum((places[:, None] >= doc_ends[None, :]).astype(jnp.int32), axis=1)
    owner = segment[:, None] == jnp.arange(lengths.shape[0], dtype=jnp.int32)[None, :]
    doc_first = jnp.sum(jnp.where(owner, doc_starts[None, :], 0), axis=1)
    return (segment, (places - doc_first).astype(jnp.float32))


def rotation(places):
    halfway = HEAD_DIM // 2
    freqs = jnp.exp(-math.log(10000.0) * jnp.arange(halfway, dtype=jnp.float32) / halfway)
    angles = places[..., None] * freqs
    return (jnp.cos(angles), jnp.sin(angles))


def rotate(factor, cos_table, sin_table):
    halfway = factor.shape[-1] // 2
    front_part = factor[..., :halfway]
    back_part = factor[..., halfway:]
    cos_part = cos_table[..., None, :]
    sin_part = sin_table[..., None, :]
    return jnp.concatenate(
        [
            front_part * cos_part - back_part * sin_part,
            front_part * sin_part + back_part * cos_part,
        ],
        axis=-1,
    )


def normalize(values, gain):
    scaling = lax.rsqrt(jnp.mean(values * values, axis=-1, keepdims=True) + EPSILON)
    unit_vals = values * scaling
    return (unit_vals * gain, unit_vals, scaling)


def norm_back(incoming, unit_vals, scaling, gain):
    unit_grad = incoming * gain
    grad_in = scaling * (
        unit_grad - unit_vals * jnp.mean(unit_grad * unit_vals, axis=-1, keepdims=True)
    )
    return (grad_in, jnp.sum(incoming * unit_vals, axis=0))


def block_scores(query_part, keys_low, seg_part, segment, place_part, places):
    scaling = HEAD_DIM ** (-0.5)
    scores = (
        jnp.einsum("thd,shd->hts", query_part, keys_low, preferred_element_type=jnp.float32)
        * scaling
    )
    allowed = (seg_part[:, None] == segment[None, :]) & (places[None, :] <= place_part[:, None])
    return jnp.where(allowed[None], scores, -1e30)


def attend_forward(queries, keys_low, values, segment):
    length = queries.shape[0]
    block_rows = min(512, length)
    places = jnp.arange(length, dtype=jnp.int32)

    def one_block(block_index):
        masked = block_scores(queries, keys_low, segment, segment, places, places)
        row_peak = jnp.max(masked, axis=-1, keepdims=True)
        exp_terms = jnp.exp(masked - row_peak)
        row_total = jnp.sum(exp_terms, axis=-1, keepdims=True)
        attn_probs = (exp_terms / row_total).astype(jnp.bfloat16)
        attended = jnp.einsum(
            "hts,shd->thd", attn_probs, values, preferred_element_type=jnp.float32
        )
        return (attended, (row_peak + jnp.log(row_total))[..., 0])

    attended, log_totals = lax.map(one_block, jnp.arange(length // block_rows, dtype=jnp.int32))
    return (attended.reshape(length, HEADS, HEAD_DIM), log_totals)


def attend_backward(queries, keys_low, values, segment, log_totals, mixed_grad):
    length = queries.shape[0]
    block_rows = min(512, length)
    places = jnp.arange(length, dtype=jnp.int32)
    scaling = HEAD_DIM ** (-0.5)

    def one_block(running, block_index):
        key_grad, value_grad = running
        masked = block_scores(queries, keys_low, segment, segment, places, places)
        attn_probs = jnp.exp(masked - log_totals[block_index][..., None])
        probs_low = attn_probs.astype(jnp.bfloat16)
        value_grad = value_grad + jnp.einsum(
            "hts,thd->shd", probs_low, mixed_grad, preferred_element_type=jnp.float32
        )
        probs_grad = jnp.einsum(
            "thd,shd->hts", mixed_grad, values, preferred_element_type=jnp.float32
        )
        inner_sum = jnp.sum(attn_probs * probs_grad, axis=-1, keepdims=True)
        score_grad = (attn_probs * (probs_grad - inner_sum)).astype(jnp.bfloat16)
        query_grad = (
            jnp.einsum("hts,shd->thd", score_grad, keys_low, preferred_element_type=jnp.float32)
            * scaling
        )
        key_grad = (
            key_grad
            + jnp.einsum("hts,thd->shd", score_grad, queries, preferred_element_type=jnp.float32)
            * scaling
        )
        return ((key_grad, value_grad), query_grad)

    empty = jnp.zeros((length, HEADS, HEAD_DIM), jnp.float32)
    (key_grad, value_grad), query_grad = lax.scan(
        one_block, (empty, empty), jnp.arange(length // block_rows, dtype=jnp.int32)
    )
    return (query_grad.reshape(length, HEADS, HEAD_DIM), key_grad, value_grad)


def factor_back(full_grad, a_part, b_part, rank_count):
    a_grad = jnp.einsum("thd,trd->trh", full_grad, b_part, precision=PRECISE) / rank_count
    b_grad = jnp.einsum("thd,trh->trd", full_grad, a_part, precision=PRECISE) / rank_count
    return (a_grad, b_grad)


def local(
    inputs,
    doc_lengths,
    w_aq,
    w_bq,
    w_ak,
    w_bk,
    w_av,
    w_bv,
    w_out,
    w_gate,
    w_up,
    w_down,
    gain_attn,
    gain_ffn,
    cotangent,
):
    length = inputs.shape[0]
    joined_local = jnp.concatenate([w_aq, w_bq, w_ak, w_bk, w_av, w_bv], axis=1)
    factor_w, out_w, gain_one = (
        lax.all_gather(joined_local, ("dp", "fsdp"), axis=0, tiled=True),
        lax.all_gather(w_out, ("dp", "fsdp"), axis=0, tiled=True),
        lax.all_gather(gain_attn, ("dp", "fsdp"), axis=0, tiled=True),
    )
    segment, places = doc_layout(doc_lengths[0], length)
    cos_table, sin_table = rotation(places)
    start_vals = inputs.astype(jnp.float32)
    normed_one, unit_one, scale_one = normalize(start_vals, gain_one.astype(jnp.float32))
    normed_low = normed_one.astype(jnp.bfloat16)
    factors = jnp.dot(normed_low, factor_w, preferred_element_type=jnp.float32)
    pieces = split_columns(factors)
    a_q = pieces[0].reshape(length, RANK_Q, HEADS)
    b_q = pieces[1].reshape(length, RANK_Q, HEAD_DIM)
    a_k = pieces[2].reshape(length, RANK_KV, HEADS)
    b_k = pieces[3].reshape(length, RANK_KV, HEAD_DIM)
    a_v = pieces[4].reshape(length, RANK_KV, HEADS)
    b_v = pieces[5].reshape(length, RANK_KV, HEAD_DIM)
    bq_rot = rotate(b_q, cos_table, sin_table)
    bk_rot = rotate(b_k, cos_table, sin_table)
    queries = (jnp.einsum("trh,trd->thd", a_q, bq_rot, precision=PRECISE) / RANK_Q).astype(
        jnp.bfloat16
    )
    keys_low = (jnp.einsum("trh,trd->thd", a_k, bk_rot, precision=PRECISE) / RANK_KV).astype(
        jnp.bfloat16
    )
    values = (jnp.einsum("trh,trd->thd", a_v, b_v, precision=PRECISE) / RANK_KV).astype(
        jnp.bfloat16
    )
    attended, log_totals = attend_forward(queries, keys_low, values, segment)
    mixed = attended.astype(jnp.bfloat16).reshape(length, HEADS * HEAD_DIM)
    resid = start_vals + jnp.dot(mixed, out_w, preferred_element_type=jnp.float32)
    gate_w, up_w, down_w, gain_two = (
        lax.all_gather(w_gate, ("dp", "fsdp"), axis=0, tiled=True),
        lax.all_gather(w_up, ("dp", "fsdp"), axis=0, tiled=True),
        lax.all_gather(w_down, ("dp", "fsdp"), axis=0, tiled=True),
        lax.all_gather(gain_ffn, ("dp", "fsdp"), axis=0, tiled=True),
    )
    normed_two, unit_two, scale_two = normalize(resid, gain_two.astype(jnp.float32))
    normed_two_low = normed_two.astype(jnp.bfloat16)
    gate_act = jnp.dot(normed_two_low, gate_w, preferred_element_type=jnp.float32)
    up_act = jnp.dot(normed_two_low, up_w, preferred_element_type=jnp.float32)
    hidden = (jax.nn.silu(gate_act) * up_act).astype(jnp.bfloat16)
    result = resid + jnp.dot(hidden, down_w, preferred_element_type=jnp.float32)
    outputs = result.astype(jnp.bfloat16)
    gate_w, up_w, down_w, gain_two = (
        lax.all_gather(w_gate, ("dp", "fsdp"), axis=0, tiled=True),
        lax.all_gather(w_up, ("dp", "fsdp"), axis=0, tiled=True),
        lax.all_gather(w_down, ("dp", "fsdp"), axis=0, tiled=True),
        lax.all_gather(gain_ffn, ("dp", "fsdp"), axis=0, tiled=True),
    )
    hidden_grad = jnp.einsum("tc,fc->tf", cotangent, down_w, preferred_element_type=jnp.float32)
    down_wgrad = jnp.einsum("tf,tc->fc", hidden, cotangent, preferred_element_type=jnp.float32)
    sig_vals = jax.nn.sigmoid(gate_act)
    gate_grad = (hidden_grad * up_act * sig_vals * (1.0 + gate_act * (1.0 - sig_vals))).astype(
        jnp.bfloat16
    )
    up_grad = (hidden_grad * jax.nn.silu(gate_act)).astype(jnp.bfloat16)
    normed_two_grad = jnp.einsum("tf,cf->tc", gate_grad, gate_w, preferred_element_type=jnp.float32)
    normed_two_grad = normed_two_grad + jnp.einsum(
        "tf,cf->tc", up_grad, up_w, preferred_element_type=jnp.float32
    )
    resid_norm_grad, gain_two_grad = norm_back(
        normed_two_grad, unit_two, scale_two, gain_two.astype(jnp.float32)
    )
    resid_grad = cotangent.astype(jnp.float32) + resid_norm_grad
    gate_rows = jnp.einsum(
        "tc,tf->cf", normed_two_low, gate_grad, preferred_element_type=jnp.float32
    )
    up_rows = jnp.einsum("tc,tf->cf", normed_two_low, up_grad, preferred_element_type=jnp.float32)
    gate_up_shard = lax.psum_scatter(
        jnp.concatenate([gate_rows, up_rows], axis=1),
        ("dp", "fsdp"),
        scatter_dimension=0,
        tiled=True,
    )
    gate_shard = gate_up_shard[:, :FF]
    up_shard = gate_up_shard[:, FF:]
    down_shard, gain_two_shard = (
        lax.psum_scatter(down_wgrad, ("dp", "fsdp"), scatter_dimension=0, tiled=True),
        lax.psum_scatter(gain_two_grad, ("dp", "fsdp"), scatter_dimension=0, tiled=True),
    )
    factor_w, out_w, gain_one = (
        lax.all_gather(joined_local, ("dp", "fsdp"), axis=0, tiled=True),
        lax.all_gather(w_out, ("dp", "fsdp"), axis=0, tiled=True),
        lax.all_gather(gain_attn, ("dp", "fsdp"), axis=0, tiled=True),
    )
    branch_grad = resid_grad.astype(jnp.bfloat16)
    out_wgrad = jnp.einsum("tc,td->cd", mixed, branch_grad, preferred_element_type=jnp.float32)
    mixed_grad = jnp.einsum("td,cd->tc", branch_grad, out_w, preferred_element_type=jnp.float32)
    mixed_grad = mixed_grad.astype(jnp.bfloat16).reshape(length, HEADS, HEAD_DIM)
    query_grad, key_grad, value_grad = attend_backward(
        queries, keys_low, values, segment, log_totals, mixed_grad
    )
    a_q_grad, bq_rot_grad = factor_back(query_grad, a_q, bq_rot, RANK_Q)
    a_k_grad, bk_rot_grad = factor_back(key_grad, a_k, bk_rot, RANK_KV)
    a_v_grad, b_v_grad = factor_back(value_grad, a_v, b_v, RANK_KV)
    neg_sin = -sin_table
    b_q_grad = rotate(bq_rot_grad, cos_table, neg_sin)
    b_k_grad = rotate(bk_rot_grad, cos_table, neg_sin)
    factor_grad = jnp.concatenate(
        [
            part.reshape(length, -1)
            for part in (a_q_grad, b_q_grad, a_k_grad, b_k_grad, a_v_grad, b_v_grad)
        ],
        axis=1,
    ).astype(jnp.bfloat16)
    factor_wgrad = jnp.einsum(
        "td,tc->dc", normed_low, factor_grad, preferred_element_type=jnp.float32
    )
    normed_one_grad = jnp.einsum(
        "tc,dc->td", factor_grad, factor_w, preferred_element_type=jnp.float32
    )
    input_norm_grad, gain_one_grad = norm_back(
        normed_one_grad, unit_one, scale_one, gain_one.astype(jnp.float32)
    )
    input_grad = resid_grad + input_norm_grad
    factor_shard, out_shard, gain_one_shard = (
        lax.psum_scatter(factor_wgrad, ("dp", "fsdp"), scatter_dimension=0, tiled=True),
        lax.psum_scatter(out_wgrad, ("dp", "fsdp"), scatter_dimension=0, tiled=True),
        lax.psum_scatter(gain_one_grad, ("dp", "fsdp"), scatter_dimension=0, tiled=True),
    )
    shard_pieces = split_columns(factor_shard)
    return (
        outputs,
        input_grad,
        shard_pieces[0],
        shard_pieces[1],
        shard_pieces[2],
        shard_pieces[3],
        shard_pieces[4],
        shard_pieces[5],
        out_shard,
        gate_shard,
        up_shard,
        down_shard,
        gain_one_shard,
        gain_two_shard,
    )


MESH_IDS = pl.DeviceIdType.MESH
HALF = FF // 2
OWN_UNITS = 88
PAD_UNITS = 96
FACTOR_PAD = 896
MIB = 2**20


def fits_pairs(mesh):
    return dict(mesh.shape) == {"dp": 2, "fsdp": 16}


def place():
    x = lax.axis_index("dp")
    f = lax.axis_index("fsdp")
    return x, lax.div(f, 4), lax.rem(lax.div(f, 2), 2), lax.rem(f, 2)


def device(x, z, y, c):
    return (x, z * 4 + y * 2 + c)


def greet(x, z, y, c):
    partners = [
        device(x, z, y, 1 - c),
        device(1 - x, z, y, c),
        device(x, z, 1 - y, c),
        device(1 - x, z, y, 1 - c),
    ]
    for step in (1, 2, 3):
        other = lax.rem(z + step, 4)
        partners += [device(x, other, y, c), device(x, other, y, 1 - c)]
    barrier = pltpu.get_barrier_semaphore()
    for partner in partners:
        pl.semaphore_signal(barrier, inc=1, device_id=partner, device_id_type=MESH_IDS)
    pl.semaphore_wait(barrier, len(partners))


class Wires:
    def __init__(self, send_sems, recv_sems, local_sems):
        self.send_sems, self.recv_sems, self.local_sems = send_sems, recv_sems, local_sems
        self.sent, self.held = 0, 0
        self.open, self.shared = [], []

    def make(self, src, dst, to):
        at = self.sent
        self.sent += 1
        return pltpu.make_async_remote_copy(
            src_ref=src,
            dst_ref=dst,
            send_sem=self.send_sems.at[at],
            recv_sem=self.recv_sems.at[at],
            device_id=to,
            device_id_type=MESH_IDS,
        )

    def go(self, copy):
        copy.start()
        self.shared.append(copy)
        return copy

    def send(self, src, dst, to):
        copy = self.make(src, dst, to)
        copy.start()
        self.open.append(copy)
        return copy

    def local(self, src, dst):
        copy = pltpu.make_async_copy(src, dst, self.local_sems.at[self.held])
        self.held += 1
        copy.start()
        return copy

    def drain(self):
        for copy in self.open:
            copy.wait_send()
        self.open = []

    def drain_shared(self):
        for copy in self.shared:
            copy.wait_send()
        self.shared = []


def arrive(copies):
    for copy in copies:
        copy.wait_recv()


BLOCKS = ((0, 512), (512, 512), (1024, 384))
TILE = 256
NT = (((1,), (1,)), ((), ()))
TN = (((0,), (0,)), ((), ()))
F32, BF16 = jnp.float32, jnp.bfloat16


def dot(a, b, dims=None):
    if dims is None:
        return jnp.dot(a, b, preferred_element_type=F32)
    return lax.dot_general(a, b, dims, preferred_element_type=F32)


def add_low(dst, src):
    dst[...] = (dst[...].astype(F32) + src[...].astype(F32)).astype(BF16)


KEPT = 1152
COS_LANES = pl.ds(896, 128)
SIN_LANES = pl.ds(1024, 128)
A_LANES = pl.ds(640, 128)
V_LANES = pl.ds(768, 128)


def lane_iota(rows, lanes=128):
    return lax.broadcasted_iota(jnp.int32, (rows, lanes), 1)


def row_iota(rows, lanes=128):
    return lax.broadcasted_iota(jnp.int32, (rows, lanes), 0)


def doc_ends_of(lengths):
    one = lengths[0, 0]
    two = one + lengths[0, 1]
    return one, two, two + lengths[0, 2]


def make_tables(lengths, cos_ref, sin_ref):
    ends = doc_ends_of(lengths)

    def tile(i, _):
        rows = pl.ds(pl.multiple_of(i * 128, 128), 128)
        places = row_iota(128) + i * 128
        first = jnp.zeros((128, 128), jnp.int32)
        for end in ends:
            first = jnp.where(places >= end, end, first)
        lane = lane_iota(128)
        turn = lax.rem(lane, 32).astype(F32)
        freqs = jnp.exp(-math.log(10000.0) * turn / 32)
        angles = (places - first).astype(F32) * freqs
        cos_ref[rows, :] = jnp.cos(angles)
        sin_vals = jnp.sin(angles)
        sin_ref[rows, :] = jnp.where(lax.rem(lane, 64) < 32, -sin_vals, sin_vals)
        return 0

    lax.fori_loop(0, 4, tile, 0)


def make_bias(lengths, bias):
    ends = doc_ends_of(lengths)

    def tile(i, _):
        rows = pl.ds(pl.multiple_of(i * 128, 128), 128)
        t = row_iota(128, 512) + i * 128
        s = lane_iota(128, 512)
        own, key = jnp.zeros((128, 512), jnp.int32), jnp.zeros((128, 512), jnp.int32)
        for end in ends:
            own += (t >= end).astype(jnp.int32)
            key += (s >= end).astype(jnp.int32)
        bias[rows, :] = jnp.where((own == key) & (s <= t), 0.0, -1e30)
        return 0

    lax.fori_loop(0, 4, tile, 0)


def make_spread(spread):
    def rank(r, _):
        head = lax.div(lane_iota(128, 1024), HEAD_DIM) + r * HEADS
        spread[r] = jnp.where(row_iota(128, 1024) == head, 1.0, 0.0).astype(BF16)
        return 0

    lax.fori_loop(0, 8, rank, 0)


def swapped(tile):
    front = lax.rem(lane_iota(tile.shape[0]), 64) < 32
    return jnp.where(front, pltpu.roll(tile, 96, 1), pltpu.roll(tile, 32, 1))


def both_halves(tile, half):
    low = lane_iota(tile.shape[0]) < 64
    other = pltpu.roll(tile, 64, 1)
    return jnp.where(low, tile, other) if half == 0 else jnp.where(low, other, tile)


def two_terms(a):
    high = a.astype(BF16)
    return high, (a - high.astype(F32)).astype(BF16)


def expand(terms, spread_r):
    return dot(terms[0], spread_r) + dot(terms[1], spread_r)


def eight(tile):
    return jnp.concatenate([tile] * 8, axis=1)


def gain_rows(fac_all, gains):
    tile = fac_all[:, :, :, :, :, V_LANES].reshape(1024, 128).astype(F32)
    gains[...] = tile.T[32:40, :]


def make_factors(x_in, gains, fac_all, n1, kept):
    def tile(i, _):
        rows = pl.ds(pl.multiple_of(i * 256, 256), 256)
        vals = x_in[rows, :].astype(F32)
        scale = lax.rsqrt(jnp.mean(vals * vals, axis=-1, keepdims=True) + EPSILON)
        low = (vals * scale * gains[0:1, :]).astype(BF16)
        n1[rows, :] = low
        kept[rows, 0:FACTOR_PAD] = dot(low, fac_all[...].reshape(1024, FACTOR_PAD))
        return 0

    lax.fori_loop(0, 2, tile, 0)


def make_heads(kept, cos_ref, sin_ref, spread, q, k, v, first, last):
    def tile(i, _):
        rows = pl.ds(pl.multiple_of(i * 128, 128), 128)
        turned = []
        for j in range(4):
            lanes = pl.ds(j * 128, 128)
            part = kept[rows, lanes]
            part = part * cos_ref[rows, :] + swapped(part) * sin_ref[rows, :]
            kept[rows, lanes] = part
            turned.append(part)
        terms = two_terms(kept[rows, A_LANES])
        total = jnp.zeros((128, 1024), F32)
        for r in range(RANK_Q):
            total += expand(terms, spread[r]) * eight(both_halves(turned[r // 2], r % 2))
        q[rows, :] = (total * (1.0 / RANK_Q)).astype(BF16) * BF16(HEAD_DIM**-0.5)
        total = jnp.zeros((128, 1024), F32)
        for r in range(RANK_KV):
            total += expand(terms, spread[RANK_Q + r]) * eight(both_halves(turned[3], r))
        k[rows, :] = (total * (1.0 / RANK_KV)).astype(BF16)
        terms = two_terms(kept[rows, V_LANES])
        plain = kept[rows, pl.ds(512, 128)]
        total = jnp.zeros((128, 1024), F32)
        for r in range(RANK_KV):
            total += expand(terms, spread[r]) * eight(both_halves(plain, r))
        v[rows, :] = (total * (1.0 / RANK_KV)).astype(BF16)
        return 0

    lax.fori_loop(first, last, tile, 0)


def only(tile, half):
    low = lane_iota(tile.shape[0]) < 64
    keep = low if half == 0 else jnp.logical_not(low)
    return jnp.where(keep, tile, jnp.zeros_like(tile))


def soft(q_rows, k_cols, bias_block):
    scores = dot(q_rows, k_cols, NT) + bias_block
    terms = jnp.exp(scores - jnp.max(scores, axis=-1, keepdims=True))
    return terms * (1.0 / jnp.sum(terms, axis=-1, keepdims=True))


def attend_pairs(q, k, v, bias, mixed, first, last):
    def pair(p, _):
        lanes = pl.ds(pl.multiple_of(p * 128, 128), 128)
        for start, extent in ((0, 256), (256, 512)):
            rows, cols = pl.ds(start, 256), pl.ds(0, extent)
            q_rows, k_cols, v_cols = q[rows, lanes], k[cols, lanes], v[cols, lanes]
            halves = []
            for half in (0, 1):
                probs = soft(only(q_rows, half), k_cols, bias[rows, cols]).astype(BF16)
                halves.append(dot(probs, v_cols))
            low = lane_iota(256) < 64
            mixed[rows, lanes] = jnp.where(low, halves[0], halves[1]).astype(BF16)
        return 0

    lax.fori_loop(first, last, pair, 0)


def make_resid(x_in, mixed, out_all, gains, resid, n2):
    def tile(i, _):
        rows = pl.ds(pl.multiple_of(i * 256, 256), 256)
        base = x_in[rows, :].astype(F32) + dot(mixed[rows, :], out_all[...].reshape(1024, 1024))
        resid[rows, :] = base
        scale = lax.rsqrt(jnp.mean(base * base, axis=-1, keepdims=True) + EPSILON)
        n2[rows, :] = (base * scale * gains[1:2, :]).astype(BF16)
        return 0

    lax.fori_loop(0, 2, tile, 0)


def head_grads(q, q_t, k, v, mg, mg_t, bias, dq, dkv_t, first, last):
    def pair(p, _):
        at = pl.multiple_of(p * 128, 128)
        lanes = pl.ds(at, 128)
        for start, extent in ((256, 512), (0, 256)):
            rows, cols = pl.ds(start, 256), pl.ds(0, extent)
            q_rows, mg_rows = q[rows, lanes], mg[rows, lanes]
            k_cols, v_cols = k[cols, lanes], v[cols, lanes]
            halves = []
            for half in (0, 1):
                own = pl.ds(pl.multiple_of(at + half * 64, 64), 64)
                probs = soft(only(q_rows, half), k_cols, bias[rows, cols])
                probs_grad = dot(only(mg_rows, half), v_cols, NT)
                inner = jnp.sum(probs * probs_grad, axis=-1, keepdims=True)
                score_grad = (probs * (probs_grad - inner)).astype(BF16)
                dv = dot(mg_t[own, rows], probs.astype(BF16))
                dk = dot(q_t[own, rows], score_grad)
                if start:
                    dkv_t[own, 0:512] = dk
                    dkv_t[own, 512:1024] = dv
                else:
                    dkv_t[own, 0:256] += dk
                    dkv_t[own, 512:768] += dv
                halves.append(dot(score_grad, k_cols))
            low = lane_iota(256) < 64
            dq[rows, lanes] = jnp.where(low, halves[0], halves[1]) * HEAD_DIM**-0.5
        return 0

    lax.fori_loop(first, last, pair, 0)


def fold(product):
    total = product[:, 0:128]
    for j in range(1, 8):
        total += product[:, j * 128 : (j + 1) * 128]
    return total + pltpu.roll(total, 64, 1)


def rank_grads(full, terms, ranks, duplicates, spread):
    a_grad, b_grads = jnp.zeros((full.shape[0], 128), F32), []
    for r, twice in zip(ranks, duplicates, strict=True):
        spread_r = spread[r]
        a_grad += dot((full * eight(twice)).astype(BF16), spread_r, NT)
        b_grads.append(fold(full * expand(terms, spread_r)))
    return a_grad, b_grads


def pick(low_half, high_half):
    return jnp.where(lane_iota(low_half.shape[0]) < 64, low_half, high_half)


def factor_grads(dq, dkv_t, kept, spread, fg, fg_at):
    def tile(i, _):
        at = pl.multiple_of(i * 128, 128)
        rows = pl.ds(at, 128)
        out = pl.ds(pl.multiple_of(fg_at + i * 128, 128), 128)
        cos_rows, sin_rows = kept[rows, COS_LANES], kept[rows, SIN_LANES]

        def turn_back(part):
            return part * cos_rows - swapped(part) * sin_rows

        tiles = [kept[rows, pl.ds(j * 128, 128)] for j in range(5)]
        terms = two_terms(kept[rows, A_LANES])
        a_q, b_q = rank_grads(
            dq[rows, :],
            terms,
            range(RANK_Q),
            [both_halves(tiles[r // 2], r % 2) for r in range(RANK_Q)],
            spread,
        )
        for j in range(RANK_Q // 2):
            part = pick(b_q[2 * j], b_q[2 * j + 1]) * (1.0 / RANK_Q)
            fg[out, pl.ds(j * 128, 128)] = turn_back(part).astype(BF16)
        a_k, b_k = rank_grads(
            dkv_t[:, rows].T,
            terms,
            range(RANK_Q, RANK_Q + RANK_KV),
            [both_halves(tiles[3], r) for r in range(RANK_KV)],
            spread,
        )
        part = pick(b_k[0], b_k[1]) * (1.0 / RANK_KV)
        fg[out, pl.ds(384, 128)] = turn_back(part).astype(BF16)
        fg[out, A_LANES] = (a_q * (1.0 / RANK_Q) + a_k * (1.0 / RANK_KV)).astype(BF16)
        a_v, b_v = rank_grads(
            dkv_t[:, pl.ds(pl.multiple_of(512 + i * 128, 128), 128)].T,
            two_terms(kept[rows, V_LANES]),
            range(RANK_KV),
            [both_halves(tiles[4], r) for r in range(RANK_KV)],
            spread,
        )
        fg[out, pl.ds(512, 128)] = (pick(b_v[0], b_v[1]) * (1.0 / RANK_KV)).astype(BF16)
        fg[out, V_LANES] = (a_v * (1.0 / RANK_KV)).astype(BF16)
        return 0

    lax.fori_loop(0, 4, tile, 0)


def whole_kernel(
    x_hbm, lengths, fac_in, wo_in, wd_in, wg_in, wu_in, cot_in,
    outputs, input_grad, gate_out, up_out, down_out, out_shard, fac_shard,
    n1_kept, kept_kept, q_kept, k_kept, v_kept, mixed_kept, resid_kept, bias_kept, spread_kept,
    n2, cot, out_acc, ng_acc, out_twin, ng_twin,
    g_buf, u_buf, d_buf, g1, u1, da1, db1, g2, u2, da2, db2, g3, u3, d3,
    po, po_twin, po_1a, po_1b, po_2a, po_2b, po_3,
    pf, pf_twin, pf_1a, pf_1b, pf_2a, pf_2b, pf_3,
    gains, wd_pad,
    ss, rs, ls,
):
    x, z, y, c = place()
    x_peer, y_peer, twin = device(1 - x, z, y, c), device(x, z, 1 - y, c), device(x, z, y, 1 - c)
    z_peers = [lax.rem(z + step, 4) for step in (1, 2, 3)]
    w = Wires(ss, rs, ls)
    upper, lower = pl.ds(0, PAD_UNITS // 2), pl.ds(PAD_UNITS // 2, PAD_UNITS // 2)
    first_rows, second_rows = pl.ds(0, 16), pl.ds(16, 16)

    def same(view, to):
        return w.make(view, view, to)

    def go(copies):
        for copy in copies:
            w.go(copy)

    def split(ref):
        return lambda core, rows: pl.ds(pl.multiple_of(core * 32, 32) + rows.start, rows.size)

    core_rows = split(None)
    gu_own, gu_z, gu_two, gu_three = [], [], [], []
    for start, size in BLOCKS:
        cols = pl.ds(start, size)
        mine = pl.ds(pl.multiple_of(c * HALF + start, 128), size)
        theirs = pl.ds(pl.multiple_of((1 - c) * HALF + start, 128), size)
        own_rows = pl.ds(pl.multiple_of(c * 32, 32), 32)
        own, first = [], []
        for src, buf in ((wg_in, g_buf), (wu_in, u_buf)):
            slot = buf.at[x, z, y, own_rows, cols]
            own.append(pltpu.make_async_copy(src.at[:, mine], slot, ls.at[w.held]))
            w.held += 1
            for zz in z_peers:
                first.append(w.make(src.at[:, mine], slot, device(x, zz, y, c)))
                first.append(w.make(src.at[:, theirs], slot, device(x, zz, y, 1 - c)))
            first.append(w.make(src.at[:, theirs], slot, twin))
        gu_own.append(own)
        gu_z.append(first)
        low, high = pl.ds(0, 32), pl.ds(32, 32)
        gu_two.append(
            [same(buf.at[x, :, y, low, cols], x_peer) for buf in (g_buf, u_buf)]
            + [same(buf.at[x, :, y, high, cols], y_peer) for buf in (g_buf, u_buf)]
        )
        gu_three.append(
            [same(buf.at[:, :, y, low, cols], y_peer) for buf in (g_buf, u_buf)]
            + [same(buf.at[x, :, :, high, cols], x_peer) for buf in (g_buf, u_buf)]
        )
    slot = d_buf.at[z, y, x]
    d_z_a = [w.make(slot.at[upper], slot.at[upper], device(x, zz, y, c)) for zz in z_peers]
    d_z_b = [w.make(slot.at[lower], slot.at[lower], device(x, zz, y, c)) for zz in z_peers]
    d_two_a, d_two_b = same(d_buf.at[:, y, x, upper], x_peer), same(d_buf.at[:, y, x, lower], y_peer)
    d_three_a = same(d_buf.at[:, y, :, upper], y_peer)
    d_three_b = same(d_buf.at[:, :, x, lower], x_peer)

    ones, twos = [], []
    for block in BLOCKS:
        cols = pl.ds(*block)
        ones.append(
            (
                w.make(u_buf.at[1 - x, :, :, :, cols], u1.at[:, :, :, cols], x_peer),
                w.make(g_buf.at[:, :, 1 - y, :, cols], g1.at[:, :, :, cols], y_peer),
            )
        )
        twos.append(
            (
                w.make(u_buf.at[x, :, 1 - y, :, cols], u2.at[:, :, cols], y_peer),
                w.make(g_buf.at[1 - x, :, y, :, cols], g2.at[:, :, cols], x_peer),
            )
        )
    n2_twin = w.make(n2.at[0:512], n2.at[512:1024], twin)
    cot_twin = w.make(cot_in, cot.at[512:1024], twin)
    ng_send = w.make(ng_acc.at[512:1024], ng_twin, twin)
    out_send = w.make(out_acc.at[512:1024], out_twin, twin)
    da_one = w.make(d_buf.at[:, 1 - y, :, upper], da1, y_peer)
    db_one = w.make(d_buf.at[:, :, 1 - x, lower], db1, x_peer)
    own_cot = pltpu.make_async_copy(cot_in, cot.at[0:512], ls.at[w.held])
    w.held += 1

    def gu_start(b):
        for copy in gu_own[b]:
            copy.start()
        go(gu_z[b])

    def gu_second(b):
        for copy in gu_own[b]:
            copy.wait()
        arrive(gu_z[b])
        go(gu_two[b])

    def gu_third(b):
        arrive(gu_two[b])
        go(gu_three[b])

    def gu_end(b):
        arrive(gu_three[b])

    def phase_one(b):
        go(ones[b])

    def phase_two(b):
        cols = pl.ds(*BLOCKS[b])
        u, g = ones[b]
        u.wait_recv()

        def add_u(i, _):
            zz, yy = lax.div(i, 2), lax.rem(i, 2)
            add_low(u_buf.at[x, zz, yy, :, cols], u1.at[zz, yy, :, cols])
            return 0

        lax.fori_loop(0, 8, add_u, 0)
        w.go(twos[b][0])
        g.wait_recv()

        def add_g(i, _):
            xx, zz = lax.div(i, 4), lax.rem(i, 4)
            add_low(g_buf.at[xx, zz, y, :, cols], g1.at[xx, zz, :, cols])
            return 0

        lax.fori_loop(0, 8, add_g, 0)
        w.go(twos[b][1])

    def phase_three(b):
        u, g = twos[b]
        cols = pl.ds(*BLOCKS[b])
        last = []
        for copy, buf, two, three in ((u, u_buf, u2, u3), (g, g_buf, g2, g3)):
            copy.wait_recv()

            def add(i, _, buf=buf, two=two):
                add_low(buf.at[x, i, y, :, cols], two.at[i, :, cols])
                return 0

            lax.fori_loop(0, 4, add, 0)
            for core, rel in ((c, 0), (1 - c, 1)):
                rows = pl.ds(pl.multiple_of(core * 32, 32), 32)
                for step, zz in enumerate(z_peers):
                    last.append(
                        w.send(
                            buf.at[x, zz, y, rows, cols],
                            three.at[rel, step + 1, :, cols],
                            device(x, zz, y, core),
                        )
                    )
            rows = pl.ds(pl.multiple_of((1 - c) * 32, 32), 32)
            last.append(w.send(buf.at[x, z, y, rows, cols], three.at[1, 0, :, cols], twin))
        return last

    def finish(buf, three, out):
        rows = pl.ds(pl.multiple_of(c * 32, 32), 32)
        own = buf[x, z, y, rows, :].astype(F32)
        for step in (1, 2, 3):
            own += three[0, step].astype(F32)
        out[c] = own
        other = three[1, 0].astype(F32)
        for step in (1, 2, 3):
            other += three[1, step].astype(F32)
        out[1 - c] = other

    def down_two():
        da_one.wait_recv()
        db_one.wait_recv()

        def add(i, _):
            zz, s = lax.div(i, 2), lax.rem(i, 2)
            add_low(d_buf.at[zz, y, s, upper], da1.at[zz, s])
            add_low(d_buf.at[zz, s, x, lower], db1.at[zz, s])
            return 0

        lax.fori_loop(0, 8, add, 0)
        da = w.send(d_buf.at[:, y, 1 - x, upper], da2, x_peer)
        return da, w.send(d_buf.at[:, 1 - y, x, lower], db2, y_peer)

    def down_three(da, db):
        da.wait_recv()
        db.wait_recv()

        def add(i, _):
            add_low(d_buf.at[i, y, x, upper], da2.at[i])
            add_low(d_buf.at[i, y, x, lower], db2.at[i])
            return 0

        lax.fori_loop(0, 4, add, 0)
        return [
            w.send(d_buf.at[zz, y, x], d3.at[step], device(x, zz, y, c))
            for step, zz in enumerate(z_peers)
        ]

    def full_zero(buf, from_twin):
        return w.send(buf.at[:, :, :, 1 - c], from_twin, twin)

    def full_one(copy, buf, from_twin, one_a, one_b):
        copy.wait_recv()

        def add(i, _):
            xx, zz, yy = lax.div(i, 8), lax.rem(lax.div(i, 2), 4), lax.rem(i, 2)
            add_low(buf.at[xx, zz, yy, c], from_twin.at[xx, zz, yy])
            return 0

        lax.fori_loop(0, 16, add, 0)
        a = w.send(buf.at[:, :, 1 - y, c, first_rows], one_a, y_peer)
        return a, w.send(buf.at[1 - x, :, :, c, second_rows], one_b, x_peer)

    def full_two(a, b, buf, one_a, one_b, two_a, two_b):
        a.wait_recv()
        b.wait_recv()

        def add(i, _):
            s, zz = lax.div(i, 4), lax.rem(i, 4)
            add_low(buf.at[s, zz, y, c, first_rows], one_a.at[s, zz])
            add_low(buf.at[x, zz, s, c, second_rows], one_b.at[zz, s])
            return 0

        lax.fori_loop(0, 8, add, 0)
        a = w.send(buf.at[1 - x, :, y, c, first_rows], two_a, x_peer)
        return a, w.send(buf.at[x, :, 1 - y, c, second_rows], two_b, y_peer)

    def full_three(a, b, buf, two_a, two_b, three):
        a.wait_recv()
        b.wait_recv()

        def add(i, _):
            add_low(buf.at[x, i, y, c, first_rows], two_a.at[i])
            add_low(buf.at[x, i, y, c, second_rows], two_b.at[i])
            return 0

        lax.fori_loop(0, 4, add, 0)
        return [
            w.send(buf.at[x, zz, y, c], three.at[step], device(x, zz, y, c))
            for step, zz in enumerate(z_peers)
        ]

    def full_end(last, buf, three, out):
        arrive(last)
        out[...] = (
            buf[x, z, y, c].astype(F32)
            + three[0].astype(F32)
            + three[1].astype(F32)
            + three[2].astype(F32)
        )

    def front(x_in, n1, kept, q, k, v, mixed, resid, bias, spread):
        cos_ref, sin_ref = kept.at[:, COS_LANES], kept.at[:, SIN_LANES]
        x_load = w.local(x_hbm, x_in)
        own_cot.start()

        def full_z(src, ref):
            own = w.local(src, ref.at[x, z, y, c])
            return own, [w.send(src, ref.at[x, z, y, c], device(x, zz, y, c)) for zz in z_peers]

        def pass_on(view, to):
            return w.send(view, view, to)

        def gather_two(ref, own, first):
            own.wait()
            arrive(first)
            a = pass_on(ref.at[x, :, y, c, first_rows], x_peer)
            b = pass_on(ref.at[x, :, y, c, second_rows], y_peer)
            return a, b, [pass_on(ref.at[x, :, y, c], twin)]

        def gather_three(ref, a, b, down):
            a.wait_recv()
            a2 = pass_on(ref.at[:, :, y, c, first_rows], y_peer)
            b.wait_recv()
            b2 = pass_on(ref.at[x, :, :, c, second_rows], x_peer)
            down.append(pass_on(ref.at[1 - x, :, y, c, first_rows], twin))
            down.append(pass_on(ref.at[x, :, 1 - y, c, second_rows], twin))
            return a2, b2

        def gather_end(ref, a2, b2, down):
            a2.wait_recv()
            down.append(pass_on(ref.at[:, :, 1 - y, c, first_rows], twin))
            b2.wait_recv()
            down.append(pass_on(ref.at[1 - x, :, :, c, second_rows], twin))

        own_f, z_f = full_z(fac_in, pf)
        rows = jnp.concatenate(
            [wd_in[...].astype(F32), jnp.zeros((PAD_UNITS - OWN_UNITS, 1024), F32)], axis=0
        )
        wd_pad[...] = rows.astype(BF16)
        swap = w.make(wd_pad, d_buf.at[z, y, 1 - x], device(1 - x, z, y, 1 - c))
        keep = pltpu.make_async_copy(wd_pad, d_buf.at[z, y, x], ls.at[w.held])
        w.held += 1

        @pl.when(x == c)
        def _():
            keep.start()

        @pl.when(x != c)
        def _():
            swap.start()

        own_o, z_o = full_z(wo_in, po)
        make_tables(lengths, cos_ref, sin_ref)
        a_f, b_f, d_f = gather_two(pf, own_f, z_f)
        gu_start(0)
        make_spread(spread)
        a2_f, b2_f = gather_three(pf, a_f, b_f, d_f)
        make_bias(lengths, bias)
        a_o, b_o, d_o = gather_two(po, own_o, z_o)

        @pl.when(x == c)
        def _():
            keep.wait()

        @pl.when(x != c)
        def _():
            swap.wait()

        go(d_z_a)
        gather_end(pf, a2_f, b2_f, d_f)
        go(d_z_b)
        a2_o, b2_o = gather_three(po, a_o, b_o, d_o)
        arrive(d_f)
        x_load.wait()
        gain_rows(pf, gains)
        make_factors(x_in, gains, pf, n1, kept)
        saves = [w.local(n1, n1_kept)]
        gu_second(0)
        w.go(cot_twin)
        make_heads(kept, cos_ref, sin_ref, spread, q, k, v, 0, 2)
        gather_end(po, a2_o, b2_o, d_o)
        gu_start(1)
        make_heads(kept, cos_ref, sin_ref, spread, q, k, v, 2, 4)
        gu_third(0)
        for src, dst in (
            (kept, kept_kept),
            (q, q_kept),
            (k, k_kept),
            (v, v_kept),
            (bias, bias_kept),
            (spread, spread_kept),
        ):
            saves.append(w.local(src, dst))
        attend_pairs(q, k, v, bias, mixed, 0, 1)
        arrive(d_z_a)
        w.go(d_two_a)
        attend_pairs(q, k, v, bias, mixed, 1, 2)
        arrive(d_z_b)
        w.go(d_two_b)
        attend_pairs(q, k, v, bias, mixed, 2, 4)
        gu_start(2)
        d_two_a.wait_recv()
        w.go(d_three_a)
        attend_pairs(q, k, v, bias, mixed, 4, 6)
        d_two_b.wait_recv()
        w.go(d_three_b)
        gu_second(1)
        attend_pairs(q, k, v, bias, mixed, 6, 8)
        saves.append(w.local(mixed, mixed_kept))
        arrive(d_o)
        make_resid(x_in, mixed, po, gains, resid, n2)
        saves.append(w.local(resid, resid_kept))
        w.go(n2_twin)
        gu_third(1)
        for copy in saves:
            copy.wait()
        w.drain()

    def feed_forward(n2_t, wd, hid, gg, ug, d_acc):
        own_cot.wait()

        def turn(i):
            rows = pl.ds(i * TILE, TILE)
            n2_t[:, rows] = n2[rows, :].T

        def forward(b, low, high):
            start, size = BLOCKS[b]
            cols = pl.ds(start, size)

            def tile(i, _):
                rows = pl.ds(pl.multiple_of(i * TILE, TILE), TILE)
                n2_rows, cot_rows = n2[rows, :], cot[rows, :]
                wg = g_buf[:, :, :, :, cols].reshape(1024, size)
                wu = u_buf[:, :, :, :, cols].reshape(1024, size)
                gate = dot(n2_rows, wg)
                up = dot(n2_rows, wu)
                hid_grad = dot(cot_rows, wd[cols, :], NT)
                sig = jax.nn.sigmoid(gate)
                silu = gate * sig
                hidden = (silu * up).astype(BF16)
                gate_grad = (hid_grad * up * sig * (1.0 + gate * (1.0 - sig))).astype(BF16)
                up_grad = (hid_grad * silu).astype(BF16)
                hid[rows, 0:size] = hidden
                gg[rows, 0:size] = gate_grad
                ug[rows, 0:size] = up_grad
                out_part = dot(hidden, wd[cols, :])
                ng_part = dot(gate_grad, wg, NT) + dot(up_grad, wu, NT)
                if b == 0:
                    out_acc[rows, :] = out_part
                    ng_acc[rows, :] = ng_part
                else:
                    out_acc[rows, :] += out_part
                    ng_acc[rows, :] += ng_part
                return 0

            lax.fori_loop(low, high, tile, 0)

        def weight_grads(b):
            ended = gu_two[b] + gu_three[b]
            for copy in ended:
                copy.wait_send()
            w.shared = [copy for copy in w.shared if all(copy is not other for other in ended)]
            start, size = BLOCKS[b]
            cols = pl.ds(start, size)

            def side(i, _):
                rows = pl.ds(pl.multiple_of(i * 512, 512), 512)
                part = dot(n2_t[rows, :], ug[:, 0:size])
                u_buf[i, :, :, :, cols] = part.astype(BF16).reshape(4, 2, 64, size)
                part = dot(n2_t[rows, :], gg[:, 0:size])
                g_buf[i, :, :, :, cols] = part.astype(BF16).reshape(4, 2, 64, size)
                return 0

            lax.fori_loop(0, 2, side, 0)
            d_acc[cols, :] = dot(hid[:, 0:size], cot[...], TN)

        turn(0)
        turn(1)
        arrive([n2_twin, cot_twin])
        turn(2)
        turn(3)
        d_three_a.wait_recv()
        d_three_b.wait_recv()

        def gather_rows(s, _):
            rows = d_buf[lax.div(s, 4), lax.rem(lax.div(s, 2), 2), lax.rem(s, 2)].astype(F32)
            d_acc[pl.ds(pl.multiple_of(s * OWN_UNITS, 8), OWN_UNITS), :] = rows[0:OWN_UNITS]
            return 0

        lax.fori_loop(0, 16, gather_rows, 0)

        def low_rows(i, _):
            rows = pl.ds(pl.multiple_of(i * 128, 128), 128)
            wd[rows, :] = d_acc[rows, :].astype(BF16)
            return 0

        lax.fori_loop(0, HALF // 128, low_rows, 0)
        gu_end(0)
        forward(0, 0, 2)
        gu_second(2)
        forward(0, 2, 4)
        weight_grads(0)
        gu_third(2)
        phase_one(0)
        gu_end(1)
        forward(1, 0, 4)
        weight_grads(1)
        phase_one(1)
        gu_end(2)
        forward(2, 2, 4)
        go([ng_send, out_send])
        forward(2, 0, 2)
        weight_grads(2)
        phase_one(2)
        phase_two(0)
        ended = [*d_z_a, *d_z_b, d_two_a, d_two_b, d_three_a, d_three_b]
        for copy in ended:
            copy.wait_send()
        w.shared = [copy for copy in w.shared if all(copy is not other for other in ended)]

        def spread_rows(s, _):
            rows = d_acc[pl.ds(pl.multiple_of(s * OWN_UNITS, 8), OWN_UNITS), :]
            rows = jnp.concatenate(
                [rows, jnp.zeros((PAD_UNITS - OWN_UNITS, rows.shape[1]), F32)], axis=0
            )
            d_buf[lax.div(s, 4), lax.rem(lax.div(s, 2), 2), lax.rem(s, 2)] = rows.astype(BF16)
            return 0

        lax.fori_loop(0, 16, spread_rows, 0)
        go([da_one, db_one])

    branch, mg = cot.at[0:512], cot.at[512:1024]

    def attention(
        resid, x_in, mixed, q, k, v, bias, kept, spread, n1, q_t, mg_t, gain_two,
        gate_sum, up_sum, d_sum,
    ):
        swap = w.make(d_sum, down_out, device(1 - x, z, y, 1 - c))
        keep = pltpu.make_async_copy(d_sum, down_out, ls.at[w.held])
        w.held += 1

        def down_end(last):
            arrive(last)
            d_sum[...] = (
                d_buf[z, y, x].astype(F32)
                + d3[0].astype(F32)
                + d3[1].astype(F32)
                + d3[2].astype(F32)
            )

            @pl.when(x == c)
            def _():
                keep.start()

            @pl.when(x != c)
            def _():
                swap.start()

        def down_close():
            @pl.when(x == c)
            def _():
                keep.wait()

            @pl.when(x != c)
            def _():
                swap.wait()

        loads = [
            w.local(src, dst)
            for src, dst in (
                (resid_kept, resid),
                (mixed_kept, mixed),
                (q_kept, q),
                (k_kept, k),
                (v_kept, v),
                (bias_kept, bias),
                (kept_kept, kept),
                (spread_kept, spread),
                (n1_kept, n1),
                (x_hbm, x_in),
            )
        ]
        phase_two(1)
        loads[0].wait()
        arrive([ng_send, out_send])

        def close(i, total):
            rows = pl.ds(pl.multiple_of(i * 128, 128), 128)
            base = resid[rows, :]
            n2[rows, :] = (base + out_acc[rows, :] + out_twin[rows, :]).astype(BF16)
            grad = ng_acc[rows, :] + ng_twin[rows, :]
            scale = lax.rsqrt(jnp.mean(base * base, axis=-1, keepdims=True) + EPSILON)
            unit = base * scale
            unit_grad = grad * gains[1:2, :]
            back = scale * (unit_grad - unit * jnp.mean(unit_grad * unit, axis=-1, keepdims=True))
            full = cot[rows, :].astype(F32) + back
            out_acc[rows, :] = full
            branch[rows, :] = full.astype(BF16)
            return total + jnp.sum((grad * unit).reshape(16, 8, 1024), axis=0)

        n2_twin.wait_send()
        w.shared = [copy for copy in w.shared if copy is not n2_twin]
        gain_two[...] = lax.fori_loop(0, 4, close, jnp.zeros((8, 1024), F32))
        results = [w.local(n2.at[0:512], outputs)]
        last = phase_three(0)
        for copy in loads[1:3]:
            copy.wait()
        for i in range(2):
            rows = pl.ds(i * 256, 256)
            part = dot(branch[rows, :], po[...].reshape(1024, 1024), NT).astype(BF16)
            mg[rows, :] = part
            mg_t[:, rows] = part.T
            q_t[:, rows] = q[rows, :].T
        for side in range(2):
            part = dot(mixed[:, side * 512 : (side + 1) * 512], branch[...], TN)
            po[side] = part.astype(BF16).reshape(4, 2, 2, 32, 1024)
        o_zero = full_zero(po, po_twin)
        phase_two(2)
        for copy in loads[3:6]:
            copy.wait()
        o_one = full_one(o_zero, po, po_twin, po_1a, po_1b)
        ng_send.wait_send()
        w.shared = [copy for copy in w.shared if copy is not ng_send]
        heads = (q, q_t, k, v, mg, mg_t, bias, out_twin, ng_acc)
        head_grads(*heads, 0, 1)
        last += phase_three(1)
        head_grads(*heads, 1, 3)
        d_two = down_two()
        head_grads(*heads, 3, 4)
        last += phase_three(2)
        head_grads(*heads, 4, 5)
        o_two = full_two(*o_one, po, po_1a, po_1b, po_2a, po_2b)
        head_grads(*heads, 5, 7)
        d_last = down_three(*d_two)
        head_grads(*heads, 7, 8)
        o_last = full_three(*o_two, po, po_2a, po_2b, po_3)
        for copy in loads[6:]:
            copy.wait()
        results[0].wait()
        factor_grads(out_twin, ng_acc, kept, spread, n2, 512)
        fg = n2.at[512:1024, 0:FACTOR_PAD]

        def first_norm(i, total):
            rows = pl.ds(pl.multiple_of(i * 128, 128), 128)
            incoming = dot(fg[rows, :], pf[...].reshape(1024, FACTOR_PAD), NT)
            vals = x_in[rows, :].astype(F32)
            scale = lax.rsqrt(jnp.mean(vals * vals, axis=-1, keepdims=True) + EPSILON)
            unit = vals * scale
            unit_grad = incoming * gains[0:1, :]
            back = scale * (unit_grad - unit * jnp.mean(unit_grad * unit, axis=-1, keepdims=True))
            out_acc[rows, :] += back
            return total + jnp.sum((incoming * unit).reshape(16, 8, 1024), axis=0)

        gain_one = lax.fori_loop(0, 4, first_norm, jnp.zeros((8, 1024), F32))
        place_row = row_iota(128, 1024)
        gain_tile = jnp.where(
            place_row == 32,
            jnp.sum(gain_one, axis=0, keepdims=True),
            jnp.where(place_row == 33, jnp.sum(gain_two[...], axis=0, keepdims=True), 0.0),
        ).T
        for side in range(2):
            part = dot(n1[:, side * 512 : (side + 1) * 512], fg[...], TN)
            part = jnp.concatenate(
                [part[:, 0:768], part[:, 768:896] + gain_tile[side * 512 : (side + 1) * 512]], axis=1
            )
            pf[side] = part.astype(BF16).reshape(4, 2, 2, 32, FACTOR_PAD)
        f_zero = full_zero(pf, pf_twin)
        results.append(w.local(out_acc.at[0:512], input_grad))
        f_one = full_one(f_zero, pf, pf_twin, pf_1a, pf_1b)
        arrive(last)
        finish(u_buf, u3, up_sum)
        finish(g_buf, g3, gate_sum)
        results += [w.local(up_sum, up_out), w.local(gate_sum, gate_out)]
        down_end(d_last)
        f_two = full_two(*f_one, pf, pf_1a, pf_1b, pf_2a, pf_2b)
        shard = out_twin.at[0:32, :]
        full_end(o_last, po, po_3, shard)
        results.append(w.local(shard, out_shard))
        f_last = full_three(*f_two, pf, pf_2a, pf_2b, pf_3)
        down_close()
        shard = out_twin.at[32:64, 0:FACTOR_PAD]
        full_end(f_last, pf, pf_3, shard)
        results.append(w.local(shard, fac_shard))
        for copy in results[1:]:
            copy.wait()
        w.drain()
        w.drain_shared()

    vmem = pltpu.VMEM
    row, turned = vmem((512, 1024), BF16), vmem((1024, 512), BF16)
    wide_row, bias_like = vmem((512, 1024), F32), vmem((512, 512), F32)
    kept_like, spread_like = vmem((512, KEPT), F32), vmem((8, 128, 1024), BF16)
    greet(x, z, y, c)
    pl.run_scoped(front, row, row, kept_like, row, row, row, row, wide_row, bias_like, spread_like)
    pl.run_scoped(
        feed_forward,
        vmem((1024, 1024), BF16), vmem((HALF, 1024), BF16), turned, turned, turned, vmem((HALF, 1024), F32),
    )
    pl.run_scoped(
        attention,
        wide_row, row, row, row, row, row, bias_like, kept_like, spread_like, row, turned, turned,
        vmem((8, 1024), F32), vmem((2, 32, HALF), F32), vmem((2, 32, HALF), F32), vmem((PAD_UNITS, 1024), F32),
    )


def whole_all(*args):
    anywhere, vmem = pl.BlockSpec(memory_space=pl.ANY), pl.BlockSpec(memory_space=pltpu.VMEM)
    big = lambda *shape: pltpu.VMEM(shape, BF16)
    wide = lambda *shape: pltpu.VMEM(shape, F32)
    half = PAD_UNITS // 2

    def full_scratch(width):
        return [
            big(2, 4, 2, 2, 32, width), big(2, 4, 2, 32, width),
            big(2, 4, 16, width), big(4, 2, 16, width), big(4, 16, width), big(4, 16, width),
            big(3, 32, width),
        ]

    row = (512, 1024)
    outs = [
        (row, BF16),
        (row, F32),
        ((2, 32, HALF), F32),
        ((2, 32, HALF), F32),
        ((PAD_UNITS, 1024), F32),
        ((32, 1024), F32),
        ((32, FACTOR_PAD), F32),
        (row, BF16),
        ((512, KEPT), F32),
        (row, BF16),
        (row, BF16),
        (row, BF16),
        (row, BF16),
        (row, F32),
        ((512, 512), F32),
        ((8, 128, 1024), BF16),
    ]
    return pl.pallas_call(
        whole_kernel,
        out_shape=[jax.ShapeDtypeStruct(*o) for o in outs],
        in_specs=[anywhere, pl.BlockSpec(memory_space=pltpu.SMEM), anywhere, anywhere, vmem]
        + [anywhere] * 3,
        out_specs=[anywhere] * len(outs),
        scratch_shapes=[
            big(1024, 1024), big(1024, 1024),
            wide(1024, 1024), wide(1024, 1024), wide(512, 1024), wide(512, 1024),
            big(2, 4, 2, 64, HALF), big(2, 4, 2, 64, HALF), big(4, 2, 2, PAD_UNITS, 1024),
            big(2, 4, 64, HALF), big(4, 2, 64, HALF), big(4, 2, half, 1024), big(4, 2, half, 1024),
            big(4, 64, HALF), big(4, 64, HALF), big(4, half, 1024), big(4, half, 1024),
            big(2, 4, 32, HALF), big(2, 4, 32, HALF), big(3, PAD_UNITS, 1024),
            *full_scratch(1024),
            *full_scratch(FACTOR_PAD),
            wide(8, 1024), big(PAD_UNITS, 1024),
            pltpu.SemaphoreType.DMA((240,)),
            pltpu.SemaphoreType.DMA((240,)),
            pltpu.SemaphoreType.DMA((64,)),
        ],
        compiler_params=pltpu.CompilerParams(
            collective_id=0, has_side_effects=True, vmem_limit_bytes=62 * MIB
        ),
        name="whole_all",
    )(*args)[:7]


def cut_kernel(fac, out_in, gate, up, down, *outs):
    at = 0
    pieces = (640, 96), (0, 384), (736, 32), (384, 128), (768, 32), (512, 128)
    for (start, size), ref in zip(pieces, outs[:6], strict=True):
        ref[...] = fac[:, start : start + size]
    outs[6][...] = out_in[...]
    for src, ref in ((gate, outs[7]), (up, outs[8])):
        ref[:, 0:HALF] = src[0]
        ref[:, HALF:FF] = src[1]
    outs[9][...] = down[0:OWN_UNITS, :]
    tile = fac[:, 768:896]
    tile = jnp.concatenate([tile, jnp.zeros((96, 128), F32)], axis=0).T
    outs[10][...] = tile[32:33, 0:32]
    outs[11][...] = tile[33:34, 0:32]


def cut_all(*args):
    shapes = [(32, n) for n in (96, 384, 32, 128, 32, 128, 1024, FF, FF)] + [(OWN_UNITS, 1024), (1, 32), (1, 32)]
    vmem = pl.BlockSpec(memory_space=pltpu.VMEM)
    return pl.pallas_call(
        cut_kernel,
        out_shape=[jax.ShapeDtypeStruct(s, F32) for s in shapes],
        in_specs=[vmem] * 5,
        out_specs=[vmem] * len(shapes),
        name="cut_all",
    )(*args)


def local_paired(
    inputs, doc_lengths, w_aq, w_bq, w_ak, w_bk, w_av, w_bv,
    w_out, w_gate, w_up, w_down, gain_attn, gain_ffn, cotangent,
):
    spare = jnp.zeros((32, FACTOR_PAD - 802), BF16)
    fac = jnp.concatenate(
        [w_bq, w_bk, w_bv, w_aq, w_ak, w_av, gain_attn[:, None], gain_ffn[:, None], spare], axis=1
    )
    outputs, input_grad, gate_sum, up_sum, down_sum, out_sum, fac_sum = whole_all(
        inputs, doc_lengths, fac, w_out, w_down, w_gate, w_up, cotangent
    )
    *cut, gain_one, gain_two = cut_all(fac_sum, out_sum, gate_sum, up_sum, down_sum)
    return (outputs, input_grad, *cut, gain_one[0], gain_two[0])


def solution(mesh):
    return jax.shard_map(
        local_paired if fits_pairs(mesh) else local,
        mesh=mesh,
        in_specs=(
            P(("dp", "fsdp"), None),
            P(("dp", "fsdp"), None),
            P(("dp", "fsdp"), None),
            P(("dp", "fsdp"), None),
            P(("dp", "fsdp"), None),
            P(("dp", "fsdp"), None),
            P(("dp", "fsdp"), None),
            P(("dp", "fsdp"), None),
            P(("dp", "fsdp"), None),
            P(("dp", "fsdp"), None),
            P(("dp", "fsdp"), None),
            P(("dp", "fsdp"), None),
            P(("dp", "fsdp")),
            P(("dp", "fsdp")),
            P(("dp", "fsdp"), None),
        ),
        out_specs=(
            P(("dp", "fsdp"), None),
            P(("dp", "fsdp"), None),
            P(("dp", "fsdp"), None),
            P(("dp", "fsdp"), None),
            P(("dp", "fsdp"), None),
            P(("dp", "fsdp"), None),
            P(("dp", "fsdp"), None),
            P(("dp", "fsdp"), None),
            P(("dp", "fsdp"), None),
            P(("dp", "fsdp"), None),
            P(("dp", "fsdp"), None),
            P(("dp", "fsdp"), None),
            P(("dp", "fsdp")),
            P(("dp", "fsdp")),
        ),
        check_vma=False,
    )
```

```python
import math

import jax
import jax.numpy as jnp
from jax import lax
from jax.experimental import pallas as pl
from jax.experimental.pallas import tpu as pltpu
from jax.sharding import PartitionSpec as P

HEADS = 16
HEAD_DIM = 64
RANK_Q = 6
RANK_KV = 2
FF = 2816


EPSILON = 1e-06
PRECISE = lax.Precision.HIGHEST


def factor_columns():
    return [
        RANK_Q * HEADS,
        RANK_Q * HEAD_DIM,
        RANK_KV * HEADS,
        RANK_KV * HEAD_DIM,
        RANK_KV * HEADS,
        RANK_KV * HEAD_DIM,
    ]


def split_columns(matrix):
    pieces = []
    offset = 0
    for columns in factor_columns():
        pieces.append(matrix[:, offset : offset + columns])
        offset += columns
    return pieces


def doc_layout(lengths, length):
    order = jnp.arange(lengths.shape[0], dtype=jnp.int32)
    doc_ends = jnp.sum(jnp.where(order[:, None] >= order[None, :], lengths[None, :], 0), axis=1)
    doc_starts = doc_ends - lengths
    places = jnp.arange(length, dtype=jnp.int32)
    segment = jnp.sum((places[:, None] >= doc_ends[None, :]).astype(jnp.int32), axis=1)
    owner = segment[:, None] == jnp.arange(lengths.shape[0], dtype=jnp.int32)[None, :]
    doc_first = jnp.sum(jnp.where(owner, doc_starts[None, :], 0), axis=1)
    return (segment, (places - doc_first).astype(jnp.float32))


def rotation(places):
    halfway = HEAD_DIM // 2
    freqs = jnp.exp(-math.log(10000.0) * jnp.arange(halfway, dtype=jnp.float32) / halfway)
    angles = places[..., None] * freqs
    return (jnp.cos(angles), jnp.sin(angles))


def rotate(factor, cos_table, sin_table):
    halfway = factor.shape[-1] // 2
    front_part = factor[..., :halfway]
    back_part = factor[..., halfway:]
    cos_part = cos_table[..., None, :]
    sin_part = sin_table[..., None, :]
    return jnp.concatenate(
        [
            front_part * cos_part - back_part * sin_part,
            front_part * sin_part + back_part * cos_part,
        ],
        axis=-1,
    )


def normalize(values, gain):
    scaling = lax.rsqrt(jnp.mean(values * values, axis=-1, keepdims=True) + EPSILON)
    unit_vals = values * scaling
    return (unit_vals * gain, unit_vals, scaling)


def norm_back(incoming, unit_vals, scaling, gain):
    unit_grad = incoming * gain
    grad_in = scaling * (
        unit_grad - unit_vals * jnp.mean(unit_grad * unit_vals, axis=-1, keepdims=True)
    )
    return (grad_in, jnp.sum(incoming * unit_vals, axis=0))


def block_scores(query_part, keys_low, seg_part, segment, place_part, places):
    scaling = HEAD_DIM ** (-0.5)
    scores = (
        jnp.einsum("thd,shd->hts", query_part, keys_low, preferred_element_type=jnp.float32)
        * scaling
    )
    allowed = (seg_part[:, None] == segment[None, :]) & (places[None, :] <= place_part[:, None])
    return jnp.where(allowed[None], scores, -1e30)


def attend_forward(queries, keys_low, values, segment):
    length = queries.shape[0]
    block_rows = min(512, length)
    places = jnp.arange(length, dtype=jnp.int32)

    def one_block(block_index):
        masked = block_scores(queries, keys_low, segment, segment, places, places)
        row_peak = jnp.max(masked, axis=-1, keepdims=True)
        exp_terms = jnp.exp(masked - row_peak)
        row_total = jnp.sum(exp_terms, axis=-1, keepdims=True)
        attn_probs = (exp_terms / row_total).astype(jnp.bfloat16)
        attended = jnp.einsum(
            "hts,shd->thd", attn_probs, values, preferred_element_type=jnp.float32
        )
        return (attended, (row_peak + jnp.log(row_total))[..., 0])

    attended, log_totals = lax.map(one_block, jnp.arange(length // block_rows, dtype=jnp.int32))
    return (attended.reshape(length, HEADS, HEAD_DIM), log_totals)


def attend_backward(queries, keys_low, values, segment, log_totals, mixed_grad):
    length = queries.shape[0]
    block_rows = min(512, length)
    places = jnp.arange(length, dtype=jnp.int32)
    scaling = HEAD_DIM ** (-0.5)

    def one_block(running, block_index):
        key_grad, value_grad = running
        masked = block_scores(queries, keys_low, segment, segment, places, places)
        attn_probs = jnp.exp(masked - log_totals[block_index][..., None])
        probs_low = attn_probs.astype(jnp.bfloat16)
        value_grad = value_grad + jnp.einsum(
            "hts,thd->shd", probs_low, mixed_grad, preferred_element_type=jnp.float32
        )
        probs_grad = jnp.einsum(
            "thd,shd->hts", mixed_grad, values, preferred_element_type=jnp.float32
        )
        inner_sum = jnp.sum(attn_probs * probs_grad, axis=-1, keepdims=True)
        score_grad = (attn_probs * (probs_grad - inner_sum)).astype(jnp.bfloat16)
        query_grad = (
            jnp.einsum("hts,shd->thd", score_grad, keys_low, preferred_element_type=jnp.float32)
            * scaling
        )
        key_grad = (
            key_grad
            + jnp.einsum("hts,thd->shd", score_grad, queries, preferred_element_type=jnp.float32)
            * scaling
        )
        return ((key_grad, value_grad), query_grad)

    empty = jnp.zeros((length, HEADS, HEAD_DIM), jnp.float32)
    (key_grad, value_grad), query_grad = lax.scan(
        one_block, (empty, empty), jnp.arange(length // block_rows, dtype=jnp.int32)
    )
    return (query_grad.reshape(length, HEADS, HEAD_DIM), key_grad, value_grad)


def factor_back(full_grad, a_part, b_part, rank_count):
    a_grad = jnp.einsum("thd,trd->trh", full_grad, b_part, precision=PRECISE) / rank_count
    b_grad = jnp.einsum("thd,trh->trd", full_grad, a_part, precision=PRECISE) / rank_count
    return (a_grad, b_grad)


def local(
    inputs,
    doc_lengths,
    w_aq,
    w_bq,
    w_ak,
    w_bk,
    w_av,
    w_bv,
    w_out,
    w_gate,
    w_up,
    w_down,
    gain_attn,
    gain_ffn,
    cotangent,
):
    length = inputs.shape[0]
    joined_local = jnp.concatenate([w_aq, w_bq, w_ak, w_bk, w_av, w_bv], axis=1)
    factor_w, out_w, gain_one = (
        lax.all_gather(joined_local, ("dp", "fsdp"), axis=0, tiled=True),
        lax.all_gather(w_out, ("dp", "fsdp"), axis=0, tiled=True),
        lax.all_gather(gain_attn, ("dp", "fsdp"), axis=0, tiled=True),
    )
    segment, places = doc_layout(doc_lengths[0], length)
    cos_table, sin_table = rotation(places)
    start_vals = inputs.astype(jnp.float32)
    normed_one, unit_one, scale_one = normalize(start_vals, gain_one.astype(jnp.float32))
    normed_low = normed_one.astype(jnp.bfloat16)
    factors = jnp.dot(normed_low, factor_w, preferred_element_type=jnp.float32)
    pieces = split_columns(factors)
    a_q = pieces[0].reshape(length, RANK_Q, HEADS)
    b_q = pieces[1].reshape(length, RANK_Q, HEAD_DIM)
    a_k = pieces[2].reshape(length, RANK_KV, HEADS)
    b_k = pieces[3].reshape(length, RANK_KV, HEAD_DIM)
    a_v = pieces[4].reshape(length, RANK_KV, HEADS)
    b_v = pieces[5].reshape(length, RANK_KV, HEAD_DIM)
    bq_rot = rotate(b_q, cos_table, sin_table)
    bk_rot = rotate(b_k, cos_table, sin_table)
    queries = (jnp.einsum("trh,trd->thd", a_q, bq_rot, precision=PRECISE) / RANK_Q).astype(
        jnp.bfloat16
    )
    keys_low = (jnp.einsum("trh,trd->thd", a_k, bk_rot, precision=PRECISE) / RANK_KV).astype(
        jnp.bfloat16
    )
    values = (jnp.einsum("trh,trd->thd", a_v, b_v, precision=PRECISE) / RANK_KV).astype(
        jnp.bfloat16
    )
    attended, log_totals = attend_forward(queries, keys_low, values, segment)
    mixed = attended.astype(jnp.bfloat16).reshape(length, HEADS * HEAD_DIM)
    resid = start_vals + jnp.dot(mixed, out_w, preferred_element_type=jnp.float32)
    gate_w, up_w, down_w, gain_two = (
        lax.all_gather(w_gate, ("dp", "fsdp"), axis=0, tiled=True),
        lax.all_gather(w_up, ("dp", "fsdp"), axis=0, tiled=True),
        lax.all_gather(w_down, ("dp", "fsdp"), axis=0, tiled=True),
        lax.all_gather(gain_ffn, ("dp", "fsdp"), axis=0, tiled=True),
    )
    normed_two, unit_two, scale_two = normalize(resid, gain_two.astype(jnp.float32))
    normed_two_low = normed_two.astype(jnp.bfloat16)
    gate_act = jnp.dot(normed_two_low, gate_w, preferred_element_type=jnp.float32)
    up_act = jnp.dot(normed_two_low, up_w, preferred_element_type=jnp.float32)
    hidden = (jax.nn.silu(gate_act) * up_act).astype(jnp.bfloat16)
    result = resid + jnp.dot(hidden, down_w, preferred_element_type=jnp.float32)
    outputs = result.astype(jnp.bfloat16)
    gate_w, up_w, down_w, gain_two = (
        lax.all_gather(w_gate, ("dp", "fsdp"), axis=0, tiled=True),
        lax.all_gather(w_up, ("dp", "fsdp"), axis=0, tiled=True),
        lax.all_gather(w_down, ("dp", "fsdp"), axis=0, tiled=True),
        lax.all_gather(gain_ffn, ("dp", "fsdp"), axis=0, tiled=True),
    )
    hidden_grad = jnp.einsum("tc,fc->tf", cotangent, down_w, preferred_element_type=jnp.float32)
    down_wgrad = jnp.einsum("tf,tc->fc", hidden, cotangent, preferred_element_type=jnp.float32)
    sig_vals = jax.nn.sigmoid(gate_act)
    gate_grad = (hidden_grad * up_act * sig_vals * (1.0 + gate_act * (1.0 - sig_vals))).astype(
        jnp.bfloat16
    )
    up_grad = (hidden_grad * jax.nn.silu(gate_act)).astype(jnp.bfloat16)
    normed_two_grad = jnp.einsum("tf,cf->tc", gate_grad, gate_w, preferred_element_type=jnp.float32)
    normed_two_grad = normed_two_grad + jnp.einsum(
        "tf,cf->tc", up_grad, up_w, preferred_element_type=jnp.float32
    )
    resid_norm_grad, gain_two_grad = norm_back(
        normed_two_grad, unit_two, scale_two, gain_two.astype(jnp.float32)
    )
    resid_grad = cotangent.astype(jnp.float32) + resid_norm_grad
    gate_rows = jnp.einsum(
        "tc,tf->cf", normed_two_low, gate_grad, preferred_element_type=jnp.float32
    )
    up_rows = jnp.einsum("tc,tf->cf", normed_two_low, up_grad, preferred_element_type=jnp.float32)
    gate_up_shard = lax.psum_scatter(
        jnp.concatenate([gate_rows, up_rows], axis=1),
        ("dp", "fsdp"),
        scatter_dimension=0,
        tiled=True,
    )
    gate_shard = gate_up_shard[:, :FF]
    up_shard = gate_up_shard[:, FF:]
    down_shard, gain_two_shard = (
        lax.psum_scatter(down_wgrad, ("dp", "fsdp"), scatter_dimension=0, tiled=True),
        lax.psum_scatter(gain_two_grad, ("dp", "fsdp"), scatter_dimension=0, tiled=True),
    )
    factor_w, out_w, gain_one = (
        lax.all_gather(joined_local, ("dp", "fsdp"), axis=0, tiled=True),
        lax.all_gather(w_out, ("dp", "fsdp"), axis=0, tiled=True),
        lax.all_gather(gain_attn, ("dp", "fsdp"), axis=0, tiled=True),
    )
    branch_grad = resid_grad.astype(jnp.bfloat16)
    out_wgrad = jnp.einsum("tc,td->cd", mixed, branch_grad, preferred_element_type=jnp.float32)
    mixed_grad = jnp.einsum("td,cd->tc", branch_grad, out_w, preferred_element_type=jnp.float32)
    mixed_grad = mixed_grad.astype(jnp.bfloat16).reshape(length, HEADS, HEAD_DIM)
    query_grad, key_grad, value_grad = attend_backward(
        queries, keys_low, values, segment, log_totals, mixed_grad
    )
    a_q_grad, bq_rot_grad = factor_back(query_grad, a_q, bq_rot, RANK_Q)
    a_k_grad, bk_rot_grad = factor_back(key_grad, a_k, bk_rot, RANK_KV)
    a_v_grad, b_v_grad = factor_back(value_grad, a_v, b_v, RANK_KV)
    neg_sin = -sin_table
    b_q_grad = rotate(bq_rot_grad, cos_table, neg_sin)
    b_k_grad = rotate(bk_rot_grad, cos_table, neg_sin)
    factor_grad = jnp.concatenate(
        [
            part.reshape(length, -1)
            for part in (a_q_grad, b_q_grad, a_k_grad, b_k_grad, a_v_grad, b_v_grad)
        ],
        axis=1,
    ).astype(jnp.bfloat16)
    factor_wgrad = jnp.einsum(
        "td,tc->dc", normed_low, factor_grad, preferred_element_type=jnp.float32
    )
    normed_one_grad = jnp.einsum(
        "tc,dc->td", factor_grad, factor_w, preferred_element_type=jnp.float32
    )
    input_norm_grad, gain_one_grad = norm_back(
        normed_one_grad, unit_one, scale_one, gain_one.astype(jnp.float32)
    )
    input_grad = resid_grad + input_norm_grad
    factor_shard, out_shard, gain_one_shard = (
        lax.psum_scatter(factor_wgrad, ("dp", "fsdp"), scatter_dimension=0, tiled=True),
        lax.psum_scatter(out_wgrad, ("dp", "fsdp"), scatter_dimension=0, tiled=True),
        lax.psum_scatter(gain_one_grad, ("dp", "fsdp"), scatter_dimension=0, tiled=True),
    )
    shard_pieces = split_columns(factor_shard)
    return (
        outputs,
        input_grad,
        shard_pieces[0],
        shard_pieces[1],
        shard_pieces[2],
        shard_pieces[3],
        shard_pieces[4],
        shard_pieces[5],
        out_shard,
        gate_shard,
        up_shard,
        down_shard,
        gain_one_shard,
        gain_two_shard,
    )


MESH_IDS = pl.DeviceIdType.MESH
HALF = FF // 2
OWN_UNITS = 88
PAD_UNITS = 96
FACTOR_PAD = 896
MIB = 2**20


def fits_pairs(mesh):
    return dict(mesh.shape) == {"dp": 2, "fsdp": 16}


def place():
    x = lax.axis_index("dp")
    f = lax.axis_index("fsdp")
    return x, lax.div(f, 4), lax.rem(lax.div(f, 2), 2), lax.rem(f, 2)


def device(x, z, y, c):
    return (x, z * 4 + y * 2 + c)


def greet(x, z, y, c):
    partners = [
        device(x, z, y, 1 - c),
        device(1 - x, z, y, c),
        device(x, z, 1 - y, c),
        device(1 - x, z, y, 1 - c),
        device(x, z, 1 - y, 1 - c),
    ]
    for step in (1, 2, 3):
        other = lax.rem(z + step, 4)
        partners += [device(x, other, y, c), device(x, other, y, 1 - c)]
    barrier = pltpu.get_barrier_semaphore()
    for partner in partners:
        pl.semaphore_signal(barrier, inc=1, device_id=partner, device_id_type=MESH_IDS)
    pl.semaphore_wait(barrier, len(partners))


class Wires:
    def __init__(self, send_sems, recv_sems, local_sems):
        self.send_sems, self.recv_sems, self.local_sems = send_sems, recv_sems, local_sems
        self.sent, self.held = 0, 0
        self.open, self.shared = [], []

    def make(self, src, dst, to):
        at = self.sent
        self.sent += 1
        return pltpu.make_async_remote_copy(
            src_ref=src,
            dst_ref=dst,
            send_sem=self.send_sems.at[at],
            recv_sem=self.recv_sems.at[at],
            device_id=to,
            device_id_type=MESH_IDS,
        )

    def go(self, copy):
        copy.start()
        self.shared.append(copy)
        return copy

    def send(self, src, dst, to):
        copy = self.make(src, dst, to)
        copy.start()
        self.open.append(copy)
        return copy

    def local(self, src, dst):
        copy = pltpu.make_async_copy(src, dst, self.local_sems.at[self.held])
        self.held += 1
        copy.start()
        return copy

    def drain(self):
        for copy in self.open:
            copy.wait_send()
        self.open = []

    def drain_shared(self):
        for copy in self.shared:
            copy.wait_send()
        self.shared = []


def arrive(copies):
    for copy in copies:
        copy.wait_recv()


BLOCKS = ((0, 512), (512, 512), (1024, 384))
TILE = 256
NT = (((1,), (1,)), ((), ()))
TN = (((0,), (0,)), ((), ()))
F32, BF16 = jnp.float32, jnp.bfloat16


def dot(a, b, dims=None):
    if dims is None:
        return jnp.dot(a, b, preferred_element_type=F32)
    return lax.dot_general(a, b, dims, preferred_element_type=F32)


def add_low(dst, src):
    dst[...] = (dst[...].astype(F32) + src[...].astype(F32)).astype(BF16)


KEPT = 1152
COS_LANES = pl.ds(896, 128)
SIN_LANES = pl.ds(1024, 128)
A_LANES = pl.ds(640, 128)
V_LANES = pl.ds(768, 128)


def lane_iota(rows, lanes=128):
    return lax.broadcasted_iota(jnp.int32, (rows, lanes), 1)


def row_iota(rows, lanes=128):
    return lax.broadcasted_iota(jnp.int32, (rows, lanes), 0)


def doc_ends_of(lengths):
    one = lengths[0, 0]
    two = one + lengths[0, 1]
    return one, two, two + lengths[0, 2]


def make_tables(lengths, cos_ref, sin_ref):
    ends = doc_ends_of(lengths)

    def tile(i, _):
        rows = pl.ds(pl.multiple_of(i * 128, 128), 128)
        places = row_iota(128) + i * 128
        first = jnp.zeros((128, 128), jnp.int32)
        for end in ends:
            first = jnp.where(places >= end, end, first)
        lane = lane_iota(128)
        turn = lax.rem(lane, 32).astype(F32)
        freqs = jnp.exp(-math.log(10000.0) * turn / 32)
        angles = (places - first).astype(F32) * freqs
        cos_ref[rows, :] = jnp.cos(angles)
        sin_vals = jnp.sin(angles)
        sin_ref[rows, :] = jnp.where(lax.rem(lane, 64) < 32, -sin_vals, sin_vals)
        return 0

    lax.fori_loop(0, 4, tile, 0)


def make_bias(lengths, bias):
    ends = doc_ends_of(lengths)

    def tile(i, _):
        rows = pl.ds(pl.multiple_of(i * 128, 128), 128)
        t = row_iota(128, 512) + i * 128
        s = lane_iota(128, 512)
        own, key = jnp.zeros((128, 512), jnp.int32), jnp.zeros((128, 512), jnp.int32)
        for end in ends:
            own += (t >= end).astype(jnp.int32)
            key += (s >= end).astype(jnp.int32)
        bias[rows, :] = jnp.where((own == key) & (s <= t), 0.0, -1e30)
        return 0

    lax.fori_loop(0, 4, tile, 0)


def make_spread(spread):
    def rank(r, _):
        head = lax.div(lane_iota(128, 1024), HEAD_DIM) + r * HEADS
        spread[r] = jnp.where(row_iota(128, 1024) == head, 1.0, 0.0).astype(BF16)
        return 0

    lax.fori_loop(0, 8, rank, 0)


def swapped(tile):
    front = lax.rem(lane_iota(tile.shape[0]), 64) < 32
    return jnp.where(front, pltpu.roll(tile, 96, 1), pltpu.roll(tile, 32, 1))


def both_halves(tile, half):
    low = lane_iota(tile.shape[0]) < 64
    other = pltpu.roll(tile, 64, 1)
    return jnp.where(low, tile, other) if half == 0 else jnp.where(low, other, tile)


def two_terms(a):
    high = a.astype(BF16)
    return high, (a - high.astype(F32)).astype(BF16)


def expand(terms, spread_r):
    return dot(terms[0], spread_r) + dot(terms[1], spread_r)


def eight(tile):
    return jnp.concatenate([tile] * 8, axis=1)


def gain_rows(fac_all, gains):
    tile = fac_all[:, :, :, :, :, V_LANES].reshape(1024, 128).astype(F32)
    gains[...] = tile.T[32:40, :]


def make_factors(x_in, gains, fac_all, n1, kept):
    def tile(i, _):
        rows = pl.ds(pl.multiple_of(i * 256, 256), 256)
        vals = x_in[rows, :].astype(F32)
        scale = lax.rsqrt(jnp.mean(vals * vals, axis=-1, keepdims=True) + EPSILON)
        low = (vals * scale * gains[0:1, :]).astype(BF16)
        n1[rows, :] = low
        kept[rows, 0:FACTOR_PAD] = dot(low, fac_all[...].reshape(1024, FACTOR_PAD))
        return 0

    lax.fori_loop(0, 2, tile, 0)


def make_heads(kept, cos_ref, sin_ref, spread, q, k, v, first, last):
    def tile(i, _):
        rows = pl.ds(pl.multiple_of(i * 128, 128), 128)
        turned = []
        for j in range(4):
            lanes = pl.ds(j * 128, 128)
            part = kept[rows, lanes]
            part = part * cos_ref[rows, :] + swapped(part) * sin_ref[rows, :]
            kept[rows, lanes] = part
            turned.append(part)
        terms = two_terms(kept[rows, A_LANES])
        total = jnp.zeros((128, 1024), F32)
        for r in range(RANK_Q):
            total += expand(terms, spread[r]) * eight(both_halves(turned[r // 2], r % 2))
        q[rows, :] = (total * (1.0 / RANK_Q)).astype(BF16) * BF16(HEAD_DIM**-0.5)
        total = jnp.zeros((128, 1024), F32)
        for r in range(RANK_KV):
            total += expand(terms, spread[RANK_Q + r]) * eight(both_halves(turned[3], r))
        k[rows, :] = (total * (1.0 / RANK_KV)).astype(BF16)
        terms = two_terms(kept[rows, V_LANES])
        plain = kept[rows, pl.ds(512, 128)]
        total = jnp.zeros((128, 1024), F32)
        for r in range(RANK_KV):
            total += expand(terms, spread[r]) * eight(both_halves(plain, r))
        v[rows, :] = (total * (1.0 / RANK_KV)).astype(BF16)
        return 0

    lax.fori_loop(first, last, tile, 0)


def only(tile, half):
    low = lane_iota(tile.shape[0]) < 64
    keep = low if half == 0 else jnp.logical_not(low)
    return jnp.where(keep, tile, jnp.zeros_like(tile))


def soft(q_rows, k_cols, bias_block):
    scores = dot(q_rows, k_cols, NT) + bias_block
    terms = jnp.exp(scores - jnp.max(scores, axis=-1, keepdims=True))
    return terms * (1.0 / jnp.sum(terms, axis=-1, keepdims=True))


def attend_pairs(q, k, v, bias, mixed, first, last):
    def pair(p, _):
        lanes = pl.ds(pl.multiple_of(p * 128, 128), 128)
        for start, extent in ((0, 256), (256, 512)):
            rows, cols = pl.ds(start, 256), pl.ds(0, extent)
            q_rows, k_cols, v_cols = q[rows, lanes], k[cols, lanes], v[cols, lanes]
            halves = []
            for half in (0, 1):
                probs = soft(only(q_rows, half), k_cols, bias[rows, cols]).astype(BF16)
                halves.append(dot(probs, v_cols))
            low = lane_iota(256) < 64
            mixed[rows, lanes] = jnp.where(low, halves[0], halves[1]).astype(BF16)
        return 0

    lax.fori_loop(first, last, pair, 0)


def make_resid(x_in, mixed, out_all, gains, resid, n2):
    def tile(i, _):
        rows = pl.ds(pl.multiple_of(i * 256, 256), 256)
        base = x_in[rows, :].astype(F32) + dot(mixed[rows, :], out_all[...].reshape(1024, 1024))
        resid[rows, :] = base
        scale = lax.rsqrt(jnp.mean(base * base, axis=-1, keepdims=True) + EPSILON)
        n2[rows, :] = (base * scale * gains[1:2, :]).astype(BF16)
        return 0

    lax.fori_loop(0, 2, tile, 0)


def head_grads(q, q_t, k, v, mg, mg_t, bias, dq, dkv_t, first, last):
    def pair(p, _):
        at = pl.multiple_of(p * 128, 128)
        lanes = pl.ds(at, 128)
        for start, extent in ((256, 512), (0, 256)):
            rows, cols = pl.ds(start, 256), pl.ds(0, extent)
            q_rows, mg_rows = q[rows, lanes], mg[rows, lanes]
            k_cols, v_cols = k[cols, lanes], v[cols, lanes]
            halves = []
            for half in (0, 1):
                own = pl.ds(pl.multiple_of(at + half * 64, 64), 64)
                probs = soft(only(q_rows, half), k_cols, bias[rows, cols])
                probs_grad = dot(only(mg_rows, half), v_cols, NT)
                inner = jnp.sum(probs * probs_grad, axis=-1, keepdims=True)
                score_grad = (probs * (probs_grad - inner)).astype(BF16)
                dv = dot(mg_t[own, rows], probs.astype(BF16))
                dk = dot(q_t[own, rows], score_grad)
                if start:
                    dkv_t[own, 0:512] = dk
                    dkv_t[own, 512:1024] = dv
                else:
                    dkv_t[own, 0:256] += dk
                    dkv_t[own, 512:768] += dv
                halves.append(dot(score_grad, k_cols))
            low = lane_iota(256) < 64
            dq[rows, lanes] = jnp.where(low, halves[0], halves[1]) * HEAD_DIM**-0.5
        return 0

    lax.fori_loop(first, last, pair, 0)


def fold(product):
    total = product[:, 0:128]
    for j in range(1, 8):
        total += product[:, j * 128 : (j + 1) * 128]
    return total + pltpu.roll(total, 64, 1)


def rank_grads(full, terms, ranks, duplicates, spread):
    a_grad, b_grads = jnp.zeros((full.shape[0], 128), F32), []
    for r, twice in zip(ranks, duplicates, strict=True):
        spread_r = spread[r]
        a_grad += dot((full * eight(twice)).astype(BF16), spread_r, NT)
        b_grads.append(fold(full * expand(terms, spread_r)))
    return a_grad, b_grads


def pick(low_half, high_half):
    return jnp.where(lane_iota(low_half.shape[0]) < 64, low_half, high_half)


def factor_grads(dq, dkv_t, kept, spread, fg, fg_at, first, last):
    def tile(i, _):
        at = pl.multiple_of(i * 128, 128)
        rows = pl.ds(at, 128)
        out = pl.ds(pl.multiple_of(fg_at + i * 128, 128), 128)
        cos_rows, sin_rows = kept[rows, COS_LANES], kept[rows, SIN_LANES]

        def turn_back(part):
            return part * cos_rows - swapped(part) * sin_rows

        tiles = [kept[rows, pl.ds(j * 128, 128)] for j in range(5)]
        terms = two_terms(kept[rows, A_LANES])
        a_q, b_q = rank_grads(
            dq[rows, :],
            terms,
            range(RANK_Q),
            [both_halves(tiles[r // 2], r % 2) for r in range(RANK_Q)],
            spread,
        )
        for j in range(RANK_Q // 2):
            part = pick(b_q[2 * j], b_q[2 * j + 1]) * (1.0 / RANK_Q)
            fg[out, pl.ds(j * 128, 128)] = turn_back(part).astype(BF16)
        a_k, b_k = rank_grads(
            dkv_t[:, rows].T,
            terms,
            range(RANK_Q, RANK_Q + RANK_KV),
            [both_halves(tiles[3], r) for r in range(RANK_KV)],
            spread,
        )
        part = pick(b_k[0], b_k[1]) * (1.0 / RANK_KV)
        fg[out, pl.ds(384, 128)] = turn_back(part).astype(BF16)
        fg[out, A_LANES] = (a_q * (1.0 / RANK_Q) + a_k * (1.0 / RANK_KV)).astype(BF16)
        a_v, b_v = rank_grads(
            dkv_t[:, pl.ds(pl.multiple_of(512 + i * 128, 128), 128)].T,
            two_terms(kept[rows, V_LANES]),
            range(RANK_KV),
            [both_halves(tiles[4], r) for r in range(RANK_KV)],
            spread,
        )
        fg[out, pl.ds(512, 128)] = (pick(b_v[0], b_v[1]) * (1.0 / RANK_KV)).astype(BF16)
        fg[out, V_LANES] = (a_v * (1.0 / RANK_KV)).astype(BF16)
        return 0

    lax.fori_loop(first, last, tile, 0)


def whole_kernel(
    x_hbm, lengths, fac_in, wo_in, wd_in, wg_in, wu_in, cot_in,
    outputs, input_grad, gate_out, up_out, down_out, out_shard, fac_shard,
    n1_kept, kept_kept, q_kept, k_kept, v_kept, mixed_kept, resid_kept, bias_kept, spread_kept,
    n2, cot, out_acc, ng_acc, out_twin, ng_twin,
    g_buf, u_buf, d_buf, g1, u1, da1, db1, g2, u2, da2, db2, g3, u3, d3,
    po, po_twin, po_1a, po_1b, po_2a, po_2b, po_3,
    pf, pf_twin, pf_1a, pf_1b, pf_2a, pf_2b, pf_3,
    gains, wd_pad,
    ss, rs, ls,
):
    x, z, y, c = place()
    x_peer, y_peer, twin = device(1 - x, z, y, c), device(x, z, 1 - y, c), device(x, z, y, 1 - c)
    z_peers = [lax.rem(z + step, 4) for step in (1, 2, 3)]
    w = Wires(ss, rs, ls)
    upper, lower = pl.ds(0, PAD_UNITS // 2), pl.ds(PAD_UNITS // 2, PAD_UNITS // 2)
    first_rows, second_rows = pl.ds(0, 16), pl.ds(16, 16)

    def same(view, to):
        return w.make(view, view, to)

    def go(copies):
        for copy in copies:
            w.go(copy)

    gu_own, gu_one, gu_z_a, gu_z_b, gu_three_a, gu_three_b = [], [], [], [], [], []
    a_rows, b_rows = first_rows, second_rows
    for start, size in BLOCKS:
        cols = pl.ds(start, size)
        mine = pl.ds(pl.multiple_of(c * HALF + start, 128), size)
        theirs = pl.ds(pl.multiple_of((1 - c) * HALF + start, 128), size)
        own, one = [], []
        for src, buf in ((wg_in, g_buf), (wu_in, u_buf)):
            slot = buf.at[x, z, y, c]
            own.append(pltpu.make_async_copy(src.at[:, mine], slot.at[:, cols], ls.at[w.held]))
            w.held += 1
            a_slot, b_slot = slot.at[a_rows, cols], slot.at[b_rows, cols]
            one.append(w.make(src.at[a_rows, mine], a_slot, x_peer))
            one.append(w.make(src.at[a_rows, theirs], a_slot, device(1 - x, z, y, 1 - c)))
            one.append(w.make(src.at[b_rows, mine], b_slot, y_peer))
            one.append(w.make(src.at[b_rows, theirs], b_slot, device(x, z, 1 - y, 1 - c)))
            one.append(w.make(src.at[:, theirs], slot.at[:, cols], twin))
        gu_own.append(own)
        gu_one.append(one)
        both = (g_buf, u_buf)
        gu_z_a.append(
            [same(buf.at[:, z, y, :, a_rows, cols], device(x, zz, y, c)) for buf in both for zz in z_peers]
        )
        gu_z_b.append(
            [same(buf.at[x, z, :, :, b_rows, cols], device(x, zz, y, c)) for buf in both for zz in z_peers]
        )
        gu_three_a.append([same(buf.at[:, :, y, :, a_rows, cols], y_peer) for buf in both])
        gu_three_b.append([same(buf.at[x, :, :, :, b_rows, cols], x_peer) for buf in both])
    slot = d_buf.at[z, y, x]
    d_z_a = [w.make(slot.at[upper], slot.at[upper], device(x, zz, y, c)) for zz in z_peers]
    d_z_b = [w.make(slot.at[lower], slot.at[lower], device(x, zz, y, c)) for zz in z_peers]
    d_two_a, d_two_b = same(d_buf.at[:, y, x, upper], x_peer), same(d_buf.at[:, y, x, lower], y_peer)
    d_three_a = same(d_buf.at[:, y, :, upper], y_peer)
    d_three_b = same(d_buf.at[:, :, x, lower], x_peer)

    ones, twos_u, twos_g, threes_u, threes_g = [], [], [], [], []
    for block in BLOCKS:
        cols = pl.ds(*block)
        ones.append(
            (
                w.make(u_buf.at[1 - x, :, :, :, :, cols], u1.at[:, :, :, :, cols], x_peer),
                w.make(g_buf.at[:, :, 1 - y, :, :, cols], g1.at[:, :, :, :, cols], y_peer),
            )
        )
        twos_u.append(
            [
                w.make(u_buf.at[x, zz, :, :, :, cols], u2.at[step, :, :, :, cols], device(x, zz, y, c))
                for step, zz in enumerate(z_peers)
            ]
        )
        twos_g.append(
            [
                w.make(g_buf.at[:, zz, y, :, :, cols], g2.at[step, :, :, :, cols], device(x, zz, y, c))
                for step, zz in enumerate(z_peers)
            ]
        )
        threes_u.append(
            [
                w.make(u_buf.at[x, z, 1 - y, c, :, cols], u3.at[0, :, cols], y_peer),
                w.make(u_buf.at[x, z, 1 - y, 1 - c, :, cols], u3.at[2, :, cols], device(x, z, 1 - y, 1 - c)),
                w.make(u_buf.at[x, z, y, 1 - c, :, cols], u3.at[1, :, cols], twin),
            ]
        )
        threes_g.append(
            [
                w.make(g_buf.at[1 - x, z, y, c, :, cols], g3.at[0, :, cols], x_peer),
                w.make(g_buf.at[1 - x, z, y, 1 - c, :, cols], g3.at[2, :, cols], device(1 - x, z, y, 1 - c)),
                w.make(g_buf.at[x, z, y, 1 - c, :, cols], g3.at[1, :, cols], twin),
            ]
        )
    n2_twin = w.make(n2.at[0:512], n2.at[512:1024], twin)
    cot_twin = w.make(cot_in, cot.at[512:1024], twin)
    ng_send = w.make(ng_acc.at[512:1024], ng_twin, twin)
    out_send = w.make(out_acc.at[512:1024], out_twin, twin)
    da_one = w.make(d_buf.at[:, 1 - y, :, upper], da1, y_peer)
    db_one = w.make(d_buf.at[:, :, 1 - x, lower], db1, x_peer)
    own_cot = pltpu.make_async_copy(cot_in, cot.at[0:512], ls.at[w.held])
    w.held += 1

    def gu_start(b):
        for copy in gu_own[b]:
            copy.start()
        go(gu_one[b])

    def gu_second(b):
        for copy in gu_own[b]:
            copy.wait()
        arrive(gu_one[b])
        go(gu_z_a[b])
        go(gu_z_b[b])

    def gu_third_a(b):
        arrive(gu_z_a[b])
        go(gu_three_a[b])

    def gu_third_b(b):
        arrive(gu_z_b[b])
        go(gu_three_b[b])

    def gu_end(b):
        arrive(gu_three_a[b])
        arrive(gu_three_b[b])

    def phase_one(b):
        go(ones[b])

    def phase_two_u(b):
        cols = pl.ds(*BLOCKS[b])
        ones[b][0].wait_recv()

        def add(i, _):
            zz, yy = lax.div(i, 2), lax.rem(i, 2)
            add_low(u_buf.at[x, zz, yy, :, :, cols], u1.at[zz, yy, :, :, cols])
            return 0

        lax.fori_loop(0, 8, add, 0)
        go(twos_u[b])

    def phase_two_g(b):
        cols = pl.ds(*BLOCKS[b])
        ones[b][1].wait_recv()

        def add(i, _):
            xx, zz = lax.div(i, 4), lax.rem(i, 4)
            add_low(g_buf.at[xx, zz, y, :, :, cols], g1.at[xx, zz, :, :, cols])
            return 0

        lax.fori_loop(0, 8, add, 0)
        go(twos_g[b])

    def add_three(dst, three):
        total = dst[...].astype(F32)
        for src in three:
            total += src[...].astype(F32)
        dst[...] = total.astype(BF16)

    def phase_three_u(b):
        cols = pl.ds(*BLOCKS[b])
        arrive(twos_u[b])

        def add(i, _):
            add_three(u_buf.at[x, z, i, :, :, cols], [u2.at[k, i, :, :, cols] for k in range(3)])
            return 0

        lax.fori_loop(0, 2, add, 0)
        go(threes_u[b])

    def phase_three_g(b):
        cols = pl.ds(*BLOCKS[b])
        arrive(twos_g[b])

        def add(i, _):
            add_three(g_buf.at[i, z, y, :, :, cols], [g2.at[k, i, :, :, cols] for k in range(3)])
            return 0

        lax.fori_loop(0, 2, add, 0)
        go(threes_g[b])

    def finish(buf, three, out):
        out[c] = buf[x, z, y, c].astype(F32) + three[0].astype(F32)
        out[1 - c] = three[1].astype(F32) + three[2].astype(F32)

    def down_two():
        da_one.wait_recv()
        db_one.wait_recv()

        def add(i, _):
            zz, s = lax.div(i, 2), lax.rem(i, 2)
            add_low(d_buf.at[zz, y, s, upper], da1.at[zz, s])
            add_low(d_buf.at[zz, s, x, lower], db1.at[zz, s])
            return 0

        lax.fori_loop(0, 8, add, 0)
        da = w.send(d_buf.at[:, y, 1 - x, upper], da2, x_peer)
        return da, w.send(d_buf.at[:, 1 - y, x, lower], db2, y_peer)

    def down_three(da, db):
        da.wait_recv()
        db.wait_recv()

        def add(i, _):
            add_low(d_buf.at[i, y, x, upper], da2.at[i])
            add_low(d_buf.at[i, y, x, lower], db2.at[i])
            return 0

        lax.fori_loop(0, 4, add, 0)
        return [
            w.send(d_buf.at[zz, y, x], d3.at[step], device(x, zz, y, c))
            for step, zz in enumerate(z_peers)
        ]

    def full_zero(buf, from_twin):
        return w.send(buf.at[:, :, :, 1 - c], from_twin, twin)

    def full_one(copy, buf, from_twin, one_a, one_b):
        copy.wait_recv()

        def add(i, _):
            xx, zz, yy = lax.div(i, 8), lax.rem(lax.div(i, 2), 4), lax.rem(i, 2)
            add_low(buf.at[xx, zz, yy, c], from_twin.at[xx, zz, yy])
            return 0

        lax.fori_loop(0, 16, add, 0)
        a = w.send(buf.at[:, :, 1 - y, c, first_rows], one_a, y_peer)
        return a, w.send(buf.at[1 - x, :, :, c, second_rows], one_b, x_peer)

    def full_two(a, b, buf, one_a, one_b, two_a, two_b):
        a.wait_recv()
        b.wait_recv()

        def add(i, _):
            s, zz = lax.div(i, 4), lax.rem(i, 4)
            add_low(buf.at[s, zz, y, c, first_rows], one_a.at[s, zz])
            add_low(buf.at[x, zz, s, c, second_rows], one_b.at[zz, s])
            return 0

        lax.fori_loop(0, 8, add, 0)
        a = w.send(buf.at[1 - x, :, y, c, first_rows], two_a, x_peer)
        return a, w.send(buf.at[x, :, 1 - y, c, second_rows], two_b, y_peer)

    def full_three(a, b, buf, two_a, two_b, three):
        a.wait_recv()
        b.wait_recv()

        def add(i, _):
            add_low(buf.at[x, i, y, c, first_rows], two_a.at[i])
            add_low(buf.at[x, i, y, c, second_rows], two_b.at[i])
            return 0

        lax.fori_loop(0, 4, add, 0)
        return [
            w.send(buf.at[x, zz, y, c], three.at[step], device(x, zz, y, c))
            for step, zz in enumerate(z_peers)
        ]

    def full_end(last, buf, three, out):
        arrive(last)
        out[...] = (
            buf[x, z, y, c].astype(F32)
            + three[0].astype(F32)
            + three[1].astype(F32)
            + three[2].astype(F32)
        )

    def front(x_in, n1, kept, q, k, v, mixed, resid, bias, spread):
        cos_ref, sin_ref = kept.at[:, COS_LANES], kept.at[:, SIN_LANES]
        x_load = w.local(x_hbm, x_in)
        own_cot.start()

        def full_z(src, ref):
            own = w.local(src, ref.at[x, z, y, c])
            return own, [w.send(src, ref.at[x, z, y, c], device(x, zz, y, c)) for zz in z_peers]

        def pass_on(view, to):
            return w.send(view, view, to)

        def gather_two(ref, own, first):
            own.wait()
            arrive(first)
            a = pass_on(ref.at[x, :, y, c, first_rows], x_peer)
            b = pass_on(ref.at[x, :, y, c, second_rows], y_peer)
            return a, b, [pass_on(ref.at[x, :, y, c], twin)]

        def gather_three(ref, a, b, down):
            a.wait_recv()
            a2 = pass_on(ref.at[:, :, y, c, first_rows], y_peer)
            b.wait_recv()
            b2 = pass_on(ref.at[x, :, :, c, second_rows], x_peer)
            down.append(pass_on(ref.at[1 - x, :, y, c, first_rows], twin))
            down.append(pass_on(ref.at[x, :, 1 - y, c, second_rows], twin))
            return a2, b2

        def gather_end(ref, a2, b2, down):
            a2.wait_recv()
            down.append(pass_on(ref.at[:, :, 1 - y, c, first_rows], twin))
            b2.wait_recv()
            down.append(pass_on(ref.at[1 - x, :, :, c, second_rows], twin))

        own_f, z_f = full_z(fac_in, pf)
        rows = jnp.concatenate(
            [wd_in[...].astype(F32), jnp.zeros((PAD_UNITS - OWN_UNITS, 1024), F32)], axis=0
        )
        wd_pad[...] = rows.astype(BF16)
        swap = w.make(wd_pad, d_buf.at[z, y, 1 - x], device(1 - x, z, y, 1 - c))
        keep = pltpu.make_async_copy(wd_pad, d_buf.at[z, y, x], ls.at[w.held])
        w.held += 1

        @pl.when(x == c)
        def _():
            keep.start()

        @pl.when(x != c)
        def _():
            swap.start()

        own_o, z_o = full_z(wo_in, po)
        for b in range(3):
            gu_start(b)
        make_tables(lengths, cos_ref, sin_ref)
        a_f, b_f, d_f = gather_two(pf, own_f, z_f)

        @pl.when(x == c)
        def _():
            keep.wait()

        @pl.when(x != c)
        def _():
            swap.wait()

        go(d_z_a)
        go(d_z_b)
        for b in range(3):
            gu_second(b)
        make_spread(spread)
        a2_f, b2_f = gather_three(pf, a_f, b_f, d_f)
        make_bias(lengths, bias)
        a_o, b_o, d_o = gather_two(po, own_o, z_o)
        w.go(cot_twin)
        gather_end(pf, a2_f, b2_f, d_f)
        arrive(d_f)
        x_load.wait()
        gain_rows(pf, gains)
        make_factors(x_in, gains, pf, n1, kept)
        saves = [w.local(n1, n1_kept)]
        a2_o, b2_o = gather_three(po, a_o, b_o, d_o)
        make_heads(kept, cos_ref, sin_ref, spread, q, k, v, 0, 2)
        arrive(d_z_a)
        w.go(d_two_a)
        make_heads(kept, cos_ref, sin_ref, spread, q, k, v, 2, 4)
        for src, dst in (
            (kept, kept_kept),
            (q, q_kept),
            (k, k_kept),
            (v, v_kept),
            (bias, bias_kept),
            (spread, spread_kept),
        ):
            saves.append(w.local(src, dst))
        attend_pairs(q, k, v, bias, mixed, 0, 1)
        gather_end(po, a2_o, b2_o, d_o)
        arrive(d_z_b)
        w.go(d_two_b)
        attend_pairs(q, k, v, bias, mixed, 1, 4)
        d_two_a.wait_recv()
        w.go(d_three_a)
        attend_pairs(q, k, v, bias, mixed, 4, 8)
        d_two_b.wait_recv()
        w.go(d_three_b)
        gu_third_a(0)
        saves.append(w.local(mixed, mixed_kept))
        arrive(d_o)
        make_resid(x_in, mixed, po, gains, resid, n2)
        saves.append(w.local(resid, resid_kept))
        w.go(n2_twin)
        for copy in saves:
            copy.wait()
        w.drain()

    def feed_forward(n2_t, wd, hid, gg, ug, d_acc):
        own_cot.wait()

        def turn(i):
            rows = pl.ds(i * TILE, TILE)
            n2_t[:, rows] = n2[rows, :].T

        def forward(b, low, high):
            start, size = BLOCKS[b]
            cols = pl.ds(start, size)

            def tile(i, _):
                rows = pl.ds(pl.multiple_of(i * TILE, TILE), TILE)
                n2_rows, cot_rows = n2[rows, :], cot[rows, :]
                wg = g_buf[:, :, :, :, :, cols].reshape(1024, size)
                wu = u_buf[:, :, :, :, :, cols].reshape(1024, size)
                gate = dot(n2_rows, wg)
                up = dot(n2_rows, wu)
                hid_grad = dot(cot_rows, wd[cols, :], NT)
                sig = jax.nn.sigmoid(gate)
                silu = gate * sig
                hidden = (silu * up).astype(BF16)
                gate_grad = (hid_grad * up * sig * (1.0 + gate * (1.0 - sig))).astype(BF16)
                up_grad = (hid_grad * silu).astype(BF16)
                hid[rows, 0:size] = hidden
                gg[rows, 0:size] = gate_grad
                ug[rows, 0:size] = up_grad
                out_part = dot(hidden, wd[cols, :])
                ng_part = dot(gate_grad, wg, NT) + dot(up_grad, wu, NT)
                if b == 0:
                    out_acc[rows, :] = out_part
                    ng_acc[rows, :] = ng_part
                else:
                    out_acc[rows, :] += out_part
                    ng_acc[rows, :] += ng_part
                return 0

            lax.fori_loop(low, high, tile, 0)

        def weight_grads(b):
            ended = gu_z_a[b] + gu_z_b[b] + gu_three_a[b] + gu_three_b[b]
            for copy in ended:
                copy.wait_send()
            w.shared = [copy for copy in w.shared if all(copy is not other for other in ended)]
            start, size = BLOCKS[b]
            cols = pl.ds(start, size)

            def side(i, _):
                rows = pl.ds(pl.multiple_of(i * 512, 512), 512)
                part = dot(n2_t[rows, :], ug[:, 0:size])
                u_buf[i, :, :, :, :, cols] = part.astype(BF16).reshape(4, 2, 2, 32, size)
                part = dot(n2_t[rows, :], gg[:, 0:size])
                g_buf[i, :, :, :, :, cols] = part.astype(BF16).reshape(4, 2, 2, 32, size)
                return 0

            lax.fori_loop(0, 2, side, 0)
            d_acc[cols, :] = dot(hid[:, 0:size], cot[...], TN)

        turn(0)
        turn(1)
        arrive([n2_twin, cot_twin])
        turn(2)
        turn(3)
        gu_third_b(0)
        d_three_a.wait_recv()
        d_three_b.wait_recv()

        def gather_rows(s, _):
            rows = d_buf[lax.div(s, 4), lax.rem(lax.div(s, 2), 2), lax.rem(s, 2)].astype(F32)
            d_acc[pl.ds(pl.multiple_of(s * OWN_UNITS, 8), OWN_UNITS), :] = rows[0:OWN_UNITS]
            return 0

        lax.fori_loop(0, 16, gather_rows, 0)

        def low_rows(i, _):
            rows = pl.ds(pl.multiple_of(i * 128, 128), 128)
            wd[rows, :] = d_acc[rows, :].astype(BF16)
            return 0

        lax.fori_loop(0, HALF // 128, low_rows, 0)
        gu_third_a(1)
        gu_end(0)
        forward(0, 0, 2)
        gu_third_b(1)
        forward(0, 2, 4)
        weight_grads(0)
        phase_one(0)
        gu_third_a(2)
        gu_end(1)
        forward(1, 0, 2)
        gu_third_b(2)
        forward(1, 2, 4)
        phase_two_g(0)
        weight_grads(1)
        phase_one(1)
        phase_two_u(0)
        gu_end(2)
        forward(2, 2, 4)
        go([ng_send, out_send])
        forward(2, 0, 2)
        weight_grads(2)
        phase_one(2)
        phase_two_g(1)
        ended = [*d_z_a, *d_z_b, d_two_a, d_two_b, d_three_a, d_three_b]
        for copy in ended:
            copy.wait_send()
        w.shared = [copy for copy in w.shared if all(copy is not other for other in ended)]

        def spread_rows(s, _):
            rows = d_acc[pl.ds(pl.multiple_of(s * OWN_UNITS, 8), OWN_UNITS), :]
            rows = jnp.concatenate(
                [rows, jnp.zeros((PAD_UNITS - OWN_UNITS, rows.shape[1]), F32)], axis=0
            )
            d_buf[lax.div(s, 4), lax.rem(lax.div(s, 2), 2), lax.rem(s, 2)] = rows.astype(BF16)
            return 0

        lax.fori_loop(0, 16, spread_rows, 0)
        go([da_one, db_one])
        phase_two_u(1)

    branch, mg = cot.at[0:512], cot.at[512:1024]

    def attention(
        resid, x_in, mixed, q, k, v, bias, kept, spread, n1, q_t, mg_t, gain_two,
        gate_sum, up_sum, d_sum,
    ):
        swap = w.make(d_sum, down_out, device(1 - x, z, y, 1 - c))
        keep = pltpu.make_async_copy(d_sum, down_out, ls.at[w.held])
        w.held += 1

        def down_end(last):
            arrive(last)
            d_sum[...] = (
                d_buf[z, y, x].astype(F32)
                + d3[0].astype(F32)
                + d3[1].astype(F32)
                + d3[2].astype(F32)
            )

            @pl.when(x == c)
            def _():
                keep.start()

            @pl.when(x != c)
            def _():
                swap.start()

        def down_close():
            @pl.when(x == c)
            def _():
                keep.wait()

            @pl.when(x != c)
            def _():
                swap.wait()

        loads = [
            w.local(src, dst)
            for src, dst in (
                (resid_kept, resid),
                (mixed_kept, mixed),
                (q_kept, q),
                (k_kept, k),
                (v_kept, v),
                (bias_kept, bias),
                (kept_kept, kept),
                (spread_kept, spread),
                (n1_kept, n1),
                (x_hbm, x_in),
            )
        ]
        loads[0].wait()
        arrive([ng_send, out_send])

        def close(i, total):
            rows = pl.ds(pl.multiple_of(i * 128, 128), 128)
            base = resid[rows, :]
            n2[rows, :] = (base + out_acc[rows, :] + out_twin[rows, :]).astype(BF16)
            grad = ng_acc[rows, :] + ng_twin[rows, :]
            scale = lax.rsqrt(jnp.mean(base * base, axis=-1, keepdims=True) + EPSILON)
            unit = base * scale
            unit_grad = grad * gains[1:2, :]
            back = scale * (unit_grad - unit * jnp.mean(unit_grad * unit, axis=-1, keepdims=True))
            full = cot[rows, :].astype(F32) + back
            out_acc[rows, :] = full
            branch[rows, :] = full.astype(BF16)
            return total + jnp.sum((grad * unit).reshape(16, 8, 1024), axis=0)

        n2_twin.wait_send()
        w.shared = [copy for copy in w.shared if copy is not n2_twin]
        gain_two[...] = lax.fori_loop(0, 4, close, jnp.zeros((8, 1024), F32))
        results = [w.local(n2.at[0:512], outputs)]
        phase_three_g(0)
        phase_three_u(0)
        for copy in loads[1:3]:
            copy.wait()
        for i in range(2):
            rows = pl.ds(i * 256, 256)
            part = dot(branch[rows, :], po[...].reshape(1024, 1024), NT).astype(BF16)
            mg[rows, :] = part
            mg_t[:, rows] = part.T
            q_t[:, rows] = q[rows, :].T
        for side in range(2):
            part = dot(mixed[:, side * 512 : (side + 1) * 512], branch[...], TN)
            po[side] = part.astype(BF16).reshape(4, 2, 2, 32, 1024)
        o_zero = full_zero(po, po_twin)
        phase_two_g(2)
        for copy in loads[3:6]:
            copy.wait()
        ng_send.wait_send()
        w.shared = [copy for copy in w.shared if copy is not ng_send]
        heads = (q, q_t, k, v, mg, mg_t, bias, out_twin, ng_acc)
        phase_two_u(2)
        head_grads(*heads, 0, 1)
        o_one = full_one(o_zero, po, po_twin, po_1a, po_1b)
        phase_three_g(1)
        head_grads(*heads, 1, 5)
        phase_three_u(1)
        head_grads(*heads, 5, 7)
        d_two = down_two()
        head_grads(*heads, 7, 8)
        phase_three_g(2)
        for copy in loads[6:]:
            copy.wait()
        results[0].wait()
        factor_grads(out_twin, ng_acc, kept, spread, n2, 512, 0, 2)
        o_two = full_two(*o_one, po, po_1a, po_1b, po_2a, po_2b)
        factor_grads(out_twin, ng_acc, kept, spread, n2, 512, 2, 4)
        fg = n2.at[512:1024, 0:FACTOR_PAD]
        incoming = out_twin
        for i in range(2):
            rows = pl.ds(i * 256, 256)
            incoming[rows, :] = dot(fg[rows, :], pf[...].reshape(1024, FACTOR_PAD), NT)
        gain_tile = jnp.where(
            row_iota(128, 1024) == 33, jnp.sum(gain_two[...], axis=0, keepdims=True), 0.0
        ).T
        for side in range(2):
            part = dot(n1[:, side * 512 : (side + 1) * 512], fg[...], TN)
            part = jnp.concatenate(
                [part[:, 0:768], part[:, 768:896] + gain_tile[side * 512 : (side + 1) * 512]], axis=1
            )
            pf[side] = part.astype(BF16).reshape(4, 2, 2, 32, FACTOR_PAD)
        f_zero = full_zero(pf, pf_twin)
        phase_three_u(2)
        d_last = down_three(*d_two)
        f_one = full_one(f_zero, pf, pf_twin, pf_1a, pf_1b)

        def first_norm(i, _):
            rows = pl.ds(pl.multiple_of(i * 128, 128), 128)
            vals = x_in[rows, :].astype(F32)
            scale = lax.rsqrt(jnp.mean(vals * vals, axis=-1, keepdims=True) + EPSILON)
            unit = vals * scale
            unit_grad = incoming[rows, :] * gains[0:1, :]
            back = scale * (unit_grad - unit * jnp.mean(unit_grad * unit, axis=-1, keepdims=True))
            out_acc[rows, :] += back
            return 0

        lax.fori_loop(0, 4, first_norm, 0)
        results.append(w.local(out_acc.at[0:512], input_grad))
        o_last = full_three(*o_two, po, po_2a, po_2b, po_3)
        f_two = full_two(*f_one, pf, pf_1a, pf_1b, pf_2a, pf_2b)
        for copies in (*threes_u, *threes_g):
            arrive(copies)
        finish(u_buf, u3, up_sum)
        finish(g_buf, g3, gate_sum)
        results += [w.local(up_sum, up_out), w.local(gate_sum, gate_out)]
        f_last = full_three(*f_two, pf, pf_2a, pf_2b, pf_3)
        down_end(d_last)
        shard = out_twin.at[0:32, :]
        full_end(o_last, po, po_3, shard)
        results.append(w.local(shard, out_shard))
        shard = out_twin.at[32:64, 0:FACTOR_PAD]
        full_end(f_last, pf, pf_3, shard)
        results.append(w.local(shard, fac_shard))
        down_close()
        for copy in results[1:]:
            copy.wait()
        w.drain()
        w.drain_shared()

    vmem = pltpu.VMEM
    row, turned = vmem((512, 1024), BF16), vmem((1024, 512), BF16)
    wide_row, bias_like = vmem((512, 1024), F32), vmem((512, 512), F32)
    kept_like, spread_like = vmem((512, KEPT), F32), vmem((8, 128, 1024), BF16)
    greet(x, z, y, c)
    pl.run_scoped(front, row, row, kept_like, row, row, row, row, wide_row, bias_like, spread_like)
    pl.run_scoped(
        feed_forward,
        vmem((1024, 1024), BF16), vmem((HALF, 1024), BF16), turned, turned, turned, vmem((HALF, 1024), F32),
    )
    pl.run_scoped(
        attention,
        wide_row, row, row, row, row, row, bias_like, kept_like, spread_like, row, turned, turned,
        vmem((8, 1024), F32), vmem((2, 32, HALF), F32), vmem((2, 32, HALF), F32), vmem((PAD_UNITS, 1024), F32),
    )


def whole_all(*args):
    anywhere, vmem = pl.BlockSpec(memory_space=pl.ANY), pl.BlockSpec(memory_space=pltpu.VMEM)
    big = lambda *shape: pltpu.VMEM(shape, BF16)
    wide = lambda *shape: pltpu.VMEM(shape, F32)
    half = PAD_UNITS // 2

    def full_scratch(width):
        return [
            big(2, 4, 2, 2, 32, width), big(2, 4, 2, 32, width),
            big(2, 4, 16, width), big(4, 2, 16, width), big(4, 16, width), big(4, 16, width),
            big(3, 32, width),
        ]

    row = (512, 1024)
    outs = [
        (row, BF16),
        (row, F32),
        ((2, 32, HALF), F32),
        ((2, 32, HALF), F32),
        ((PAD_UNITS, 1024), F32),
        ((32, 1024), F32),
        ((32, FACTOR_PAD), F32),
        (row, BF16),
        ((512, KEPT), F32),
        (row, BF16),
        (row, BF16),
        (row, BF16),
        (row, BF16),
        (row, F32),
        ((512, 512), F32),
        ((8, 128, 1024), BF16),
    ]
    return pl.pallas_call(
        whole_kernel,
        out_shape=[jax.ShapeDtypeStruct(*o) for o in outs],
        in_specs=[anywhere, pl.BlockSpec(memory_space=pltpu.SMEM), anywhere, anywhere, vmem]
        + [anywhere] * 3,
        out_specs=[anywhere] * len(outs),
        scratch_shapes=[
            big(1024, 1024), big(1024, 1024),
            wide(1024, 1024), wide(1024, 1024), wide(512, 1024), wide(512, 1024),
            big(2, 4, 2, 2, 32, HALF), big(2, 4, 2, 2, 32, HALF), big(4, 2, 2, PAD_UNITS, 1024),
            big(2, 4, 2, 32, HALF), big(4, 2, 2, 32, HALF), big(4, 2, half, 1024), big(4, 2, half, 1024),
            big(3, 2, 2, 32, HALF), big(3, 2, 2, 32, HALF), big(4, half, 1024), big(4, half, 1024),
            big(3, 32, HALF), big(3, 32, HALF), big(3, PAD_UNITS, 1024),
            *full_scratch(1024),
            *full_scratch(FACTOR_PAD),
            wide(8, 1024), big(PAD_UNITS, 1024),
            pltpu.SemaphoreType.DMA((240,)),
            pltpu.SemaphoreType.DMA((240,)),
            pltpu.SemaphoreType.DMA((64,)),
        ],
        compiler_params=pltpu.CompilerParams(
            collective_id=0, has_side_effects=True, vmem_limit_bytes=62 * MIB
        ),
        name="whole_all",
    )(*args)[:7]


def cut_kernel(big_out, big_grad, fac_in, fac, out_in, gate, up, down, *refs):
    outs, (held_out, held_grad, sems) = refs[:-3], refs[-3:]
    loads, stores = [], []
    for part in range(4):
        rows = pl.ds(part * 128, 128)
        for src, held, dst in ((big_grad, held_grad, outs[1]), (big_out, held_out, outs[0])):
            at = len(loads)
            loads.append(pltpu.make_async_copy(src.at[rows], held.at[rows], sems.at[0, at]))
            stores.append(pltpu.make_async_copy(held.at[rows], dst.at[rows], sems.at[1, at]))
    for copy in loads:
        copy.start()
    pieces = (640, 96), (0, 384), (736, 32), (384, 128), (768, 32), (512, 128)
    for (start, size), ref in zip(pieces, outs[2:8], strict=True):
        ref[...] = fac[:, start : start + size]
    for load, store in zip(loads[:4], stores[:4], strict=True):
        load.wait()
        store.start()
    outs[8][...] = out_in[...]
    for src, ref in ((gate, outs[9]), (up, outs[10])):
        ref[:, 0:HALF] = src[0]
        ref[:, HALF:FF] = src[1]
    for load, store in zip(loads[4:], stores[4:], strict=True):
        load.wait()
        store.start()
    outs[11][...] = down[0:OWN_UNITS, :]
    maps = fac_in[...].astype(F32)
    lanes = lane_iota(32, FACTOR_PAD)
    total = jnp.sum(jnp.where(lanes < 800, maps * fac[...], 0.0), axis=-1, keepdims=True)
    gain = jnp.sum(jnp.where(lanes == 800, maps, 0.0), axis=-1, keepdims=True)
    tile = jnp.where(lane_iota(32) == 32, total / gain, fac[:, 768:896])
    tile = jnp.concatenate([tile, jnp.zeros((96, 128), F32)], axis=0).T
    outs[12][...] = tile[32:33, 0:32]
    outs[13][...] = tile[33:34, 0:32]
    for copy in stores:
        copy.wait()


def cut_all(*args):
    shapes = [(32, n) for n in (96, 384, 32, 128, 32, 128, 1024, FF, FF)] + [(OWN_UNITS, 1024), (1, 32), (1, 32)]
    anywhere, vmem = pl.BlockSpec(memory_space=pl.ANY), pl.BlockSpec(memory_space=pltpu.VMEM)
    return pl.pallas_call(
        cut_kernel,
        out_shape=[jax.ShapeDtypeStruct((512, 1024), BF16), jax.ShapeDtypeStruct((512, 1024), F32)]
        + [jax.ShapeDtypeStruct(s, F32) for s in shapes],
        in_specs=[anywhere] * 2 + [vmem] * 6,
        out_specs=[anywhere] * 2 + [vmem] * len(shapes),
        scratch_shapes=[
            pltpu.VMEM((512, 1024), BF16),
            pltpu.VMEM((512, 1024), F32),
            pltpu.SemaphoreType.DMA((2, 8)),
        ],
        compiler_params=pltpu.CompilerParams(vmem_limit_bytes=61 * MIB),
        name="cut_all",
    )(*args)


def local_paired(
    inputs, doc_lengths, w_aq, w_bq, w_ak, w_bk, w_av, w_bv,
    w_out, w_gate, w_up, w_down, gain_attn, gain_ffn, cotangent,
):
    spare = jnp.zeros((32, FACTOR_PAD - 802), BF16)
    fac = jnp.concatenate(
        [w_bq, w_bk, w_bv, w_aq, w_ak, w_av, gain_attn[:, None], gain_ffn[:, None], spare], axis=1
    )
    outputs, input_grad, gate_sum, up_sum, down_sum, out_sum, fac_sum = whole_all(
        inputs, doc_lengths, fac, w_out, w_down, w_gate, w_up, cotangent
    )
    *cut, gain_one, gain_two = cut_all(
        outputs, input_grad, fac, fac_sum, out_sum, gate_sum, up_sum, down_sum
    )
    return (*cut, gain_one[0], gain_two[0])


def solution(mesh):
    return jax.shard_map(
        local_paired if fits_pairs(mesh) else local,
        mesh=mesh,
        in_specs=(
            P(("dp", "fsdp"), None),
            P(("dp", "fsdp"), None),
            P(("dp", "fsdp"), None),
            P(("dp", "fsdp"), None),
            P(("dp", "fsdp"), None),
            P(("dp", "fsdp"), None),
            P(("dp", "fsdp"), None),
            P(("dp", "fsdp"), None),
            P(("dp", "fsdp"), None),
            P(("dp", "fsdp"), None),
            P(("dp", "fsdp"), None),
            P(("dp", "fsdp"), None),
            P(("dp", "fsdp")),
            P(("dp", "fsdp")),
            P(("dp", "fsdp"), None),
        ),
        out_specs=(
            P(("dp", "fsdp"), None),
            P(("dp", "fsdp"), None),
            P(("dp", "fsdp"), None),
            P(("dp", "fsdp"), None),
            P(("dp", "fsdp"), None),
            P(("dp", "fsdp"), None),
            P(("dp", "fsdp"), None),
            P(("dp", "fsdp"), None),
            P(("dp", "fsdp"), None),
            P(("dp", "fsdp"), None),
            P(("dp", "fsdp"), None),
            P(("dp", "fsdp"), None),
            P(("dp", "fsdp")),
            P(("dp", "fsdp")),
        ),
        check_vma=False,
    )
```

```python
import math

import jax
import jax.numpy as jnp
from jax import lax
from jax.experimental import pallas as pl
from jax.experimental.pallas import tpu as pltpu
from jax.sharding import PartitionSpec as P

HEADS = 16
HEAD_DIM = 64
RANK_Q = 6
RANK_KV = 2
FF = 2816


EPSILON = 1e-06
PRECISE = lax.Precision.HIGHEST


def factor_columns():
    return [
        RANK_Q * HEADS,
        RANK_Q * HEAD_DIM,
        RANK_KV * HEADS,
        RANK_KV * HEAD_DIM,
        RANK_KV * HEADS,
        RANK_KV * HEAD_DIM,
    ]


def split_columns(matrix):
    pieces = []
    offset = 0
    for columns in factor_columns():
        pieces.append(matrix[:, offset : offset + columns])
        offset += columns
    return pieces


def doc_layout(lengths, length):
    order = jnp.arange(lengths.shape[0], dtype=jnp.int32)
    doc_ends = jnp.sum(jnp.where(order[:, None] >= order[None, :], lengths[None, :], 0), axis=1)
    doc_starts = doc_ends - lengths
    places = jnp.arange(length, dtype=jnp.int32)
    segment = jnp.sum((places[:, None] >= doc_ends[None, :]).astype(jnp.int32), axis=1)
    owner = segment[:, None] == jnp.arange(lengths.shape[0], dtype=jnp.int32)[None, :]
    doc_first = jnp.sum(jnp.where(owner, doc_starts[None, :], 0), axis=1)
    return (segment, (places - doc_first).astype(jnp.float32))


def rotation(places):
    halfway = HEAD_DIM // 2
    freqs = jnp.exp(-math.log(10000.0) * jnp.arange(halfway, dtype=jnp.float32) / halfway)
    angles = places[..., None] * freqs
    return (jnp.cos(angles), jnp.sin(angles))


def rotate(factor, cos_table, sin_table):
    halfway = factor.shape[-1] // 2
    front_part = factor[..., :halfway]
    back_part = factor[..., halfway:]
    cos_part = cos_table[..., None, :]
    sin_part = sin_table[..., None, :]
    return jnp.concatenate(
        [
            front_part * cos_part - back_part * sin_part,
            front_part * sin_part + back_part * cos_part,
        ],
        axis=-1,
    )


def normalize(values, gain):
    scaling = lax.rsqrt(jnp.mean(values * values, axis=-1, keepdims=True) + EPSILON)
    unit_vals = values * scaling
    return (unit_vals * gain, unit_vals, scaling)


def norm_back(incoming, unit_vals, scaling, gain):
    unit_grad = incoming * gain
    grad_in = scaling * (
        unit_grad - unit_vals * jnp.mean(unit_grad * unit_vals, axis=-1, keepdims=True)
    )
    return (grad_in, jnp.sum(incoming * unit_vals, axis=0))


def block_scores(query_part, keys_low, seg_part, segment, place_part, places):
    scaling = HEAD_DIM ** (-0.5)
    scores = (
        jnp.einsum("thd,shd->hts", query_part, keys_low, preferred_element_type=jnp.float32)
        * scaling
    )
    allowed = (seg_part[:, None] == segment[None, :]) & (places[None, :] <= place_part[:, None])
    return jnp.where(allowed[None], scores, -1e30)


def attend_forward(queries, keys_low, values, segment):
    length = queries.shape[0]
    block_rows = min(512, length)
    places = jnp.arange(length, dtype=jnp.int32)

    def one_block(block_index):
        masked = block_scores(queries, keys_low, segment, segment, places, places)
        row_peak = jnp.max(masked, axis=-1, keepdims=True)
        exp_terms = jnp.exp(masked - row_peak)
        row_total = jnp.sum(exp_terms, axis=-1, keepdims=True)
        attn_probs = (exp_terms / row_total).astype(jnp.bfloat16)
        attended = jnp.einsum(
            "hts,shd->thd", attn_probs, values, preferred_element_type=jnp.float32
        )
        return (attended, (row_peak + jnp.log(row_total))[..., 0])

    attended, log_totals = lax.map(one_block, jnp.arange(length // block_rows, dtype=jnp.int32))
    return (attended.reshape(length, HEADS, HEAD_DIM), log_totals)


def attend_backward(queries, keys_low, values, segment, log_totals, mixed_grad):
    length = queries.shape[0]
    block_rows = min(512, length)
    places = jnp.arange(length, dtype=jnp.int32)
    scaling = HEAD_DIM ** (-0.5)

    def one_block(running, block_index):
        key_grad, value_grad = running
        masked = block_scores(queries, keys_low, segment, segment, places, places)
        attn_probs = jnp.exp(masked - log_totals[block_index][..., None])
        probs_low = attn_probs.astype(jnp.bfloat16)
        value_grad = value_grad + jnp.einsum(
            "hts,thd->shd", probs_low, mixed_grad, preferred_element_type=jnp.float32
        )
        probs_grad = jnp.einsum(
            "thd,shd->hts", mixed_grad, values, preferred_element_type=jnp.float32
        )
        inner_sum = jnp.sum(attn_probs * probs_grad, axis=-1, keepdims=True)
        score_grad = (attn_probs * (probs_grad - inner_sum)).astype(jnp.bfloat16)
        query_grad = (
            jnp.einsum("hts,shd->thd", score_grad, keys_low, preferred_element_type=jnp.float32)
            * scaling
        )
        key_grad = (
            key_grad
            + jnp.einsum("hts,thd->shd", score_grad, queries, preferred_element_type=jnp.float32)
            * scaling
        )
        return ((key_grad, value_grad), query_grad)

    empty = jnp.zeros((length, HEADS, HEAD_DIM), jnp.float32)
    (key_grad, value_grad), query_grad = lax.scan(
        one_block, (empty, empty), jnp.arange(length // block_rows, dtype=jnp.int32)
    )
    return (query_grad.reshape(length, HEADS, HEAD_DIM), key_grad, value_grad)


def factor_back(full_grad, a_part, b_part, rank_count):
    a_grad = jnp.einsum("thd,trd->trh", full_grad, b_part, precision=PRECISE) / rank_count
    b_grad = jnp.einsum("thd,trh->trd", full_grad, a_part, precision=PRECISE) / rank_count
    return (a_grad, b_grad)


def local(
    inputs,
    doc_lengths,
    w_aq,
    w_bq,
    w_ak,
    w_bk,
    w_av,
    w_bv,
    w_out,
    w_gate,
    w_up,
    w_down,
    gain_attn,
    gain_ffn,
    cotangent,
):
    length = inputs.shape[0]
    joined_local = jnp.concatenate([w_aq, w_bq, w_ak, w_bk, w_av, w_bv], axis=1)
    factor_w, out_w, gain_one = (
        lax.all_gather(joined_local, ("dp", "fsdp"), axis=0, tiled=True),
        lax.all_gather(w_out, ("dp", "fsdp"), axis=0, tiled=True),
        lax.all_gather(gain_attn, ("dp", "fsdp"), axis=0, tiled=True),
    )
    segment, places = doc_layout(doc_lengths[0], length)
    cos_table, sin_table = rotation(places)
    start_vals = inputs.astype(jnp.float32)
    normed_one, unit_one, scale_one = normalize(start_vals, gain_one.astype(jnp.float32))
    normed_low = normed_one.astype(jnp.bfloat16)
    factors = jnp.dot(normed_low, factor_w, preferred_element_type=jnp.float32)
    pieces = split_columns(factors)
    a_q = pieces[0].reshape(length, RANK_Q, HEADS)
    b_q = pieces[1].reshape(length, RANK_Q, HEAD_DIM)
    a_k = pieces[2].reshape(length, RANK_KV, HEADS)
    b_k = pieces[3].reshape(length, RANK_KV, HEAD_DIM)
    a_v = pieces[4].reshape(length, RANK_KV, HEADS)
    b_v = pieces[5].reshape(length, RANK_KV, HEAD_DIM)
    bq_rot = rotate(b_q, cos_table, sin_table)
    bk_rot = rotate(b_k, cos_table, sin_table)
    queries = (jnp.einsum("trh,trd->thd", a_q, bq_rot, precision=PRECISE) / RANK_Q).astype(
        jnp.bfloat16
    )
    keys_low = (jnp.einsum("trh,trd->thd", a_k, bk_rot, precision=PRECISE) / RANK_KV).astype(
        jnp.bfloat16
    )
    values = (jnp.einsum("trh,trd->thd", a_v, b_v, precision=PRECISE) / RANK_KV).astype(
        jnp.bfloat16
    )
    attended, log_totals = attend_forward(queries, keys_low, values, segment)
    mixed = attended.astype(jnp.bfloat16).reshape(length, HEADS * HEAD_DIM)
    resid = start_vals + jnp.dot(mixed, out_w, preferred_element_type=jnp.float32)
    gate_w, up_w, down_w, gain_two = (
        lax.all_gather(w_gate, ("dp", "fsdp"), axis=0, tiled=True),
        lax.all_gather(w_up, ("dp", "fsdp"), axis=0, tiled=True),
        lax.all_gather(w_down, ("dp", "fsdp"), axis=0, tiled=True),
        lax.all_gather(gain_ffn, ("dp", "fsdp"), axis=0, tiled=True),
    )
    normed_two, unit_two, scale_two = normalize(resid, gain_two.astype(jnp.float32))
    normed_two_low = normed_two.astype(jnp.bfloat16)
    gate_act = jnp.dot(normed_two_low, gate_w, preferred_element_type=jnp.float32)
    up_act = jnp.dot(normed_two_low, up_w, preferred_element_type=jnp.float32)
    hidden = (jax.nn.silu(gate_act) * up_act).astype(jnp.bfloat16)
    result = resid + jnp.dot(hidden, down_w, preferred_element_type=jnp.float32)
    outputs = result.astype(jnp.bfloat16)
    gate_w, up_w, down_w, gain_two = (
        lax.all_gather(w_gate, ("dp", "fsdp"), axis=0, tiled=True),
        lax.all_gather(w_up, ("dp", "fsdp"), axis=0, tiled=True),
        lax.all_gather(w_down, ("dp", "fsdp"), axis=0, tiled=True),
        lax.all_gather(gain_ffn, ("dp", "fsdp"), axis=0, tiled=True),
    )
    hidden_grad = jnp.einsum("tc,fc->tf", cotangent, down_w, preferred_element_type=jnp.float32)
    down_wgrad = jnp.einsum("tf,tc->fc", hidden, cotangent, preferred_element_type=jnp.float32)
    sig_vals = jax.nn.sigmoid(gate_act)
    gate_grad = (hidden_grad * up_act * sig_vals * (1.0 + gate_act * (1.0 - sig_vals))).astype(
        jnp.bfloat16
    )
    up_grad = (hidden_grad * jax.nn.silu(gate_act)).astype(jnp.bfloat16)
    normed_two_grad = jnp.einsum("tf,cf->tc", gate_grad, gate_w, preferred_element_type=jnp.float32)
    normed_two_grad = normed_two_grad + jnp.einsum(
        "tf,cf->tc", up_grad, up_w, preferred_element_type=jnp.float32
    )
    resid_norm_grad, gain_two_grad = norm_back(
        normed_two_grad, unit_two, scale_two, gain_two.astype(jnp.float32)
    )
    resid_grad = cotangent.astype(jnp.float32) + resid_norm_grad
    gate_rows = jnp.einsum(
        "tc,tf->cf", normed_two_low, gate_grad, preferred_element_type=jnp.float32
    )
    up_rows = jnp.einsum("tc,tf->cf", normed_two_low, up_grad, preferred_element_type=jnp.float32)
    gate_up_shard = lax.psum_scatter(
        jnp.concatenate([gate_rows, up_rows], axis=1),
        ("dp", "fsdp"),
        scatter_dimension=0,
        tiled=True,
    )
    gate_shard = gate_up_shard[:, :FF]
    up_shard = gate_up_shard[:, FF:]
    down_shard, gain_two_shard = (
        lax.psum_scatter(down_wgrad, ("dp", "fsdp"), scatter_dimension=0, tiled=True),
        lax.psum_scatter(gain_two_grad, ("dp", "fsdp"), scatter_dimension=0, tiled=True),
    )
    factor_w, out_w, gain_one = (
        lax.all_gather(joined_local, ("dp", "fsdp"), axis=0, tiled=True),
        lax.all_gather(w_out, ("dp", "fsdp"), axis=0, tiled=True),
        lax.all_gather(gain_attn, ("dp", "fsdp"), axis=0, tiled=True),
    )
    branch_grad = resid_grad.astype(jnp.bfloat16)
    out_wgrad = jnp.einsum("tc,td->cd", mixed, branch_grad, preferred_element_type=jnp.float32)
    mixed_grad = jnp.einsum("td,cd->tc", branch_grad, out_w, preferred_element_type=jnp.float32)
    mixed_grad = mixed_grad.astype(jnp.bfloat16).reshape(length, HEADS, HEAD_DIM)
    query_grad, key_grad, value_grad = attend_backward(
        queries, keys_low, values, segment, log_totals, mixed_grad
    )
    a_q_grad, bq_rot_grad = factor_back(query_grad, a_q, bq_rot, RANK_Q)
    a_k_grad, bk_rot_grad = factor_back(key_grad, a_k, bk_rot, RANK_KV)
    a_v_grad, b_v_grad = factor_back(value_grad, a_v, b_v, RANK_KV)
    neg_sin = -sin_table
    b_q_grad = rotate(bq_rot_grad, cos_table, neg_sin)
    b_k_grad = rotate(bk_rot_grad, cos_table, neg_sin)
    factor_grad = jnp.concatenate(
        [
            part.reshape(length, -1)
            for part in (a_q_grad, b_q_grad, a_k_grad, b_k_grad, a_v_grad, b_v_grad)
        ],
        axis=1,
    ).astype(jnp.bfloat16)
    factor_wgrad = jnp.einsum(
        "td,tc->dc", normed_low, factor_grad, preferred_element_type=jnp.float32
    )
    normed_one_grad = jnp.einsum(
        "tc,dc->td", factor_grad, factor_w, preferred_element_type=jnp.float32
    )
    input_norm_grad, gain_one_grad = norm_back(
        normed_one_grad, unit_one, scale_one, gain_one.astype(jnp.float32)
    )
    input_grad = resid_grad + input_norm_grad
    factor_shard, out_shard, gain_one_shard = (
        lax.psum_scatter(factor_wgrad, ("dp", "fsdp"), scatter_dimension=0, tiled=True),
        lax.psum_scatter(out_wgrad, ("dp", "fsdp"), scatter_dimension=0, tiled=True),
        lax.psum_scatter(gain_one_grad, ("dp", "fsdp"), scatter_dimension=0, tiled=True),
    )
    shard_pieces = split_columns(factor_shard)
    return (
        outputs,
        input_grad,
        shard_pieces[0],
        shard_pieces[1],
        shard_pieces[2],
        shard_pieces[3],
        shard_pieces[4],
        shard_pieces[5],
        out_shard,
        gate_shard,
        up_shard,
        down_shard,
        gain_one_shard,
        gain_two_shard,
    )


MESH_IDS = pl.DeviceIdType.MESH
HALF = FF // 2
OWN_UNITS = 88
DOWN_ROWS = 2 * OWN_UNITS
DOWN_A = 96
FACTOR_PAD = 896
MIB = 2**20


def fits_pairs(mesh):
    return dict(mesh.shape) == {"dp": 2, "fsdp": 16}


def place():
    x = lax.axis_index("dp")
    f = lax.axis_index("fsdp")
    return x, lax.div(f, 4), lax.rem(lax.div(f, 2), 2), lax.rem(f, 2)


def device(x, z, y, c):
    return (x, z * 4 + y * 2 + c)


def greet(x, z, y, c):
    partners = [
        device(x, z, y, 1 - c),
        device(1 - x, z, y, c),
        device(x, z, 1 - y, c),
        device(1 - x, z, y, 1 - c),
        device(x, z, 1 - y, 1 - c),
    ]
    for step in (1, 2, 3):
        other = lax.rem(z + step, 4)
        partners += [device(x, other, y, c), device(x, other, y, 1 - c)]
    barrier = pltpu.get_barrier_semaphore()
    for partner in partners:
        pl.semaphore_signal(barrier, inc=1, device_id=partner, device_id_type=MESH_IDS)
    pl.semaphore_wait(barrier, len(partners))


class Wires:
    def __init__(self, send_sems, recv_sems, local_sems):
        self.send_sems, self.recv_sems, self.local_sems = send_sems, recv_sems, local_sems
        self.sent, self.held = 0, 0
        self.open, self.shared = [], []

    def make(self, src, dst, to):
        at = self.sent
        self.sent += 1
        return pltpu.make_async_remote_copy(
            src_ref=src,
            dst_ref=dst,
            send_sem=self.send_sems.at[at],
            recv_sem=self.recv_sems.at[at],
            device_id=to,
            device_id_type=MESH_IDS,
        )

    def go(self, copy):
        copy.start()
        self.shared.append(copy)
        return copy

    def send(self, src, dst, to):
        copy = self.make(src, dst, to)
        copy.start()
        self.open.append(copy)
        return copy

    def local(self, src, dst):
        copy = pltpu.make_async_copy(src, dst, self.local_sems.at[self.held])
        self.held += 1
        copy.start()
        return copy

    def drain(self):
        for copy in self.open:
            copy.wait_send()
        self.open = []

    def drain_shared(self):
        for copy in self.shared:
            copy.wait_send()
        self.shared = []


def arrive(copies):
    for copy in copies:
        copy.wait_recv()


BLOCKS = ((0, 512), (512, 512), (1024, 384))
TILE = 256
NT = (((1,), (1,)), ((), ()))
TN = (((0,), (0,)), ((), ()))
F32, BF16 = jnp.float32, jnp.bfloat16


def dot(a, b, dims=None):
    if dims is None:
        return jnp.dot(a, b, preferred_element_type=F32)
    return lax.dot_general(a, b, dims, preferred_element_type=F32)


def add_low(dst, src):
    dst[...] = (dst[...].astype(F32) + src[...].astype(F32)).astype(BF16)


KEPT = 1152
COS_LANES = pl.ds(896, 128)
SIN_LANES = pl.ds(1024, 128)
A_LANES = pl.ds(640, 128)
V_LANES = pl.ds(768, 128)


def lane_iota(rows, lanes=128):
    return lax.broadcasted_iota(jnp.int32, (rows, lanes), 1)


def row_iota(rows, lanes=128):
    return lax.broadcasted_iota(jnp.int32, (rows, lanes), 0)


def doc_ends_of(lengths):
    one = lengths[0, 0]
    two = one + lengths[0, 1]
    return one, two, two + lengths[0, 2]


def make_tables(lengths, cos_ref, sin_ref):
    ends = doc_ends_of(lengths)

    def tile(i, _):
        rows = pl.ds(pl.multiple_of(i * 128, 128), 128)
        places = row_iota(128) + i * 128
        first = jnp.zeros((128, 128), jnp.int32)
        for end in ends:
            first = jnp.where(places >= end, end, first)
        lane = lane_iota(128)
        turn = lax.rem(lane, 32).astype(F32)
        freqs = jnp.exp(-math.log(10000.0) * turn / 32)
        angles = (places - first).astype(F32) * freqs
        cos_ref[rows, :] = jnp.cos(angles)
        sin_vals = jnp.sin(angles)
        sin_ref[rows, :] = jnp.where(lax.rem(lane, 64) < 32, -sin_vals, sin_vals)
        return 0

    lax.fori_loop(0, 4, tile, 0)


def make_bias(lengths, bias):
    ends = doc_ends_of(lengths)

    def tile(i, _):
        rows = pl.ds(pl.multiple_of(i * 128, 128), 128)
        t = row_iota(128, 512) + i * 128
        s = lane_iota(128, 512)
        own, key = jnp.zeros((128, 512), jnp.int32), jnp.zeros((128, 512), jnp.int32)
        for end in ends:
            own += (t >= end).astype(jnp.int32)
            key += (s >= end).astype(jnp.int32)
        bias[rows, :] = jnp.where((own == key) & (s <= t), 0.0, -1e30)
        return 0

    lax.fori_loop(0, 4, tile, 0)


def make_spread(spread):
    def rank(r, _):
        head = lax.div(lane_iota(128, 1024), HEAD_DIM) + r * HEADS
        spread[r] = jnp.where(row_iota(128, 1024) == head, 1.0, 0.0).astype(BF16)
        return 0

    lax.fori_loop(0, 8, rank, 0)


def swapped(tile):
    front = lax.rem(lane_iota(tile.shape[0]), 64) < 32
    return jnp.where(front, pltpu.roll(tile, 96, 1), pltpu.roll(tile, 32, 1))


def both_halves(tile, half):
    low = lane_iota(tile.shape[0]) < 64
    other = pltpu.roll(tile, 64, 1)
    return jnp.where(low, tile, other) if half == 0 else jnp.where(low, other, tile)


def two_terms(a):
    high = a.astype(BF16)
    return high, (a - high.astype(F32)).astype(BF16)


def expand(terms, spread_r):
    return dot(terms[0], spread_r) + dot(terms[1], spread_r)


def eight(tile):
    return jnp.concatenate([tile] * 8, axis=1)


def gain_rows(fac_all, gains):
    tile = fac_all[:, :, :, :, :, V_LANES].reshape(1024, 128).astype(F32)
    gains[...] = tile.T[32:40, :]


def make_factors(x_in, gains, fac_all, n1, kept, first, last):
    def tile(i, _):
        rows = pl.ds(pl.multiple_of(i * 256, 256), 256)
        vals = x_in[rows, :].astype(F32)
        scale = lax.rsqrt(jnp.mean(vals * vals, axis=-1, keepdims=True) + EPSILON)
        low = (vals * scale * gains[0:1, :]).astype(BF16)
        n1[rows, :] = low
        kept[rows, 0:FACTOR_PAD] = dot(low, fac_all[...].reshape(1024, FACTOR_PAD))
        return 0

    lax.fori_loop(first, last, tile, 0)


def make_heads(kept, cos_ref, sin_ref, spread, q, k, v, first, last):
    def tile(i, _):
        rows = pl.ds(pl.multiple_of(i * 128, 128), 128)
        turned = []
        for j in range(4):
            lanes = pl.ds(j * 128, 128)
            part = kept[rows, lanes]
            part = part * cos_ref[rows, :] + swapped(part) * sin_ref[rows, :]
            kept[rows, lanes] = part
            turned.append(part)
        terms = two_terms(kept[rows, A_LANES])
        total = jnp.zeros((128, 1024), F32)
        for r in range(RANK_Q):
            total += expand(terms, spread[r]) * eight(both_halves(turned[r // 2], r % 2))
        q[rows, :] = (total * (1.0 / RANK_Q)).astype(BF16) * BF16(HEAD_DIM**-0.5)
        total = jnp.zeros((128, 1024), F32)
        for r in range(RANK_KV):
            total += expand(terms, spread[RANK_Q + r]) * eight(both_halves(turned[3], r))
        k[rows, :] = (total * (1.0 / RANK_KV)).astype(BF16)
        terms = two_terms(kept[rows, V_LANES])
        plain = kept[rows, pl.ds(512, 128)]
        total = jnp.zeros((128, 1024), F32)
        for r in range(RANK_KV):
            total += expand(terms, spread[r]) * eight(both_halves(plain, r))
        v[rows, :] = (total * (1.0 / RANK_KV)).astype(BF16)
        return 0

    lax.fori_loop(first, last, tile, 0)


def only(tile, half):
    low = lane_iota(tile.shape[0]) < 64
    keep = low if half == 0 else jnp.logical_not(low)
    return jnp.where(keep, tile, jnp.zeros_like(tile))


def soft(q_rows, k_cols, bias_block):
    scores = dot(q_rows, k_cols, NT) + bias_block
    terms = jnp.exp(scores - jnp.max(scores, axis=-1, keepdims=True))
    return terms * (1.0 / jnp.sum(terms, axis=-1, keepdims=True))


def attend_pairs(q, k, v, bias, mixed, first, last):
    def pair(p, _):
        lanes = pl.ds(pl.multiple_of(p * 128, 128), 128)
        for start, extent in ((0, 256), (256, 512)):
            rows, cols = pl.ds(start, 256), pl.ds(0, extent)
            q_rows, k_cols, v_cols = q[rows, lanes], k[cols, lanes], v[cols, lanes]
            halves = []
            for half in (0, 1):
                probs = soft(only(q_rows, half), k_cols, bias[rows, cols]).astype(BF16)
                halves.append(dot(probs, v_cols))
            low = lane_iota(256) < 64
            mixed[rows, lanes] = jnp.where(low, halves[0], halves[1]).astype(BF16)
        return 0

    lax.fori_loop(first, last, pair, 0)


def make_resid(x_in, mixed, out_all, gains, resid, n2, first, last):
    def tile(i, _):
        rows = pl.ds(pl.multiple_of(i * 256, 256), 256)
        base = x_in[rows, :].astype(F32) + dot(mixed[rows, :], out_all[...].reshape(1024, 1024))
        resid[rows, :] = base
        scale = lax.rsqrt(jnp.mean(base * base, axis=-1, keepdims=True) + EPSILON)
        n2[rows, :] = (base * scale * gains[1:2, :]).astype(BF16)
        return 0

    lax.fori_loop(first, last, tile, 0)


def head_grads(q, q_t, k, v, mg, mg_t, bias, dq, dkv_t, first, last):
    def pair(p, _):
        at = pl.multiple_of(p * 128, 128)
        lanes = pl.ds(at, 128)
        for start, extent in ((256, 512), (0, 256)):
            rows, cols = pl.ds(start, 256), pl.ds(0, extent)
            q_rows, mg_rows = q[rows, lanes], mg[rows, lanes]
            k_cols, v_cols = k[cols, lanes], v[cols, lanes]
            halves = []
            for half in (0, 1):
                own = pl.ds(pl.multiple_of(at + half * 64, 64), 64)
                probs = soft(only(q_rows, half), k_cols, bias[rows, cols])
                probs_grad = dot(only(mg_rows, half), v_cols, NT)
                inner = jnp.sum(probs * probs_grad, axis=-1, keepdims=True)
                score_grad = (probs * (probs_grad - inner)).astype(BF16)
                dv = dot(mg_t[own, rows], probs.astype(BF16))
                dk = dot(q_t[own, rows], score_grad)
                if start:
                    dkv_t[own, 0:512] = dk
                    dkv_t[own, 512:1024] = dv
                else:
                    dkv_t[own, 0:256] += dk
                    dkv_t[own, 512:768] += dv
                halves.append(dot(score_grad, k_cols))
            low = lane_iota(256) < 64
            dq[rows, lanes] = jnp.where(low, halves[0], halves[1]) * HEAD_DIM**-0.5
        return 0

    lax.fori_loop(first, last, pair, 0)


def fold(product):
    total = product[:, 0:128]
    for j in range(1, 8):
        total += product[:, j * 128 : (j + 1) * 128]
    return total + pltpu.roll(total, 64, 1)


def rank_grads(full, terms, ranks, duplicates, spread):
    a_grad, b_grads = jnp.zeros((full.shape[0], 128), F32), []
    for r, twice in zip(ranks, duplicates, strict=True):
        spread_r = spread[r]
        a_grad += dot((full * eight(twice)).astype(BF16), spread_r, NT)
        b_grads.append(fold(full * expand(terms, spread_r)))
    return a_grad, b_grads


def pick(low_half, high_half):
    return jnp.where(lane_iota(low_half.shape[0]) < 64, low_half, high_half)


def factor_grads(dq, dkv_t, kept, spread, fg, fg_at, first, last):
    def tile(i, _):
        at = pl.multiple_of(i * 128, 128)
        rows = pl.ds(at, 128)
        out = pl.ds(pl.multiple_of(fg_at + i * 128, 128), 128)
        cos_rows, sin_rows = kept[rows, COS_LANES], kept[rows, SIN_LANES]

        def turn_back(part):
            return part * cos_rows - swapped(part) * sin_rows

        tiles = [kept[rows, pl.ds(j * 128, 128)] for j in range(5)]
        terms = two_terms(kept[rows, A_LANES])
        a_q, b_q = rank_grads(
            dq[rows, :],
            terms,
            range(RANK_Q),
            [both_halves(tiles[r // 2], r % 2) for r in range(RANK_Q)],
            spread,
        )
        for j in range(RANK_Q // 2):
            part = pick(b_q[2 * j], b_q[2 * j + 1]) * (1.0 / RANK_Q)
            fg[out, pl.ds(j * 128, 128)] = turn_back(part).astype(BF16)
        a_k, b_k = rank_grads(
            dkv_t[:, rows].T,
            terms,
            range(RANK_Q, RANK_Q + RANK_KV),
            [both_halves(tiles[3], r) for r in range(RANK_KV)],
            spread,
        )
        part = pick(b_k[0], b_k[1]) * (1.0 / RANK_KV)
        fg[out, pl.ds(384, 128)] = turn_back(part).astype(BF16)
        fg[out, A_LANES] = (a_q * (1.0 / RANK_Q) + a_k * (1.0 / RANK_KV)).astype(BF16)
        a_v, b_v = rank_grads(
            dkv_t[:, pl.ds(pl.multiple_of(512 + i * 128, 128), 128)].T,
            two_terms(kept[rows, V_LANES]),
            range(RANK_KV),
            [both_halves(tiles[4], r) for r in range(RANK_KV)],
            spread,
        )
        fg[out, pl.ds(512, 128)] = (pick(b_v[0], b_v[1]) * (1.0 / RANK_KV)).astype(BF16)
        fg[out, V_LANES] = (a_v * (1.0 / RANK_KV)).astype(BF16)
        return 0

    lax.fori_loop(first, last, tile, 0)


def whole_kernel(
    x_hbm, lengths, fac_in, wo_in, wd_in, wg_in, wu_in, cot_in,
    outputs, input_grad, gate_out, up_out, down_out, out_shard, fac_shard,
    n1_kept, kept_kept, q_kept, k_kept, v_kept, mixed_kept, resid_kept, bias_kept, spread_kept,
    n2, cot, out_acc, ng_acc, out_twin, ng_twin,
    g_buf, u_buf, d_buf, g1, u1, da1, db1, g2, u2, gz2, uz2, da2, db2, g3, u3, gz3, uz3, d3,
    po, po_twin, po_1a, po_1b, po_2a, po_2b, po_3,
    pf, pf_twin, pf_1a, pf_1b, pf_2a, pf_2b, pf_3,
    gains, wd_own,
    ss, rs, ls,
):
    x, z, y, c = place()
    x_peer, y_peer, twin = device(1 - x, z, y, c), device(x, z, 1 - y, c), device(x, z, y, 1 - c)
    z_peers = [lax.rem(z + step, 4) for step in (1, 2, 3)]
    w = Wires(ss, rs, ls)
    a_rows, b_rows = pl.ds(0, 16), pl.ds(16, 16)
    a_down, b_down = pl.ds(0, DOWN_A), pl.ds(DOWN_A, DOWN_ROWS - DOWN_A)

    def same(view, to):
        return w.make(view, view, to)

    def own_copy(src, dst):
        w.held += 1
        return pltpu.make_async_copy(src, dst, ls.at[w.held - 1])

    def go(*copies):
        for copy in copies:
            w.go(copy)

    def ended(copies):
        for copy in copies:
            copy.wait_send()
        w.shared = [copy for copy in w.shared if all(copy is not other for other in copies)]

    class Whole:
        def __init__(self, src, ref, from_twin, one_a, one_b, two_a, two_b, three):
            self.ref, self.from_twin, self.one, self.two, self.three = (
                ref, from_twin, (one_a, one_b), (two_a, two_b), three,
            )
            slot = ref.at[x, z, y, c]
            self.own = own_copy(src, slot)
            self.z = [w.make(src, slot, device(x, zz, y, c)) for zz in z_peers]
            self.two_a = same(ref.at[x, :, y, c, a_rows], x_peer)
            self.two_b = same(ref.at[x, :, y, c, b_rows], y_peer)
            self.three_a = same(ref.at[:, :, y, c, a_rows], y_peer)
            self.three_b = same(ref.at[x, :, :, c, b_rows], x_peer)
            self.passed = [
                same(ref.at[x, :, y, c], twin),
                same(ref.at[1 - x, :, y, c, a_rows], twin),
                same(ref.at[x, :, 1 - y, c, b_rows], twin),
                same(ref.at[:, :, 1 - y, c, a_rows], twin),
                same(ref.at[1 - x, :, :, c, b_rows], twin),
            ]
            self.g_twin = w.make(ref.at[:, :, :, 1 - c], from_twin, twin)
            self.g_one_a = w.make(ref.at[:, :, 1 - y, c, a_rows], one_a, y_peer)
            self.g_one_b = w.make(ref.at[1 - x, :, :, c, b_rows], one_b, x_peer)
            self.g_two_a = w.make(ref.at[1 - x, :, y, c, a_rows], two_a, x_peer)
            self.g_two_b = w.make(ref.at[x, :, 1 - y, c, b_rows], two_b, y_peer)
            self.g_z = [
                w.make(ref.at[x, zz, y, c], three.at[step], device(x, zz, y, c))
                for step, zz in enumerate(z_peers)
            ]

        def start(self):
            self.own.start()
            go(*self.z)

        def step_two(self):
            self.own.wait()
            arrive(self.z)
            go(self.two_a, self.two_b, self.passed[0])

        def step_three_a(self):
            self.two_a.wait_recv()
            go(self.three_a, self.passed[1])

        def step_three_b(self):
            self.two_b.wait_recv()
            go(self.three_b, self.passed[2])

        def pass_a(self):
            self.three_a.wait_recv()
            go(self.passed[3])

        def pass_b(self):
            self.three_b.wait_recv()
            go(self.passed[4])

        def here(self):
            arrive(self.passed)

        def gathered(self):
            ended([*self.z, self.two_a, self.two_b, self.three_a, self.three_b, *self.passed])

        def sum_zero(self):
            go(self.g_twin)

        def sum_one(self):
            self.g_twin.wait_recv()

            def add(i, _):
                xx, zz, yy = lax.div(i, 8), lax.rem(lax.div(i, 2), 4), lax.rem(i, 2)
                add_low(self.ref.at[xx, zz, yy, c], self.from_twin.at[xx, zz, yy])
                return 0

            lax.fori_loop(0, 16, add, 0)
            go(self.g_one_a, self.g_one_b)

        def sum_two_a(self):
            self.g_one_a.wait_recv()

            def add(i, _):
                s, zz = lax.div(i, 4), lax.rem(i, 4)
                add_low(self.ref.at[s, zz, y, c, a_rows], self.one[0].at[s, zz])
                return 0

            lax.fori_loop(0, 8, add, 0)
            go(self.g_two_a)

        def sum_two_b(self):
            self.g_one_b.wait_recv()

            def add(i, _):
                zz, s = lax.div(i, 2), lax.rem(i, 2)
                add_low(self.ref.at[x, zz, s, c, b_rows], self.one[1].at[zz, s])
                return 0

            lax.fori_loop(0, 8, add, 0)
            go(self.g_two_b)

        def sum_three(self):
            arrive([self.g_two_a, self.g_two_b])

            def add(i, _):
                add_low(self.ref.at[x, i, y, c, a_rows], self.two[0].at[i])
                add_low(self.ref.at[x, i, y, c, b_rows], self.two[1].at[i])
                return 0

            lax.fori_loop(0, 4, add, 0)
            go(*self.g_z)

        def sum_end(self, out):
            arrive(self.g_z)
            out[...] = (
                self.ref[x, z, y, c].astype(F32)
                + self.three[0].astype(F32)
                + self.three[1].astype(F32)
                + self.three[2].astype(F32)
            )

    maps = Whole(fac_in, pf, pf_twin, pf_1a, pf_1b, pf_2a, pf_2b, pf_3)
    proj = Whole(wo_in, po, po_twin, po_1a, po_1b, po_2a, po_2b, po_3)
    both = (g_buf, u_buf)

    class Block:
        def __init__(self, b, gather_z_first, sum_z_last):
            start, size = BLOCKS[b]
            self.z_first, self.z_last, self.size = gather_z_first, sum_z_last, size
            self.cols = cols = pl.ds(start, size)
            mine = pl.ds(pl.multiple_of(c * HALF + start, 128), size)
            theirs = pl.ds(pl.multiple_of((1 - c) * HALF + start, 128), size)
            self.own, self.first = [], []
            for src, buf in ((wg_in, g_buf), (wu_in, u_buf)):
                slot = buf.at[x, z, y, c]
                self.own.append(own_copy(src.at[:, mine], slot.at[:, cols]))
                if gather_z_first:
                    for zz in z_peers:
                        self.first.append(w.make(src.at[:, mine], slot.at[:, cols], device(x, zz, y, c)))
                        self.first.append(w.make(src.at[:, theirs], slot.at[:, cols], device(x, zz, y, 1 - c)))
                else:
                    a_slot, b_slot = slot.at[a_rows, cols], slot.at[b_rows, cols]
                    self.first += [
                        w.make(src.at[a_rows, mine], a_slot, x_peer),
                        w.make(src.at[a_rows, theirs], a_slot, device(1 - x, z, y, 1 - c)),
                        w.make(src.at[b_rows, mine], b_slot, y_peer),
                        w.make(src.at[b_rows, theirs], b_slot, device(x, z, 1 - y, 1 - c)),
                    ]
                self.first.append(w.make(src.at[:, theirs], slot.at[:, cols], twin))
            if gather_z_first:
                self.second_a = [same(buf.at[x, :, y, :, a_rows, cols], x_peer) for buf in both]
                self.second_b = [same(buf.at[x, :, y, :, b_rows, cols], y_peer) for buf in both]
            else:
                self.second_a = [
                    same(buf.at[:, z, y, :, a_rows, cols], device(x, zz, y, c)) for buf in both for zz in z_peers
                ]
                self.second_b = [
                    same(buf.at[x, z, :, :, b_rows, cols], device(x, zz, y, c)) for buf in both for zz in z_peers
                ]
            self.third_a = [same(buf.at[:, :, y, :, a_rows, cols], y_peer) for buf in both]
            self.third_b = [same(buf.at[x, :, :, :, b_rows, cols], x_peer) for buf in both]
            self.one_u = w.make(u_buf.at[1 - x, :, :, :, :, cols], u1.at[:, :, :, :, cols], x_peer)
            self.one_g = w.make(g_buf.at[:, :, 1 - y, :, :, cols], g1.at[:, :, :, :, cols], y_peer)
            if sum_z_last:
                self.two_u = [w.make(u_buf.at[x, :, 1 - y, :, :, cols], uz2, y_peer)]
                self.two_g = [w.make(g_buf.at[1 - x, :, y, :, :, cols], gz2, x_peer)]
                self.three_u, self.three_g = [], []
                for copies, buf, three in ((self.three_u, u_buf, uz3), (self.three_g, g_buf, gz3)):
                    for core, rel in ((c, 0), (1 - c, 1)):
                        for step, zz in enumerate(z_peers):
                            copies.append(
                                w.make(buf.at[x, zz, y, core, :, cols], three.at[rel, step + 1], device(x, zz, y, core))
                            )
                    copies.append(w.make(buf.at[x, z, y, 1 - c, :, cols], three.at[1, 0], twin))
            else:
                self.two_u = [
                    w.make(u_buf.at[x, zz, :, :, :, cols], u2.at[step, :, :, :, cols], device(x, zz, y, c))
                    for step, zz in enumerate(z_peers)
                ]
                self.two_g = [
                    w.make(g_buf.at[:, zz, y, :, :, cols], g2.at[step, :, :, :, cols], device(x, zz, y, c))
                    for step, zz in enumerate(z_peers)
                ]
                self.three_u = [
                    w.make(u_buf.at[x, z, 1 - y, c, :, cols], u3.at[0, :, cols], y_peer),
                    w.make(u_buf.at[x, z, 1 - y, 1 - c, :, cols], u3.at[2, :, cols], device(x, z, 1 - y, 1 - c)),
                    w.make(u_buf.at[x, z, y, 1 - c, :, cols], u3.at[1, :, cols], twin),
                ]
                self.three_g = [
                    w.make(g_buf.at[1 - x, z, y, c, :, cols], g3.at[0, :, cols], x_peer),
                    w.make(g_buf.at[1 - x, z, y, 1 - c, :, cols], g3.at[2, :, cols], device(1 - x, z, y, 1 - c)),
                    w.make(g_buf.at[x, z, y, 1 - c, :, cols], g3.at[1, :, cols], twin),
                ]

        def start(self):
            for copy in self.own:
                copy.start()
            go(*self.first)

        def second(self):
            for copy in self.own:
                copy.wait()
            arrive(self.first)
            go(*self.second_a, *self.second_b)

        def step_three_a(self):
            arrive(self.second_a)
            go(*self.third_a)

        def step_three_b(self):
            arrive(self.second_b)
            go(*self.third_b)

        def here(self):
            arrive(self.third_a)
            arrive(self.third_b)

        def gathered(self):
            ended([*self.second_a, *self.second_b, *self.third_a, *self.third_b])

        def sum_one(self):
            go(self.one_u, self.one_g)

        def sum_two_u(self):
            self.one_u.wait_recv()

            def add(i, _):
                zz, yy = lax.div(i, 2), lax.rem(i, 2)
                add_low(u_buf.at[x, zz, yy, :, :, self.cols], u1.at[zz, yy, :, :, self.cols])
                return 0

            lax.fori_loop(0, 8, add, 0)
            go(*self.two_u)

        def sum_two_g(self):
            self.one_g.wait_recv()

            def add(i, _):
                xx, zz = lax.div(i, 4), lax.rem(i, 4)
                add_low(g_buf.at[xx, zz, y, :, :, self.cols], g1.at[xx, zz, :, :, self.cols])
                return 0

            lax.fori_loop(0, 8, add, 0)
            go(*self.two_g)

        def sum_three_u(self):
            arrive(self.two_u)
            cols = self.cols
            if self.z_last:

                def add(i, _):
                    add_low(u_buf.at[x, i, y, :, :, cols], uz2.at[i])
                    return 0

                lax.fori_loop(0, 4, add, 0)
            else:

                def add(i, _):
                    add_three(u_buf.at[x, z, i, :, :, cols], [u2.at[k, i, :, :, cols] for k in range(3)])
                    return 0

                lax.fori_loop(0, 2, add, 0)
            go(*self.three_u)

        def sum_three_g(self):
            arrive(self.two_g)
            cols = self.cols
            if self.z_last:

                def add(i, _):
                    add_low(g_buf.at[x, i, y, :, :, cols], gz2.at[i])
                    return 0

                lax.fori_loop(0, 4, add, 0)
            else:

                def add(i, _):
                    add_three(g_buf.at[i, z, y, :, :, cols], [g2.at[k, i, :, :, cols] for k in range(3)])
                    return 0

                lax.fori_loop(0, 2, add, 0)
            go(*self.three_g)

        def sum_end(self, gate_sum, up_sum):
            arrive(self.three_u)
            arrive(self.three_g)
            cols = self.cols
            for buf, three, last, out in ((g_buf, g3, gz3, gate_sum), (u_buf, u3, uz3, up_sum)):
                own = buf[x, z, y, c, :, cols].astype(F32)
                if self.z_last:
                    for step in (1, 2, 3):
                        own += last[0, step].astype(F32)
                    other = last[1, 0].astype(F32)
                    for step in (1, 2, 3):
                        other += last[1, step].astype(F32)
                else:
                    own += three[0, :, cols].astype(F32)
                    other = three[1, :, cols].astype(F32) + three[2, :, cols].astype(F32)
                out[c, :, cols] = own
                out[1 - c, :, cols] = other

    def add_three(dst, three):
        total = dst[...].astype(F32)
        for src in three:
            total += src[...].astype(F32)
        dst[...] = total.astype(BF16)

    blocks = [Block(0, True, False), Block(1, False, False), Block(2, False, True)]

    other_core = device(1 - x, z, y, 1 - c)
    d_swap = w.make(wd_own, d_buf.at[z, y, 1 - x], other_core)
    d_keep = own_copy(wd_own, d_buf.at[z, y, x])
    slot = d_buf.at[z, y, x]
    d_z_a = [same(slot.at[a_down], device(x, zz, y, c)) for zz in z_peers]
    d_z_b = [same(slot.at[b_down], device(x, zz, y, c)) for zz in z_peers]
    d_two_a, d_two_b = same(d_buf.at[:, y, x, a_down], x_peer), same(d_buf.at[:, y, x, b_down], y_peer)
    d_three_a, d_three_b = same(d_buf.at[:, y, :, a_down], y_peer), same(d_buf.at[:, :, x, b_down], x_peer)
    d_one_ga = w.make(d_buf.at[:, 1 - y, :, a_down], da1, y_peer)
    d_one_gb = w.make(d_buf.at[:, :, 1 - x, b_down], db1, x_peer)
    d_two_ga = w.make(d_buf.at[:, y, 1 - x, a_down], da2, x_peer)
    d_two_gb = w.make(d_buf.at[:, 1 - y, x, b_down], db2, y_peer)
    d_z_g = [w.make(d_buf.at[zz, y, x], d3.at[step], device(x, zz, y, c)) for step, zz in enumerate(z_peers)]

    def either(kept, swapped, verb):
        @pl.when(x == c)
        def _():
            getattr(kept, verb)()

        @pl.when(x != c)
        def _():
            getattr(swapped, verb)()

    def down_second():
        either(d_keep, d_swap, "wait")
        go(*d_z_a, *d_z_b)

    def down_two_a():
        arrive(d_z_a)
        go(d_two_a)

    def down_two_b():
        arrive(d_z_b)
        go(d_two_b)

    def down_three_a():
        d_two_a.wait_recv()
        go(d_three_a)

    def down_three_b():
        d_two_b.wait_recv()
        go(d_three_b)

    def down_sum_two_a():
        d_one_ga.wait_recv()

        def add(i, _):
            zz, s = lax.div(i, 2), lax.rem(i, 2)
            add_low(d_buf.at[zz, y, s, a_down], da1.at[zz, s])
            return 0

        lax.fori_loop(0, 8, add, 0)
        go(d_two_ga)

    def down_sum_two_b():
        d_one_gb.wait_recv()

        def add(i, _):
            zz, s = lax.div(i, 2), lax.rem(i, 2)
            add_low(d_buf.at[zz, s, x, b_down], db1.at[zz, s])
            return 0

        lax.fori_loop(0, 8, add, 0)
        go(d_two_gb)

    def down_sum_three():
        arrive([d_two_ga, d_two_gb])

        def add(i, _):
            add_low(d_buf.at[i, y, x, a_down], da2.at[i])
            add_low(d_buf.at[i, y, x, b_down], db2.at[i])
            return 0

        lax.fori_loop(0, 4, add, 0)
        go(*d_z_g)

    n2_twin = w.make(n2.at[0:512], n2.at[512:1024], twin)
    cot_twin = w.make(cot_in, cot.at[512:1024], twin)
    ng_send = w.make(ng_acc.at[512:1024], ng_twin, twin)
    out_send = w.make(out_acc.at[512:1024], out_twin, twin)
    own_cot = own_copy(cot_in, cot.at[0:512])

    def front(x_in, n1, kept, q, k, v, mixed, resid, bias, spread):
        cos_ref, sin_ref = kept.at[:, COS_LANES], kept.at[:, SIN_LANES]
        x_load = w.local(x_hbm, x_in)
        own_cot.start()
        proj.start()
        maps.start()
        rows = wd_in[...].astype(F32)
        rows = jnp.concatenate([rows[:, 0:512], rows[:, 512:1024]], axis=0)
        wd_own[...] = rows.astype(BF16)
        either(d_keep, d_swap, "start")
        for block in (blocks[1], blocks[2], blocks[0]):
            block.start()
        make_tables(lengths, cos_ref, sin_ref)
        make_spread(spread)
        make_bias(lengths, bias)
        down_second()
        blocks[1].second()
        blocks[2].second()
        proj.step_two()
        proj.step_three_a()
        proj.step_three_b()
        maps.step_two()
        go(cot_twin)
        proj.pass_a()
        proj.pass_b()
        maps.step_three_b()
        maps.step_three_a()
        blocks[0].second()
        x_load.wait()
        maps.pass_b()
        maps.pass_a()
        maps.here()
        gain_rows(pf, gains)
        make_factors(x_in, gains, pf, n1, kept, 0, 1)
        down_two_a()
        make_factors(x_in, gains, pf, n1, kept, 1, 2)
        saves = [w.local(n1, n1_kept)]
        blocks[0].step_three_a()
        make_heads(kept, cos_ref, sin_ref, spread, q, k, v, 0, 1)
        blocks[0].step_three_b()
        make_heads(kept, cos_ref, sin_ref, spread, q, k, v, 1, 4)
        down_two_b()
        for src, dst in (
            (kept, kept_kept),
            (q, q_kept),
            (k, k_kept),
            (v, v_kept),
            (bias, bias_kept),
            (spread, spread_kept),
        ):
            saves.append(w.local(src, dst))
        attend_pairs(q, k, v, bias, mixed, 0, 2)
        down_three_a()
        attend_pairs(q, k, v, bias, mixed, 2, 7)
        blocks[1].step_three_a()
        attend_pairs(q, k, v, bias, mixed, 7, 8)
        saves.append(w.local(mixed, mixed_kept))
        proj.here()
        make_resid(x_in, mixed, po, gains, resid, n2, 0, 1)
        down_three_b()
        make_resid(x_in, mixed, po, gains, resid, n2, 1, 2)
        saves.append(w.local(resid, resid_kept))
        go(n2_twin)
        for copy in saves:
            copy.wait()

    def feed_forward(n2_t, wd, hid, gg, ug, d_acc):
        own_cot.wait()

        def turn(i):
            rows = pl.ds(i * TILE, TILE)
            n2_t[:, rows] = n2[rows, :].T

        def forward(b, low, high):
            start, size = BLOCKS[b]
            cols = pl.ds(start, size)

            def tile(i, _):
                rows = pl.ds(pl.multiple_of(i * TILE, TILE), TILE)
                n2_rows, cot_rows = n2[rows, :], cot[rows, :]
                wg = g_buf[:, :, :, :, :, cols].reshape(1024, size)
                wu = u_buf[:, :, :, :, :, cols].reshape(1024, size)
                gate = dot(n2_rows, wg)
                up = dot(n2_rows, wu)
                hid_grad = dot(cot_rows, wd[cols, :], NT)
                sig = jax.nn.sigmoid(gate)
                silu = gate * sig
                hidden = (silu * up).astype(BF16)
                gate_grad = (hid_grad * up * sig * (1.0 + gate * (1.0 - sig))).astype(BF16)
                up_grad = (hid_grad * silu).astype(BF16)
                hid[rows, 0:size] = hidden
                gg[rows, 0:size] = gate_grad
                ug[rows, 0:size] = up_grad
                out_part = dot(hidden, wd[cols, :])
                ng_part = dot(gate_grad, wg, NT) + dot(up_grad, wu, NT)
                if b == 0:
                    out_acc[rows, :] = out_part
                    ng_acc[rows, :] = ng_part
                else:
                    out_acc[rows, :] += out_part
                    ng_acc[rows, :] += ng_part
                return 0

            lax.fori_loop(low, high, tile, 0)

        def weight_grads(b):
            blocks[b].gathered()
            start, size = BLOCKS[b]
            cols = pl.ds(start, size)

            def side(i, _):
                rows = pl.ds(pl.multiple_of(i * 512, 512), 512)
                part = dot(n2_t[rows, :], ug[:, 0:size])
                u_buf[i, :, :, :, :, cols] = part.astype(BF16).reshape(4, 2, 2, 32, size)
                part = dot(n2_t[rows, :], gg[:, 0:size])
                g_buf[i, :, :, :, :, cols] = part.astype(BF16).reshape(4, 2, 2, 32, size)
                return 0

            lax.fori_loop(0, 2, side, 0)
            blocks[b].sum_one()
            d_acc[cols, :] = dot(hid[:, 0:size], cot[...], TN)

        turn(0)
        turn(1)
        arrive([n2_twin, cot_twin])
        turn(2)
        turn(3)
        blocks[1].step_three_b()
        blocks[2].step_three_a()
        d_three_a.wait_recv()
        d_three_b.wait_recv()

        def gather_rows(s, _):
            rows = d_buf[lax.div(s, 4), lax.rem(lax.div(s, 2), 2), lax.rem(s, 2)].astype(F32)
            at = pl.ds(pl.multiple_of(s * OWN_UNITS, 8), OWN_UNITS)
            d_acc[at, 0:512] = rows[0:OWN_UNITS]
            d_acc[at, 512:1024] = rows[OWN_UNITS:DOWN_ROWS]
            return 0

        lax.fori_loop(0, 16, gather_rows, 0)

        def low_rows(i, _):
            rows = pl.ds(pl.multiple_of(i * 128, 128), 128)
            wd[rows, :] = d_acc[rows, :].astype(BF16)
            return 0

        lax.fori_loop(0, HALF // 128, low_rows, 0)
        blocks[0].here()
        forward(0, 0, 2)
        blocks[2].step_three_b()
        forward(0, 2, 4)
        weight_grads(0)
        blocks[1].here()
        forward(1, 0, 4)
        weight_grads(1)
        blocks[2].here()
        forward(2, 2, 4)
        go(ng_send, out_send)
        blocks[0].sum_two_g()
        blocks[0].sum_two_u()
        forward(2, 0, 2)
        weight_grads(2)
        ended([*d_z_a, *d_z_b, d_two_a, d_two_b, d_three_a, d_three_b])

        def spread_rows(s, _):
            rows = d_acc[pl.ds(pl.multiple_of(s * OWN_UNITS, 8), OWN_UNITS), :]
            rows = jnp.concatenate([rows[:, 0:512], rows[:, 512:1024]], axis=0)
            d_buf[lax.div(s, 4), lax.rem(lax.div(s, 2), 2), lax.rem(s, 2)] = rows.astype(BF16)
            return 0

        lax.fori_loop(0, 16, spread_rows, 0)
        go(d_one_ga, d_one_gb)

    branch, mg = cot.at[0:512], cot.at[512:1024]

    def attention(
        resid, x_in, mixed, q, k, v, bias, kept, spread, n1, q_t, mg_t, gain_two,
        gate_sum, up_sum, d_sum,
    ):
        d_back = w.make(d_sum, down_out, other_core)
        d_stay = own_copy(d_sum, down_out)
        loads = [
            w.local(src, dst)
            for src, dst in (
                (resid_kept, resid),
                (mixed_kept, mixed),
                (q_kept, q),
                (k_kept, k),
                (v_kept, v),
                (bias_kept, bias),
                (kept_kept, kept),
                (spread_kept, spread),
                (n1_kept, n1),
                (x_hbm, x_in),
            )
        ]
        blocks[1].sum_two_g()
        loads[0].wait()
        arrive([ng_send, out_send])

        def close(i, total):
            rows = pl.ds(pl.multiple_of(i * 128, 128), 128)
            base = resid[rows, :]
            n2[rows, :] = (base + out_acc[rows, :] + out_twin[rows, :]).astype(BF16)
            grad = ng_acc[rows, :] + ng_twin[rows, :]
            scale = lax.rsqrt(jnp.mean(base * base, axis=-1, keepdims=True) + EPSILON)
            unit = base * scale
            unit_grad = grad * gains[1:2, :]
            back = scale * (unit_grad - unit * jnp.mean(unit_grad * unit, axis=-1, keepdims=True))
            full = cot[rows, :].astype(F32) + back
            out_acc[rows, :] = full
            branch[rows, :] = full.astype(BF16)
            return total + jnp.sum((grad * unit).reshape(16, 8, 1024), axis=0)

        ended([n2_twin])
        gain_two[...] = lax.fori_loop(0, 2, close, jnp.zeros((8, 1024), F32))
        blocks[1].sum_two_u()
        blocks[0].sum_three_g()
        gain_two[...] += lax.fori_loop(2, 4, close, jnp.zeros((8, 1024), F32))
        results = [w.local(n2.at[0:512], outputs)]
        for copy in loads[1:3]:
            copy.wait()
        for i in range(2):
            rows = pl.ds(i * 256, 256)
            part = dot(branch[rows, :], po[...].reshape(1024, 1024), NT).astype(BF16)
            mg[rows, :] = part
            mg_t[:, rows] = part.T
            q_t[:, rows] = q[rows, :].T
        blocks[2].sum_two_g()
        proj.gathered()
        for side in range(2):
            part = dot(mixed[:, side * 512 : (side + 1) * 512], branch[...], TN)
            po[side] = part.astype(BF16).reshape(4, 2, 2, 32, 1024)
        proj.sum_zero()
        blocks[2].sum_two_u()
        for copy in loads[3:6]:
            copy.wait()
        ended([ng_send])
        heads = (q, q_t, k, v, mg, mg_t, bias, out_twin, ng_acc)
        head_grads(*heads, 0, 2)
        blocks[0].sum_three_u()
        proj.sum_one()
        head_grads(*heads, 2, 5)
        down_sum_two_a()
        head_grads(*heads, 5, 6)
        blocks[1].sum_three_g()
        down_sum_two_b()
        blocks[2].sum_three_u()
        head_grads(*heads, 6, 7)
        blocks[2].sum_three_g()
        head_grads(*heads, 7, 8)
        for copy in loads[6:]:
            copy.wait()
        results[0].wait()
        factor_grads(out_twin, ng_acc, kept, spread, n2, 512, 0, 1)
        proj.sum_two_a()
        proj.sum_two_b()
        blocks[1].sum_three_u()
        factor_grads(out_twin, ng_acc, kept, spread, n2, 512, 1, 4)
        down_sum_three()
        fg = n2.at[512:1024, 0:FACTOR_PAD]
        incoming = out_twin
        for i in range(2):
            rows = pl.ds(i * 256, 256)
            incoming[rows, :] = dot(fg[rows, :], pf[...].reshape(1024, FACTOR_PAD), NT)
        gain_tile = jnp.where(
            row_iota(128, 1024) == 33, jnp.sum(gain_two[...], axis=0, keepdims=True), 0.0
        ).T
        maps.gathered()
        for side in range(2):
            part = dot(n1[:, side * 512 : (side + 1) * 512], fg[...], TN)
            part = jnp.concatenate(
                [part[:, 0:768], part[:, 768:896] + gain_tile[side * 512 : (side + 1) * 512]], axis=1
            )
            pf[side] = part.astype(BF16).reshape(4, 2, 2, 32, FACTOR_PAD)
        maps.sum_zero()
        proj.sum_three()

        def first_norm(i, _):
            rows = pl.ds(pl.multiple_of(i * 128, 128), 128)
            vals = x_in[rows, :].astype(F32)
            scale = lax.rsqrt(jnp.mean(vals * vals, axis=-1, keepdims=True) + EPSILON)
            unit = vals * scale
            unit_grad = incoming[rows, :] * gains[0:1, :]
            back = scale * (unit_grad - unit * jnp.mean(unit_grad * unit, axis=-1, keepdims=True))
            out_acc[rows, :] += back
            return 0

        lax.fori_loop(0, 4, first_norm, 0)
        maps.sum_one()
        results.append(w.local(out_acc.at[0:512], input_grad))
        blocks[0].sum_end(gate_sum, up_sum)
        blocks[1].sum_end(gate_sum, up_sum)
        maps.sum_two_a()
        maps.sum_two_b()
        blocks[2].sum_end(gate_sum, up_sum)
        results += [w.local(up_sum, up_out), w.local(gate_sum, gate_out)]
        arrive(d_z_g)
        d_sum[...] = (
            d_buf[z, y, x].astype(F32)
            + d3[0].astype(F32)
            + d3[1].astype(F32)
            + d3[2].astype(F32)
        )
        either(d_stay, d_back, "start")
        maps.sum_three()
        shard = out_twin.at[0:32, :]
        proj.sum_end(shard)
        results.append(w.local(shard, out_shard))
        shard = out_twin.at[32:64, 0:FACTOR_PAD]
        maps.sum_end(shard)
        results.append(w.local(shard, fac_shard))
        either(d_stay, d_back, "wait")
        for copy in results[1:]:
            copy.wait()
        w.drain_shared()

    vmem = pltpu.VMEM
    row, turned = vmem((512, 1024), BF16), vmem((1024, 512), BF16)
    wide_row, bias_like = vmem((512, 1024), F32), vmem((512, 512), F32)
    kept_like, spread_like = vmem((512, KEPT), F32), vmem((8, 128, 1024), BF16)
    greet(x, z, y, c)
    pl.run_scoped(front, row, row, kept_like, row, row, row, row, wide_row, bias_like, spread_like)
    pl.run_scoped(
        feed_forward,
        vmem((1024, 1024), BF16), vmem((HALF, 1024), BF16), turned, turned, turned, vmem((HALF, 1024), F32),
    )
    pl.run_scoped(
        attention,
        wide_row, row, row, row, row, row, bias_like, kept_like, spread_like, row, turned, turned,
        vmem((8, 1024), F32), vmem((2, 32, HALF), F32), vmem((2, 32, HALF), F32), vmem((DOWN_ROWS, 512), F32),
    )


def whole_all(*args):
    anywhere, vmem = pl.BlockSpec(memory_space=pl.ANY), pl.BlockSpec(memory_space=pltpu.VMEM)
    big = lambda *shape: pltpu.VMEM(shape, BF16)
    wide = lambda *shape: pltpu.VMEM(shape, F32)
    down_b = DOWN_ROWS - DOWN_A
    early, late = BLOCKS[2][0], BLOCKS[2][1]

    def full_scratch(width):
        return [
            big(2, 4, 2, 2, 32, width), big(2, 4, 2, 32, width),
            big(2, 4, 16, width), big(4, 2, 16, width), big(4, 16, width), big(4, 16, width),
            big(3, 32, width),
        ]

    row = (512, 1024)
    outs = [
        (row, BF16),
        (row, F32),
        ((2, 32, HALF), F32),
        ((2, 32, HALF), F32),
        ((DOWN_ROWS, 512), F32),
        ((32, 1024), F32),
        ((32, FACTOR_PAD), F32),
        (row, BF16),
        ((512, KEPT), F32),
        (row, BF16),
        (row, BF16),
        (row, BF16),
        (row, BF16),
        (row, F32),
        ((512, 512), F32),
        ((8, 128, 1024), BF16),
    ]
    return pl.pallas_call(
        whole_kernel,
        out_shape=[jax.ShapeDtypeStruct(*o) for o in outs],
        in_specs=[anywhere, pl.BlockSpec(memory_space=pltpu.SMEM), anywhere, anywhere, vmem]
        + [anywhere] * 3,
        out_specs=[anywhere] * len(outs),
        scratch_shapes=[
            big(1024, 1024), big(1024, 1024),
            wide(1024, 1024), wide(1024, 1024), wide(512, 1024), wide(512, 1024),
            big(2, 4, 2, 2, 32, HALF), big(2, 4, 2, 2, 32, HALF), big(4, 2, 2, DOWN_ROWS, 512),
            big(2, 4, 2, 32, HALF), big(4, 2, 2, 32, HALF), big(4, 2, DOWN_A, 512), big(4, 2, down_b, 512),
            big(3, 2, 2, 32, early), big(3, 2, 2, 32, early), big(4, 2, 32, late), big(4, 2, 32, late),
            big(4, DOWN_A, 512), big(4, down_b, 512),
            big(3, 32, early), big(3, 32, early), big(2, 4, 32, late), big(2, 4, 32, late),
            big(3, DOWN_ROWS, 512),
            *full_scratch(1024),
            *full_scratch(FACTOR_PAD),
            wide(8, 1024), big(DOWN_ROWS, 512),
            pltpu.SemaphoreType.DMA((240,)),
            pltpu.SemaphoreType.DMA((240,)),
            pltpu.SemaphoreType.DMA((64,)),
        ],
        compiler_params=pltpu.CompilerParams(
            collective_id=0, has_side_effects=True, vmem_limit_bytes=62 * MIB
        ),
        name="whole_all",
    )(*args)[:7]


def cut_kernel(big_out, big_grad, fac_in, fac, out_in, gate, up, down, *refs):
    outs, (held_out, held_grad, sems) = refs[:-3], refs[-3:]
    loads, stores = [], []
    for part in range(4):
        rows = pl.ds(part * 128, 128)
        for src, held, dst in ((big_grad, held_grad, outs[1]), (big_out, held_out, outs[0])):
            at = len(loads)
            loads.append(pltpu.make_async_copy(src.at[rows], held.at[rows], sems.at[0, at]))
            stores.append(pltpu.make_async_copy(held.at[rows], dst.at[rows], sems.at[1, at]))
    for copy in loads:
        copy.start()
    pieces = (640, 96), (0, 384), (736, 32), (384, 128), (768, 32), (512, 128)
    for (start, size), ref in zip(pieces, outs[2:8], strict=True):
        ref[...] = fac[:, start : start + size]
    for load, store in zip(loads[:4], stores[:4], strict=True):
        load.wait()
        store.start()
    outs[8][...] = out_in[...]
    for src, ref in ((gate, outs[9]), (up, outs[10])):
        ref[:, 0:HALF] = src[0]
        ref[:, HALF:FF] = src[1]
    for load, store in zip(loads[4:], stores[4:], strict=True):
        load.wait()
        store.start()
    outs[11][:, 0:512] = down[0:OWN_UNITS, :]
    outs[11][:, 512:1024] = down[OWN_UNITS:DOWN_ROWS, :]
    maps = fac_in[...].astype(F32)
    lanes = lane_iota(32, FACTOR_PAD)
    total = jnp.sum(jnp.where(lanes < 800, maps * fac[...], 0.0), axis=-1, keepdims=True)
    gain = jnp.sum(jnp.where(lanes == 800, maps, 0.0), axis=-1, keepdims=True)
    tile = jnp.where(lane_iota(32) == 32, total / gain, fac[:, 768:896])
    tile = jnp.concatenate([tile, jnp.zeros((96, 128), F32)], axis=0).T
    outs[12][...] = tile[32:33, 0:32]
    outs[13][...] = tile[33:34, 0:32]
    for copy in stores:
        copy.wait()


def cut_all(*args):
    shapes = [(32, n) for n in (96, 384, 32, 128, 32, 128, 1024, FF, FF)] + [(OWN_UNITS, 1024), (1, 32), (1, 32)]
    anywhere, vmem = pl.BlockSpec(memory_space=pl.ANY), pl.BlockSpec(memory_space=pltpu.VMEM)
    return pl.pallas_call(
        cut_kernel,
        out_shape=[jax.ShapeDtypeStruct((512, 1024), BF16), jax.ShapeDtypeStruct((512, 1024), F32)]
        + [jax.ShapeDtypeStruct(s, F32) for s in shapes],
        in_specs=[anywhere] * 2 + [vmem] * 6,
        out_specs=[anywhere] * 2 + [vmem] * len(shapes),
        scratch_shapes=[
            pltpu.VMEM((512, 1024), BF16),
            pltpu.VMEM((512, 1024), F32),
            pltpu.SemaphoreType.DMA((2, 8)),
        ],
        compiler_params=pltpu.CompilerParams(vmem_limit_bytes=61 * MIB),
        name="cut_all",
    )(*args)


def local_paired(
    inputs, doc_lengths, w_aq, w_bq, w_ak, w_bk, w_av, w_bv,
    w_out, w_gate, w_up, w_down, gain_attn, gain_ffn, cotangent,
):
    spare = jnp.zeros((32, FACTOR_PAD - 802), BF16)
    fac = jnp.concatenate(
        [w_bq, w_bk, w_bv, w_aq, w_ak, w_av, gain_attn[:, None], gain_ffn[:, None], spare], axis=1
    )
    outputs, input_grad, gate_sum, up_sum, down_sum, out_sum, fac_sum = whole_all(
        inputs, doc_lengths, fac, w_out, w_down, w_gate, w_up, cotangent
    )
    *cut, gain_one, gain_two = cut_all(
        outputs, input_grad, fac, fac_sum, out_sum, gate_sum, up_sum, down_sum
    )
    return (*cut, gain_one[0], gain_two[0])


def solution(mesh):
    return jax.shard_map(
        local_paired if fits_pairs(mesh) else local,
        mesh=mesh,
        in_specs=(
            P(("dp", "fsdp"), None),
            P(("dp", "fsdp"), None),
            P(("dp", "fsdp"), None),
            P(("dp", "fsdp"), None),
            P(("dp", "fsdp"), None),
            P(("dp", "fsdp"), None),
            P(("dp", "fsdp"), None),
            P(("dp", "fsdp"), None),
            P(("dp", "fsdp"), None),
            P(("dp", "fsdp"), None),
            P(("dp", "fsdp"), None),
            P(("dp", "fsdp"), None),
            P(("dp", "fsdp")),
            P(("dp", "fsdp")),
            P(("dp", "fsdp"), None),
        ),
        out_specs=(
            P(("dp", "fsdp"), None),
            P(("dp", "fsdp"), None),
            P(("dp", "fsdp"), None),
            P(("dp", "fsdp"), None),
            P(("dp", "fsdp"), None),
            P(("dp", "fsdp"), None),
            P(("dp", "fsdp"), None),
            P(("dp", "fsdp"), None),
            P(("dp", "fsdp"), None),
            P(("dp", "fsdp"), None),
            P(("dp", "fsdp"), None),
            P(("dp", "fsdp"), None),
            P(("dp", "fsdp")),
            P(("dp", "fsdp")),
        ),
        check_vma=False,
    )
```

```python
import math

import jax
import jax.numpy as jnp
from jax import lax
from jax.experimental import pallas as pl
from jax.experimental.pallas import tpu as pltpu
from jax.sharding import PartitionSpec as P

HEADS = 16
HEAD_DIM = 64
RANK_Q = 6
RANK_KV = 2
FF = 2816


EPSILON = 1e-06
PRECISE = lax.Precision.HIGHEST


def factor_columns():
    return [
        RANK_Q * HEADS,
        RANK_Q * HEAD_DIM,
        RANK_KV * HEADS,
        RANK_KV * HEAD_DIM,
        RANK_KV * HEADS,
        RANK_KV * HEAD_DIM,
    ]


def split_columns(matrix):
    pieces = []
    offset = 0
    for columns in factor_columns():
        pieces.append(matrix[:, offset : offset + columns])
        offset += columns
    return pieces


def doc_layout(lengths, length):
    order = jnp.arange(lengths.shape[0], dtype=jnp.int32)
    doc_ends = jnp.sum(jnp.where(order[:, None] >= order[None, :], lengths[None, :], 0), axis=1)
    doc_starts = doc_ends - lengths
    places = jnp.arange(length, dtype=jnp.int32)
    segment = jnp.sum((places[:, None] >= doc_ends[None, :]).astype(jnp.int32), axis=1)
    owner = segment[:, None] == jnp.arange(lengths.shape[0], dtype=jnp.int32)[None, :]
    doc_first = jnp.sum(jnp.where(owner, doc_starts[None, :], 0), axis=1)
    return (segment, (places - doc_first).astype(jnp.float32))


def rotation(places):
    halfway = HEAD_DIM // 2
    freqs = jnp.exp(-math.log(10000.0) * jnp.arange(halfway, dtype=jnp.float32) / halfway)
    angles = places[..., None] * freqs
    return (jnp.cos(angles), jnp.sin(angles))


def rotate(factor, cos_table, sin_table):
    halfway = factor.shape[-1] // 2
    front_part = factor[..., :halfway]
    back_part = factor[..., halfway:]
    cos_part = cos_table[..., None, :]
    sin_part = sin_table[..., None, :]
    return jnp.concatenate(
        [
            front_part * cos_part - back_part * sin_part,
            front_part * sin_part + back_part * cos_part,
        ],
        axis=-1,
    )


def normalize(values, gain):
    scaling = lax.rsqrt(jnp.mean(values * values, axis=-1, keepdims=True) + EPSILON)
    unit_vals = values * scaling
    return (unit_vals * gain, unit_vals, scaling)


def norm_back(incoming, unit_vals, scaling, gain):
    unit_grad = incoming * gain
    grad_in = scaling * (
        unit_grad - unit_vals * jnp.mean(unit_grad * unit_vals, axis=-1, keepdims=True)
    )
    return (grad_in, jnp.sum(incoming * unit_vals, axis=0))


def block_scores(query_part, keys_low, seg_part, segment, place_part, places):
    scaling = HEAD_DIM ** (-0.5)
    scores = (
        jnp.einsum("thd,shd->hts", query_part, keys_low, preferred_element_type=jnp.float32)
        * scaling
    )
    allowed = (seg_part[:, None] == segment[None, :]) & (places[None, :] <= place_part[:, None])
    return jnp.where(allowed[None], scores, -1e30)


def attend_forward(queries, keys_low, values, segment):
    length = queries.shape[0]
    block_rows = min(512, length)
    places = jnp.arange(length, dtype=jnp.int32)

    def one_block(block_index):
        masked = block_scores(queries, keys_low, segment, segment, places, places)
        row_peak = jnp.max(masked, axis=-1, keepdims=True)
        exp_terms = jnp.exp(masked - row_peak)
        row_total = jnp.sum(exp_terms, axis=-1, keepdims=True)
        attn_probs = (exp_terms / row_total).astype(jnp.bfloat16)
        attended = jnp.einsum(
            "hts,shd->thd", attn_probs, values, preferred_element_type=jnp.float32
        )
        return (attended, (row_peak + jnp.log(row_total))[..., 0])

    attended, log_totals = lax.map(one_block, jnp.arange(length // block_rows, dtype=jnp.int32))
    return (attended.reshape(length, HEADS, HEAD_DIM), log_totals)


def attend_backward(queries, keys_low, values, segment, log_totals, mixed_grad):
    length = queries.shape[0]
    block_rows = min(512, length)
    places = jnp.arange(length, dtype=jnp.int32)
    scaling = HEAD_DIM ** (-0.5)

    def one_block(running, block_index):
        key_grad, value_grad = running
        masked = block_scores(queries, keys_low, segment, segment, places, places)
        attn_probs = jnp.exp(masked - log_totals[block_index][..., None])
        probs_low = attn_probs.astype(jnp.bfloat16)
        value_grad = value_grad + jnp.einsum(
            "hts,thd->shd", probs_low, mixed_grad, preferred_element_type=jnp.float32
        )
        probs_grad = jnp.einsum(
            "thd,shd->hts", mixed_grad, values, preferred_element_type=jnp.float32
        )
        inner_sum = jnp.sum(attn_probs * probs_grad, axis=-1, keepdims=True)
        score_grad = (attn_probs * (probs_grad - inner_sum)).astype(jnp.bfloat16)
        query_grad = (
            jnp.einsum("hts,shd->thd", score_grad, keys_low, preferred_element_type=jnp.float32)
            * scaling
        )
        key_grad = (
            key_grad
            + jnp.einsum("hts,thd->shd", score_grad, queries, preferred_element_type=jnp.float32)
            * scaling
        )
        return ((key_grad, value_grad), query_grad)

    empty = jnp.zeros((length, HEADS, HEAD_DIM), jnp.float32)
    (key_grad, value_grad), query_grad = lax.scan(
        one_block, (empty, empty), jnp.arange(length // block_rows, dtype=jnp.int32)
    )
    return (query_grad.reshape(length, HEADS, HEAD_DIM), key_grad, value_grad)


def factor_back(full_grad, a_part, b_part, rank_count):
    a_grad = jnp.einsum("thd,trd->trh", full_grad, b_part, precision=PRECISE) / rank_count
    b_grad = jnp.einsum("thd,trh->trd", full_grad, a_part, precision=PRECISE) / rank_count
    return (a_grad, b_grad)


def local(
    inputs,
    doc_lengths,
    w_aq,
    w_bq,
    w_ak,
    w_bk,
    w_av,
    w_bv,
    w_out,
    w_gate,
    w_up,
    w_down,
    gain_attn,
    gain_ffn,
    cotangent,
):
    length = inputs.shape[0]
    joined_local = jnp.concatenate([w_aq, w_bq, w_ak, w_bk, w_av, w_bv], axis=1)
    factor_w, out_w, gain_one = (
        lax.all_gather(joined_local, ("dp", "fsdp"), axis=0, tiled=True),
        lax.all_gather(w_out, ("dp", "fsdp"), axis=0, tiled=True),
        lax.all_gather(gain_attn, ("dp", "fsdp"), axis=0, tiled=True),
    )
    segment, places = doc_layout(doc_lengths[0], length)
    cos_table, sin_table = rotation(places)
    start_vals = inputs.astype(jnp.float32)
    normed_one, unit_one, scale_one = normalize(start_vals, gain_one.astype(jnp.float32))
    normed_low = normed_one.astype(jnp.bfloat16)
    factors = jnp.dot(normed_low, factor_w, preferred_element_type=jnp.float32)
    pieces = split_columns(factors)
    a_q = pieces[0].reshape(length, RANK_Q, HEADS)
    b_q = pieces[1].reshape(length, RANK_Q, HEAD_DIM)
    a_k = pieces[2].reshape(length, RANK_KV, HEADS)
    b_k = pieces[3].reshape(length, RANK_KV, HEAD_DIM)
    a_v = pieces[4].reshape(length, RANK_KV, HEADS)
    b_v = pieces[5].reshape(length, RANK_KV, HEAD_DIM)
    bq_rot = rotate(b_q, cos_table, sin_table)
    bk_rot = rotate(b_k, cos_table, sin_table)
    queries = (jnp.einsum("trh,trd->thd", a_q, bq_rot, precision=PRECISE) / RANK_Q).astype(
        jnp.bfloat16
    )
    keys_low = (jnp.einsum("trh,trd->thd", a_k, bk_rot, precision=PRECISE) / RANK_KV).astype(
        jnp.bfloat16
    )
    values = (jnp.einsum("trh,trd->thd", a_v, b_v, precision=PRECISE) / RANK_KV).astype(
        jnp.bfloat16
    )
    attended, log_totals = attend_forward(queries, keys_low, values, segment)
    mixed = attended.astype(jnp.bfloat16).reshape(length, HEADS * HEAD_DIM)
    resid = start_vals + jnp.dot(mixed, out_w, preferred_element_type=jnp.float32)
    gate_w, up_w, down_w, gain_two = (
        lax.all_gather(w_gate, ("dp", "fsdp"), axis=0, tiled=True),
        lax.all_gather(w_up, ("dp", "fsdp"), axis=0, tiled=True),
        lax.all_gather(w_down, ("dp", "fsdp"), axis=0, tiled=True),
        lax.all_gather(gain_ffn, ("dp", "fsdp"), axis=0, tiled=True),
    )
    normed_two, unit_two, scale_two = normalize(resid, gain_two.astype(jnp.float32))
    normed_two_low = normed_two.astype(jnp.bfloat16)
    gate_act = jnp.dot(normed_two_low, gate_w, preferred_element_type=jnp.float32)
    up_act = jnp.dot(normed_two_low, up_w, preferred_element_type=jnp.float32)
    hidden = (jax.nn.silu(gate_act) * up_act).astype(jnp.bfloat16)
    result = resid + jnp.dot(hidden, down_w, preferred_element_type=jnp.float32)
    outputs = result.astype(jnp.bfloat16)
    gate_w, up_w, down_w, gain_two = (
        lax.all_gather(w_gate, ("dp", "fsdp"), axis=0, tiled=True),
        lax.all_gather(w_up, ("dp", "fsdp"), axis=0, tiled=True),
        lax.all_gather(w_down, ("dp", "fsdp"), axis=0, tiled=True),
        lax.all_gather(gain_ffn, ("dp", "fsdp"), axis=0, tiled=True),
    )
    hidden_grad = jnp.einsum("tc,fc->tf", cotangent, down_w, preferred_element_type=jnp.float32)
    down_wgrad = jnp.einsum("tf,tc->fc", hidden, cotangent, preferred_element_type=jnp.float32)
    sig_vals = jax.nn.sigmoid(gate_act)
    gate_grad = (hidden_grad * up_act * sig_vals * (1.0 + gate_act * (1.0 - sig_vals))).astype(
        jnp.bfloat16
    )
    up_grad = (hidden_grad * jax.nn.silu(gate_act)).astype(jnp.bfloat16)
    normed_two_grad = jnp.einsum("tf,cf->tc", gate_grad, gate_w, preferred_element_type=jnp.float32)
    normed_two_grad = normed_two_grad + jnp.einsum(
        "tf,cf->tc", up_grad, up_w, preferred_element_type=jnp.float32
    )
    resid_norm_grad, gain_two_grad = norm_back(
        normed_two_grad, unit_two, scale_two, gain_two.astype(jnp.float32)
    )
    resid_grad = cotangent.astype(jnp.float32) + resid_norm_grad
    gate_rows = jnp.einsum(
        "tc,tf->cf", normed_two_low, gate_grad, preferred_element_type=jnp.float32
    )
    up_rows = jnp.einsum("tc,tf->cf", normed_two_low, up_grad, preferred_element_type=jnp.float32)
    gate_up_shard = lax.psum_scatter(
        jnp.concatenate([gate_rows, up_rows], axis=1),
        ("dp", "fsdp"),
        scatter_dimension=0,
        tiled=True,
    )
    gate_shard = gate_up_shard[:, :FF]
    up_shard = gate_up_shard[:, FF:]
    down_shard, gain_two_shard = (
        lax.psum_scatter(down_wgrad, ("dp", "fsdp"), scatter_dimension=0, tiled=True),
        lax.psum_scatter(gain_two_grad, ("dp", "fsdp"), scatter_dimension=0, tiled=True),
    )
    factor_w, out_w, gain_one = (
        lax.all_gather(joined_local, ("dp", "fsdp"), axis=0, tiled=True),
        lax.all_gather(w_out, ("dp", "fsdp"), axis=0, tiled=True),
        lax.all_gather(gain_attn, ("dp", "fsdp"), axis=0, tiled=True),
    )
    branch_grad = resid_grad.astype(jnp.bfloat16)
    out_wgrad = jnp.einsum("tc,td->cd", mixed, branch_grad, preferred_element_type=jnp.float32)
    mixed_grad = jnp.einsum("td,cd->tc", branch_grad, out_w, preferred_element_type=jnp.float32)
    mixed_grad = mixed_grad.astype(jnp.bfloat16).reshape(length, HEADS, HEAD_DIM)
    query_grad, key_grad, value_grad = attend_backward(
        queries, keys_low, values, segment, log_totals, mixed_grad
    )
    a_q_grad, bq_rot_grad = factor_back(query_grad, a_q, bq_rot, RANK_Q)
    a_k_grad, bk_rot_grad = factor_back(key_grad, a_k, bk_rot, RANK_KV)
    a_v_grad, b_v_grad = factor_back(value_grad, a_v, b_v, RANK_KV)
    neg_sin = -sin_table
    b_q_grad = rotate(bq_rot_grad, cos_table, neg_sin)
    b_k_grad = rotate(bk_rot_grad, cos_table, neg_sin)
    factor_grad = jnp.concatenate(
        [
            part.reshape(length, -1)
            for part in (a_q_grad, b_q_grad, a_k_grad, b_k_grad, a_v_grad, b_v_grad)
        ],
        axis=1,
    ).astype(jnp.bfloat16)
    factor_wgrad = jnp.einsum(
        "td,tc->dc", normed_low, factor_grad, preferred_element_type=jnp.float32
    )
    normed_one_grad = jnp.einsum(
        "tc,dc->td", factor_grad, factor_w, preferred_element_type=jnp.float32
    )
    input_norm_grad, gain_one_grad = norm_back(
        normed_one_grad, unit_one, scale_one, gain_one.astype(jnp.float32)
    )
    input_grad = resid_grad + input_norm_grad
    factor_shard, out_shard, gain_one_shard = (
        lax.psum_scatter(factor_wgrad, ("dp", "fsdp"), scatter_dimension=0, tiled=True),
        lax.psum_scatter(out_wgrad, ("dp", "fsdp"), scatter_dimension=0, tiled=True),
        lax.psum_scatter(gain_one_grad, ("dp", "fsdp"), scatter_dimension=0, tiled=True),
    )
    shard_pieces = split_columns(factor_shard)
    return (
        outputs,
        input_grad,
        shard_pieces[0],
        shard_pieces[1],
        shard_pieces[2],
        shard_pieces[3],
        shard_pieces[4],
        shard_pieces[5],
        out_shard,
        gate_shard,
        up_shard,
        down_shard,
        gain_one_shard,
        gain_two_shard,
    )


MESH_IDS = pl.DeviceIdType.MESH
HALF = FF // 2
OWN_UNITS = 88
DOWN_ROWS = 2 * OWN_UNITS
DOWN_A = 96
FACTOR_PAD = 896
MIB = 2**20


def fits_pairs(mesh):
    return dict(mesh.shape) == {"dp": 2, "fsdp": 16}


def place():
    x = lax.axis_index("dp")
    f = lax.axis_index("fsdp")
    return x, lax.div(f, 4), lax.rem(lax.div(f, 2), 2), lax.rem(f, 2)


def device(x, z, y, c):
    return (x, z * 4 + y * 2 + c)


def greet(x, z, y, c):
    partners = [
        device(x, z, y, 1 - c),
        device(1 - x, z, y, c),
        device(x, z, 1 - y, c),
        device(1 - x, z, y, 1 - c),
        device(x, z, 1 - y, 1 - c),
    ]
    for step in (1, 2, 3):
        other = lax.rem(z + step, 4)
        partners += [device(x, other, y, c), device(x, other, y, 1 - c)]
    barrier = pltpu.get_barrier_semaphore()
    for partner in partners:
        pl.semaphore_signal(barrier, inc=1, device_id=partner, device_id_type=MESH_IDS)
    return len(partners)


class Wires:
    def __init__(self, send_sems, recv_sems, local_sems):
        self.send_sems, self.recv_sems, self.local_sems = send_sems, recv_sems, local_sems
        self.sent, self.held = 0, 0
        self.open, self.shared = [], []

    def make(self, src, dst, to):
        at = self.sent
        self.sent += 1
        return pltpu.make_async_remote_copy(
            src_ref=src,
            dst_ref=dst,
            send_sem=self.send_sems.at[at],
            recv_sem=self.recv_sems.at[at],
            device_id=to,
            device_id_type=MESH_IDS,
        )

    def go(self, copy):
        copy.start()
        self.shared.append(copy)
        return copy

    def send(self, src, dst, to):
        copy = self.make(src, dst, to)
        copy.start()
        self.open.append(copy)
        return copy

    def local(self, src, dst):
        copy = pltpu.make_async_copy(src, dst, self.local_sems.at[self.held])
        self.held += 1
        copy.start()
        return copy

    def drain(self):
        for copy in self.open:
            copy.wait_send()
        self.open = []

    def drain_shared(self):
        for copy in self.shared:
            copy.wait_send()
        self.shared = []


def arrive(copies):
    for copy in copies:
        copy.wait_recv()


BLOCKS = ((0, 256), (256, 512), (768, 384), (1152, 256))
TILE = 256
NT = (((1,), (1,)), ((), ()))
TN = (((0,), (0,)), ((), ()))
F32, BF16 = jnp.float32, jnp.bfloat16


def dot(a, b, dims=None):
    if dims is None:
        return jnp.dot(a, b, preferred_element_type=F32)
    return lax.dot_general(a, b, dims, preferred_element_type=F32)


def add_low(dst, src):
    dst[...] = (dst[...].astype(F32) + src[...].astype(F32)).astype(BF16)


KEPT = 1152
COS_LANES = pl.ds(896, 128)
SIN_LANES = pl.ds(1024, 128)
A_LANES = pl.ds(640, 128)
V_LANES = pl.ds(768, 128)


def lane_iota(rows, lanes=128):
    return lax.broadcasted_iota(jnp.int32, (rows, lanes), 1)


def row_iota(rows, lanes=128):
    return lax.broadcasted_iota(jnp.int32, (rows, lanes), 0)


def doc_ends_of(lengths):
    one = lengths[0, 0]
    two = one + lengths[0, 1]
    return one, two, two + lengths[0, 2]


def make_tables(lengths, cos_ref, sin_ref):
    ends = doc_ends_of(lengths)

    def tile(i, _):
        rows = pl.ds(pl.multiple_of(i * 128, 128), 128)
        places = row_iota(128) + i * 128
        first = jnp.zeros((128, 128), jnp.int32)
        for end in ends:
            first = jnp.where(places >= end, end, first)
        lane = lane_iota(128)
        turn = lax.rem(lane, 32).astype(F32)
        freqs = jnp.exp(-math.log(10000.0) * turn / 32)
        angles = (places - first).astype(F32) * freqs
        cos_ref[rows, :] = jnp.cos(angles)
        sin_vals = jnp.sin(angles)
        sin_ref[rows, :] = jnp.where(lax.rem(lane, 64) < 32, -sin_vals, sin_vals)
        return 0

    lax.fori_loop(0, 4, tile, 0)


def make_bias(lengths, bias):
    ends = doc_ends_of(lengths)

    def tile(i, _):
        rows = pl.ds(pl.multiple_of(i * 128, 128), 128)
        t = row_iota(128, 512) + i * 128
        s = lane_iota(128, 512)
        own, key = jnp.zeros((128, 512), jnp.int32), jnp.zeros((128, 512), jnp.int32)
        for end in ends:
            own += (t >= end).astype(jnp.int32)
            key += (s >= end).astype(jnp.int32)
        bias[rows, :] = jnp.where((own == key) & (s <= t), 0.0, -1e30)
        return 0

    lax.fori_loop(0, 4, tile, 0)


def make_spread(spread):
    def rank(r, _):
        head = lax.div(lane_iota(128, 1024), HEAD_DIM) + r * HEADS
        spread[r] = jnp.where(row_iota(128, 1024) == head, 1.0, 0.0).astype(BF16)
        return 0

    lax.fori_loop(0, 8, rank, 0)


def swapped(tile):
    front = lax.rem(lane_iota(tile.shape[0]), 64) < 32
    return jnp.where(front, pltpu.roll(tile, 96, 1), pltpu.roll(tile, 32, 1))


def both_halves(tile, half):
    low = lane_iota(tile.shape[0]) < 64
    other = pltpu.roll(tile, 64, 1)
    return jnp.where(low, tile, other) if half == 0 else jnp.where(low, other, tile)


def two_terms(a):
    high = a.astype(BF16)
    return high, (a - high.astype(F32)).astype(BF16)


def expand(terms, spread_r):
    return dot(terms[0], spread_r) + dot(terms[1], spread_r)


def eight(tile):
    return jnp.concatenate([tile] * 8, axis=1)


def gain_rows(fac_all, gains):
    tile = fac_all[:, :, :, :, :, V_LANES].reshape(1024, 128).astype(F32)
    gains[...] = tile.T[32:40, :]


def make_factors(x_in, gains, fac_all, n1, kept, first, last):
    def tile(i, _):
        rows = pl.ds(pl.multiple_of(i * 256, 256), 256)
        vals = x_in[rows, :].astype(F32)
        scale = lax.rsqrt(jnp.mean(vals * vals, axis=-1, keepdims=True) + EPSILON)
        low = (vals * scale * gains[0:1, :]).astype(BF16)
        n1[rows, :] = low
        kept[rows, 0:FACTOR_PAD] = dot(low, fac_all[...].reshape(1024, FACTOR_PAD))
        return 0

    lax.fori_loop(first, last, tile, 0)


def make_heads(kept, cos_ref, sin_ref, spread, q, k, v, first, last):
    def tile(i, _):
        rows = pl.ds(pl.multiple_of(i * 128, 128), 128)
        turned = []
        for j in range(4):
            lanes = pl.ds(j * 128, 128)
            part = kept[rows, lanes]
            part = part * cos_ref[rows, :] + swapped(part) * sin_ref[rows, :]
            kept[rows, lanes] = part
            turned.append(part)
        terms = two_terms(kept[rows, A_LANES])
        total = jnp.zeros((128, 1024), F32)
        for r in range(RANK_Q):
            total += expand(terms, spread[r]) * eight(both_halves(turned[r // 2], r % 2))
        q[rows, :] = (total * (1.0 / RANK_Q)).astype(BF16) * BF16(HEAD_DIM**-0.5)
        total = jnp.zeros((128, 1024), F32)
        for r in range(RANK_KV):
            total += expand(terms, spread[RANK_Q + r]) * eight(both_halves(turned[3], r))
        k[rows, :] = (total * (1.0 / RANK_KV)).astype(BF16)
        terms = two_terms(kept[rows, V_LANES])
        plain = kept[rows, pl.ds(512, 128)]
        total = jnp.zeros((128, 1024), F32)
        for r in range(RANK_KV):
            total += expand(terms, spread[r]) * eight(both_halves(plain, r))
        v[rows, :] = (total * (1.0 / RANK_KV)).astype(BF16)
        return 0

    lax.fori_loop(first, last, tile, 0)


def only(tile, half):
    low = lane_iota(tile.shape[0]) < 64
    keep = low if half == 0 else jnp.logical_not(low)
    return jnp.where(keep, tile, jnp.zeros_like(tile))


def soft(q_rows, k_cols, bias_block):
    scores = dot(q_rows, k_cols, NT) + bias_block
    terms = jnp.exp(scores - jnp.max(scores, axis=-1, keepdims=True))
    return terms * (1.0 / jnp.sum(terms, axis=-1, keepdims=True))


def attend_pairs(q, k, v, bias, mixed, first, last):
    def pair(p, _):
        lanes = pl.ds(pl.multiple_of(p * 128, 128), 128)
        for start, extent in ((0, 256), (256, 512)):
            rows, cols = pl.ds(start, 256), pl.ds(0, extent)
            q_rows, k_cols, v_cols = q[rows, lanes], k[cols, lanes], v[cols, lanes]
            halves = []
            for half in (0, 1):
                probs = soft(only(q_rows, half), k_cols, bias[rows, cols]).astype(BF16)
                halves.append(dot(probs, v_cols))
            low = lane_iota(256) < 64
            mixed[rows, lanes] = jnp.where(low, halves[0], halves[1]).astype(BF16)
        return 0

    lax.fori_loop(first, last, pair, 0)


def make_resid(x_in, mixed, out_all, gains, resid, n2, first, last):
    def tile(i, _):
        rows = pl.ds(pl.multiple_of(i * 256, 256), 256)
        base = x_in[rows, :].astype(F32) + dot(mixed[rows, :], out_all[...].reshape(1024, 1024))
        resid[rows, :] = base
        scale = lax.rsqrt(jnp.mean(base * base, axis=-1, keepdims=True) + EPSILON)
        n2[rows, :] = (base * scale * gains[1:2, :]).astype(BF16)
        return 0

    lax.fori_loop(first, last, tile, 0)


def head_grads(q, q_t, k, v, mg, mg_t, bias, dq, dkv_t, first, last):
    def pair(p, _):
        at = pl.multiple_of(p * 128, 128)
        lanes = pl.ds(at, 128)
        for start, extent in ((256, 512), (0, 256)):
            rows, cols = pl.ds(start, 256), pl.ds(0, extent)
            q_rows, mg_rows = q[rows, lanes], mg[rows, lanes]
            k_cols, v_cols = k[cols, lanes], v[cols, lanes]
            halves = []
            for half in (0, 1):
                own = pl.ds(pl.multiple_of(at + half * 64, 64), 64)
                probs = soft(only(q_rows, half), k_cols, bias[rows, cols])
                probs_grad = dot(only(mg_rows, half), v_cols, NT)
                inner = jnp.sum(probs * probs_grad, axis=-1, keepdims=True)
                score_grad = (probs * (probs_grad - inner)).astype(BF16)
                dv = dot(mg_t[own, rows], probs.astype(BF16))
                dk = dot(q_t[own, rows], score_grad)
                if start:
                    dkv_t[own, 0:512] = dk
                    dkv_t[own, 512:1024] = dv
                else:
                    dkv_t[own, 0:256] += dk
                    dkv_t[own, 512:768] += dv
                halves.append(dot(score_grad, k_cols))
            low = lane_iota(256) < 64
            dq[rows, lanes] = jnp.where(low, halves[0], halves[1]) * HEAD_DIM**-0.5
        return 0

    lax.fori_loop(first, last, pair, 0)


def fold(product):
    total = product[:, 0:128]
    for j in range(1, 8):
        total += product[:, j * 128 : (j + 1) * 128]
    return total + pltpu.roll(total, 64, 1)


def rank_grads(full, terms, ranks, duplicates, spread):
    a_grad, b_grads = jnp.zeros((full.shape[0], 128), F32), []
    for r, twice in zip(ranks, duplicates, strict=True):
        spread_r = spread[r]
        a_grad += dot((full * eight(twice)).astype(BF16), spread_r, NT)
        b_grads.append(fold(full * expand(terms, spread_r)))
    return a_grad, b_grads


def pick(low_half, high_half):
    return jnp.where(lane_iota(low_half.shape[0]) < 64, low_half, high_half)


def factor_grads(dq, dkv_t, kept, spread, fg, fg_at, first, last):
    def tile(i, _):
        at = pl.multiple_of(i * 128, 128)
        rows = pl.ds(at, 128)
        out = pl.ds(pl.multiple_of(fg_at + i * 128, 128), 128)
        cos_rows, sin_rows = kept[rows, COS_LANES], kept[rows, SIN_LANES]

        def turn_back(part):
            return part * cos_rows - swapped(part) * sin_rows

        tiles = [kept[rows, pl.ds(j * 128, 128)] for j in range(5)]
        terms = two_terms(kept[rows, A_LANES])
        a_q, b_q = rank_grads(
            dq[rows, :],
            terms,
            range(RANK_Q),
            [both_halves(tiles[r // 2], r % 2) for r in range(RANK_Q)],
            spread,
        )
        for j in range(RANK_Q // 2):
            part = pick(b_q[2 * j], b_q[2 * j + 1]) * (1.0 / RANK_Q)
            fg[out, pl.ds(j * 128, 128)] = turn_back(part).astype(BF16)
        a_k, b_k = rank_grads(
            dkv_t[:, rows].T,
            terms,
            range(RANK_Q, RANK_Q + RANK_KV),
            [both_halves(tiles[3], r) for r in range(RANK_KV)],
            spread,
        )
        part = pick(b_k[0], b_k[1]) * (1.0 / RANK_KV)
        fg[out, pl.ds(384, 128)] = turn_back(part).astype(BF16)
        fg[out, A_LANES] = (a_q * (1.0 / RANK_Q) + a_k * (1.0 / RANK_KV)).astype(BF16)
        a_v, b_v = rank_grads(
            dkv_t[:, pl.ds(pl.multiple_of(512 + i * 128, 128), 128)].T,
            two_terms(kept[rows, V_LANES]),
            range(RANK_KV),
            [both_halves(tiles[4], r) for r in range(RANK_KV)],
            spread,
        )
        fg[out, pl.ds(512, 128)] = (pick(b_v[0], b_v[1]) * (1.0 / RANK_KV)).astype(BF16)
        fg[out, V_LANES] = (a_v * (1.0 / RANK_KV)).astype(BF16)
        return 0

    lax.fori_loop(first, last, tile, 0)


def whole_kernel(
    x_hbm, lengths, w_bq, w_bk, w_bv, w_aq, w_ak, w_av, gains_in, wo_in, wd_in, wg_in, wu_in, cot_in,
    outputs, input_grad, gate_out, up_out, down_out, out_shard, fac_shard,
    n1_kept, kept_kept, q_kept, k_kept, v_kept, mixed_kept, resid_kept, bias_kept, spread_kept,
    n2, cot, out_acc, ng_acc, out_twin, ng_twin,
    g_buf, u_buf, d_buf, g1, u1, da1, db1, g2, u2, da2, db2, g3, u3, d3,
    po, po_twin, po_1a, po_1b, po_2a, po_2b, po_3,
    pf, pf_twin, pf_1a, pf_1b, pf_2a, pf_2b, pf_3,
    gains, wd_own, fac_own,
    ss, rs, ls,
):
    x, z, y, c = place()
    x_peer, y_peer, twin = device(1 - x, z, y, c), device(x, z, 1 - y, c), device(x, z, y, 1 - c)
    z_peers = [3 - z, lax.rem(z + 2, 4), z + 1 - 2 * lax.rem(z, 2)]
    w = Wires(ss, rs, ls)
    a_rows, b_rows = pl.ds(0, 16), pl.ds(16, 16)
    a_down, b_down = pl.ds(0, DOWN_A), pl.ds(DOWN_A, DOWN_ROWS - DOWN_A)

    def same(view, to):
        return w.make(view, view, to)

    def own_copy(src, dst):
        w.held += 1
        return pltpu.make_async_copy(src, dst, ls.at[w.held - 1])

    def go(*copies):
        for copy in copies:
            w.go(copy)

    def ended(copies):
        for copy in copies:
            copy.wait_send()
        w.shared = [copy for copy in w.shared if all(copy is not other for other in copies)]

    class Whole:
        def __init__(self, src, ref, from_twin, one_a, one_b, two_a, two_b, three):
            self.ref, self.from_twin, self.one, self.two, self.three = (
                ref, from_twin, (one_a, one_b), (two_a, two_b), three,
            )
            slot = ref.at[x, z, y, c]
            self.own = own_copy(src, slot)
            self.z = [w.make(src, slot, device(x, zz, y, c)) for zz in z_peers]
            self.two_a = same(ref.at[x, :, y, c, a_rows], x_peer)
            self.two_b = same(ref.at[x, :, y, c, b_rows], y_peer)
            self.three_a = same(ref.at[:, :, y, c, a_rows], y_peer)
            self.three_b = same(ref.at[x, :, :, c, b_rows], x_peer)
            self.passed = [
                same(ref.at[x, :, y, c], twin),
                same(ref.at[1 - x, :, y, c, a_rows], twin),
                same(ref.at[x, :, 1 - y, c, b_rows], twin),
                same(ref.at[:, :, 1 - y, c, a_rows], twin),
                same(ref.at[1 - x, :, :, c, b_rows], twin),
            ]
            self.g_twin = w.make(ref.at[:, :, :, 1 - c], from_twin, twin)
            self.g_one_a = w.make(ref.at[:, :, 1 - y, c, a_rows], one_a, y_peer)
            self.g_one_b = w.make(ref.at[1 - x, :, :, c, b_rows], one_b, x_peer)
            self.g_two_a = w.make(ref.at[1 - x, :, y, c, a_rows], two_a, x_peer)
            self.g_two_b = w.make(ref.at[x, :, 1 - y, c, b_rows], two_b, y_peer)
            self.g_z = [
                w.make(ref.at[x, zz, y, c], three.at[step], device(x, zz, y, c))
                for step, zz in enumerate(z_peers)
            ]

        def start(self):
            self.own.start()
            go(*self.z)

        def step_two(self):
            self.own.wait()
            arrive(self.z)
            go(self.two_a, self.two_b, self.passed[0])

        def step_three_a(self):
            self.two_a.wait_recv()
            go(self.three_a, self.passed[1])

        def step_three_b(self):
            self.two_b.wait_recv()
            go(self.three_b, self.passed[2])

        def pass_a(self):
            self.three_a.wait_recv()
            go(self.passed[3])

        def pass_b(self):
            self.three_b.wait_recv()
            go(self.passed[4])

        def here(self):
            arrive(self.passed)

        def gathered(self):
            ended([*self.z, self.two_a, self.two_b, self.three_a, self.three_b, *self.passed])

        def sum_zero(self):
            go(self.g_twin)

        def sum_one(self):
            self.g_twin.wait_recv()

            def add(i, _):
                xx, zz, yy = lax.div(i, 8), lax.rem(lax.div(i, 2), 4), lax.rem(i, 2)
                add_low(self.ref.at[xx, zz, yy, c], self.from_twin.at[xx, zz, yy])
                return 0

            lax.fori_loop(0, 16, add, 0)
            go(self.g_one_a, self.g_one_b)

        def sum_two_a(self):
            self.g_one_a.wait_recv()

            def add(i, _):
                s, zz = lax.div(i, 4), lax.rem(i, 4)
                add_low(self.ref.at[s, zz, y, c, a_rows], self.one[0].at[s, zz])
                return 0

            lax.fori_loop(0, 8, add, 0)
            go(self.g_two_a)

        def sum_two_b(self):
            self.g_one_b.wait_recv()

            def add(i, _):
                zz, s = lax.div(i, 2), lax.rem(i, 2)
                add_low(self.ref.at[x, zz, s, c, b_rows], self.one[1].at[zz, s])
                return 0

            lax.fori_loop(0, 8, add, 0)
            go(self.g_two_b)

        def sum_three(self):
            arrive([self.g_two_a, self.g_two_b])

            def add(i, _):
                add_low(self.ref.at[x, i, y, c, a_rows], self.two[0].at[i])
                add_low(self.ref.at[x, i, y, c, b_rows], self.two[1].at[i])
                return 0

            lax.fori_loop(0, 4, add, 0)
            go(*self.g_z)

        def sum_end(self, out):
            arrive(self.g_z)
            out[...] = (
                self.ref[x, z, y, c].astype(F32)
                + self.three[0].astype(F32)
                + self.three[1].astype(F32)
                + self.three[2].astype(F32)
            )

    maps = Whole(fac_own, pf, pf_twin, pf_1a, pf_1b, pf_2a, pf_2b, pf_3)
    proj = Whole(wo_in, po, po_twin, po_1a, po_1b, po_2a, po_2b, po_3)
    both = (g_buf, u_buf)

    class Block:
        def __init__(self, b, gather_z_first):
            start, size = BLOCKS[b]
            self.cols = cols = pl.ds(start, size)
            mine = pl.ds(pl.multiple_of(c * HALF + start, 128), size)
            theirs = pl.ds(pl.multiple_of((1 - c) * HALF + start, 128), size)
            self.own, self.first = [], []
            for src, buf in ((wg_in, g_buf), (wu_in, u_buf)):
                slot = buf.at[x, z, y, c]
                self.own.append(own_copy(src.at[:, mine], slot.at[:, cols]))
                if gather_z_first:
                    for zz in z_peers:
                        self.first.append(w.make(src.at[:, mine], slot.at[:, cols], device(x, zz, y, c)))
                        self.first.append(w.make(src.at[:, theirs], slot.at[:, cols], device(x, zz, y, 1 - c)))
                else:
                    a_slot, b_slot = slot.at[a_rows, cols], slot.at[b_rows, cols]
                    self.first += [
                        w.make(src.at[a_rows, mine], a_slot, x_peer),
                        w.make(src.at[a_rows, theirs], a_slot, device(1 - x, z, y, 1 - c)),
                        w.make(src.at[b_rows, mine], b_slot, y_peer),
                        w.make(src.at[b_rows, theirs], b_slot, device(x, z, 1 - y, 1 - c)),
                    ]
                self.first.append(w.make(src.at[:, theirs], slot.at[:, cols], twin))
            if gather_z_first:
                self.second_a = [same(buf.at[x, :, y, :, a_rows, cols], x_peer) for buf in both]
                self.second_b = [same(buf.at[x, :, y, :, b_rows, cols], y_peer) for buf in both]
            else:
                self.second_a = [
                    same(buf.at[:, z, y, :, a_rows, cols], device(x, zz, y, c)) for buf in both for zz in z_peers
                ]
                self.second_b = [
                    same(buf.at[x, z, :, :, b_rows, cols], device(x, zz, y, c)) for buf in both for zz in z_peers
                ]
            self.third_a = [same(buf.at[:, :, y, :, a_rows, cols], y_peer) for buf in both]
            self.third_b = [same(buf.at[x, :, :, :, b_rows, cols], x_peer) for buf in both]
            self.one_u = w.make(u_buf.at[1 - x, :, :, :, :, cols], u1.at[:, :, :, :, cols], x_peer)
            self.one_g = w.make(g_buf.at[:, :, 1 - y, :, :, cols], g1.at[:, :, :, :, cols], y_peer)
            self.two_u = [
                w.make(u_buf.at[x, zz, :, :, :, cols], u2.at[step, :, :, :, cols], device(x, zz, y, c))
                for step, zz in enumerate(z_peers)
            ]
            self.two_g = [
                w.make(g_buf.at[:, zz, y, :, :, cols], g2.at[step, :, :, :, cols], device(x, zz, y, c))
                for step, zz in enumerate(z_peers)
            ]
            self.three_u = [
                w.make(u_buf.at[x, z, 1 - y, c, :, cols], u3.at[0, :, cols], y_peer),
                w.make(u_buf.at[x, z, 1 - y, 1 - c, :, cols], u3.at[2, :, cols], device(x, z, 1 - y, 1 - c)),
                w.make(u_buf.at[x, z, y, 1 - c, :, cols], u3.at[1, :, cols], twin),
            ]
            self.three_g = [
                w.make(g_buf.at[1 - x, z, y, c, :, cols], g3.at[0, :, cols], x_peer),
                w.make(g_buf.at[1 - x, z, y, 1 - c, :, cols], g3.at[2, :, cols], device(1 - x, z, y, 1 - c)),
                w.make(g_buf.at[x, z, y, 1 - c, :, cols], g3.at[1, :, cols], twin),
            ]

        def start(self):
            for copy in self.own:
                copy.start()
            go(*self.first)

        def second(self):
            for copy in self.own:
                copy.wait()
            arrive(self.first)
            go(*self.second_a, *self.second_b)

        def step_three_a(self):
            arrive(self.second_a)
            go(*self.third_a)

        def step_three_b(self):
            arrive(self.second_b)
            go(*self.third_b)

        def here(self):
            arrive(self.third_a)
            arrive(self.third_b)

        def gathered(self):
            ended([*self.second_a, *self.second_b, *self.third_a, *self.third_b])

        def sum_one(self):
            go(self.one_u, self.one_g)

        def sum_two_u(self):
            self.one_u.wait_recv()

            def add(i, _):
                zz, yy = lax.div(i, 2), lax.rem(i, 2)
                add_low(u_buf.at[x, zz, yy, :, :, self.cols], u1.at[zz, yy, :, :, self.cols])
                return 0

            lax.fori_loop(0, 8, add, 0)
            go(*self.two_u)

        def sum_two_g(self):
            self.one_g.wait_recv()

            def add(i, _):
                xx, zz = lax.div(i, 4), lax.rem(i, 4)
                add_low(g_buf.at[xx, zz, y, :, :, self.cols], g1.at[xx, zz, :, :, self.cols])
                return 0

            lax.fori_loop(0, 8, add, 0)
            go(*self.two_g)

        def sum_three_u(self):
            arrive(self.two_u)
            cols = self.cols

            def add(i, _):
                add_three(u_buf.at[x, z, i, :, :, cols], [u2.at[k, i, :, :, cols] for k in range(3)])
                return 0

            lax.fori_loop(0, 2, add, 0)
            go(*self.three_u)

        def sum_three_g(self):
            arrive(self.two_g)
            cols = self.cols

            def add(i, _):
                add_three(g_buf.at[i, z, y, :, :, cols], [g2.at[k, i, :, :, cols] for k in range(3)])
                return 0

            lax.fori_loop(0, 2, add, 0)
            go(*self.three_g)

        def sum_end(self, gate_sum, up_sum):
            arrive(self.three_u)
            arrive(self.three_g)
            cols = self.cols
            for buf, three, out in ((g_buf, g3, gate_sum), (u_buf, u3, up_sum)):
                out[c, :, cols] = buf[x, z, y, c, :, cols].astype(F32) + three[0, :, cols].astype(F32)
                out[1 - c, :, cols] = three[1, :, cols].astype(F32) + three[2, :, cols].astype(F32)

    def add_three(dst, three):
        total = dst[...].astype(F32)
        for src in three:
            total += src[...].astype(F32)
        dst[...] = total.astype(BF16)

    blocks = [Block(0, True), Block(1, False), Block(2, False), Block(3, False)]

    other_core = device(1 - x, z, y, 1 - c)
    d_swap = w.make(wd_own, d_buf.at[z, y, 1 - x], other_core)
    d_keep = own_copy(wd_own, d_buf.at[z, y, x])
    slot = d_buf.at[z, y, x]
    d_z_a = [same(slot.at[a_down], device(x, zz, y, c)) for zz in z_peers]
    d_z_b = [same(slot.at[b_down], device(x, zz, y, c)) for zz in z_peers]
    d_two_a, d_two_b = same(d_buf.at[:, y, x, a_down], x_peer), same(d_buf.at[:, y, x, b_down], y_peer)
    d_three_a, d_three_b = same(d_buf.at[:, y, :, a_down], y_peer), same(d_buf.at[:, :, x, b_down], x_peer)
    d_one_ga = w.make(d_buf.at[:, 1 - y, :, a_down], da1, y_peer)
    d_one_gb = w.make(d_buf.at[:, :, 1 - x, b_down], db1, x_peer)
    d_two_ga = w.make(d_buf.at[:, y, 1 - x, a_down], da2, x_peer)
    d_two_gb = w.make(d_buf.at[:, 1 - y, x, b_down], db2, y_peer)
    d_z_g = [w.make(d_buf.at[zz, y, x], d3.at[step], device(x, zz, y, c)) for step, zz in enumerate(z_peers)]

    def either(kept, swapped, verb):
        @pl.when(x == c)
        def _():
            getattr(kept, verb)()

        @pl.when(x != c)
        def _():
            getattr(swapped, verb)()

    def down_second():
        either(d_keep, d_swap, "wait")
        go(*d_z_a, *d_z_b)

    def down_two_a():
        arrive(d_z_a)
        go(d_two_a)

    def down_two_b():
        arrive(d_z_b)
        go(d_two_b)

    def down_three_a():
        d_two_a.wait_recv()
        go(d_three_a)

    def down_three_b():
        d_two_b.wait_recv()
        go(d_three_b)

    def down_sum_two_a():
        d_one_ga.wait_recv()

        def add(i, _):
            zz, s = lax.div(i, 2), lax.rem(i, 2)
            add_low(d_buf.at[zz, y, s, a_down], da1.at[zz, s])
            return 0

        lax.fori_loop(0, 8, add, 0)
        go(d_two_ga)

    def down_sum_two_b():
        d_one_gb.wait_recv()

        def add(i, _):
            zz, s = lax.div(i, 2), lax.rem(i, 2)
            add_low(d_buf.at[zz, s, x, b_down], db1.at[zz, s])
            return 0

        lax.fori_loop(0, 8, add, 0)
        go(d_two_gb)

    def down_sum_three():
        arrive([d_two_ga, d_two_gb])

        def add(i, _):
            add_low(d_buf.at[i, y, x, a_down], da2.at[i])
            add_low(d_buf.at[i, y, x, b_down], db2.at[i])
            return 0

        lax.fori_loop(0, 4, add, 0)
        go(*d_z_g)

    n2_twin = w.make(n2.at[0:512], n2.at[512:1024], twin)
    cot_twin = w.make(cot_in, cot.at[512:1024], twin)
    ng_send = w.make(ng_acc.at[512:1024], ng_twin, twin)
    out_send = w.make(out_acc.at[512:1024], out_twin, twin)
    own_cot = own_copy(cot_in, cot.at[0:512])

    def front(x_in, n1, kept, q, k, v, mixed, resid, bias, spread):
        cos_ref, sin_ref = kept.at[:, COS_LANES], kept.at[:, SIN_LANES]
        x_load = w.local(x_hbm, x_in)
        own_cot.start()
        for ref, at in ((w_bq, 0), (w_bk, 384), (w_bv, 512)):
            fac_own[:, at : at + ref.shape[1]] = ref[...]
        heads_tile = jnp.concatenate([w_aq[...].astype(F32), w_ak[...].astype(F32)], axis=1)
        fac_own[:, A_LANES] = heads_tile.astype(BF16)
        tile = jnp.concatenate([w_av[...].astype(F32), jnp.zeros((32, 96), F32)], axis=1)
        for row in (0, 1):
            gain = jnp.where(row_iota(32, 32) == lane_iota(32, 32), gains_in[row : row + 1, :].astype(F32), 0.0)
            gain = jnp.sum(gain, axis=1, keepdims=True)
            tile = jnp.where(lane_iota(32) == 32 + row, gain, tile)
        fac_own[:, V_LANES] = tile.astype(BF16)
        rows = wd_in[...].astype(F32)
        rows = jnp.concatenate([rows[:, 0:512], rows[:, 512:1024]], axis=0)
        wd_own[...] = rows.astype(BF16)
        pl.semaphore_wait(pltpu.get_barrier_semaphore(), partners)
        maps.start()
        blocks[0].start()
        proj.start()
        either(d_keep, d_swap, "start")
        for block in blocks[1:]:
            block.start()
        make_tables(lengths, cos_ref, sin_ref)
        make_spread(spread)
        make_bias(lengths, bias)
        down_second()
        blocks[1].second()
        maps.step_two()
        blocks[2].second()
        blocks[3].second()
        maps.step_three_a()
        maps.step_three_b()
        blocks[0].second()
        go(cot_twin)
        maps.pass_a()
        maps.pass_b()
        proj.step_two()
        x_load.wait()
        maps.here()
        gain_rows(pf, gains)
        make_factors(x_in, gains, pf, n1, kept, 0, 1)
        blocks[0].step_three_a()
        blocks[0].step_three_b()
        make_factors(x_in, gains, pf, n1, kept, 1, 2)
        saves = [w.local(n1, n1_kept)]
        proj.step_three_b()
        proj.step_three_a()
        make_heads(kept, cos_ref, sin_ref, spread, q, k, v, 0, 2)
        down_two_a()
        make_heads(kept, cos_ref, sin_ref, spread, q, k, v, 2, 4)
        for src, dst in (
            (kept, kept_kept),
            (q, q_kept),
            (k, k_kept),
            (v, v_kept),
            (bias, bias_kept),
            (spread, spread_kept),
        ):
            saves.append(w.local(src, dst))
        attend_pairs(q, k, v, bias, mixed, 0, 3)
        down_two_b()
        attend_pairs(q, k, v, bias, mixed, 3, 4)
        proj.pass_a()
        proj.pass_b()
        attend_pairs(q, k, v, bias, mixed, 4, 8)
        down_three_a()
        saves.append(w.local(mixed, mixed_kept))
        proj.here()
        make_resid(x_in, mixed, po, gains, resid, n2, 0, 1)
        down_three_b()
        blocks[1].step_three_a()
        make_resid(x_in, mixed, po, gains, resid, n2, 1, 2)
        saves.append(w.local(resid, resid_kept))
        go(n2_twin)
        for copy in saves:
            copy.wait()

    def feed_forward(n2_t, wd, hid, gg, ug, d_acc):
        own_cot.wait()

        def turn(i):
            rows = pl.ds(i * TILE, TILE)
            n2_t[:, rows] = n2[rows, :].T

        def forward(b, low, high):
            start, size = BLOCKS[b]
            cols = pl.ds(start, size)

            def tile(i, _):
                rows = pl.ds(pl.multiple_of(i * TILE, TILE), TILE)
                n2_rows, cot_rows = n2[rows, :], cot[rows, :]
                wg = g_buf[:, :, :, :, :, cols].reshape(1024, size)
                wu = u_buf[:, :, :, :, :, cols].reshape(1024, size)
                gate = dot(n2_rows, wg)
                up = dot(n2_rows, wu)
                hid_grad = dot(cot_rows, wd[cols, :], NT)
                sig = jax.nn.sigmoid(gate)
                silu = gate * sig
                hidden = (silu * up).astype(BF16)
                gate_grad = (hid_grad * up * sig * (1.0 + gate * (1.0 - sig))).astype(BF16)
                up_grad = (hid_grad * silu).astype(BF16)
                hid[rows, 0:size] = hidden
                gg[rows, 0:size] = gate_grad
                ug[rows, 0:size] = up_grad
                out_part = dot(hidden, wd[cols, :])
                ng_part = dot(gate_grad, wg, NT) + dot(up_grad, wu, NT)
                if b == 0:
                    out_acc[rows, :] = out_part
                    ng_acc[rows, :] = ng_part
                else:
                    out_acc[rows, :] += out_part
                    ng_acc[rows, :] += ng_part
                return 0

            lax.fori_loop(low, high, tile, 0)

        def column_grads(b):
            blocks[b].gathered()
            start, size = BLOCKS[b]
            cols = pl.ds(start, size)

            def side(i, _):
                rows = pl.ds(pl.multiple_of(i * 512, 512), 512)
                part = dot(n2_t[rows, :], ug[:, 0:size])
                u_buf[i, :, :, :, :, cols] = part.astype(BF16).reshape(4, 2, 2, 32, size)
                part = dot(n2_t[rows, :], gg[:, 0:size])
                g_buf[i, :, :, :, :, cols] = part.astype(BF16).reshape(4, 2, 2, 32, size)
                return 0

            lax.fori_loop(0, 2, side, 0)

        def row_grads(b):
            start, size = BLOCKS[b]
            d_acc[pl.ds(start, size), :] = dot(hid[:, 0:size], cot[...], TN)

        turn(0)
        turn(1)
        arrive([n2_twin, cot_twin])
        turn(2)
        turn(3)
        blocks[1].step_three_b()

        def gather_rows(at, lanes):
            def slot_rows(s, _):
                rows = d_buf[lax.div(s, 4), lax.rem(lax.div(s, 2), 2), lax.rem(s, 2), at : at + OWN_UNITS]
                d_acc[pl.ds(pl.multiple_of(s * OWN_UNITS, 8), OWN_UNITS), lanes] = rows.astype(F32)
                return 0

            lax.fori_loop(0, 16, slot_rows, 0)

            def low_rows(i, _):
                rows = pl.ds(pl.multiple_of(i * 128, 128), 128)
                wd[rows, lanes] = d_acc[rows, lanes].astype(BF16)
                return 0

            lax.fori_loop(0, HALF // 128, low_rows, 0)

        d_three_a.wait_recv()
        gather_rows(0, pl.ds(0, 512))
        d_three_b.wait_recv()
        gather_rows(OWN_UNITS, pl.ds(512, 512))
        blocks[2].step_three_a()
        blocks[0].here()
        forward(0, 0, 4)
        column_grads(0)
        blocks[0].sum_one()
        row_grads(0)
        blocks[2].step_three_b()
        blocks[1].here()
        forward(1, 0, 4)
        blocks[0].sum_two_u()
        blocks[3].step_three_a()
        column_grads(1)
        row_grads(1)
        blocks[0].sum_two_g()
        blocks[3].step_three_b()
        blocks[1].sum_one()
        blocks[2].here()
        forward(2, 0, 2)
        blocks[0].sum_three_u()
        forward(2, 2, 4)
        column_grads(2)
        row_grads(2)
        blocks[0].sum_three_g()
        blocks[2].sum_one()
        blocks[3].here()
        forward(3, 2, 4)
        go(ng_send, out_send)
        forward(3, 0, 2)
        row_grads(3)
        blocks[1].sum_two_g()
        ended([*d_z_a, *d_z_b, d_two_a, d_two_b, d_three_a, d_three_b])

        def spread_rows(s, _):
            rows = d_acc[pl.ds(pl.multiple_of(s * OWN_UNITS, 8), OWN_UNITS), :]
            rows = jnp.concatenate([rows[:, 0:512], rows[:, 512:1024]], axis=0)
            d_buf[lax.div(s, 4), lax.rem(lax.div(s, 2), 2), lax.rem(s, 2)] = rows.astype(BF16)
            return 0

        lax.fori_loop(0, 16, spread_rows, 0)
        go(d_one_ga, d_one_gb)
        column_grads(3)
        blocks[1].sum_two_u()
        blocks[3].sum_one()

    branch, mg = cot.at[0:512], cot.at[512:1024]

    def attention(
        resid, x_in, mixed, q, k, v, bias, kept, spread, n1, q_t, mg_t, gain_two,
        gate_sum, up_sum, d_sum,
    ):
        d_back = w.make(d_sum, down_out, other_core)
        d_stay = own_copy(d_sum, down_out)
        loads = [
            w.local(src, dst)
            for src, dst in (
                (resid_kept, resid),
                (mixed_kept, mixed),
                (q_kept, q),
                (k_kept, k),
                (v_kept, v),
                (bias_kept, bias),
                (kept_kept, kept),
                (spread_kept, spread),
                (n1_kept, n1),
                (x_hbm, x_in),
            )
        ]
        loads[0].wait()
        arrive([ng_send, out_send])

        def close(i, total):
            rows = pl.ds(pl.multiple_of(i * 128, 128), 128)
            base = resid[rows, :]
            n2[rows, :] = (base + out_acc[rows, :] + out_twin[rows, :]).astype(BF16)
            grad = ng_acc[rows, :] + ng_twin[rows, :]
            scale = lax.rsqrt(jnp.mean(base * base, axis=-1, keepdims=True) + EPSILON)
            unit = base * scale
            unit_grad = grad * gains[1:2, :]
            back = scale * (unit_grad - unit * jnp.mean(unit_grad * unit, axis=-1, keepdims=True))
            full = cot[rows, :].astype(F32) + back
            out_acc[rows, :] = full
            branch[rows, :] = full.astype(BF16)
            return total + jnp.sum((grad * unit).reshape(16, 8, 1024), axis=0)

        ended([n2_twin])
        gain_two[...] = lax.fori_loop(0, 4, close, jnp.zeros((8, 1024), F32))
        blocks[2].sum_two_g()
        results = [w.local(n2.at[0:512], outputs)]
        for copy in loads[1:3]:
            copy.wait()
        for i in range(2):
            rows = pl.ds(i * 256, 256)
            part = dot(branch[rows, :], po[...].reshape(1024, 1024), NT).astype(BF16)
            mg[rows, :] = part
            mg_t[:, rows] = part.T
            q_t[:, rows] = q[rows, :].T
        blocks[2].sum_two_u()
        blocks[1].sum_three_g()
        proj.gathered()
        for side in range(2):
            part = dot(mixed[:, side * 512 : (side + 1) * 512], branch[...], TN)
            po[side] = part.astype(BF16).reshape(4, 2, 2, 32, 1024)
        proj.sum_zero()
        for copy in loads[3:6]:
            copy.wait()
        ended([ng_send])
        heads = (q, q_t, k, v, mg, mg_t, bias, out_twin, ng_acc)
        head_grads(*heads, 0, 2)
        proj.sum_one()
        head_grads(*heads, 2, 4)
        blocks[1].sum_three_u()
        down_sum_two_a()
        head_grads(*heads, 4, 5)
        down_sum_two_b()
        head_grads(*heads, 5, 6)
        blocks[3].sum_two_g()
        head_grads(*heads, 6, 7)
        blocks[2].sum_three_g()
        blocks[3].sum_two_u()
        head_grads(*heads, 7, 8)
        proj.sum_two_a()
        for copy in loads[6:]:
            copy.wait()
        results[0].wait()
        factor_grads(out_twin, ng_acc, kept, spread, n2, 512, 0, 1)
        proj.sum_two_b()
        factor_grads(out_twin, ng_acc, kept, spread, n2, 512, 1, 2)
        blocks[2].sum_three_u()
        factor_grads(out_twin, ng_acc, kept, spread, n2, 512, 2, 4)
        down_sum_three()
        blocks[3].sum_three_g()
        fg = n2.at[512:1024, 0:FACTOR_PAD]
        incoming = out_twin
        for i in range(2):
            rows = pl.ds(i * 256, 256)
            incoming[rows, :] = dot(fg[rows, :], pf[...].reshape(1024, FACTOR_PAD), NT)
        gain_tile = jnp.where(
            row_iota(128, 1024) == 33, jnp.sum(gain_two[...], axis=0, keepdims=True), 0.0
        ).T
        maps.gathered()
        for side in range(2):
            part = dot(n1[:, side * 512 : (side + 1) * 512], fg[...], TN)
            part = jnp.concatenate(
                [part[:, 0:768], part[:, 768:896] + gain_tile[side * 512 : (side + 1) * 512]], axis=1
            )
            pf[side] = part.astype(BF16).reshape(4, 2, 2, 32, FACTOR_PAD)
        maps.sum_zero()
        proj.sum_three()
        blocks[3].sum_three_u()

        def first_norm(i, _):
            rows = pl.ds(pl.multiple_of(i * 128, 128), 128)
            vals = x_in[rows, :].astype(F32)
            scale = lax.rsqrt(jnp.mean(vals * vals, axis=-1, keepdims=True) + EPSILON)
            unit = vals * scale
            unit_grad = incoming[rows, :] * gains[0:1, :]
            back = scale * (unit_grad - unit * jnp.mean(unit_grad * unit, axis=-1, keepdims=True))
            out_acc[rows, :] += back
            return 0

        lax.fori_loop(0, 4, first_norm, 0)
        maps.sum_one()
        results.append(w.local(out_acc.at[0:512], input_grad))
        for block in blocks:
            block.sum_end(gate_sum, up_sum)
        maps.sum_two_a()
        maps.sum_two_b()
        results += [w.local(up_sum, up_out), w.local(gate_sum, gate_out)]
        arrive(d_z_g)
        d_sum[...] = (
            d_buf[z, y, x].astype(F32)
            + d3[0].astype(F32)
            + d3[1].astype(F32)
            + d3[2].astype(F32)
        )
        either(d_stay, d_back, "start")
        maps.sum_three()
        shard = out_twin.at[0:32, :]
        proj.sum_end(shard)
        results.append(w.local(shard, out_shard))
        shard = out_twin.at[32:64, 0:FACTOR_PAD]
        maps.sum_end(shard)
        own_maps, lanes = fac_own[...].astype(F32), lane_iota(32, FACTOR_PAD)
        total = jnp.sum(jnp.where(lanes < 800, own_maps * shard[...], 0.0), axis=-1, keepdims=True)
        gain = jnp.sum(jnp.where(lanes == 800, own_maps, 0.0), axis=-1, keepdims=True)
        tile_ref = out_twin.at[32:64, V_LANES]
        tile_ref[...] = jnp.where(lane_iota(32) == 32, total / gain, tile_ref[...])
        results.append(w.local(shard, fac_shard))
        either(d_stay, d_back, "wait")
        for copy in results[1:]:
            copy.wait()
        w.drain_shared()

    vmem = pltpu.VMEM
    row, turned = vmem((512, 1024), BF16), vmem((1024, 512), BF16)
    wide_row, bias_like = vmem((512, 1024), F32), vmem((512, 512), F32)
    kept_like, spread_like = vmem((512, KEPT), F32), vmem((8, 128, 1024), BF16)
    partners = greet(x, z, y, c)
    pl.run_scoped(front, row, row, kept_like, row, row, row, row, wide_row, bias_like, spread_like)
    pl.run_scoped(
        feed_forward,
        vmem((1024, 1024), BF16), vmem((HALF, 1024), BF16), turned, turned, turned, vmem((HALF, 1024), F32),
    )
    pl.run_scoped(
        attention,
        wide_row, row, row, row, row, row, bias_like, kept_like, spread_like, row, turned, turned,
        vmem((8, 1024), F32), vmem((2, 32, HALF), F32), vmem((2, 32, HALF), F32), vmem((DOWN_ROWS, 512), F32),
    )


def whole_all(*args):
    anywhere, vmem = pl.BlockSpec(memory_space=pl.ANY), pl.BlockSpec(memory_space=pltpu.VMEM)
    big = lambda *shape: pltpu.VMEM(shape, BF16)
    wide = lambda *shape: pltpu.VMEM(shape, F32)
    down_b = DOWN_ROWS - DOWN_A

    def full_scratch(width):
        return [
            big(2, 4, 2, 2, 32, width), big(2, 4, 2, 32, width),
            big(2, 4, 16, width), big(4, 2, 16, width), big(4, 16, width), big(4, 16, width),
            big(3, 32, width),
        ]

    row = (512, 1024)
    outs = [
        (row, BF16),
        (row, F32),
        ((2, 32, HALF), F32),
        ((2, 32, HALF), F32),
        ((DOWN_ROWS, 512), F32),
        ((32, 1024), F32),
        ((32, FACTOR_PAD), F32),
        (row, BF16),
        ((512, KEPT), F32),
        (row, BF16),
        (row, BF16),
        (row, BF16),
        (row, BF16),
        (row, F32),
        ((512, 512), F32),
        ((8, 128, 1024), BF16),
    ]
    return pl.pallas_call(
        whole_kernel,
        out_shape=[jax.ShapeDtypeStruct(*o) for o in outs],
        in_specs=[anywhere, pl.BlockSpec(memory_space=pltpu.SMEM)]
        + [vmem] * 7
        + [anywhere, vmem]
        + [anywhere] * 3,
        out_specs=[anywhere] * len(outs),
        scratch_shapes=[
            big(1024, 1024), big(1024, 1024),
            wide(1024, 1024), wide(1024, 1024), wide(512, 1024), wide(512, 1024),
            big(2, 4, 2, 2, 32, HALF), big(2, 4, 2, 2, 32, HALF), big(4, 2, 2, DOWN_ROWS, 512),
            big(2, 4, 2, 32, HALF), big(4, 2, 2, 32, HALF), big(4, 2, DOWN_A, 512), big(4, 2, down_b, 512),
            big(3, 2, 2, 32, HALF), big(3, 2, 2, 32, HALF),
            big(4, DOWN_A, 512), big(4, down_b, 512),
            big(3, 32, HALF), big(3, 32, HALF),
            big(3, DOWN_ROWS, 512),
            *full_scratch(1024),
            *full_scratch(FACTOR_PAD),
            wide(8, 1024), big(DOWN_ROWS, 512), big(32, FACTOR_PAD),
            pltpu.SemaphoreType.DMA((280,)),
            pltpu.SemaphoreType.DMA((280,)),
            pltpu.SemaphoreType.DMA((64,)),
        ],
        compiler_params=pltpu.CompilerParams(
            collective_id=0, has_side_effects=True, vmem_limit_bytes=62 * MIB
        ),
        name="whole_all",
    )(*args)[:7]


def cut_kernel(big_out, big_grad, *refs):
    smalls, outs, (held_out, held_grad, fac, out_in, gate, up, down, sems) = refs[:5], refs[5:-8], refs[-8:]
    loads, stores = [], []
    for part in range(4):
        rows = pl.ds(part * 128, 128)
        for src, held, dst in ((big_grad, held_grad, outs[1]), (big_out, held_out, outs[0])):
            at = len(loads)
            loads.append(pltpu.make_async_copy(src.at[rows], held.at[rows], sems.at[0, at]))
            stores.append(pltpu.make_async_copy(held.at[rows], dst.at[rows], sems.at[1, at]))
    first = [
        pltpu.make_async_copy(src, dst, sems.at[2, at])
        for at, (src, dst) in enumerate(zip(smalls, (fac, out_in, gate, up, down), strict=True))
    ]
    for copy in (*loads[:4], *first, *loads[4:]):
        copy.start()
    for load, store in zip(loads[:4], stores[:4], strict=True):
        load.wait()
        store.start()
    for copy in first:
        copy.wait()
    for load, store in zip(loads[4:], stores[4:], strict=True):
        load.wait()
        store.start()
    pieces = (640, 96), (0, 384), (736, 32), (384, 128), (768, 32), (512, 128)
    for (start, size), ref in zip(pieces, outs[2:8], strict=True):
        ref[...] = fac[:, start : start + size]
    outs[8][...] = out_in[...]
    for src, ref in ((gate, outs[9]), (up, outs[10])):
        ref[:, 0:HALF] = src[0]
        ref[:, HALF:FF] = src[1]
    outs[11][:, 0:512] = down[0:OWN_UNITS, :]
    outs[11][:, 512:1024] = down[OWN_UNITS:DOWN_ROWS, :]
    tile = jnp.concatenate([fac[:, 768:896], jnp.zeros((96, 128), F32)], axis=0).T
    outs[12][...] = tile[32:33, 0:32]
    outs[13][...] = tile[33:34, 0:32]
    for copy in stores:
        copy.wait()


def cut_all(*args):
    shapes = [(32, n) for n in (96, 384, 32, 128, 32, 128, 1024, FF, FF)] + [(OWN_UNITS, 1024), (1, 32), (1, 32)]
    anywhere, vmem = pl.BlockSpec(memory_space=pl.ANY), pl.BlockSpec(memory_space=pltpu.VMEM)
    wide = lambda *shape: pltpu.VMEM(shape, F32)
    return pl.pallas_call(
        cut_kernel,
        out_shape=[jax.ShapeDtypeStruct((512, 1024), BF16), jax.ShapeDtypeStruct((512, 1024), F32)]
        + [jax.ShapeDtypeStruct(s, F32) for s in shapes],
        in_specs=[anywhere] * 7,
        out_specs=[anywhere] * 2 + [vmem] * len(shapes),
        scratch_shapes=[
            pltpu.VMEM((512, 1024), BF16), wide(512, 1024), wide(32, FACTOR_PAD), wide(32, 1024),
            wide(2, 32, HALF), wide(2, 32, HALF), wide(DOWN_ROWS, 512),
            pltpu.SemaphoreType.DMA((3, 8)),
        ],
        compiler_params=pltpu.CompilerParams(vmem_limit_bytes=61 * MIB),
        name="cut_all",
    )(*args)


def local_paired(
    inputs, doc_lengths, w_aq, w_bq, w_ak, w_bk, w_av, w_bv,
    w_out, w_gate, w_up, w_down, gain_attn, gain_ffn, cotangent,
):
    outputs, input_grad, gate_sum, up_sum, down_sum, out_sum, fac_sum = whole_all(
        inputs, doc_lengths, w_bq, w_bk, w_bv, w_aq, w_ak, w_av, jnp.stack([gain_attn, gain_ffn]),
        w_out, w_down, w_gate, w_up, cotangent,
    )
    *cut, gain_one, gain_two = cut_all(
        outputs, input_grad, fac_sum, out_sum, gate_sum, up_sum, down_sum
    )
    return (*cut, gain_one[0], gain_two[0])


def solution(mesh):
    return jax.shard_map(
        local_paired if fits_pairs(mesh) else local,
        mesh=mesh,
        in_specs=(
            P(("dp", "fsdp"), None),
            P(("dp", "fsdp"), None),
            P(("dp", "fsdp"), None),
            P(("dp", "fsdp"), None),
            P(("dp", "fsdp"), None),
            P(("dp", "fsdp"), None),
            P(("dp", "fsdp"), None),
            P(("dp", "fsdp"), None),
            P(("dp", "fsdp"), None),
            P(("dp", "fsdp"), None),
            P(("dp", "fsdp"), None),
            P(("dp", "fsdp"), None),
            P(("dp", "fsdp")),
            P(("dp", "fsdp")),
            P(("dp", "fsdp"), None),
        ),
        out_specs=(
            P(("dp", "fsdp"), None),
            P(("dp", "fsdp"), None),
            P(("dp", "fsdp"), None),
            P(("dp", "fsdp"), None),
            P(("dp", "fsdp"), None),
            P(("dp", "fsdp"), None),
            P(("dp", "fsdp"), None),
            P(("dp", "fsdp"), None),
            P(("dp", "fsdp"), None),
            P(("dp", "fsdp"), None),
            P(("dp", "fsdp"), None),
            P(("dp", "fsdp"), None),
            P(("dp", "fsdp")),
            P(("dp", "fsdp")),
        ),
        check_vma=False,
    )
```

```python
import math

import jax
import jax.numpy as jnp
from jax import lax
from jax.experimental import pallas as pl
from jax.experimental.pallas import tpu as pltpu
from jax.sharding import PartitionSpec as P

HEADS = 16
HEAD_DIM = 64
RANK_Q = 6
RANK_KV = 2
FF = 2816


EPSILON = 1e-06
PRECISE = lax.Precision.HIGHEST


def factor_columns():
    return [
        RANK_Q * HEADS,
        RANK_Q * HEAD_DIM,
        RANK_KV * HEADS,
        RANK_KV * HEAD_DIM,
        RANK_KV * HEADS,
        RANK_KV * HEAD_DIM,
    ]


def split_columns(matrix):
    pieces = []
    offset = 0
    for columns in factor_columns():
        pieces.append(matrix[:, offset : offset + columns])
        offset += columns
    return pieces


def doc_layout(lengths, length):
    order = jnp.arange(lengths.shape[0], dtype=jnp.int32)
    doc_ends = jnp.sum(jnp.where(order[:, None] >= order[None, :], lengths[None, :], 0), axis=1)
    doc_starts = doc_ends - lengths
    places = jnp.arange(length, dtype=jnp.int32)
    segment = jnp.sum((places[:, None] >= doc_ends[None, :]).astype(jnp.int32), axis=1)
    owner = segment[:, None] == jnp.arange(lengths.shape[0], dtype=jnp.int32)[None, :]
    doc_first = jnp.sum(jnp.where(owner, doc_starts[None, :], 0), axis=1)
    return (segment, (places - doc_first).astype(jnp.float32))


def rotation(places):
    halfway = HEAD_DIM // 2
    freqs = jnp.exp(-math.log(10000.0) * jnp.arange(halfway, dtype=jnp.float32) / halfway)
    angles = places[..., None] * freqs
    return (jnp.cos(angles), jnp.sin(angles))


def rotate(factor, cos_table, sin_table):
    halfway = factor.shape[-1] // 2
    front_part = factor[..., :halfway]
    back_part = factor[..., halfway:]
    cos_part = cos_table[..., None, :]
    sin_part = sin_table[..., None, :]
    return jnp.concatenate(
        [
            front_part * cos_part - back_part * sin_part,
            front_part * sin_part + back_part * cos_part,
        ],
        axis=-1,
    )


def normalize(values, gain):
    scaling = lax.rsqrt(jnp.mean(values * values, axis=-1, keepdims=True) + EPSILON)
    unit_vals = values * scaling
    return (unit_vals * gain, unit_vals, scaling)


def norm_back(incoming, unit_vals, scaling, gain):
    unit_grad = incoming * gain
    grad_in = scaling * (
        unit_grad - unit_vals * jnp.mean(unit_grad * unit_vals, axis=-1, keepdims=True)
    )
    return (grad_in, jnp.sum(incoming * unit_vals, axis=0))


def block_scores(query_part, keys_low, seg_part, segment, place_part, places):
    scaling = HEAD_DIM ** (-0.5)
    scores = (
        jnp.einsum("thd,shd->hts", query_part, keys_low, preferred_element_type=jnp.float32)
        * scaling
    )
    allowed = (seg_part[:, None] == segment[None, :]) & (places[None, :] <= place_part[:, None])
    return jnp.where(allowed[None], scores, -1e30)


def attend_forward(queries, keys_low, values, segment):
    length = queries.shape[0]
    block_rows = min(512, length)
    places = jnp.arange(length, dtype=jnp.int32)

    def one_block(block_index):
        masked = block_scores(queries, keys_low, segment, segment, places, places)
        row_peak = jnp.max(masked, axis=-1, keepdims=True)
        exp_terms = jnp.exp(masked - row_peak)
        row_total = jnp.sum(exp_terms, axis=-1, keepdims=True)
        attn_probs = (exp_terms / row_total).astype(jnp.bfloat16)
        attended = jnp.einsum(
            "hts,shd->thd", attn_probs, values, preferred_element_type=jnp.float32
        )
        return (attended, (row_peak + jnp.log(row_total))[..., 0])

    attended, log_totals = lax.map(one_block, jnp.arange(length // block_rows, dtype=jnp.int32))
    return (attended.reshape(length, HEADS, HEAD_DIM), log_totals)


def attend_backward(queries, keys_low, values, segment, log_totals, mixed_grad):
    length = queries.shape[0]
    block_rows = min(512, length)
    places = jnp.arange(length, dtype=jnp.int32)
    scaling = HEAD_DIM ** (-0.5)

    def one_block(running, block_index):
        key_grad, value_grad = running
        masked = block_scores(queries, keys_low, segment, segment, places, places)
        attn_probs = jnp.exp(masked - log_totals[block_index][..., None])
        probs_low = attn_probs.astype(jnp.bfloat16)
        value_grad = value_grad + jnp.einsum(
            "hts,thd->shd", probs_low, mixed_grad, preferred_element_type=jnp.float32
        )
        probs_grad = jnp.einsum(
            "thd,shd->hts", mixed_grad, values, preferred_element_type=jnp.float32
        )
        inner_sum = jnp.sum(attn_probs * probs_grad, axis=-1, keepdims=True)
        score_grad = (attn_probs * (probs_grad - inner_sum)).astype(jnp.bfloat16)
        query_grad = (
            jnp.einsum("hts,shd->thd", score_grad, keys_low, preferred_element_type=jnp.float32)
            * scaling
        )
        key_grad = (
            key_grad
            + jnp.einsum("hts,thd->shd", score_grad, queries, preferred_element_type=jnp.float32)
            * scaling
        )
        return ((key_grad, value_grad), query_grad)

    empty = jnp.zeros((length, HEADS, HEAD_DIM), jnp.float32)
    (key_grad, value_grad), query_grad = lax.scan(
        one_block, (empty, empty), jnp.arange(length // block_rows, dtype=jnp.int32)
    )
    return (query_grad.reshape(length, HEADS, HEAD_DIM), key_grad, value_grad)


def factor_back(full_grad, a_part, b_part, rank_count):
    a_grad = jnp.einsum("thd,trd->trh", full_grad, b_part, precision=PRECISE) / rank_count
    b_grad = jnp.einsum("thd,trh->trd", full_grad, a_part, precision=PRECISE) / rank_count
    return (a_grad, b_grad)


def local(
    inputs,
    doc_lengths,
    w_aq,
    w_bq,
    w_ak,
    w_bk,
    w_av,
    w_bv,
    w_out,
    w_gate,
    w_up,
    w_down,
    gain_attn,
    gain_ffn,
    cotangent,
):
    length = inputs.shape[0]
    joined_local = jnp.concatenate([w_aq, w_bq, w_ak, w_bk, w_av, w_bv], axis=1)
    factor_w, out_w, gain_one = (
        lax.all_gather(joined_local, ("dp", "fsdp"), axis=0, tiled=True),
        lax.all_gather(w_out, ("dp", "fsdp"), axis=0, tiled=True),
        lax.all_gather(gain_attn, ("dp", "fsdp"), axis=0, tiled=True),
    )
    segment, places = doc_layout(doc_lengths[0], length)
    cos_table, sin_table = rotation(places)
    start_vals = inputs.astype(jnp.float32)
    normed_one, unit_one, scale_one = normalize(start_vals, gain_one.astype(jnp.float32))
    normed_low = normed_one.astype(jnp.bfloat16)
    factors = jnp.dot(normed_low, factor_w, preferred_element_type=jnp.float32)
    pieces = split_columns(factors)
    a_q = pieces[0].reshape(length, RANK_Q, HEADS)
    b_q = pieces[1].reshape(length, RANK_Q, HEAD_DIM)
    a_k = pieces[2].reshape(length, RANK_KV, HEADS)
    b_k = pieces[3].reshape(length, RANK_KV, HEAD_DIM)
    a_v = pieces[4].reshape(length, RANK_KV, HEADS)
    b_v = pieces[5].reshape(length, RANK_KV, HEAD_DIM)
    bq_rot = rotate(b_q, cos_table, sin_table)
    bk_rot = rotate(b_k, cos_table, sin_table)
    queries = (jnp.einsum("trh,trd->thd", a_q, bq_rot, precision=PRECISE) / RANK_Q).astype(
        jnp.bfloat16
    )
    keys_low = (jnp.einsum("trh,trd->thd", a_k, bk_rot, precision=PRECISE) / RANK_KV).astype(
        jnp.bfloat16
    )
    values = (jnp.einsum("trh,trd->thd", a_v, b_v, precision=PRECISE) / RANK_KV).astype(
        jnp.bfloat16
    )
    attended, log_totals = attend_forward(queries, keys_low, values, segment)
    mixed = attended.astype(jnp.bfloat16).reshape(length, HEADS * HEAD_DIM)
    resid = start_vals + jnp.dot(mixed, out_w, preferred_element_type=jnp.float32)
    gate_w, up_w, down_w, gain_two = (
        lax.all_gather(w_gate, ("dp", "fsdp"), axis=0, tiled=True),
        lax.all_gather(w_up, ("dp", "fsdp"), axis=0, tiled=True),
        lax.all_gather(w_down, ("dp", "fsdp"), axis=0, tiled=True),
        lax.all_gather(gain_ffn, ("dp", "fsdp"), axis=0, tiled=True),
    )
    normed_two, unit_two, scale_two = normalize(resid, gain_two.astype(jnp.float32))
    normed_two_low = normed_two.astype(jnp.bfloat16)
    gate_act = jnp.dot(normed_two_low, gate_w, preferred_element_type=jnp.float32)
    up_act = jnp.dot(normed_two_low, up_w, preferred_element_type=jnp.float32)
    hidden = (jax.nn.silu(gate_act) * up_act).astype(jnp.bfloat16)
    result = resid + jnp.dot(hidden, down_w, preferred_element_type=jnp.float32)
    outputs = result.astype(jnp.bfloat16)
    gate_w, up_w, down_w, gain_two = (
        lax.all_gather(w_gate, ("dp", "fsdp"), axis=0, tiled=True),
        lax.all_gather(w_up, ("dp", "fsdp"), axis=0, tiled=True),
        lax.all_gather(w_down, ("dp", "fsdp"), axis=0, tiled=True),
        lax.all_gather(gain_ffn, ("dp", "fsdp"), axis=0, tiled=True),
    )
    hidden_grad = jnp.einsum("tc,fc->tf", cotangent, down_w, preferred_element_type=jnp.float32)
    down_wgrad = jnp.einsum("tf,tc->fc", hidden, cotangent, preferred_element_type=jnp.float32)
    sig_vals = jax.nn.sigmoid(gate_act)
    gate_grad = (hidden_grad * up_act * sig_vals * (1.0 + gate_act * (1.0 - sig_vals))).astype(
        jnp.bfloat16
    )
    up_grad = (hidden_grad * jax.nn.silu(gate_act)).astype(jnp.bfloat16)
    normed_two_grad = jnp.einsum("tf,cf->tc", gate_grad, gate_w, preferred_element_type=jnp.float32)
    normed_two_grad = normed_two_grad + jnp.einsum(
        "tf,cf->tc", up_grad, up_w, preferred_element_type=jnp.float32
    )
    resid_norm_grad, gain_two_grad = norm_back(
        normed_two_grad, unit_two, scale_two, gain_two.astype(jnp.float32)
    )
    resid_grad = cotangent.astype(jnp.float32) + resid_norm_grad
    gate_rows = jnp.einsum(
        "tc,tf->cf", normed_two_low, gate_grad, preferred_element_type=jnp.float32
    )
    up_rows = jnp.einsum("tc,tf->cf", normed_two_low, up_grad, preferred_element_type=jnp.float32)
    gate_up_shard = lax.psum_scatter(
        jnp.concatenate([gate_rows, up_rows], axis=1),
        ("dp", "fsdp"),
        scatter_dimension=0,
        tiled=True,
    )
    gate_shard = gate_up_shard[:, :FF]
    up_shard = gate_up_shard[:, FF:]
    down_shard, gain_two_shard = (
        lax.psum_scatter(down_wgrad, ("dp", "fsdp"), scatter_dimension=0, tiled=True),
        lax.psum_scatter(gain_two_grad, ("dp", "fsdp"), scatter_dimension=0, tiled=True),
    )
    factor_w, out_w, gain_one = (
        lax.all_gather(joined_local, ("dp", "fsdp"), axis=0, tiled=True),
        lax.all_gather(w_out, ("dp", "fsdp"), axis=0, tiled=True),
        lax.all_gather(gain_attn, ("dp", "fsdp"), axis=0, tiled=True),
    )
    branch_grad = resid_grad.astype(jnp.bfloat16)
    out_wgrad = jnp.einsum("tc,td->cd", mixed, branch_grad, preferred_element_type=jnp.float32)
    mixed_grad = jnp.einsum("td,cd->tc", branch_grad, out_w, preferred_element_type=jnp.float32)
    mixed_grad = mixed_grad.astype(jnp.bfloat16).reshape(length, HEADS, HEAD_DIM)
    query_grad, key_grad, value_grad = attend_backward(
        queries, keys_low, values, segment, log_totals, mixed_grad
    )
    a_q_grad, bq_rot_grad = factor_back(query_grad, a_q, bq_rot, RANK_Q)
    a_k_grad, bk_rot_grad = factor_back(key_grad, a_k, bk_rot, RANK_KV)
    a_v_grad, b_v_grad = factor_back(value_grad, a_v, b_v, RANK_KV)
    neg_sin = -sin_table
    b_q_grad = rotate(bq_rot_grad, cos_table, neg_sin)
    b_k_grad = rotate(bk_rot_grad, cos_table, neg_sin)
    factor_grad = jnp.concatenate(
        [
            part.reshape(length, -1)
            for part in (a_q_grad, b_q_grad, a_k_grad, b_k_grad, a_v_grad, b_v_grad)
        ],
        axis=1,
    ).astype(jnp.bfloat16)
    factor_wgrad = jnp.einsum(
        "td,tc->dc", normed_low, factor_grad, preferred_element_type=jnp.float32
    )
    normed_one_grad = jnp.einsum(
        "tc,dc->td", factor_grad, factor_w, preferred_element_type=jnp.float32
    )
    input_norm_grad, gain_one_grad = norm_back(
        normed_one_grad, unit_one, scale_one, gain_one.astype(jnp.float32)
    )
    input_grad = resid_grad + input_norm_grad
    factor_shard, out_shard, gain_one_shard = (
        lax.psum_scatter(factor_wgrad, ("dp", "fsdp"), scatter_dimension=0, tiled=True),
        lax.psum_scatter(out_wgrad, ("dp", "fsdp"), scatter_dimension=0, tiled=True),
        lax.psum_scatter(gain_one_grad, ("dp", "fsdp"), scatter_dimension=0, tiled=True),
    )
    shard_pieces = split_columns(factor_shard)
    return (
        outputs,
        input_grad,
        shard_pieces[0],
        shard_pieces[1],
        shard_pieces[2],
        shard_pieces[3],
        shard_pieces[4],
        shard_pieces[5],
        out_shard,
        gate_shard,
        up_shard,
        down_shard,
        gain_one_shard,
        gain_two_shard,
    )


MESH_IDS = pl.DeviceIdType.MESH
HALF = FF // 2
OWN_UNITS = 88
DOWN_ROWS = 2 * OWN_UNITS
DOWN_A = 96
FACTOR_PAD = 896
MIB = 2**20


def fits_pairs(mesh):
    return dict(mesh.shape) == {"dp": 2, "fsdp": 16}


def place():
    x = lax.axis_index("dp")
    f = lax.axis_index("fsdp")
    return x, lax.div(f, 4), lax.rem(lax.div(f, 2), 2), lax.rem(f, 2)


def device(x, z, y, c):
    return (x, z * 4 + y * 2 + c)


def greet(x, z, y, c):
    partners = [
        device(x, z, y, 1 - c),
        device(1 - x, z, y, c),
        device(x, z, 1 - y, c),
        device(1 - x, z, y, 1 - c),
        device(x, z, 1 - y, 1 - c),
    ]
    for step in (1, 2, 3):
        other = lax.rem(z + step, 4)
        partners += [device(x, other, y, c), device(x, other, y, 1 - c)]
    barrier = pltpu.get_barrier_semaphore()
    for partner in partners:
        pl.semaphore_signal(barrier, inc=1, device_id=partner, device_id_type=MESH_IDS)
    return len(partners)


class Wires:
    def __init__(self, send_sems, recv_sems, local_sems):
        self.send_sems, self.recv_sems, self.local_sems = send_sems, recv_sems, local_sems
        self.sent, self.held = 0, 0
        self.open, self.shared = [], []

    def make(self, src, dst, to):
        at = self.sent
        self.sent += 1
        return pltpu.make_async_remote_copy(
            src_ref=src,
            dst_ref=dst,
            send_sem=self.send_sems.at[at],
            recv_sem=self.recv_sems.at[at],
            device_id=to,
            device_id_type=MESH_IDS,
        )

    def go(self, copy):
        copy.start()
        self.shared.append(copy)
        return copy

    def send(self, src, dst, to):
        copy = self.make(src, dst, to)
        copy.start()
        self.open.append(copy)
        return copy

    def local(self, src, dst):
        copy = pltpu.make_async_copy(src, dst, self.local_sems.at[self.held])
        self.held += 1
        copy.start()
        return copy

    def drain(self):
        for copy in self.open:
            copy.wait_send()
        self.open = []

    def drain_shared(self):
        for copy in self.shared:
            copy.wait_send()
        self.shared = []


def arrive(copies):
    for copy in copies:
        copy.wait_recv()


BLOCKS = ((0, 256), (256, 512), (768, 384), (1152, 256))
TILE = 256
NT = (((1,), (1,)), ((), ()))
TN = (((0,), (0,)), ((), ()))
F32, BF16 = jnp.float32, jnp.bfloat16


def dot(a, b, dims=None):
    if dims is None:
        return jnp.dot(a, b, preferred_element_type=F32)
    return lax.dot_general(a, b, dims, preferred_element_type=F32)


def add_low(dst, src):
    dst[...] = (dst[...].astype(F32) + src[...].astype(F32)).astype(BF16)


KEPT = 1152
COS_LANES = pl.ds(896, 128)
SIN_LANES = pl.ds(1024, 128)
A_LANES = pl.ds(640, 128)
V_LANES = pl.ds(768, 128)


def lane_iota(rows, lanes=128):
    return lax.broadcasted_iota(jnp.int32, (rows, lanes), 1)


def row_iota(rows, lanes=128):
    return lax.broadcasted_iota(jnp.int32, (rows, lanes), 0)


def doc_ends_of(lengths):
    one = lengths[0, 0]
    two = one + lengths[0, 1]
    return one, two, two + lengths[0, 2]


def make_tables(lengths, cos_ref, sin_ref):
    ends = doc_ends_of(lengths)

    def tile(i, _):
        rows = pl.ds(pl.multiple_of(i * 128, 128), 128)
        places = row_iota(128) + i * 128
        first = jnp.zeros((128, 128), jnp.int32)
        for end in ends:
            first = jnp.where(places >= end, end, first)
        lane = lane_iota(128)
        turn = lax.rem(lane, 32).astype(F32)
        freqs = jnp.exp(-math.log(10000.0) * turn / 32)
        angles = (places - first).astype(F32) * freqs
        cos_ref[rows, :] = jnp.cos(angles)
        sin_vals = jnp.sin(angles)
        sin_ref[rows, :] = jnp.where(lax.rem(lane, 64) < 32, -sin_vals, sin_vals)
        return 0

    lax.fori_loop(0, 4, tile, 0)


def make_bias(lengths, bias):
    ends = doc_ends_of(lengths)

    def tile(i, _):
        rows = pl.ds(pl.multiple_of(i * 128, 128), 128)
        t = row_iota(128, 512) + i * 128
        s = lane_iota(128, 512)
        own, key = jnp.zeros((128, 512), jnp.int32), jnp.zeros((128, 512), jnp.int32)
        for end in ends:
            own += (t >= end).astype(jnp.int32)
            key += (s >= end).astype(jnp.int32)
        bias[rows, :] = jnp.where((own == key) & (s <= t), 0.0, -1e30)
        return 0

    lax.fori_loop(0, 4, tile, 0)


def make_spread(spread):
    def rank(r, _):
        head = lax.div(lane_iota(128, 1024), HEAD_DIM) + r * HEADS
        spread[r] = jnp.where(row_iota(128, 1024) == head, 1.0, 0.0).astype(BF16)
        return 0

    lax.fori_loop(0, 8, rank, 0)


def swapped(tile):
    front = lax.rem(lane_iota(tile.shape[0]), 64) < 32
    return jnp.where(front, pltpu.roll(tile, 96, 1), pltpu.roll(tile, 32, 1))


def both_halves(tile, half):
    low = lane_iota(tile.shape[0]) < 64
    other = pltpu.roll(tile, 64, 1)
    return jnp.where(low, tile, other) if half == 0 else jnp.where(low, other, tile)


def two_terms(a):
    high = a.astype(BF16)
    return high, (a - high.astype(F32)).astype(BF16)


def expand(terms, spread_r):
    return dot(terms[0], spread_r) + dot(terms[1], spread_r)


def eight(tile):
    return jnp.concatenate([tile] * 8, axis=1)


def gain_rows(fac_all, gains):
    tile = fac_all[:, :, :, :, :, V_LANES].reshape(1024, 128).astype(F32)
    gains[...] = tile.T[32:40, :]


def make_factors(x_in, gains, fac_all, n1, kept, first, last):
    def tile(i, _):
        rows = pl.ds(pl.multiple_of(i * 256, 256), 256)
        vals = x_in[rows, :].astype(F32)
        scale = lax.rsqrt(jnp.mean(vals * vals, axis=-1, keepdims=True) + EPSILON)
        low = (vals * scale * gains[0:1, :]).astype(BF16)
        n1[rows, :] = low
        kept[rows, 0:FACTOR_PAD] = dot(low, fac_all[...].reshape(1024, FACTOR_PAD))
        return 0

    lax.fori_loop(first, last, tile, 0)


def make_heads(kept, cos_ref, sin_ref, spread, q, k, v, first, last):
    def tile(i, _):
        rows = pl.ds(pl.multiple_of(i * 128, 128), 128)
        turned = []
        for j in range(4):
            lanes = pl.ds(j * 128, 128)
            part = kept[rows, lanes]
            part = part * cos_ref[rows, :] + swapped(part) * sin_ref[rows, :]
            kept[rows, lanes] = part
            turned.append(part)
        terms = two_terms(kept[rows, A_LANES])
        total = jnp.zeros((128, 1024), F32)
        for r in range(RANK_Q):
            total += expand(terms, spread[r]) * eight(both_halves(turned[r // 2], r % 2))
        q[rows, :] = (total * (1.0 / RANK_Q)).astype(BF16) * BF16(HEAD_DIM**-0.5)
        total = jnp.zeros((128, 1024), F32)
        for r in range(RANK_KV):
            total += expand(terms, spread[RANK_Q + r]) * eight(both_halves(turned[3], r))
        k[rows, :] = (total * (1.0 / RANK_KV)).astype(BF16)
        terms = two_terms(kept[rows, V_LANES])
        plain = kept[rows, pl.ds(512, 128)]
        total = jnp.zeros((128, 1024), F32)
        for r in range(RANK_KV):
            total += expand(terms, spread[r]) * eight(both_halves(plain, r))
        v[rows, :] = (total * (1.0 / RANK_KV)).astype(BF16)
        return 0

    lax.fori_loop(first, last, tile, 0)


def only(tile, half):
    low = lane_iota(tile.shape[0]) < 64
    keep = low if half == 0 else jnp.logical_not(low)
    return jnp.where(keep, tile, jnp.zeros_like(tile))


def soft(q_rows, k_cols, bias_block):
    scores = dot(q_rows, k_cols, NT) + bias_block
    terms = jnp.exp(scores - jnp.max(scores, axis=-1, keepdims=True))
    return terms * (1.0 / jnp.sum(terms, axis=-1, keepdims=True))


def attend_pairs(q, k, v, bias, mixed, first, last):
    def pair(p, _):
        lanes = pl.ds(pl.multiple_of(p * 128, 128), 128)
        for start, extent in ((0, 256), (256, 512)):
            rows, cols = pl.ds(start, 256), pl.ds(0, extent)
            q_rows, k_cols, v_cols = q[rows, lanes], k[cols, lanes], v[cols, lanes]
            halves = []
            for half in (0, 1):
                probs = soft(only(q_rows, half), k_cols, bias[rows, cols]).astype(BF16)
                halves.append(dot(probs, v_cols))
            low = lane_iota(256) < 64
            mixed[rows, lanes] = jnp.where(low, halves[0], halves[1]).astype(BF16)
        return 0

    lax.fori_loop(first, last, pair, 0)


def make_resid(x_in, mixed, out_all, gains, resid, n2, first, last):
    def tile(i, _):
        rows = pl.ds(pl.multiple_of(i * 256, 256), 256)
        base = x_in[rows, :].astype(F32) + dot(mixed[rows, :], out_all[...].reshape(1024, 1024))
        resid[rows, :] = base
        scale = lax.rsqrt(jnp.mean(base * base, axis=-1, keepdims=True) + EPSILON)
        n2[rows, :] = (base * scale * gains[1:2, :]).astype(BF16)
        return 0

    lax.fori_loop(first, last, tile, 0)


def head_grads(q, q_t, k, v, mg, mg_t, bias, dq, dkv_t, first, last):
    def pair(p, _):
        at = pl.multiple_of(p * 128, 128)
        lanes = pl.ds(at, 128)
        for start, extent in ((256, 512), (0, 256)):
            rows, cols = pl.ds(start, 256), pl.ds(0, extent)
            q_rows, mg_rows = q[rows, lanes], mg[rows, lanes]
            k_cols, v_cols = k[cols, lanes], v[cols, lanes]
            halves = []
            for half in (0, 1):
                own = pl.ds(pl.multiple_of(at + half * 64, 64), 64)
                probs = soft(only(q_rows, half), k_cols, bias[rows, cols])
                probs_grad = dot(only(mg_rows, half), v_cols, NT)
                inner = jnp.sum(probs * probs_grad, axis=-1, keepdims=True)
                score_grad = (probs * (probs_grad - inner)).astype(BF16)
                dv = dot(mg_t[own, rows], probs.astype(BF16))
                dk = dot(q_t[own, rows], score_grad)
                if start:
                    dkv_t[own, 0:512] = dk
                    dkv_t[own, 512:1024] = dv
                else:
                    dkv_t[own, 0:256] += dk
                    dkv_t[own, 512:768] += dv
                halves.append(dot(score_grad, k_cols))
            low = lane_iota(256) < 64
            dq[rows, lanes] = jnp.where(low, halves[0], halves[1]) * HEAD_DIM**-0.5
        return 0

    lax.fori_loop(first, last, pair, 0)


def fold(product):
    total = product[:, 0:128]
    for j in range(1, 8):
        total += product[:, j * 128 : (j + 1) * 128]
    return total + pltpu.roll(total, 64, 1)


def rank_grads(full, terms, ranks, duplicates, spread):
    a_grad, b_grads = jnp.zeros((full.shape[0], 128), F32), []
    for r, twice in zip(ranks, duplicates, strict=True):
        spread_r = spread[r]
        a_grad += dot((full * eight(twice)).astype(BF16), spread_r, NT)
        b_grads.append(fold(full * expand(terms, spread_r)))
    return a_grad, b_grads


def pick(low_half, high_half):
    return jnp.where(lane_iota(low_half.shape[0]) < 64, low_half, high_half)


def factor_grads(dq, dkv_t, kept, spread, fg, fg_at, first, last):
    def tile(i, _):
        at = pl.multiple_of(i * 128, 128)
        rows = pl.ds(at, 128)
        out = pl.ds(pl.multiple_of(fg_at + i * 128, 128), 128)
        cos_rows, sin_rows = kept[rows, COS_LANES], kept[rows, SIN_LANES]

        def turn_back(part):
            return part * cos_rows - swapped(part) * sin_rows

        tiles = [kept[rows, pl.ds(j * 128, 128)] for j in range(5)]
        terms = two_terms(kept[rows, A_LANES])
        a_q, b_q = rank_grads(
            dq[rows, :],
            terms,
            range(RANK_Q),
            [both_halves(tiles[r // 2], r % 2) for r in range(RANK_Q)],
            spread,
        )
        for j in range(RANK_Q // 2):
            part = pick(b_q[2 * j], b_q[2 * j + 1]) * (1.0 / RANK_Q)
            fg[out, pl.ds(j * 128, 128)] = turn_back(part).astype(BF16)
        a_k, b_k = rank_grads(
            dkv_t[:, rows].T,
            terms,
            range(RANK_Q, RANK_Q + RANK_KV),
            [both_halves(tiles[3], r) for r in range(RANK_KV)],
            spread,
        )
        part = pick(b_k[0], b_k[1]) * (1.0 / RANK_KV)
        fg[out, pl.ds(384, 128)] = turn_back(part).astype(BF16)
        fg[out, A_LANES] = (a_q * (1.0 / RANK_Q) + a_k * (1.0 / RANK_KV)).astype(BF16)
        a_v, b_v = rank_grads(
            dkv_t[:, pl.ds(pl.multiple_of(512 + i * 128, 128), 128)].T,
            two_terms(kept[rows, V_LANES]),
            range(RANK_KV),
            [both_halves(tiles[4], r) for r in range(RANK_KV)],
            spread,
        )
        fg[out, pl.ds(512, 128)] = (pick(b_v[0], b_v[1]) * (1.0 / RANK_KV)).astype(BF16)
        fg[out, V_LANES] = (a_v * (1.0 / RANK_KV)).astype(BF16)
        return 0

    lax.fori_loop(first, last, tile, 0)


def whole_kernel(
    x_hbm, lengths, w_bq, w_bk, w_bv, w_aq, w_ak, w_av, gains_in, wo_in, wd_in, wg_in, wu_in, cot_in,
    outputs, input_grad, gate_out, up_out, down_out, out_shard, fac_shard,
    n1_kept, kept_kept, q_kept, k_kept, v_kept, mixed_kept, resid_kept, bias_kept, spread_kept,
    n2, cot, out_acc, ng_acc, out_twin, ng_twin,
    g_buf, u_buf, d_buf, g1, u1, da1, db1, g2, u2, da2, db2, g3, u3, d3,
    po, po_twin, po_1a, po_1b, po_2a, po_2b, po_3,
    pf, pf_twin, pf_1a, pf_1b, pf_2a, pf_2b, pf_3,
    gains, wd_own, fac_own,
    ss, rs, ls,
):
    x, z, y, c = place()
    x_peer, y_peer, twin = device(1 - x, z, y, c), device(x, z, 1 - y, c), device(x, z, y, 1 - c)
    z_peers = [3 - z, lax.rem(z + 2, 4), z + 1 - 2 * lax.rem(z, 2)]
    w = Wires(ss, rs, ls)
    a_rows, b_rows = pl.ds(0, 16), pl.ds(16, 16)
    a_down, b_down = pl.ds(0, DOWN_A), pl.ds(DOWN_A, DOWN_ROWS - DOWN_A)

    def same(view, to):
        return w.make(view, view, to)

    def own_copy(src, dst):
        w.held += 1
        return pltpu.make_async_copy(src, dst, ls.at[w.held - 1])

    def go(*copies):
        for copy in copies:
            w.go(copy)

    def ended(copies):
        for copy in copies:
            copy.wait_send()
        w.shared = [copy for copy in w.shared if all(copy is not other for other in copies)]

    class Whole:
        def __init__(self, src, ref, from_twin, one_a, one_b, two_a, two_b, three):
            self.ref, self.from_twin, self.one, self.two, self.three = (
                ref, from_twin, (one_a, one_b), (two_a, two_b), three,
            )
            slot = ref.at[x, z, y, c]
            self.own = own_copy(src, slot)
            self.z = [w.make(src, slot, device(x, zz, y, c)) for zz in z_peers]
            self.two_a = same(ref.at[x, :, y, c, a_rows], x_peer)
            self.two_b = same(ref.at[x, :, y, c, b_rows], y_peer)
            self.three_a = same(ref.at[:, :, y, c, a_rows], y_peer)
            self.three_b = same(ref.at[x, :, :, c, b_rows], x_peer)
            self.passed = [
                same(ref.at[x, :, y, c], twin),
                same(ref.at[1 - x, :, y, c, a_rows], twin),
                same(ref.at[x, :, 1 - y, c, b_rows], twin),
                same(ref.at[:, :, 1 - y, c, a_rows], twin),
                same(ref.at[1 - x, :, :, c, b_rows], twin),
            ]
            self.g_twin = w.make(ref.at[:, :, :, 1 - c], from_twin, twin)
            self.g_one_a = w.make(ref.at[:, :, 1 - y, c, a_rows], one_a, y_peer)
            self.g_one_b = w.make(ref.at[1 - x, :, :, c, b_rows], one_b, x_peer)
            self.g_two_a = w.make(ref.at[1 - x, :, y, c, a_rows], two_a, x_peer)
            self.g_two_b = w.make(ref.at[x, :, 1 - y, c, b_rows], two_b, y_peer)
            self.g_z = [
                w.make(ref.at[x, zz, y, c], three.at[step], device(x, zz, y, c))
                for step, zz in enumerate(z_peers)
            ]

        def start(self):
            self.own.start()
            go(*self.z)

        def step_two(self):
            self.own.wait()
            arrive(self.z)
            go(self.two_a, self.two_b, self.passed[0])

        def step_three_a(self):
            self.two_a.wait_recv()
            go(self.three_a, self.passed[1])

        def step_three_b(self):
            self.two_b.wait_recv()
            go(self.three_b, self.passed[2])

        def pass_a(self):
            self.three_a.wait_recv()
            go(self.passed[3])

        def pass_b(self):
            self.three_b.wait_recv()
            go(self.passed[4])

        def here(self):
            arrive(self.passed)

        def gathered(self):
            ended([*self.z, self.two_a, self.two_b, self.three_a, self.three_b, *self.passed])

        def sum_zero(self):
            go(self.g_twin)

        def sum_one(self):
            self.g_twin.wait_recv()

            def add(i, _):
                xx, zz, yy = lax.div(i, 8), lax.rem(lax.div(i, 2), 4), lax.rem(i, 2)
                add_low(self.ref.at[xx, zz, yy, c], self.from_twin.at[xx, zz, yy])
                return 0

            lax.fori_loop(0, 16, add, 0)
            go(self.g_one_a, self.g_one_b)

        def sum_two_a(self):
            self.g_one_a.wait_recv()

            def add(i, _):
                s, zz = lax.div(i, 4), lax.rem(i, 4)
                add_low(self.ref.at[s, zz, y, c, a_rows], self.one[0].at[s, zz])
                return 0

            lax.fori_loop(0, 8, add, 0)
            go(self.g_two_a)

        def sum_two_b(self):
            self.g_one_b.wait_recv()

            def add(i, _):
                zz, s = lax.div(i, 2), lax.rem(i, 2)
                add_low(self.ref.at[x, zz, s, c, b_rows], self.one[1].at[zz, s])
                return 0

            lax.fori_loop(0, 8, add, 0)
            go(self.g_two_b)

        def sum_three(self):
            arrive([self.g_two_a, self.g_two_b])

            def add(i, _):
                add_low(self.ref.at[x, i, y, c, a_rows], self.two[0].at[i])
                add_low(self.ref.at[x, i, y, c, b_rows], self.two[1].at[i])
                return 0

            lax.fori_loop(0, 4, add, 0)
            go(*self.g_z)

        def sum_end(self, out):
            arrive(self.g_z)
            out[...] = (
                self.ref[x, z, y, c].astype(F32)
                + self.three[0].astype(F32)
                + self.three[1].astype(F32)
                + self.three[2].astype(F32)
            )

    maps = Whole(fac_own, pf, pf_twin, pf_1a, pf_1b, pf_2a, pf_2b, pf_3)
    proj = Whole(wo_in, po, po_twin, po_1a, po_1b, po_2a, po_2b, po_3)
    both = (g_buf, u_buf)

    class Block:
        def __init__(self, b, gather_z_first):
            start, size = BLOCKS[b]
            self.cols = cols = pl.ds(start, size)
            mine = pl.ds(pl.multiple_of(c * HALF + start, 128), size)
            theirs = pl.ds(pl.multiple_of((1 - c) * HALF + start, 128), size)
            self.own, self.first = [], []
            for src, buf in ((wg_in, g_buf), (wu_in, u_buf)):
                slot = buf.at[x, z, y, c]
                self.own.append(own_copy(src.at[:, mine], slot.at[:, cols]))
                if gather_z_first:
                    for zz in z_peers:
                        self.first.append(w.make(src.at[:, mine], slot.at[:, cols], device(x, zz, y, c)))
                        self.first.append(w.make(src.at[:, theirs], slot.at[:, cols], device(x, zz, y, 1 - c)))
                else:
                    a_slot, b_slot = slot.at[a_rows, cols], slot.at[b_rows, cols]
                    self.first += [
                        w.make(src.at[a_rows, mine], a_slot, x_peer),
                        w.make(src.at[a_rows, theirs], a_slot, device(1 - x, z, y, 1 - c)),
                        w.make(src.at[b_rows, mine], b_slot, y_peer),
                        w.make(src.at[b_rows, theirs], b_slot, device(x, z, 1 - y, 1 - c)),
                    ]
                self.first.append(w.make(src.at[:, theirs], slot.at[:, cols], twin))
            if gather_z_first:
                self.second_a = [same(buf.at[x, :, y, :, a_rows, cols], x_peer) for buf in both]
                self.second_b = [same(buf.at[x, :, y, :, b_rows, cols], y_peer) for buf in both]
            else:
                self.second_a = [
                    same(buf.at[:, z, y, :, a_rows, cols], device(x, zz, y, c)) for buf in both for zz in z_peers
                ]
                self.second_b = [
                    same(buf.at[x, z, :, :, b_rows, cols], device(x, zz, y, c)) for buf in both for zz in z_peers
                ]
            self.third_a = [same(buf.at[:, :, y, :, a_rows, cols], y_peer) for buf in both]
            self.third_b = [same(buf.at[x, :, :, :, b_rows, cols], x_peer) for buf in both]
            self.one_u = w.make(u_buf.at[1 - x, :, :, :, :, cols], u1.at[:, :, :, :, cols], x_peer)
            self.one_g = w.make(g_buf.at[:, :, 1 - y, :, :, cols], g1.at[:, :, :, :, cols], y_peer)
            self.two_u = [
                w.make(u_buf.at[x, zz, :, :, :, cols], u2.at[step, :, :, :, cols], device(x, zz, y, c))
                for step, zz in enumerate(z_peers)
            ]
            self.two_g = [
                w.make(g_buf.at[:, zz, y, :, :, cols], g2.at[step, :, :, :, cols], device(x, zz, y, c))
                for step, zz in enumerate(z_peers)
            ]
            self.three_u = [
                w.make(u_buf.at[x, z, 1 - y, c, :, cols], u3.at[0, :, cols], y_peer),
                w.make(u_buf.at[x, z, 1 - y, 1 - c, :, cols], u3.at[2, :, cols], device(x, z, 1 - y, 1 - c)),
                w.make(u_buf.at[x, z, y, 1 - c, :, cols], u3.at[1, :, cols], twin),
            ]
            self.three_g = [
                w.make(g_buf.at[1 - x, z, y, c, :, cols], g3.at[0, :, cols], x_peer),
                w.make(g_buf.at[1 - x, z, y, 1 - c, :, cols], g3.at[2, :, cols], device(1 - x, z, y, 1 - c)),
                w.make(g_buf.at[x, z, y, 1 - c, :, cols], g3.at[1, :, cols], twin),
            ]

        def start(self):
            for copy in self.own:
                copy.start()
            go(*self.first)

        def second(self):
            for copy in self.own:
                copy.wait()
            arrive(self.first)
            go(*self.second_a, *self.second_b)

        def step_three_a(self):
            arrive(self.second_a)
            go(*self.third_a)

        def step_three_b(self):
            arrive(self.second_b)
            go(*self.third_b)

        def here(self):
            arrive(self.third_a)
            arrive(self.third_b)

        def gathered(self):
            ended([*self.second_a, *self.second_b, *self.third_a, *self.third_b])

        def sum_one(self):
            go(self.one_u, self.one_g)

        def sum_two_u(self):
            self.one_u.wait_recv()

            def add(i, _):
                zz, yy = lax.div(i, 2), lax.rem(i, 2)
                add_low(u_buf.at[x, zz, yy, :, :, self.cols], u1.at[zz, yy, :, :, self.cols])
                return 0

            lax.fori_loop(0, 8, add, 0)
            go(*self.two_u)

        def sum_two_g(self):
            self.one_g.wait_recv()

            def add(i, _):
                xx, zz = lax.div(i, 4), lax.rem(i, 4)
                add_low(g_buf.at[xx, zz, y, :, :, self.cols], g1.at[xx, zz, :, :, self.cols])
                return 0

            lax.fori_loop(0, 8, add, 0)
            go(*self.two_g)

        def sum_three_u(self):
            arrive(self.two_u)
            cols = self.cols

            def add(i, _):
                add_three(u_buf.at[x, z, i, :, :, cols], [u2.at[k, i, :, :, cols] for k in range(3)])
                return 0

            lax.fori_loop(0, 2, add, 0)
            go(*self.three_u)

        def sum_three_g(self):
            arrive(self.two_g)
            cols = self.cols

            def add(i, _):
                add_three(g_buf.at[i, z, y, :, :, cols], [g2.at[k, i, :, :, cols] for k in range(3)])
                return 0

            lax.fori_loop(0, 2, add, 0)
            go(*self.three_g)

        def sum_end(self, gate_sum, up_sum):
            arrive(self.three_u)
            arrive(self.three_g)
            cols = self.cols
            for buf, three, out in ((g_buf, g3, gate_sum), (u_buf, u3, up_sum)):
                out[c, :, cols] = buf[x, z, y, c, :, cols].astype(F32) + three[0, :, cols].astype(F32)
                out[1 - c, :, cols] = three[1, :, cols].astype(F32) + three[2, :, cols].astype(F32)

    def add_three(dst, three):
        total = dst[...].astype(F32)
        for src in three:
            total += src[...].astype(F32)
        dst[...] = total.astype(BF16)

    blocks = [Block(0, True), Block(1, False), Block(2, False), Block(3, False)]

    other_core = device(1 - x, z, y, 1 - c)
    d_swap = w.make(wd_own, d_buf.at[z, y, 1 - x], other_core)
    d_keep = own_copy(wd_own, d_buf.at[z, y, x])
    slot = d_buf.at[z, y, x]
    d_z_a = [same(slot.at[a_down], device(x, zz, y, c)) for zz in z_peers]
    d_z_b = [same(slot.at[b_down], device(x, zz, y, c)) for zz in z_peers]
    d_two_a, d_two_b = same(d_buf.at[:, y, x, a_down], x_peer), same(d_buf.at[:, y, x, b_down], y_peer)
    d_three_a, d_three_b = same(d_buf.at[:, y, :, a_down], y_peer), same(d_buf.at[:, :, x, b_down], x_peer)
    d_one_ga = w.make(d_buf.at[:, 1 - y, :, a_down], da1, y_peer)
    d_one_gb = w.make(d_buf.at[:, :, 1 - x, b_down], db1, x_peer)
    d_two_ga = w.make(d_buf.at[:, y, 1 - x, a_down], da2, x_peer)
    d_two_gb = w.make(d_buf.at[:, 1 - y, x, b_down], db2, y_peer)
    d_z_g = [w.make(d_buf.at[zz, y, x], d3.at[step], device(x, zz, y, c)) for step, zz in enumerate(z_peers)]

    def either(kept, swapped, verb):
        @pl.when(x == c)
        def _():
            getattr(kept, verb)()

        @pl.when(x != c)
        def _():
            getattr(swapped, verb)()

    def down_second():
        either(d_keep, d_swap, "wait")
        go(*d_z_a, *d_z_b)

    def down_two_a():
        arrive(d_z_a)
        go(d_two_a)

    def down_two_b():
        arrive(d_z_b)
        go(d_two_b)

    def down_three_a():
        d_two_a.wait_recv()
        go(d_three_a)

    def down_three_b():
        d_two_b.wait_recv()
        go(d_three_b)

    def down_sum_two_a():
        d_one_ga.wait_recv()

        def add(i, _):
            zz, s = lax.div(i, 2), lax.rem(i, 2)
            add_low(d_buf.at[zz, y, s, a_down], da1.at[zz, s])
            return 0

        lax.fori_loop(0, 8, add, 0)
        go(d_two_ga)

    def down_sum_two_b():
        d_one_gb.wait_recv()

        def add(i, _):
            zz, s = lax.div(i, 2), lax.rem(i, 2)
            add_low(d_buf.at[zz, s, x, b_down], db1.at[zz, s])
            return 0

        lax.fori_loop(0, 8, add, 0)
        go(d_two_gb)

    def down_sum_three():
        arrive([d_two_ga, d_two_gb])

        def add(i, _):
            add_low(d_buf.at[i, y, x, a_down], da2.at[i])
            add_low(d_buf.at[i, y, x, b_down], db2.at[i])
            return 0

        lax.fori_loop(0, 4, add, 0)
        go(*d_z_g)

    n2_twin = w.make(n2.at[0:512], n2.at[512:1024], twin)
    cot_twin = w.make(cot_in, cot.at[512:1024], twin)
    ng_send = w.make(ng_acc.at[512:1024], ng_twin, twin)
    out_send = w.make(out_acc.at[512:1024], out_twin, twin)
    own_cot = own_copy(cot_in, cot.at[0:512])

    def front(x_in, n1, kept, q, k, v, mixed, resid, bias, spread):
        cos_ref, sin_ref = kept.at[:, COS_LANES], kept.at[:, SIN_LANES]
        x_load = w.local(x_hbm, x_in)
        own_cot.start()
        for ref, at in ((w_bq, 0), (w_bk, 384), (w_bv, 512)):
            fac_own[:, at : at + ref.shape[1]] = ref[...]
        heads_tile = jnp.concatenate([w_aq[...].astype(F32), w_ak[...].astype(F32)], axis=1)
        fac_own[:, A_LANES] = heads_tile.astype(BF16)
        tile = jnp.concatenate([w_av[...].astype(F32), jnp.zeros((32, 96), F32)], axis=1)
        for row in (0, 1):
            gain = jnp.where(row_iota(32, 32) == lane_iota(32, 32), gains_in[row : row + 1, :].astype(F32), 0.0)
            gain = jnp.sum(gain, axis=1, keepdims=True)
            tile = jnp.where(lane_iota(32) == 32 + row, gain, tile)
        fac_own[:, V_LANES] = tile.astype(BF16)
        rows = wd_in[...].astype(F32)
        rows = jnp.concatenate([rows[:, 0:512], rows[:, 512:1024]], axis=0)
        wd_own[...] = rows.astype(BF16)
        pl.semaphore_wait(pltpu.get_barrier_semaphore(), partners)
        maps.start()
        blocks[0].start()
        proj.start()
        either(d_keep, d_swap, "start")
        for block in blocks[1:]:
            block.start()
        make_tables(lengths, cos_ref, sin_ref)
        make_spread(spread)
        make_bias(lengths, bias)
        down_second()
        blocks[1].second()
        maps.step_two()
        blocks[2].second()
        blocks[3].second()
        maps.step_three_a()
        maps.step_three_b()
        blocks[0].second()
        go(cot_twin)
        maps.pass_a()
        maps.pass_b()
        proj.step_two()
        x_load.wait()
        maps.here()
        gain_rows(pf, gains)
        make_factors(x_in, gains, pf, n1, kept, 0, 1)
        blocks[0].step_three_a()
        blocks[0].step_three_b()
        make_factors(x_in, gains, pf, n1, kept, 1, 2)
        saves = [w.local(n1, n1_kept)]
        proj.step_three_b()
        proj.step_three_a()
        make_heads(kept, cos_ref, sin_ref, spread, q, k, v, 0, 2)
        down_two_a()
        make_heads(kept, cos_ref, sin_ref, spread, q, k, v, 2, 4)
        for src, dst in (
            (kept, kept_kept),
            (q, q_kept),
            (k, k_kept),
            (v, v_kept),
            (bias, bias_kept),
            (spread, spread_kept),
        ):
            saves.append(w.local(src, dst))
        attend_pairs(q, k, v, bias, mixed, 0, 3)
        down_two_b()
        attend_pairs(q, k, v, bias, mixed, 3, 4)
        proj.pass_a()
        proj.pass_b()
        attend_pairs(q, k, v, bias, mixed, 4, 8)
        down_three_a()
        saves.append(w.local(mixed, mixed_kept))
        proj.here()
        make_resid(x_in, mixed, po, gains, resid, n2, 0, 1)
        down_three_b()
        blocks[1].step_three_a()
        make_resid(x_in, mixed, po, gains, resid, n2, 1, 2)
        saves.append(w.local(resid, resid_kept))
        go(n2_twin)
        for copy in saves:
            copy.wait()

    def feed_forward(n2_t, wd, hid, gg, ug, d_acc):
        own_cot.wait()

        def turn(i):
            rows = pl.ds(i * TILE, TILE)
            n2_t[:, rows] = n2[rows, :].T

        def forward(b, low, high):
            start, size = BLOCKS[b]
            cols = pl.ds(start, size)

            def tile(i, _):
                rows = pl.ds(pl.multiple_of(i * TILE, TILE), TILE)
                n2_rows, cot_rows = n2[rows, :], cot[rows, :]
                wg = g_buf[:, :, :, :, :, cols].reshape(1024, size)
                wu = u_buf[:, :, :, :, :, cols].reshape(1024, size)
                gate = dot(n2_rows, wg)
                up = dot(n2_rows, wu)
                hid_grad = dot(cot_rows, wd[cols, :], NT)
                sig = jax.nn.sigmoid(gate)
                silu = gate * sig
                hidden = (silu * up).astype(BF16)
                gate_grad = (hid_grad * up * sig * (1.0 + gate * (1.0 - sig))).astype(BF16)
                up_grad = (hid_grad * silu).astype(BF16)
                hid[rows, 0:size] = hidden
                gg[rows, 0:size] = gate_grad
                ug[rows, 0:size] = up_grad
                out_part = dot(hidden, wd[cols, :])
                ng_part = dot(gate_grad, wg, NT) + dot(up_grad, wu, NT)
                if b == 0:
                    out_acc[rows, :] = out_part
                    ng_acc[rows, :] = ng_part
                else:
                    out_acc[rows, :] += out_part
                    ng_acc[rows, :] += ng_part
                return 0

            lax.fori_loop(low, high, tile, 0)

        def column_grads(b):
            blocks[b].gathered()
            start, size = BLOCKS[b]
            cols = pl.ds(start, size)

            def side(i, _):
                rows = pl.ds(pl.multiple_of(i * 512, 512), 512)
                part = dot(n2_t[rows, :], ug[:, 0:size])
                u_buf[i, :, :, :, :, cols] = part.astype(BF16).reshape(4, 2, 2, 32, size)
                part = dot(n2_t[rows, :], gg[:, 0:size])
                g_buf[i, :, :, :, :, cols] = part.astype(BF16).reshape(4, 2, 2, 32, size)
                return 0

            lax.fori_loop(0, 2, side, 0)

        def row_grads(b):
            start, size = BLOCKS[b]
            d_acc[pl.ds(start, size), :] = dot(hid[:, 0:size], cot[...], TN)

        turn(0)
        turn(1)
        arrive([n2_twin, cot_twin])
        turn(2)
        turn(3)
        blocks[1].step_three_b()

        def gather_rows(at, skip, lanes):
            def slot_rows(s, _):
                rows = d_buf[lax.div(s, 4), lax.rem(lax.div(s, 2), 2), lax.rem(s, 2), at : at + DOWN_A]
                rows = rows.astype(F32)[skip : skip + OWN_UNITS]
                d_acc[pl.ds(pl.multiple_of(s * OWN_UNITS, 8), OWN_UNITS), lanes] = rows
                return 0

            lax.fori_loop(0, 16, slot_rows, 0)

            def low_rows(i, _):
                rows = pl.ds(pl.multiple_of(i * 128, 128), 128)
                wd[rows, lanes] = d_acc[rows, lanes].astype(BF16)
                return 0

            lax.fori_loop(0, HALF // 128, low_rows, 0)

        d_three_a.wait_recv()
        gather_rows(0, 0, pl.ds(0, 512))
        d_three_b.wait_recv()
        gather_rows(DOWN_ROWS - DOWN_A, OWN_UNITS - (DOWN_ROWS - DOWN_A), pl.ds(512, 512))
        blocks[2].step_three_a()
        blocks[0].here()
        forward(0, 0, 4)
        column_grads(0)
        blocks[0].sum_one()
        row_grads(0)
        blocks[2].step_three_b()
        blocks[1].here()
        forward(1, 0, 4)
        blocks[0].sum_two_u()
        blocks[3].step_three_a()
        column_grads(1)
        row_grads(1)
        blocks[0].sum_two_g()
        blocks[3].step_three_b()
        blocks[1].sum_one()
        blocks[2].here()
        forward(2, 0, 2)
        blocks[0].sum_three_u()
        forward(2, 2, 4)
        column_grads(2)
        row_grads(2)
        blocks[0].sum_three_g()
        blocks[2].sum_one()
        blocks[3].here()
        forward(3, 2, 4)
        go(ng_send, out_send)
        forward(3, 0, 2)
        row_grads(3)
        blocks[1].sum_two_g()
        ended([*d_z_a, *d_z_b, d_two_a, d_two_b, d_three_a, d_three_b])

        def spread_rows(s, _):
            rows = d_acc[pl.ds(pl.multiple_of(s * OWN_UNITS, 8), OWN_UNITS), :]
            rows = jnp.concatenate([rows[:, 0:512], rows[:, 512:1024]], axis=0)
            d_buf[lax.div(s, 4), lax.rem(lax.div(s, 2), 2), lax.rem(s, 2)] = rows.astype(BF16)
            return 0

        lax.fori_loop(0, 16, spread_rows, 0)
        go(d_one_ga, d_one_gb)
        column_grads(3)
        blocks[1].sum_two_u()
        blocks[3].sum_one()

    branch, mg = cot.at[0:512], cot.at[512:1024]

    def attention(
        resid, x_in, mixed, q, k, v, bias, kept, spread, n1, q_t, mg_t, gain_two,
        gate_sum, up_sum, d_sum,
    ):
        d_back = w.make(d_sum, down_out, other_core)
        d_stay = own_copy(d_sum, down_out)
        loads = [
            w.local(src, dst)
            for src, dst in (
                (resid_kept, resid),
                (mixed_kept, mixed),
                (q_kept, q),
                (k_kept, k),
                (v_kept, v),
                (bias_kept, bias),
                (kept_kept, kept),
                (spread_kept, spread),
                (n1_kept, n1),
                (x_hbm, x_in),
            )
        ]
        loads[0].wait()
        arrive([ng_send, out_send])

        def close(i, total):
            rows = pl.ds(pl.multiple_of(i * 128, 128), 128)
            base = resid[rows, :]
            n2[rows, :] = (base + out_acc[rows, :] + out_twin[rows, :]).astype(BF16)
            grad = ng_acc[rows, :] + ng_twin[rows, :]
            scale = lax.rsqrt(jnp.mean(base * base, axis=-1, keepdims=True) + EPSILON)
            unit = base * scale
            unit_grad = grad * gains[1:2, :]
            back = scale * (unit_grad - unit * jnp.mean(unit_grad * unit, axis=-1, keepdims=True))
            full = cot[rows, :].astype(F32) + back
            out_acc[rows, :] = full
            branch[rows, :] = full.astype(BF16)
            return total + jnp.sum((grad * unit).reshape(16, 8, 1024), axis=0)

        ended([n2_twin])
        gain_two[...] = lax.fori_loop(0, 4, close, jnp.zeros((8, 1024), F32))
        blocks[2].sum_two_g()
        results = [w.local(n2.at[0:512], outputs)]
        for copy in loads[1:3]:
            copy.wait()
        for i in range(2):
            rows = pl.ds(i * 256, 256)
            part = dot(branch[rows, :], po[...].reshape(1024, 1024), NT).astype(BF16)
            mg[rows, :] = part
            mg_t[:, rows] = part.T
            q_t[:, rows] = q[rows, :].T
        blocks[2].sum_two_u()
        blocks[1].sum_three_g()
        proj.gathered()
        for side in range(2):
            part = dot(mixed[:, side * 512 : (side + 1) * 512], branch[...], TN)
            po[side] = part.astype(BF16).reshape(4, 2, 2, 32, 1024)
        proj.sum_zero()
        for copy in loads[3:6]:
            copy.wait()
        ended([ng_send])
        heads = (q, q_t, k, v, mg, mg_t, bias, out_twin, ng_acc)
        head_grads(*heads, 0, 2)
        proj.sum_one()
        head_grads(*heads, 2, 4)
        blocks[1].sum_three_u()
        down_sum_two_a()
        head_grads(*heads, 4, 5)
        down_sum_two_b()
        head_grads(*heads, 5, 6)
        blocks[3].sum_two_g()
        head_grads(*heads, 6, 7)
        blocks[2].sum_three_g()
        blocks[3].sum_two_u()
        head_grads(*heads, 7, 8)
        proj.sum_two_a()
        for copy in loads[6:]:
            copy.wait()
        results[0].wait()
        factor_grads(out_twin, ng_acc, kept, spread, n2, 512, 0, 1)
        proj.sum_two_b()
        factor_grads(out_twin, ng_acc, kept, spread, n2, 512, 1, 2)
        blocks[2].sum_three_u()
        factor_grads(out_twin, ng_acc, kept, spread, n2, 512, 2, 4)
        down_sum_three()
        blocks[3].sum_three_g()
        fg = n2.at[512:1024, 0:FACTOR_PAD]
        incoming = out_twin
        for i in range(2):
            rows = pl.ds(i * 256, 256)
            incoming[rows, :] = dot(fg[rows, :], pf[...].reshape(1024, FACTOR_PAD), NT)
        gain_tile = jnp.where(
            row_iota(128, 1024) == 33, jnp.sum(gain_two[...], axis=0, keepdims=True), 0.0
        ).T
        maps.gathered()
        for side in range(2):
            part = dot(n1[:, side * 512 : (side + 1) * 512], fg[...], TN)
            part = jnp.concatenate(
                [part[:, 0:768], part[:, 768:896] + gain_tile[side * 512 : (side + 1) * 512]], axis=1
            )
            pf[side] = part.astype(BF16).reshape(4, 2, 2, 32, FACTOR_PAD)
        maps.sum_zero()
        proj.sum_three()
        blocks[3].sum_three_u()

        def first_norm(i, _):
            rows = pl.ds(pl.multiple_of(i * 128, 128), 128)
            vals = x_in[rows, :].astype(F32)
            scale = lax.rsqrt(jnp.mean(vals * vals, axis=-1, keepdims=True) + EPSILON)
            unit = vals * scale
            unit_grad = incoming[rows, :] * gains[0:1, :]
            back = scale * (unit_grad - unit * jnp.mean(unit_grad * unit, axis=-1, keepdims=True))
            out_acc[rows, :] += back
            return 0

        lax.fori_loop(0, 4, first_norm, 0)
        maps.sum_one()
        results.append(w.local(out_acc.at[0:512], input_grad))
        for block in blocks:
            block.sum_end(gate_sum, up_sum)
        maps.sum_two_a()
        maps.sum_two_b()
        results += [w.local(up_sum, up_out), w.local(gate_sum, gate_out)]
        arrive(d_z_g)
        d_sum[...] = (
            d_buf[z, y, x].astype(F32)
            + d3[0].astype(F32)
            + d3[1].astype(F32)
            + d3[2].astype(F32)
        )
        either(d_stay, d_back, "start")
        maps.sum_three()
        shard = out_twin.at[0:32, :]
        proj.sum_end(shard)
        results.append(w.local(shard, out_shard))
        shard = out_twin.at[32:64, 0:FACTOR_PAD]
        maps.sum_end(shard)
        own_maps, lanes = fac_own[...].astype(F32), lane_iota(32, FACTOR_PAD)
        total = jnp.sum(jnp.where(lanes < 800, own_maps * shard[...], 0.0), axis=-1, keepdims=True)
        gain = jnp.sum(jnp.where(lanes == 800, own_maps, 0.0), axis=-1, keepdims=True)
        tile_ref = out_twin.at[32:64, V_LANES]
        tile_ref[...] = jnp.where(lane_iota(32) == 32, total / gain, tile_ref[...])
        results.append(w.local(shard, fac_shard))
        either(d_stay, d_back, "wait")
        for copy in results[1:]:
            copy.wait()
        w.drain_shared()

    vmem = pltpu.VMEM
    row, turned = vmem((512, 1024), BF16), vmem((1024, 512), BF16)
    wide_row, bias_like = vmem((512, 1024), F32), vmem((512, 512), F32)
    kept_like, spread_like = vmem((512, KEPT), F32), vmem((8, 128, 1024), BF16)
    partners = greet(x, z, y, c)
    pl.run_scoped(front, row, row, kept_like, row, row, row, row, wide_row, bias_like, spread_like)
    pl.run_scoped(
        feed_forward,
        vmem((1024, 1024), BF16), vmem((HALF, 1024), BF16), turned, turned, turned, vmem((HALF, 1024), F32),
    )
    pl.run_scoped(
        attention,
        wide_row, row, row, row, row, row, bias_like, kept_like, spread_like, row, turned, turned,
        vmem((8, 1024), F32), vmem((2, 32, HALF), F32), vmem((2, 32, HALF), F32), vmem((DOWN_ROWS, 512), F32),
    )


def whole_all(*args):
    anywhere, vmem = pl.BlockSpec(memory_space=pl.ANY), pl.BlockSpec(memory_space=pltpu.VMEM)
    big = lambda *shape: pltpu.VMEM(shape, BF16)
    wide = lambda *shape: pltpu.VMEM(shape, F32)
    down_b = DOWN_ROWS - DOWN_A

    def full_scratch(width):
        return [
            big(2, 4, 2, 2, 32, width), big(2, 4, 2, 32, width),
            big(2, 4, 16, width), big(4, 2, 16, width), big(4, 16, width), big(4, 16, width),
            big(3, 32, width),
        ]

    row = (512, 1024)
    outs = [
        (row, BF16),
        (row, F32),
        ((2, 32, HALF), F32),
        ((2, 32, HALF), F32),
        ((DOWN_ROWS, 512), F32),
        ((32, 1024), F32),
        ((32, FACTOR_PAD), F32),
        (row, BF16),
        ((512, KEPT), F32),
        (row, BF16),
        (row, BF16),
        (row, BF16),
        (row, BF16),
        (row, F32),
        ((512, 512), F32),
        ((8, 128, 1024), BF16),
    ]
    return pl.pallas_call(
        whole_kernel,
        out_shape=[jax.ShapeDtypeStruct(*o) for o in outs],
        in_specs=[anywhere, pl.BlockSpec(memory_space=pltpu.SMEM)]
        + [vmem] * 7
        + [anywhere, vmem]
        + [anywhere] * 3,
        out_specs=[anywhere] * len(outs),
        scratch_shapes=[
            big(1024, 1024), big(1024, 1024),
            wide(1024, 1024), wide(1024, 1024), wide(512, 1024), wide(512, 1024),
            big(2, 4, 2, 2, 32, HALF), big(2, 4, 2, 2, 32, HALF), big(4, 2, 2, DOWN_ROWS, 512),
            big(2, 4, 2, 32, HALF), big(4, 2, 2, 32, HALF), big(4, 2, DOWN_A, 512), big(4, 2, down_b, 512),
            big(3, 2, 2, 32, HALF), big(3, 2, 2, 32, HALF),
            big(4, DOWN_A, 512), big(4, down_b, 512),
            big(3, 32, HALF), big(3, 32, HALF),
            big(3, DOWN_ROWS, 512),
            *full_scratch(1024),
            *full_scratch(FACTOR_PAD),
            wide(8, 1024), big(DOWN_ROWS, 512), big(32, FACTOR_PAD),
            pltpu.SemaphoreType.DMA((280,)),
            pltpu.SemaphoreType.DMA((280,)),
            pltpu.SemaphoreType.DMA((64,)),
        ],
        compiler_params=pltpu.CompilerParams(
            collective_id=0, has_side_effects=True, vmem_limit_bytes=62 * MIB
        ),
        name="whole_all",
    )(*args)[:7]


def cut_kernel(big_out, big_grad, *refs):
    smalls, outs, (held_out, held_grad, fac, out_in, gate, up, down, sems) = refs[:5], refs[5:-8], refs[-8:]
    loads, stores = [], []
    for part in range(4):
        rows = pl.ds(part * 128, 128)
        for src, held, dst in ((big_grad, held_grad, outs[1]), (big_out, held_out, outs[0])):
            at = len(loads)
            loads.append(pltpu.make_async_copy(src.at[rows], held.at[rows], sems.at[0, at]))
            stores.append(pltpu.make_async_copy(held.at[rows], dst.at[rows], sems.at[1, at]))
    first = [
        pltpu.make_async_copy(src, dst, sems.at[2, at])
        for at, (src, dst) in enumerate(zip(smalls, (fac, out_in, gate, up, down), strict=True))
    ]
    for copy in (*loads[:4], *first, *loads[4:]):
        copy.start()
    for load, store in zip(loads[:4], stores[:4], strict=True):
        load.wait()
        store.start()
    for copy in first:
        copy.wait()
    for load, store in zip(loads[4:], stores[4:], strict=True):
        load.wait()
        store.start()
    pieces = (640, 96), (0, 384), (736, 32), (384, 128), (768, 32), (512, 128)
    for (start, size), ref in zip(pieces, outs[2:8], strict=True):
        ref[...] = fac[:, start : start + size]
    outs[8][...] = out_in[...]
    for src, ref in ((gate, outs[9]), (up, outs[10])):
        ref[:, 0:HALF] = src[0]
        ref[:, HALF:FF] = src[1]
    outs[11][:, 0:512] = down[0:OWN_UNITS, :]
    outs[11][:, 512:1024] = down[OWN_UNITS:DOWN_ROWS, :]
    tile = jnp.concatenate([fac[:, 768:896], jnp.zeros((96, 128), F32)], axis=0).T
    outs[12][...] = tile[32:33, 0:32]
    outs[13][...] = tile[33:34, 0:32]
    for copy in stores:
        copy.wait()


def cut_all(*args):
    shapes = [(32, n) for n in (96, 384, 32, 128, 32, 128, 1024, FF, FF)] + [(OWN_UNITS, 1024), (1, 32), (1, 32)]
    anywhere, vmem = pl.BlockSpec(memory_space=pl.ANY), pl.BlockSpec(memory_space=pltpu.VMEM)
    wide = lambda *shape: pltpu.VMEM(shape, F32)
    return pl.pallas_call(
        cut_kernel,
        out_shape=[jax.ShapeDtypeStruct((512, 1024), BF16), jax.ShapeDtypeStruct((512, 1024), F32)]
        + [jax.ShapeDtypeStruct(s, F32) for s in shapes],
        in_specs=[anywhere] * 7,
        out_specs=[anywhere] * 2 + [vmem] * len(shapes),
        scratch_shapes=[
            pltpu.VMEM((512, 1024), BF16), wide(512, 1024), wide(32, FACTOR_PAD), wide(32, 1024),
            wide(2, 32, HALF), wide(2, 32, HALF), wide(DOWN_ROWS, 512),
            pltpu.SemaphoreType.DMA((3, 8)),
        ],
        compiler_params=pltpu.CompilerParams(vmem_limit_bytes=61 * MIB),
        name="cut_all",
    )(*args)


def local_paired(
    inputs, doc_lengths, w_aq, w_bq, w_ak, w_bk, w_av, w_bv,
    w_out, w_gate, w_up, w_down, gain_attn, gain_ffn, cotangent,
):
    outputs, input_grad, gate_sum, up_sum, down_sum, out_sum, fac_sum = whole_all(
        inputs, doc_lengths, w_bq, w_bk, w_bv, w_aq, w_ak, w_av, jnp.stack([gain_attn, gain_ffn]),
        w_out, w_down, w_gate, w_up, cotangent,
    )
    *cut, gain_one, gain_two = cut_all(
        outputs, input_grad, fac_sum, out_sum, gate_sum, up_sum, down_sum
    )
    return (*cut, gain_one[0], gain_two[0])


def solution(mesh):
    return jax.shard_map(
        local_paired if fits_pairs(mesh) else local,
        mesh=mesh,
        in_specs=(
            P(("dp", "fsdp"), None),
            P(("dp", "fsdp"), None),
            P(("dp", "fsdp"), None),
            P(("dp", "fsdp"), None),
            P(("dp", "fsdp"), None),
            P(("dp", "fsdp"), None),
            P(("dp", "fsdp"), None),
            P(("dp", "fsdp"), None),
            P(("dp", "fsdp"), None),
            P(("dp", "fsdp"), None),
            P(("dp", "fsdp"), None),
            P(("dp", "fsdp"), None),
            P(("dp", "fsdp")),
            P(("dp", "fsdp")),
            P(("dp", "fsdp"), None),
        ),
        out_specs=(
            P(("dp", "fsdp"), None),
            P(("dp", "fsdp"), None),
            P(("dp", "fsdp"), None),
            P(("dp", "fsdp"), None),
            P(("dp", "fsdp"), None),
            P(("dp", "fsdp"), None),
            P(("dp", "fsdp"), None),
            P(("dp", "fsdp"), None),
            P(("dp", "fsdp"), None),
            P(("dp", "fsdp"), None),
            P(("dp", "fsdp"), None),
            P(("dp", "fsdp"), None),
            P(("dp", "fsdp")),
            P(("dp", "fsdp")),
        ),
        check_vma=False,
    )
```
